32 devices in a mesh: dp: 32 (over z, y, x, core).
Axes of the slice: x: 2, y: 2, z: 4, core: 2. Of those that a mesh axis runs over, the one named last changes fastest.
Arguments:
- inputs: bfloat16 [2, 32, 64, 1152], P(None, 'dp'), may hold values from -32 to 32
- segment_ids: int32 [2, 32, 64], P(None, 'dp'), may hold values from 0 to 3, never falling along the last dimension, each value on 1 to 32 neighbouring positions
- valid_mask: int32 [2, 32, 64], P(None, 'dp'), may hold values from 0 to 1, as said below
- attn_in: bfloat16 [1536, 1152], P('dp'), may hold values from -0.1875 to 0.1875
- attn_out: bfloat16 [1024, 1152], P('dp'), may hold values from -0.1875 to 0.1875
- ffw_in: bfloat16 [13824, 1152], P('dp'), may hold values from -0.1875 to 0.1875
- ffw_out: bfloat16 [6912, 1152], P('dp'), may hold values from -0.078125 to 0.078125
- norm_gains: float32 [4, 1152], replicated, may hold values from 0.1 to 1.9
- head_gains: float32 [2, 256], replicated, may hold values from 0.1 to 1.9
- cotangent: bfloat16 [2, 32, 64, 1152], P(None, 'dp'), may hold values from -32 to 32
Outputs:
- layer_out: bfloat16 [2, 32, 64, 1152], P(None, 'dp')
- input_grad: float32 [2, 32, 64, 1152], P(None, 'dp')
- attn_in_grad: float32 [1536, 1152], P('dp')
- attn_out_grad: float32 [1024, 1152], P('dp')
- ffw_in_grad: float32 [13824, 1152], P('dp')
- ffw_out_grad: float32 [6912, 1152], P('dp')
- norm_grad: float32 [4, 1152], replicated
- head_grad: float32 [2, 256], replicated
- rms_values: float32 [4], replicated
The draws below stay inside these ranges and needn't reach their ends.
Inputs may be any that keep to these rules, and one draw needn't show every extreme that they name: `segment_ids`: within a sequence the numbers never fall; each of the 4 documents holds 1 to 32 tokens. `valid_mask`: in each sequence the first tokens, 32 of them or more, are 1 and the rest 0.
All inputs are finite; a program needn't handle non-finite values.
Results may differ from the reference program's by a relative error of at most 0.015.
Values may be sent and summed in bfloat16 or wider, within the bound.
A program may use at most 320 MiB of HBM per device.

```python
import math
import jax
import jax.numpy as jnp
import numpy as np
from jax import lax

D = 1152
HEADS = 4
HD = 256
FF = 6912
LEN = 64
MICRO = 2
DOCS = 4
SEQS = 32
ATT = 1024
QKV = 1536


def draw_inputs(key, part):
    key = jax.random.fold_in(key, 11)
    first, second = jax.random.split(key)
    shape = (MICRO, SEQS, LEN, D)
    rising = jnp.arange(SEQS, dtype=jnp.float32) / max(SEQS - 1, 1)
    noise = jnp.clip(jax.random.normal(first, shape, jnp.float32), -4.0, 4.0)
    scale = 0.5 + rising
    rough = jnp.exp(0.35 * jnp.clip(jax.random.normal(second, (MICRO, SEQS, LEN, 1), jnp.float32), -3.0, 3.0))
    return (noise * scale[None, :, None, None] * rough).astype(jnp.bfloat16)


def draw_cotangent(key, part):
    key = jax.random.fold_in(key, 12)
    first, second = jax.random.split(key)
    shape = (MICRO, SEQS, LEN, D)
    rising = jnp.arange(SEQS, dtype=jnp.float32) / max(SEQS - 1, 1)
    noise = jnp.clip(jax.random.normal(first, shape, jnp.float32), -4.0, 4.0)
    scale = 0.5 + rising
    rough = jnp.exp(0.35 * jnp.clip(jax.random.normal(second, (MICRO, SEQS, LEN, 1), jnp.float32), -3.0, 3.0))
    return (noise * scale[None, :, None, None] * rough).astype(jnp.bfloat16)


def draw_valid_mask(key, part):
    key = jax.random.fold_in(key, 13)
    counts = jax.random.randint(key, (MICRO, SEQS, 1), LEN // 2, LEN + 1)
    counts = counts.at[0, 0, 0].set(LEN // 2)
    places = jnp.arange(LEN, dtype=jnp.int32)
    return (places[None, None, :] < counts).astype(jnp.int32)


def levels(own_key, extent, shards, least, high):
    loudness = 1.0
    for dim, blocks in shards:
        steps = jax.random.uniform(jax.random.fold_in(jax.random.fold_in(own_key, 6), dim), (blocks,), jnp.float32, least / len(shards), high / len(shards))
        loudness = loudness * jnp.repeat(jnp.exp(steps), extent[dim] // blocks).reshape((-1,) + (1,) * (len(extent) - 1 - dim))
    return loudness


def length_profile(number_of, total, most, skew):
    weights = [(1 << 20) // math.isqrt(rank ** skew) + 1 for rank in range(2, number_of + 1)]
    surplus, holding = total - most - (number_of - 1), [1] * (number_of - 1)
    while surplus > 0:
        free = [i for i in range(number_of - 1) if holding[i] < most]
        mass, budget = sum([weights[i] for i in free]), surplus
        for i in free:
            extra = min(most - holding[i], max(1, budget * weights[i] // mass), surplus)
            holding[i] = holding[i] + extra
            surplus = surplus - extra
    return np.array([most] + holding)


def uneven(key, number_of, total, bound, slope):
    if number_of == 2:
        one = jax.random.randint(key, (), max(1, total - bound), min(bound, total - 1) + 1)
        return jnp.stack([one, total - one])
    sizes = jnp.asarray(length_profile(number_of, total, bound, slope), jnp.int32)
    pairs = (number_of - 1) // 2
    giver, receiver = sizes[1:1 + 2 * pairs:2], sizes[2:2 + 2 * pairs:2]
    margin = jnp.minimum(giver - 1, bound - receiver)
    shifted = jax.random.randint(jax.random.fold_in(key, 1), (pairs,), 0, 1 << 20) % (margin + 1)
    sizes = sizes.at[1:1 + 2 * pairs:2].set(giver - shifted).at[2:2 + 2 * pairs:2].set(receiver + shifted)
    return sizes[jax.random.permutation(jax.random.fold_in(key, 2), number_of)]


def centred(own_key, extent, deviation, limit, pieces=(), kind=jnp.bfloat16):
    loudness = levels(own_key, extent, pieces, -0.22, 0.18) if pieces else 1.0
    drawn = jax.random.normal(own_key, extent, jnp.float32) * deviation * loudness
    return jnp.minimum(jnp.maximum(drawn, -limit), limit).astype(kind)


def setup_inputs(seed: int = 0) -> dict:
    key_of = jax.random.split(jax.random.key(seed), 11)
    inputs = draw_inputs(jax.random.fold_in(key_of[10], 71), 0)
    segment_ids = jax.vmap(lambda own: jnp.searchsorted(jnp.cumsum(uneven(own, DOCS, LEN, LEN // 2, 0)), jnp.arange(LEN), side="right"))(jax.random.split(key_of[1], MICRO * SEQS)).reshape((MICRO, SEQS, LEN)).astype(jnp.int32)
    valid_mask = draw_valid_mask(jax.random.fold_in(key_of[10], 71), 0)
    attn_in = centred(key_of[3], (QKV, D), D ** -0.5, 0.1875, ((0, 32),))
    attn_out = centred(key_of[4], (ATT, D), ATT ** -0.5, 0.1875, ((0, 32),))
    ffw_in = centred(key_of[5], (2 * FF, D), D ** -0.5, 0.1875, ((0, 32),))
    ffw_out = centred(key_of[6], (FF, D), FF ** -0.5, 0.078125, ((0, 32),))
    norm_gains = jnp.clip(1.0 + 0.18 * jax.random.normal(key_of[7], (4, D), jnp.float32), 0.1, 1.9)
    head_gains = jnp.clip(1.0 + 0.18 * jax.random.normal(key_of[8], (2, HD), jnp.float32), 0.1, 1.9)
    cotangent = draw_cotangent(jax.random.fold_in(key_of[10], 71), 0)
    return {"inputs": inputs, "segment_ids": segment_ids, "valid_mask": valid_mask, "attn_in": attn_in, "attn_out": attn_out, "ffw_in": ffw_in, "ffw_out": ffw_out, "norm_gains": norm_gains, "head_gains": head_gains, "cotangent": cotangent}


EPSILON = 1e-06
SCALE_FACTOR = 0.0625
THETA = 10000.0
NEGATIVE = -1e+30

@jax.custom_vjp
def low(v):
    return lax.optimization_barrier(v.astype(jnp.bfloat16)).astype(jnp.float32)

@jax.custom_vjp
def low_back(v):
    return v

def low_keep(v):
    return (low(v), None)

def low_pass(kept, grad):
    return (grad,)

def back_keep(v):
    return (v, None)

def back_low(kept, grad):
    return (low(grad),)
low.defvjp(low_keep, low_pass)
low_back.defvjp(back_keep, back_low)

def norm_rows(values, gain):
    return values * lax.rsqrt(lax.optimization_barrier(jnp.mean(values * values, -1, keepdims=True)) + EPSILON) * gain

def rotate(values, cosine, sine):
    half = values.shape[-1] // 2
    first = values[..., :half]
    second = values[..., half:]
    return jnp.concatenate([first * cosine - second * sine, second * cosine + first * sine], -1)

def doc_tables(segments, validity, head_size):
    length = segments.shape[-1]
    places = jnp.arange(length, dtype=jnp.int32)
    same_doc = segments[..., :, None] == segments[..., None, :]
    earlier = places[None, :] < places[:, None]
    position = lax.optimization_barrier(jnp.sum(jnp.logical_and(same_doc, earlier).astype(jnp.int32), -1))
    reach = places[None, :] <= places[:, None]
    usable = jnp.logical_or(validity[..., None, :] > 0, places[None, :] == places[:, None])
    allowed = jnp.logical_and(jnp.logical_and(same_doc, reach), usable)
    freqs = jnp.exp(jnp.arange(head_size // 2, dtype=jnp.float32) * (-2.0 * math.log(THETA) / head_size))
    angles = position.astype(jnp.float32)[..., None] * freqs
    return (allowed, jnp.cos(angles), jnp.sin(angles))

def prepare(projected, head_gains, cosine, sine):
    width = HEADS * HD
    query = projected[..., :width].reshape(projected.shape[:-1] + (HEADS, HD))
    keys = projected[..., width:width + HD]
    values = projected[..., width + HD:]
    query = rotate(norm_rows(query, head_gains[0]), cosine[..., None, :], sine[..., None, :])
    keys = rotate(norm_rows(keys, head_gains[1]), cosine, sine)
    return (query, keys, values)

def layer(stream, weight_in, weight_out, weight_ffin, weight_ffout, gains, heads_gain, allowed, cosine, sine):
    top = lax.Precision.HIGHEST
    normed_in = low(norm_rows(stream, gains[0]))
    projected = low_back(jnp.einsum('gtd,od->gto', normed_in, weight_in, precision=top))
    query, keys, values = prepare(projected, heads_gain, cosine, sine)
    query = low(query)
    keys = low(keys)
    values = low(values)
    scores = low_back(jnp.einsum('gqhd,gkd->ghqk', query, keys, precision=top) * SCALE_FACTOR)
    visible = allowed[:, None]
    masked = jnp.where(visible, scores, NEGATIVE)
    peak = lax.optimization_barrier(jnp.max(masked, -1, keepdims=True))
    expo = jnp.where(visible, jnp.exp(masked - peak), 0.0)
    probs = low(expo / lax.optimization_barrier(jnp.sum(expo, -1, keepdims=True)))
    mixed = jnp.einsum('ghqk,gkd->gqhd', probs, values, precision=top)
    mixed = low(low_back(mixed.reshape(mixed.shape[:2] + (HEADS * HD,))))
    attn_proj = low_back(jnp.einsum('gto,od->gtd', mixed, weight_out, precision=top))
    attn_branch = norm_rows(attn_proj, gains[1])
    middle = stream + attn_branch
    normed_mid = low(norm_rows(middle, gains[2]))
    gate_up = low_back(jnp.einsum('gtd,od->gto', normed_mid, weight_ffin, precision=top))
    hidden = low(jax.nn.gelu(gate_up[..., :FF], approximate=True) * gate_up[..., FF:])
    ffw_proj = low_back(jnp.einsum('gtf,fd->gtd', hidden, weight_ffout, precision=top))
    ffw_branch = norm_rows(ffw_proj, gains[3])
    return (middle + ffw_branch, (middle, attn_branch, ffw_branch))

def reference(inputs, segment_ids, valid_mask, attn_in, attn_out, ffw_in, ffw_out, norm_gains, head_gains, cotangent):
    group = math.gcd(SEQS, max(1, 4096 // LEN))
    count = MICRO * SEQS // group
    streams = inputs.astype(jnp.float32).reshape(count, group, LEN, D)
    cotangents = cotangent.astype(jnp.float32).reshape(count, group, LEN, D)
    segments = segment_ids.reshape(count, group, LEN)
    validity = valid_mask.reshape(count, group, LEN)
    params = (attn_in.astype(jnp.float32), attn_out.astype(jnp.float32), ffw_in.astype(jnp.float32), ffw_out.astype(jnp.float32), norm_gains.astype(jnp.float32), head_gains.astype(jnp.float32))

    def step(carry, item):
        grads, stats = carry
        stream, segment, valid, cot = item
        allowed, cosine, sine = doc_tables(segment, valid, HD)

        def forward(values, weight_in, weight_out, weight_ffin, weight_ffout, gains, heads_gain):
            return layer(values, weight_in, weight_out, weight_ffin, weight_ffout, gains, heads_gain, allowed, cosine, sine)
        result, backward, extras = jax.vjp(forward, stream, params[0], params[1], params[2], params[3], params[4], params[5], has_aux=True)
        parts = backward(cot)
        grads = tuple((total + part for total, part in zip(grads, parts[1:])))
        weight = valid.astype(jnp.float32)
        middle, attn_branch, ffw_branch = extras
        sums = [jnp.sum(weight * lax.optimization_barrier(jnp.sum(value * value, -1))) for value in (stream, middle, attn_branch, ffw_branch)]
        sums.append(jnp.sum(weight))
        return ((grads, stats + jnp.stack(sums)), (result.astype(jnp.bfloat16), parts[0]))
    start = (tuple((jnp.zeros_like(param) for param in params)), jnp.zeros((5,), jnp.float32))
    (grads, stats), (results, input_grads) = lax.scan(step, start, (streams, segments, validity, cotangents))
    rms_values = jnp.sqrt(stats[:4] / (stats[4] * D))
    return (results.reshape(MICRO, SEQS, LEN, D), input_grads.reshape(MICRO, SEQS, LEN, D), grads[0], grads[1], grads[2], grads[3], grads[4], grads[5], rms_values)
```

```python
import math

import jax
import jax.numpy as jnp
from jax import lax
from jax.experimental import pallas as pl
from jax.experimental.pallas import tpu as pltpu
from jax.sharding import PartitionSpec as P

D = 1152
HEADS = 4
HD = 256
FF = 6912
MICRO = 2


EPSILON = 1e-06
SCALE_FACTOR = 0.0625
THETA = 10000.0
NEGATIVE = -1e30


def shortened(x):

    def short(part):
        return part.astype(jnp.bfloat16) if part.dtype == jnp.float32 else part

    return jax.tree.map(short, x)


def swapped(block, axis, stride):
    count = lax.axis_size(axis)
    route = []
    for low in range(count):
        high = low | 1 << stride
        if high != low and high < count:
            route += [(low, high), (high, low)]
    return lax.ppermute(block, axis, route)


def norm_rows(values, gain):
    return values * lax.rsqrt(jnp.mean(values * values, -1, keepdims=True) + EPSILON) * gain


def rotate(values, cosine, sine):
    half = values.shape[-1] // 2
    first = values[..., :half]
    second = values[..., half:]
    return jnp.concatenate([first * cosine - second * sine, second * cosine + first * sine], -1)


def doc_tables(segments, validity, head_size):
    length = segments.shape[-1]
    places = jnp.arange(length, dtype=jnp.int32)
    same_doc = segments[..., :, None] == segments[..., None, :]
    earlier = places[None, :] < places[:, None]
    position = jnp.sum(jnp.logical_and(same_doc, earlier).astype(jnp.int32), -1)
    reach = places[None, :] <= places[:, None]
    usable = jnp.logical_or(validity[..., None, :] > 0, places[None, :] == places[:, None])
    allowed = jnp.logical_and(jnp.logical_and(same_doc, reach), usable)
    freqs = jnp.exp(
        jnp.arange(head_size // 2, dtype=jnp.float32) * (-2.0 * math.log(THETA) / head_size)
    )
    angles = position.astype(jnp.float32)[..., None] * freqs
    return (allowed, jnp.cos(angles), jnp.sin(angles))


def prepare(projected, head_gains, cosine, sine):
    width = HEADS * HD
    query = projected[..., :width].reshape(projected.shape[:-1] + (HEADS, HD))
    keys = projected[..., width : width + HD]
    values = projected[..., width + HD :]
    query = rotate(norm_rows(query, head_gains[0]), cosine[..., None, :], sine[..., None, :])
    keys = rotate(norm_rows(keys, head_gains[1]), cosine, sine)
    return (query, keys, values)


def across(left, piece):
    return lax.dot_general(
        left, piece, (((1,), (1,)), ((), ())), preferred_element_type=jnp.float32
    )


def over_rows(left, right):
    return lax.dot_general(
        left, right, (((0,), (0,)), ((), ())), preferred_element_type=jnp.float32
    )


def score_table(query_low, keys_low):
    return (
        jnp.einsum("qhd,kd->hqk", query_low, keys_low, preferred_element_type=jnp.float32)
        * SCALE_FACTOR
    )


def attend(query_low, keys_low, values_low, allowed):
    scores = score_table(query_low, keys_low)
    masked = jnp.where(allowed[None], scores, NEGATIVE)
    peak = jnp.max(masked, -1, keepdims=True)
    expo = jnp.where(allowed[None], jnp.exp(masked - peak), 0.0)
    totals = jnp.sum(expo, -1, keepdims=True)
    probs = expo / totals
    mixed = jnp.einsum(
        "hqk,kd->qhd", probs.astype(jnp.bfloat16), values_low, preferred_element_type=jnp.float32
    )
    return (mixed, peak + jnp.log(totals))


def attend_back(query_low, keys_low, values_low, allowed, log_sum, grad_low):
    scores = score_table(query_low, keys_low)
    probs = jnp.where(allowed[None], jnp.exp(scores - log_sum), 0.0)
    grad_probs = jnp.einsum("qhd,kd->hqk", grad_low, values_low, preferred_element_type=jnp.float32)
    grad_values = jnp.einsum(
        "hqk,qhd->kd", probs.astype(jnp.bfloat16), grad_low, preferred_element_type=jnp.float32
    )
    center = jnp.sum(grad_probs * probs, -1, keepdims=True)
    grad_scores = (probs * (grad_probs - center)).astype(jnp.bfloat16)
    grad_query = (
        jnp.einsum("hqk,kd->qhd", grad_scores, keys_low, preferred_element_type=jnp.float32)
        * SCALE_FACTOR
    )
    grad_keys = (
        jnp.einsum("hqk,qhd->kd", grad_scores, query_low, preferred_element_type=jnp.float32)
        * SCALE_FACTOR
    )
    return (grad_query, grad_keys, grad_values)


def gated(gate, upward):
    return jax.nn.gelu(gate, approximate=True) * upward


def general_shards(
    inputs,
    segment_ids,
    valid_mask,
    attn_in,
    attn_out,
    ffw_in,
    ffw_out,
    norm_gains,
    head_gains,
    cotangent,
):
    width = HEADS * HD
    kept_proj = []
    kept_normed_in = []
    kept_mixed = []
    kept_attn = []
    kept_gate = []
    kept_normed_mid = []
    kept_hidden = []
    kept_ffw = []
    gain_sums = jnp.zeros((4, D), jnp.float32)
    head_sums = jnp.zeros((2, HD), jnp.float32)
    stats = jnp.zeros((5,), jnp.float32)
    results = []
    input_grads = []
    for step in range(MICRO):
        full_in, full_out = (
            lax.all_gather(attn_in, "dp", axis=0, tiled=True),
            lax.all_gather(attn_out, "dp", axis=0, tiled=True),
        )
        full_ffin, full_ffout = (
            lax.all_gather(ffw_in, "dp", axis=0, tiled=True),
            lax.all_gather(ffw_out, "dp", axis=0, tiled=True),
        )
        stream = inputs[step, 0].astype(jnp.float32)
        length = stream.shape[0]
        allowed, cosine, sine = doc_tables(segment_ids[step, 0], valid_mask[step, 0], HD)
        normed_in = norm_rows(stream, norm_gains[0]).astype(jnp.bfloat16)
        projected = across(normed_in, full_in)
        query, keys, values = prepare(projected, head_gains, cosine, sine)
        query_low = query.astype(jnp.bfloat16)
        keys_low = keys.astype(jnp.bfloat16)
        values_low = values.astype(jnp.bfloat16)
        mixed, log_sum = attend(query_low, keys_low, values_low, allowed)
        mixed_low = mixed.reshape(length, width).astype(jnp.bfloat16)
        attn_proj = jnp.dot(mixed_low, full_out, preferred_element_type=jnp.float32)
        attn_branch = norm_rows(attn_proj, norm_gains[1])
        middle = stream + attn_branch
        normed_mid = norm_rows(middle, norm_gains[2]).astype(jnp.bfloat16)
        gate_up = across(normed_mid, full_ffin)
        gate = gate_up[:, :FF]
        upward = gate_up[:, FF:]
        hidden = gated(gate, upward).astype(jnp.bfloat16)
        ffw_proj = jnp.dot(hidden, full_ffout, preferred_element_type=jnp.float32)
        ffw_branch = norm_rows(ffw_proj, norm_gains[3])
        results.append((middle + ffw_branch).astype(jnp.bfloat16))
        weight = valid_mask[step, 0].astype(jnp.float32)
        sums = [
            jnp.sum(weight * jnp.sum(value * value, -1))
            for value in (stream, middle, attn_branch, ffw_branch)
        ]
        sums.append(jnp.sum(weight))
        stats = stats + jnp.stack(sums)
        upstream = cotangent[step, 0].astype(jnp.float32)
        _, back_ffw = jax.vjp(norm_rows, ffw_proj, norm_gains[3])
        grad_ffw_proj, gain_three = back_ffw(upstream)
        grad_ffw_low = grad_ffw_proj.astype(jnp.bfloat16)
        grad_hidden = across(grad_ffw_low, full_ffout)
        _, back_gated = jax.vjp(gated, gate, upward)
        grad_gate, grad_upward = back_gated(grad_hidden)
        grad_gate_up = jnp.concatenate([grad_gate, grad_upward], 1).astype(jnp.bfloat16)
        grad_normed_mid = jnp.dot(grad_gate_up, full_ffin, preferred_element_type=jnp.float32)
        _, back_mid = jax.vjp(norm_rows, middle, norm_gains[2])
        grad_mid_part, gain_two = back_mid(grad_normed_mid)
        grad_middle = upstream + grad_mid_part
        _, back_attn = jax.vjp(norm_rows, attn_proj, norm_gains[1])
        grad_attn_proj, gain_one = back_attn(grad_middle)
        grad_attn_low = grad_attn_proj.astype(jnp.bfloat16)
        grad_mixed = across(grad_attn_low, full_out)
        grad_mixed_low = grad_mixed.astype(jnp.bfloat16).reshape(length, HEADS, HD)
        grad_query, grad_keys, grad_values = attend_back(
            query_low, keys_low, values_low, allowed, log_sum, grad_mixed_low
        )
        _, back_prep = jax.vjp(
            lambda table, gains: prepare(table, gains, cosine, sine), projected, head_gains
        )
        grad_projected, grad_heads = back_prep((grad_query, grad_keys, grad_values))
        grad_proj_low = grad_projected.astype(jnp.bfloat16)
        grad_normed_in = jnp.dot(grad_proj_low, full_in, preferred_element_type=jnp.float32)
        _, back_in = jax.vjp(norm_rows, stream, norm_gains[0])
        grad_stream, gain_zero = back_in(grad_normed_in)
        input_grads.append(grad_middle + grad_stream)
        gain_sums = gain_sums + jnp.stack([gain_zero, gain_one, gain_two, gain_three])
        head_sums = head_sums + grad_heads
        kept_proj.append(grad_proj_low)
        kept_normed_in.append(normed_in)
        kept_mixed.append(mixed_low)
        kept_attn.append(grad_attn_low)
        kept_gate.append(grad_gate_up)
        kept_normed_mid.append(normed_mid)
        kept_hidden.append(hidden)
        kept_ffw.append(grad_ffw_low)
    pairs = [
        (jnp.concatenate(kept_proj, 0), jnp.concatenate(kept_normed_in, 0)),
        (jnp.concatenate(kept_mixed, 0), jnp.concatenate(kept_attn, 0)),
        (jnp.concatenate(kept_gate, 0), jnp.concatenate(kept_normed_mid, 0)),
        (jnp.concatenate(kept_hidden, 0), jnp.concatenate(kept_ffw, 0)),
    ]
    levels = lax.axis_size("dp").bit_length() - 1
    place = lax.axis_index("dp")
    top_bit = place >> levels - 1 & 1
    kept_parts = []
    sent_parts = []
    for left, right in pairs:
        half_cols = left.shape[1] // 2
        kept_parts.append(
            over_rows(lax.dynamic_slice_in_dim(left, top_bit * half_cols, half_cols, 1), right)
        )
        sent_parts.append(
            over_rows(
                lax.dynamic_slice_in_dim(left, (1 - top_bit) * half_cols, half_cols, 1), right
            )
        )
    current = tuple(kept_parts)
    outgoing = tuple(sent_parts)
    for level in range(levels):
        bit = levels - 1 - level
        arrived = jax.tree.map(
            lambda part, own: part.astype(own.dtype),
            swapped(shortened(outgoing), "dp", bit),
            outgoing,
        )
        current = tuple((mine + theirs for mine, theirs in zip(current, arrived)))
        if level + 1 < levels:
            next_bit = place >> bit - 1 & 1
            halves = [piece.shape[0] // 2 for piece in current]
            outgoing = tuple(
                (
                    lax.dynamic_slice_in_dim(piece, (1 - next_bit) * rows, rows, 0)
                    for piece, rows in zip(current, halves)
                )
            )
            current = tuple(
                (
                    lax.dynamic_slice_in_dim(piece, next_bit * rows, rows, 0)
                    for piece, rows in zip(current, halves)
                )
            )
    shard_in, shard_out, shard_ffin, shard_ffout = current
    gain_total, head_total, stat_total = lax.psum((gain_sums, head_sums, stats), "dp")
    rms_values = jnp.sqrt(stat_total[:4] / (stat_total[4] * D))
    layer_out = jnp.stack(results)[:, None]
    input_grad = jnp.stack(input_grads)[:, None]
    return (
        layer_out,
        input_grad,
        shard_in,
        shard_out,
        shard_ffin,
        shard_ffout,
        gain_total,
        head_total,
        rms_values,
    )


BLOCK = 216
PADDED = 224
WIDE = 2 * PADDED
MINE = 128
VMEM_BYTES = 56 << 20
SQRT_2_OVER_PI = math.sqrt(2.0 / math.pi)
CUBIC = 0.044715
MESH = pl.DeviceIdType.MESH


def spots():
    me = lax.axis_index("dp")
    return me, me // 8, me // 4 % 2, me // 2 % 2, me % 2


def at(z, y, x, c):
    return z * 8 + y * 4 + x * 2 + c


def z_peer(z, k):
    if k == 0:
        return z
    if k == 1:
        return z + 1 - 2 * (z % 2)
    if k == 2:
        return (z + 2) % 4
    return 3 - z


def remote(src, dst, send_sem, recv_sem, device):
    return pltpu.make_async_remote_copy(
        src_ref=src,
        dst_ref=dst,
        send_sem=send_sem,
        recv_sem=recv_sem,
        device_id=(device,),
        device_id_type=MESH,
    )


def greet(devices):
    barrier = pltpu.get_barrier_semaphore()
    for device in devices:
        pl.semaphore_signal(barrier, inc=1, device_id=(device,), device_id_type=MESH)
    pl.semaphore_wait(barrier, len(devices))


def greet_all(me):
    barrier = pltpu.get_barrier_semaphore()

    def one(step, carry):
        pl.semaphore_signal(barrier, inc=1, device_id=((me + step) % 32,), device_id_type=MESH)
        return carry

    lax.fori_loop(1, 32, one, 0)
    pl.semaphore_wait(barrier, 31)


def weights_kernel(
    ain, aout, gu, dn, all_in, all_out, all_gu, all_dn, local, sa, ra, sb, rb, sw, rw, sd, rd
):
    me, z, y, x, c = spots()
    greet_all(me)
    xp, yp, cp = at(z, y, 1 - x, c), at(z, 1 - y, x, c), at(z, y, x, 1 - c)
    mine_in, mine_out = all_in.at[z, y, x, c], all_out.at[z, y, x, c]
    keep_in = pltpu.make_async_copy(ain, mine_in, local.at[0])
    keep_out = pltpu.make_async_copy(aout, mine_out, local.at[1])
    keep_in.start()
    keep_out.start()
    sent = []

    def send(src, dst, send_sem, recv_sem, device):
        copy = remote(src, dst, send_sem, recv_sem, device)
        copy.start()
        sent.append(copy)

    def got(block, send_sem, recv_sem):
        remote(block, block, send_sem, recv_sem, cp).wait_recv()

    for k in (1, 2, 3):
        send(ain, mine_in, sa.at[k], ra.at[k], at(z_peer(z, k), y, x, c))
    send(ain, mine_in, sa.at[4], ra.at[4], xp)
    for k in (1, 2, 3):
        send(aout, mine_out, sb.at[k], rb.at[k], at(z_peer(z, k), y, x, c))
    send(aout, mine_out, sb.at[4], rb.at[4], yp)
    kind, goal = z // 2, 2 * (z % 2) + x
    down_z, down_y = 2 * (z // 2) + y, z % 2
    moves = [
        (
            jnp.logical_and(goal == z, x == h),
            gu.at[h],
            all_gu.at[kind, h, c],
            sw.at[h],
            rw.at[kind],
            at(goal, y, h, c),
        )
        for h in range(2)
    ]
    moves.append(
        (down_y == y, dn, all_dn.at[c, x], sw.at[2], rw.at[2], at(down_z, down_y, x, c))
    )
    for stays, src, dst, send_sem, recv_sem, device in moves:

        @pl.when(stays)
        def _():
            pltpu.make_async_copy(src, dst, recv_sem).start()

        @pl.when(jnp.logical_not(stays))
        def _():
            remote(src, dst, send_sem, recv_sem, device).start()

    for k in (1, 2, 3):
        there = z_peer(z, k)
        block = all_in.at[there, y, x, c]
        got(block, sa.at[k], ra.at[k])
        send(block, block, sa.at[4 + k], ra.at[4 + k], xp)
        block = all_out.at[there, y, x, c]
        got(block, sb.at[k], rb.at[k])
        send(block, block, sb.at[4 + k], rb.at[4 + k], yp)
    keep_in.wait()
    keep_out.wait()
    for k in range(4):
        there = z_peer(z, k)
        got(all_in.at[there, y, 1 - x, c], sa.at[4 + k], ra.at[4 + k])
        pair = all_in.at[there, y, :, c]
        send(pair, pair, sa.at[8 + k], ra.at[8 + k], yp)
        got(all_out.at[there, 1 - y, x, c], sb.at[4 + k], rb.at[4 + k])
        pair = all_out.at[there, :, x, c]
        send(pair, pair, sb.at[8 + k], rb.at[8 + k], xp)
    for t in range(2):
        block = all_gu.at[t, x, c]
        got(block, sw.at[t], rw.at[t])
        send(block, block, sd.at[t], rd.at[t], xp)
    block = all_dn.at[c, x]
    got(block, sw.at[2], rw.at[2])
    send(block, block, sd.at[2], rd.at[2], xp)
    near = all_in.at[:, y, :, c]
    send(near, near, sd.at[3], rd.at[3], cp)
    near = all_out.at[:, :, x, c]
    send(near, near, sd.at[4], rd.at[4], cp)
    for k in range(4):
        there = z_peer(z, k)
        got(all_in.at[there, 1 - y, :, c], sa.at[8 + k], ra.at[8 + k])
        got(all_out.at[there, :, 1 - x, c], sb.at[8 + k], rb.at[8 + k])
    far = all_in.at[:, 1 - y, :, c]
    send(far, far, sd.at[5], rd.at[5], cp)
    far = all_out.at[:, :, 1 - x, c]
    send(far, far, sd.at[6], rd.at[6], cp)
    for t in range(2):
        got(all_gu.at[t, 1 - x, c], sd.at[t], rd.at[t])
    got(all_dn.at[c, 1 - x], sd.at[2], rd.at[2])
    send(all_gu.at[:, :, c], all_gu.at[:, :, c], sd.at[7], rd.at[7], cp)
    send(all_dn.at[c], all_dn.at[c], sd.at[8], rd.at[8], cp)
    got(all_in.at[:, y, :, 1 - c], sd.at[3], rd.at[3])
    got(all_out.at[:, :, x, 1 - c], sd.at[4], rd.at[4])
    got(all_in.at[:, 1 - y, :, 1 - c], sd.at[5], rd.at[5])
    got(all_out.at[:, :, 1 - x, 1 - c], sd.at[6], rd.at[6])
    got(all_gu.at[:, :, 1 - c], sd.at[7], rd.at[7])
    got(all_dn.at[1 - c], sd.at[8], rd.at[8])
    for copy in sent:
        copy.wait_send()
    for stays, src, dst, send_sem, recv_sem, device in moves:

        @pl.when(jnp.logical_not(stays))
        def _():
            remote(src, dst, send_sem, recv_sem, device).wait_send()


def dma(count):
    return pltpu.SemaphoreType.DMA((count,))


def gather_weights(ain, aout, gu, dn):
    low = jnp.bfloat16
    any_place = pl.BlockSpec(memory_space=pl.ANY)
    return pl.pallas_call(
        weights_kernel,
        out_shape=(
            jax.ShapeDtypeStruct((4, 2, 2, 2) + ain.shape, low),
            jax.ShapeDtypeStruct((4, 2, 2, 2) + aout.shape, low),
            jax.ShapeDtypeStruct((2, 2, 2, PADDED, D), low),
            jax.ShapeDtypeStruct((2, 2, PADDED, D), low),
        ),
        in_specs=[any_place] * 4,
        out_specs=(any_place,) * 4,
        scratch_shapes=[dma(2)] + [dma(12)] * 4 + [dma(3)] * 2 + [dma(9)] * 2,
        compiler_params=pltpu.CompilerParams(
            collective_id=1, has_side_effects=True, vmem_limit_bytes=VMEM_BYTES
        ),
        name="gather_weights",
    )(ain, aout, gu, dn)


def nt(left, right):
    return lax.dot_general(
        left, right, (((1,), (1,)), ((), ())), preferred_element_type=jnp.float32
    )


def nn(left, right):
    return lax.dot_general(
        left, right, (((1,), (0,)), ((), ())), preferred_element_type=jnp.float32
    )


def tn(left, right):
    return lax.dot_general(
        left, right, (((0,), (0,)), ((), ())), preferred_element_type=jnp.float32
    )


def moved(rows, got_all, total, pairs, buffers, sems):
    acc, keep, send_y, recv_y, send_z, recv_z = buffers
    gsz, grz, gsy, gry, ssy, sry, ssz, srz = sems
    me, z, y, x, c = spots()
    yp = at(z, 1 - y, x, c)
    peers = [at(z_peer(z, k), y, x, c) for k in (1, 2, 3)]
    greet(peers + [yp])
    sent = []

    def send(src, dst, send_sem, recv_sem, device):
        copy = remote(src, dst, send_sem, recv_sem, device)
        copy.start()
        sent.append(copy)

    for k in (1, 2, 3):
        send(rows, got_all.at[z, y], gsz.at[k - 1], grz.at[k - 1], peers[k - 1])
    send(rows, got_all.at[z, y], gsy.at[0], gry.at[0], yp)
    got_all[z, y] = rows[...]

    def finish(k):
        there = z_peer(z, k)
        remote(recv_y.at[k], recv_y.at[k], ssy.at[k], sry.at[k], yp).wait_recv()
        if k == 0:
            total[...] = keep[0] + recv_y[0].astype(jnp.float32)
        else:
            send_z[k - 1] = (keep[k] + recv_y[k].astype(jnp.float32)).astype(jnp.bfloat16)
            send(
                send_z.at[k - 1],
                recv_z.at[k - 1],
                ssz.at[k - 1],
                srz.at[k - 1],
                at(there, y, x, c),
            )

    for k in range(4):
        there = z_peer(z, k)
        if k < 3:
            block = got_all.at[z_peer(z, k + 1), y]
            remote(block, block, gsz.at[k], grz.at[k], yp).wait_recv()
            send(block, block, gsy.at[k + 1], gry.at[k + 1], yp)
        block = got_all.at[there, 1 - y]
        remote(block, block, gsy.at[k], gry.at[k], yp).wait_recv()
        pairs(there, acc)
        keep[k] = acc[y]
        send_y[k] = acc[1 - y].astype(jnp.bfloat16)
        send(send_y.at[k], recv_y.at[k], ssy.at[k], sry.at[k], yp)
        if k:
            finish(k - 1)
    return sent, finish


def settle(total, recv_z, ssz, srz):
    me, z, y, x, c = spots()
    for k in (1, 2, 3):
        block = recv_z.at[k - 1]
        remote(block, block, ssz.at[k - 1], srz.at[k - 1], at(z, 1 - y, x, c)).wait_recv()
        total[...] += recv_z[k - 1].astype(jnp.float32)


def forward_kernel(
    rows, w_gu, w_dn, total, got_all, hidden, slope_gate, slope_up, *scratch
):
    buffers, sems = scratch[:6], scratch[6:]

    def pairs(there, acc):
        def half(h, carry):
            block = got_all[there].reshape(2 * MINE, D)
            gate = nt(block, w_gu[0, h])
            upward = nt(block, w_gu[1, h])
            square = gate * gate
            tanh = jnp.tanh(SQRT_2_OVER_PI * gate * (1.0 + CUBIC * square))
            side = 0.5 * (1.0 + tanh)
            gelu = gate * side
            slope = side + 0.5 * gate * (1.0 - tanh * tanh) * (
                SQRT_2_OVER_PI * (1.0 + 3.0 * CUBIC * square)
            )
            low = (gelu * upward).astype(jnp.bfloat16)
            hidden[h, there] = low
            slope_gate[h, there] = (upward * slope).astype(jnp.bfloat16)
            slope_up[h, there] = gelu.astype(jnp.bfloat16)
            part = nn(low, w_dn[h]).reshape(2, MINE, D)

            @pl.when(h == 0)
            def _():
                acc[...] = part

            @pl.when(h == 1)
            def _():
                acc[...] += part

            return carry

        lax.fori_loop(0, 2, half, 0)

    sent, finish = moved(rows, got_all, total, pairs, buffers, sems)
    finish(3)
    settle(total, buffers[5], sems[6], sems[7])
    for copy in sent:
        copy.wait_send()


def backward_kernel(
    rows,
    w_gu,
    w_dn,
    mids,
    hidden,
    slope_gate,
    slope_up,
    total,
    d_gu,
    d_dn,
    got_all,
    grad_gate,
    grad_up,
    *scratch,
):
    buffers, sems = scratch[:6], scratch[6:]

    def pairs(there, acc):
        def half(h, carry):
            block = got_all[there].reshape(2 * MINE, D)
            back = nt(block, w_dn[h])
            gate = (back * slope_gate[h, there].astype(jnp.float32)).astype(jnp.bfloat16)
            upward = (back * slope_up[h, there].astype(jnp.float32)).astype(jnp.bfloat16)
            grad_gate[h, there] = gate
            grad_up[h, there] = upward
            part = (nn(gate, w_gu[0, h]) + nn(upward, w_gu[1, h])).reshape(2, MINE, D)

            @pl.when(h == 0)
            def _():
                acc[...] = part

            @pl.when(h == 1)
            def _():
                acc[...] += part

            return carry

        lax.fori_loop(0, 2, half, 0)

    sent, finish = moved(rows, got_all, total, pairs, buffers, sems)
    step = 128

    def column(j, carry):
        cols = pl.ds(pl.multiple_of(j * step, step), step)
        ups = got_all[:, :, :, cols].reshape(8 * MINE, step)
        mid = mids[:, :, :, cols].reshape(8 * MINE, step)
        for h in range(2):
            d_dn[h, :, cols] = tn(hidden[h].reshape(8 * MINE, WIDE), ups).astype(jnp.bfloat16)
            d_gu[0, h, :, cols] = tn(grad_gate[h].reshape(8 * MINE, WIDE), mid).astype(jnp.bfloat16)
            d_gu[1, h, :, cols] = tn(grad_up[h].reshape(8 * MINE, WIDE), mid).astype(jnp.bfloat16)
        return carry

    finish(3)
    lax.fori_loop(0, D // step, column, 0)
    settle(total, buffers[5], sems[6], sems[7])
    for copy in sent:
        copy.wait_send()


def move_scratch():
    low = jnp.bfloat16
    return [
        pltpu.VMEM((2, MINE, D), jnp.float32),
        pltpu.VMEM((4, MINE, D), jnp.float32),
        pltpu.VMEM((4, MINE, D), low),
        pltpu.VMEM((4, MINE, D), low),
        pltpu.VMEM((3, MINE, D), low),
        pltpu.VMEM((3, MINE, D), low),
    ] + [dma(3), dma(3), dma(4), dma(4), dma(4), dma(4), dma(3), dma(3)]


def ffw_forward(rows, w_gu, w_dn):
    low = jnp.bfloat16
    wide = jax.ShapeDtypeStruct((2, 4, 2 * MINE, WIDE), low)
    vmem = pl.BlockSpec(memory_space=pltpu.VMEM)
    return pl.pallas_call(
        forward_kernel,
        out_shape=(
            jax.ShapeDtypeStruct((MINE, D), jnp.float32),
            jax.ShapeDtypeStruct((4, 2, MINE, D), low),
            wide,
            wide,
            wide,
        ),
        in_specs=[vmem] * 3,
        out_specs=(vmem,) * 5,
        scratch_shapes=move_scratch(),
        compiler_params=pltpu.CompilerParams(
            collective_id=2, has_side_effects=True, vmem_limit_bytes=VMEM_BYTES
        ),
        name="ffw_forward",
    )(rows, w_gu, w_dn)


def ffw_backward(rows, w_gu, w_dn, mids, hidden, slope_gate, slope_up):
    low = jnp.bfloat16
    vmem = pl.BlockSpec(memory_space=pltpu.VMEM)
    wide = pltpu.VMEM((2, 4, 2 * MINE, WIDE), low)
    return pl.pallas_call(
        backward_kernel,
        out_shape=(
            jax.ShapeDtypeStruct((MINE, D), jnp.float32),
            jax.ShapeDtypeStruct((2, 2, WIDE, D), low),
            jax.ShapeDtypeStruct((2, WIDE, D), low),
        ),
        in_specs=[vmem] * 7,
        out_specs=(vmem,) * 3,
        scratch_shapes=[pltpu.VMEM((4, 2, MINE, D), low), wide, wide] + move_scratch(),
        compiler_params=pltpu.CompilerParams(
            collective_id=3, has_side_effects=True, vmem_limit_bytes=VMEM_BYTES
        ),
        name="ffw_backward",
    )(rows, w_gu, w_dn, mids, hidden, slope_gate, slope_up)


def added(left, right):
    return (left.astype(jnp.float32) + right.astype(jnp.float32)).astype(jnp.bfloat16)


def return_kernel(
    d_in,
    d_out,
    d_gu,
    d_dn,
    small,
    o_in,
    o_out,
    o_gu,
    o_dn,
    o_small,
    a0,
    a1,
    a2,
    a3,
    ta,
    ta1,
    ta2,
    b0,
    b1,
    b2,
    b3,
    tb,
    tb1,
    tb2,
    g0,
    g1,
    g2,
    tg,
    tg1,
    n0,
    n1,
    n2,
    tn0,
    tn1,
    sv,
    ss,
    rs,
    sv_s,
    sv_r,
    so,
    ro,
):
    me, z, y, x, c = spots()
    greet_all(me)
    xp, yp, cp = at(z, y, 1 - x, c), at(z, 1 - y, x, c), at(z, y, x, 1 - c)
    sent = []

    def send(src, dst, slot, device):
        copy = remote(src, dst, ss.at[slot], rs.at[slot], device)
        copy.start()
        sent.append(copy)

    def got(block, slot):
        remote(block, block, ss.at[slot], rs.at[slot], cp).wait_recv()

    def send_small(src, dst, slot, device):
        copy = remote(src, dst, sv_s.at[slot], sv_r.at[slot], device)
        copy.start()
        sent.append(copy)

    def got_small(slot):
        remote(sv.at[slot], sv.at[slot], sv_s.at[slot], sv_r.at[slot], cp).wait_recv()

    send_small(small, sv.at[0], 0, cp)
    send(d_out.at[:, :, :, 1 - c], b0, 0, cp)
    send(d_in.at[:, :, :, 1 - c], a0, 1, cp)
    send(d_dn.at[1 - c], n0, 2, cp)
    send(d_gu.at[:, :, 1 - c], g0, 3, cp)
    got_small(0)
    o_small[...] = small[...] + sv[0]
    sv[6] = o_small[...]
    send_small(sv.at[6], sv.at[1], 1, xp)

    got(b0, 0)

    def sum_out(i, carry):
        p, q, r = i // 4, i // 2 % 2, i % 2
        tb[p, q, r] = added(d_out[p, q, r, c], b0[p, q, r])
        return carry

    lax.fori_loop(0, 16, sum_out, 0)
    send(tb.at[:, :, 1 - x], b1, 4, xp)
    got(a0, 1)

    def sum_in(i, carry):
        p, q, r = i // 4, i // 2 % 2, i % 2
        ta[p, q, r] = added(d_in[p, q, r, c], a0[p, q, r])
        return carry

    lax.fori_loop(0, 16, sum_in, 0)
    send(ta.at[:, 1 - y], a1, 5, yp)
    got(n0, 2)
    for q in range(2):
        tn0[q] = added(d_dn[c, q], n0[q])
    send(tn0.at[1 - x], n1, 6, xp)
    got(g0, 3)
    for t in range(2):
        for h in range(2):
            tg[t, h] = added(d_gu[t, h, c], g0[t, h])
    send(tg.at[:, 1 - x], g1, 7, xp)
    got_small(1)
    o_small[...] += sv[1]
    sv[7] = o_small[...]
    send_small(sv.at[7], sv.at[2], 2, yp)

    got(b1, 4)

    def sum_out1(i, carry):
        p, q = i // 2, i % 2
        tb1[p, q] = added(tb[p, q, x], b1[p, q])
        return carry

    lax.fori_loop(0, 8, sum_out1, 0)
    send(tb1.at[:, 1 - y], b2, 8, yp)
    got(a1, 5)

    def sum_in1(i, carry):
        p, q = i // 2, i % 2
        ta1[p, q] = added(ta[p, y, q], a1[p, q])
        return carry

    lax.fori_loop(0, 8, sum_in1, 0)
    send(ta1.at[:, 1 - x], a2, 9, xp)
    got_small(2)
    o_small[...] += sv[2]
    sv[8] = o_small[...]
    for k in (1, 2, 3):
        send_small(sv.at[8], sv.at[2 + k], 2 + k, at(z_peer(z, k), y, x, c))

    got(n1, 6)
    tn1[...] = added(tn0[x], n1[...])
    got(g1, 7)
    for t in range(2):
        tg1[t] = added(tg[t, x], g1[t])
    home_z, home_y = 2 * (z // 2) + y, z % 2
    source_z, source_x = z // 2, z % 2
    moves = [
        (home_y == y, tn1, n2, so.at[2], ro.at[2], at(home_z, home_y, x, c)),
        (
            jnp.logical_and(source_z == z, source_x == x),
            tg1.at[0],
            g2.at[x],
            so.at[0],
            ro.at[x],
            at(source_z, y, source_x, c),
        ),
        (
            jnp.logical_and(source_z + 2 == z, source_x == x),
            tg1.at[1],
            g2.at[x],
            so.at[1],
            ro.at[x],
            at(source_z + 2, y, source_x, c),
        ),
    ]
    for stays, src, dst, send_sem, recv_sem, device in moves:

        @pl.when(stays)
        def _():
            pltpu.make_async_copy(src, dst, recv_sem).start()

        @pl.when(jnp.logical_not(stays))
        def _():
            remote(src, dst, send_sem, recv_sem, device).start()

    got(b2, 8)
    for p in range(4):
        tb2[p] = added(tb1[p, y], b2[p])
    for k in (1, 2, 3):
        there = z_peer(z, k)
        send(tb2.at[there], b3.at[k - 1], 9 + k, at(there, y, x, c))
    got(a2, 9)
    for p in range(4):
        ta2[p] = added(ta1[p, x], a2[p])
    for k in (1, 2, 3):
        there = z_peer(z, k)
        send(ta2.at[there], a3.at[k - 1], 12 + k, at(there, y, x, c))
    for k in (1, 2, 3):
        got_small(2 + k)
    first = sv[8] + sv[3]
    second = sv[4] + sv[5]
    o_small[...] = first + second

    for k in (1, 2, 3):
        got(b3.at[k - 1], 9 + k)
    o_out[...] = (tb2[z].astype(jnp.float32) + b3[0].astype(jnp.float32)) + (
        b3[1].astype(jnp.float32) + b3[2].astype(jnp.float32)
    )
    for k in (1, 2, 3):
        got(a3.at[k - 1], 12 + k)
    o_in[...] = (ta2[z].astype(jnp.float32) + a3[0].astype(jnp.float32)) + (
        a3[1].astype(jnp.float32) + a3[2].astype(jnp.float32)
    )
    remote(n2, n2, so.at[2], ro.at[2], cp).wait_recv()
    o_dn[...] = n2[...].astype(jnp.float32)
    for h in range(2):
        remote(g2.at[h], g2.at[h], so.at[h], ro.at[h], cp).wait_recv()
        o_gu[h] = g2[h].astype(jnp.float32)
    for copy in sent:
        copy.wait_send()
    for stays, src, dst, send_sem, recv_sem, device in moves:

        @pl.when(jnp.logical_not(stays))
        def _():
            remote(src, dst, send_sem, recv_sem, device).wait_send()


def return_grads(d_in, d_out, d_gu, d_dn, small):
    low = jnp.bfloat16
    f32 = jnp.float32
    vmem = pl.BlockSpec(memory_space=pltpu.VMEM)

    def leg(*lead):
        return pltpu.VMEM(lead + (D,), low)

    scratch = []
    for rows in (48, 32):
        scratch += [leg(4, 2, 2, rows), leg(4, 2, rows), leg(4, rows), leg(3, rows)]
        scratch += [leg(4, 2, 2, rows), leg(4, 2, rows), leg(4, rows)]
    scratch += [leg(2, 2, PADDED), leg(2, PADDED), leg(2, PADDED)]
    scratch += [leg(2, 2, PADDED), leg(2, PADDED)]
    scratch += [leg(2, PADDED), leg(PADDED), leg(PADDED)]
    scratch += [leg(2, PADDED), leg(PADDED)]
    scratch += [pltpu.VMEM((9,) + small.shape, f32)]
    scratch += [dma(16), dma(16), dma(6), dma(6), dma(3), dma(3)]
    return pl.pallas_call(
        return_kernel,
        out_shape=(
            jax.ShapeDtypeStruct((48, D), f32),
            jax.ShapeDtypeStruct((32, D), f32),
            jax.ShapeDtypeStruct((2, PADDED, D), f32),
            jax.ShapeDtypeStruct((PADDED, D), f32),
            jax.ShapeDtypeStruct(small.shape, f32),
        ),
        in_specs=[vmem] * 5,
        out_specs=(vmem,) * 5,
        scratch_shapes=scratch,
        compiler_params=pltpu.CompilerParams(
            collective_id=4, has_side_effects=True, vmem_limit_bytes=VMEM_BYTES
        ),
        name="return_grads",
    )(d_in, d_out, d_gu, d_dn, small)


def padded_rows(rows):
    return jnp.pad(rows, ((0, 0), (0, PADDED - BLOCK), (0, 0)))


def split_shards(
    inputs,
    segment_ids,
    valid_mask,
    attn_in,
    attn_out,
    ffw_in,
    ffw_out,
    norm_gains,
    head_gains,
    cotangent,
):
    width = HEADS * HD
    length = inputs.shape[2]
    rows = MICRO * length
    all_in, all_out, all_gu, all_dn = gather_weights(
        attn_in,
        attn_out,
        padded_rows(ffw_in.reshape(2, BLOCK, D)),
        padded_rows(ffw_out.reshape(1, BLOCK, D))[0],
    )
    full_in = all_in.reshape(width + 2 * HD, D)
    full_out = all_out.reshape(width, D)
    w_gu = all_gu.reshape(2, 2, WIDE, D)
    w_dn = all_dn.reshape(2, WIDE, D)
    stream = inputs.reshape(rows, D).astype(jnp.float32)
    upstream = cotangent.reshape(rows, D).astype(jnp.float32)
    allowed, cosine, sine = doc_tables(segment_ids[:, 0], valid_mask[:, 0], HD)
    cosine, sine = cosine.reshape(rows, -1), sine.reshape(rows, -1)
    normed_in = norm_rows(stream, norm_gains[0]).astype(jnp.bfloat16)
    projected = across(normed_in, full_in)
    query, keys, values = prepare(projected, head_gains, cosine, sine)
    query_low = query.astype(jnp.bfloat16).reshape(MICRO, length, HEADS, HD)
    keys_low = keys.astype(jnp.bfloat16).reshape(MICRO, length, HD)
    values_low = values.astype(jnp.bfloat16).reshape(MICRO, length, HD)
    mixed, log_sum = jax.vmap(attend)(query_low, keys_low, values_low, allowed)
    mixed_low = mixed.reshape(rows, width).astype(jnp.bfloat16)
    attn_proj = jnp.dot(mixed_low, full_out, preferred_element_type=jnp.float32)
    attn_branch = norm_rows(attn_proj, norm_gains[1])
    middle = stream + attn_branch
    normed_mid = norm_rows(middle, norm_gains[2]).astype(jnp.bfloat16)
    ffw_proj, mids, hidden, slope_gate, slope_up = ffw_forward(normed_mid, w_gu, w_dn)
    ffw_branch = norm_rows(ffw_proj, norm_gains[3])
    layer_out = (middle + ffw_branch).astype(jnp.bfloat16)
    weight = valid_mask.reshape(rows).astype(jnp.float32)
    sums = [
        jnp.sum(weight * jnp.sum(value * value, -1))
        for value in (stream, middle, attn_branch, ffw_branch)
    ]
    sums.append(jnp.sum(weight))
    _, back_ffw = jax.vjp(norm_rows, ffw_proj, norm_gains[3])
    grad_ffw_proj, gain_three = back_ffw(upstream)
    grad_normed_mid, d_gu, d_dn = ffw_backward(
        grad_ffw_proj.astype(jnp.bfloat16), w_gu, w_dn, mids, hidden, slope_gate, slope_up
    )
    _, back_mid = jax.vjp(norm_rows, middle, norm_gains[2])
    grad_mid_part, gain_two = back_mid(grad_normed_mid)
    grad_middle = upstream + grad_mid_part
    _, back_attn = jax.vjp(norm_rows, attn_proj, norm_gains[1])
    grad_attn_proj, gain_one = back_attn(grad_middle)
    grad_attn_low = grad_attn_proj.astype(jnp.bfloat16)
    grad_mixed = across(grad_attn_low, full_out)
    grad_mixed_low = grad_mixed.astype(jnp.bfloat16).reshape(MICRO, length, HEADS, HD)
    grad_query, grad_keys, grad_values = jax.vmap(attend_back)(
        query_low, keys_low, values_low, allowed, log_sum, grad_mixed_low
    )
    _, back_prep = jax.vjp(
        lambda table, gains: prepare(table, gains, cosine, sine), projected, head_gains
    )
    grad_projected, grad_heads = back_prep(
        (
            grad_query.reshape(rows, HEADS, HD),
            grad_keys.reshape(rows, HD),
            grad_values.reshape(rows, HD),
        )
    )
    grad_proj_low = grad_projected.astype(jnp.bfloat16)
    d_in = over_rows(grad_proj_low, normed_in).astype(jnp.bfloat16)
    d_out = over_rows(mixed_low, grad_attn_low).astype(jnp.bfloat16)
    grad_normed_in = jnp.dot(grad_proj_low, full_in, preferred_element_type=jnp.float32)
    _, back_in = jax.vjp(norm_rows, stream, norm_gains[0])
    grad_stream, gain_zero = back_in(grad_normed_in)
    input_grad = grad_middle + grad_stream
    flat = jnp.concatenate(
        [gain_zero, gain_one, gain_two, gain_three, grad_heads.reshape(-1), jnp.stack(sums)]
    )
    small = jnp.pad(flat, (0, 48 * 128 - flat.shape[0])).reshape(48, 128)
    shard_in, shard_out, shard_gu, shard_dn, small = return_grads(
        d_in.reshape(4, 2, 2, 2, 48, D),
        d_out.reshape(4, 2, 2, 2, 32, D),
        d_gu.reshape(2, 2, 2, PADDED, D),
        d_dn.reshape(2, 2, PADDED, D),
        small,
    )
    flat = small.reshape(-1)
    gain_total = flat[: 4 * D].reshape(4, D)
    head_total = flat[4 * D : 4 * D + 2 * HD].reshape(2, HD)
    stat_total = flat[4 * D + 2 * HD : 4 * D + 2 * HD + 5]
    rms_values = jnp.sqrt(stat_total[:4] / (stat_total[4] * D))
    return (
        layer_out.reshape(inputs.shape),
        input_grad.reshape(inputs.shape),
        shard_in,
        shard_out,
        shard_gu[:, :BLOCK].reshape(2 * BLOCK, D),
        shard_dn[:BLOCK],
        gain_total,
        head_total,
        rms_values,
    )


def solution(mesh):
    placed = (
        P(None, "dp", None, None),
        P(None, "dp", None),
        P(None, "dp", None),
        P("dp", None),
        P("dp", None),
        P("dp", None),
        P("dp", None),
        P(),
        P(),
        P(None, "dp", None, None),
    )
    return jax.shard_map(
        split_shards if mesh.shape["dp"] == 32 else general_shards,
        mesh=mesh,
        in_specs=placed,
        out_specs=(
            P(None, "dp", None, None),
            P(None, "dp", None, None),
            P("dp", None),
            P("dp", None),
            P("dp", None),
            P("dp", None),
            P(),
            P(),
            P(),
        ),
        check_vma=False,
    )
```

```python
import math

import jax
import jax.numpy as jnp
from jax import lax
from jax.experimental import pallas as pl
from jax.experimental.pallas import tpu as pltpu
from jax.sharding import PartitionSpec as P

D = 1152
HEADS = 4
HD = 256
FF = 6912
MICRO = 2


EPSILON = 1e-06
SCALE_FACTOR = 0.0625
THETA = 10000.0
NEGATIVE = -1e30


def shortened(x):

    def short(part):
        return part.astype(jnp.bfloat16) if part.dtype == jnp.float32 else part

    return jax.tree.map(short, x)


def swapped(block, axis, stride):
    count = lax.axis_size(axis)
    route = []
    for low in range(count):
        high = low | 1 << stride
        if high != low and high < count:
            route += [(low, high), (high, low)]
    return lax.ppermute(block, axis, route)


def norm_rows(values, gain):
    return values * lax.rsqrt(jnp.mean(values * values, -1, keepdims=True) + EPSILON) * gain


def rotate(values, cosine, sine):
    half = values.shape[-1] // 2
    first = values[..., :half]
    second = values[..., half:]
    return jnp.concatenate([first * cosine - second * sine, second * cosine + first * sine], -1)


def doc_tables(segments, validity, head_size):
    length = segments.shape[-1]
    places = jnp.arange(length, dtype=jnp.int32)
    same_doc = segments[..., :, None] == segments[..., None, :]
    earlier = places[None, :] < places[:, None]
    position = jnp.sum(jnp.logical_and(same_doc, earlier).astype(jnp.int32), -1)
    reach = places[None, :] <= places[:, None]
    usable = jnp.logical_or(validity[..., None, :] > 0, places[None, :] == places[:, None])
    allowed = jnp.logical_and(jnp.logical_and(same_doc, reach), usable)
    freqs = jnp.exp(
        jnp.arange(head_size // 2, dtype=jnp.float32) * (-2.0 * math.log(THETA) / head_size)
    )
    angles = position.astype(jnp.float32)[..., None] * freqs
    return (allowed, jnp.cos(angles), jnp.sin(angles))


def prepare(projected, head_gains, cosine, sine):
    width = HEADS * HD
    query = projected[..., :width].reshape(projected.shape[:-1] + (HEADS, HD))
    keys = projected[..., width : width + HD]
    values = projected[..., width + HD :]
    query = rotate(norm_rows(query, head_gains[0]), cosine[..., None, :], sine[..., None, :])
    keys = rotate(norm_rows(keys, head_gains[1]), cosine, sine)
    return (query, keys, values)


def across(left, piece):
    return lax.dot_general(
        left, piece, (((1,), (1,)), ((), ())), preferred_element_type=jnp.float32
    )


def over_rows(left, right):
    return lax.dot_general(
        left, right, (((0,), (0,)), ((), ())), preferred_element_type=jnp.float32
    )


def score_table(query_low, keys_low):
    return (
        jnp.einsum("qhd,kd->hqk", query_low, keys_low, preferred_element_type=jnp.float32)
        * SCALE_FACTOR
    )


def attend(query_low, keys_low, values_low, allowed):
    scores = score_table(query_low, keys_low)
    masked = jnp.where(allowed[None], scores, NEGATIVE)
    peak = jnp.max(masked, -1, keepdims=True)
    expo = jnp.where(allowed[None], jnp.exp(masked - peak), 0.0)
    totals = jnp.sum(expo, -1, keepdims=True)
    probs = expo / totals
    mixed = jnp.einsum(
        "hqk,kd->qhd", probs.astype(jnp.bfloat16), values_low, preferred_element_type=jnp.float32
    )
    return (mixed, peak + jnp.log(totals))


def attend_back(query_low, keys_low, values_low, allowed, log_sum, grad_low):
    scores = score_table(query_low, keys_low)
    probs = jnp.where(allowed[None], jnp.exp(scores - log_sum), 0.0)
    grad_probs = jnp.einsum("qhd,kd->hqk", grad_low, values_low, preferred_element_type=jnp.float32)
    grad_values = jnp.einsum(
        "hqk,qhd->kd", probs.astype(jnp.bfloat16), grad_low, preferred_element_type=jnp.float32
    )
    center = jnp.sum(grad_probs * probs, -1, keepdims=True)
    grad_scores = (probs * (grad_probs - center)).astype(jnp.bfloat16)
    grad_query = (
        jnp.einsum("hqk,kd->qhd", grad_scores, keys_low, preferred_element_type=jnp.float32)
        * SCALE_FACTOR
    )
    grad_keys = (
        jnp.einsum("hqk,qhd->kd", grad_scores, query_low, preferred_element_type=jnp.float32)
        * SCALE_FACTOR
    )
    return (grad_query, grad_keys, grad_values)


def gated(gate, upward):
    return jax.nn.gelu(gate, approximate=True) * upward


def general_shards(
    inputs,
    segment_ids,
    valid_mask,
    attn_in,
    attn_out,
    ffw_in,
    ffw_out,
    norm_gains,
    head_gains,
    cotangent,
):
    width = HEADS * HD
    kept_proj = []
    kept_normed_in = []
    kept_mixed = []
    kept_attn = []
    kept_gate = []
    kept_normed_mid = []
    kept_hidden = []
    kept_ffw = []
    gain_sums = jnp.zeros((4, D), jnp.float32)
    head_sums = jnp.zeros((2, HD), jnp.float32)
    stats = jnp.zeros((5,), jnp.float32)
    results = []
    input_grads = []
    for step in range(MICRO):
        full_in, full_out = (
            lax.all_gather(attn_in, "dp", axis=0, tiled=True),
            lax.all_gather(attn_out, "dp", axis=0, tiled=True),
        )
        full_ffin, full_ffout = (
            lax.all_gather(ffw_in, "dp", axis=0, tiled=True),
            lax.all_gather(ffw_out, "dp", axis=0, tiled=True),
        )
        stream = inputs[step, 0].astype(jnp.float32)
        length = stream.shape[0]
        allowed, cosine, sine = doc_tables(segment_ids[step, 0], valid_mask[step, 0], HD)
        normed_in = norm_rows(stream, norm_gains[0]).astype(jnp.bfloat16)
        projected = across(normed_in, full_in)
        query, keys, values = prepare(projected, head_gains, cosine, sine)
        query_low = query.astype(jnp.bfloat16)
        keys_low = keys.astype(jnp.bfloat16)
        values_low = values.astype(jnp.bfloat16)
        mixed, log_sum = attend(query_low, keys_low, values_low, allowed)
        mixed_low = mixed.reshape(length, width).astype(jnp.bfloat16)
        attn_proj = jnp.dot(mixed_low, full_out, preferred_element_type=jnp.float32)
        attn_branch = norm_rows(attn_proj, norm_gains[1])
        middle = stream + attn_branch
        normed_mid = norm_rows(middle, norm_gains[2]).astype(jnp.bfloat16)
        gate_up = across(normed_mid, full_ffin)
        gate = gate_up[:, :FF]
        upward = gate_up[:, FF:]
        hidden = gated(gate, upward).astype(jnp.bfloat16)
        ffw_proj = jnp.dot(hidden, full_ffout, preferred_element_type=jnp.float32)
        ffw_branch = norm_rows(ffw_proj, norm_gains[3])
        results.append((middle + ffw_branch).astype(jnp.bfloat16))
        weight = valid_mask[step, 0].astype(jnp.float32)
        sums = [
            jnp.sum(weight * jnp.sum(value * value, -1))
            for value in (stream, middle, attn_branch, ffw_branch)
        ]
        sums.append(jnp.sum(weight))
        stats = stats + jnp.stack(sums)
        upstream = cotangent[step, 0].astype(jnp.float32)
        _, back_ffw = jax.vjp(norm_rows, ffw_proj, norm_gains[3])
        grad_ffw_proj, gain_three = back_ffw(upstream)
        grad_ffw_low = grad_ffw_proj.astype(jnp.bfloat16)
        grad_hidden = across(grad_ffw_low, full_ffout)
        _, back_gated = jax.vjp(gated, gate, upward)
        grad_gate, grad_upward = back_gated(grad_hidden)
        grad_gate_up = jnp.concatenate([grad_gate, grad_upward], 1).astype(jnp.bfloat16)
        grad_normed_mid = jnp.dot(grad_gate_up, full_ffin, preferred_element_type=jnp.float32)
        _, back_mid = jax.vjp(norm_rows, middle, norm_gains[2])
        grad_mid_part, gain_two = back_mid(grad_normed_mid)
        grad_middle = upstream + grad_mid_part
        _, back_attn = jax.vjp(norm_rows, attn_proj, norm_gains[1])
        grad_attn_proj, gain_one = back_attn(grad_middle)
        grad_attn_low = grad_attn_proj.astype(jnp.bfloat16)
        grad_mixed = across(grad_attn_low, full_out)
        grad_mixed_low = grad_mixed.astype(jnp.bfloat16).reshape(length, HEADS, HD)
        grad_query, grad_keys, grad_values = attend_back(
            query_low, keys_low, values_low, allowed, log_sum, grad_mixed_low
        )
        _, back_prep = jax.vjp(
            lambda table, gains: prepare(table, gains, cosine, sine), projected, head_gains
        )
        grad_projected, grad_heads = back_prep((grad_query, grad_keys, grad_values))
        grad_proj_low = grad_projected.astype(jnp.bfloat16)
        grad_normed_in = jnp.dot(grad_proj_low, full_in, preferred_element_type=jnp.float32)
        _, back_in = jax.vjp(norm_rows, stream, norm_gains[0])
        grad_stream, gain_zero = back_in(grad_normed_in)
        input_grads.append(grad_middle + grad_stream)
        gain_sums = gain_sums + jnp.stack([gain_zero, gain_one, gain_two, gain_three])
        head_sums = head_sums + grad_heads
        kept_proj.append(grad_proj_low)
        kept_normed_in.append(normed_in)
        kept_mixed.append(mixed_low)
        kept_attn.append(grad_attn_low)
        kept_gate.append(grad_gate_up)
        kept_normed_mid.append(normed_mid)
        kept_hidden.append(hidden)
        kept_ffw.append(grad_ffw_low)
    pairs = [
        (jnp.concatenate(kept_proj, 0), jnp.concatenate(kept_normed_in, 0)),
        (jnp.concatenate(kept_mixed, 0), jnp.concatenate(kept_attn, 0)),
        (jnp.concatenate(kept_gate, 0), jnp.concatenate(kept_normed_mid, 0)),
        (jnp.concatenate(kept_hidden, 0), jnp.concatenate(kept_ffw, 0)),
    ]
    levels = lax.axis_size("dp").bit_length() - 1
    place = lax.axis_index("dp")
    top_bit = place >> levels - 1 & 1
    kept_parts = []
    sent_parts = []
    for left, right in pairs:
        half_cols = left.shape[1] // 2
        kept_parts.append(
            over_rows(lax.dynamic_slice_in_dim(left, top_bit * half_cols, half_cols, 1), right)
        )
        sent_parts.append(
            over_rows(
                lax.dynamic_slice_in_dim(left, (1 - top_bit) * half_cols, half_cols, 1), right
            )
        )
    current = tuple(kept_parts)
    outgoing = tuple(sent_parts)
    for level in range(levels):
        bit = levels - 1 - level
        arrived = jax.tree.map(
            lambda part, own: part.astype(own.dtype),
            swapped(shortened(outgoing), "dp", bit),
            outgoing,
        )
        current = tuple((mine + theirs for mine, theirs in zip(current, arrived)))
        if level + 1 < levels:
            next_bit = place >> bit - 1 & 1
            halves = [piece.shape[0] // 2 for piece in current]
            outgoing = tuple(
                (
                    lax.dynamic_slice_in_dim(piece, (1 - next_bit) * rows, rows, 0)
                    for piece, rows in zip(current, halves)
                )
            )
            current = tuple(
                (
                    lax.dynamic_slice_in_dim(piece, next_bit * rows, rows, 0)
                    for piece, rows in zip(current, halves)
                )
            )
    shard_in, shard_out, shard_ffin, shard_ffout = current
    gain_total, head_total, stat_total = lax.psum((gain_sums, head_sums, stats), "dp")
    rms_values = jnp.sqrt(stat_total[:4] / (stat_total[4] * D))
    layer_out = jnp.stack(results)[:, None]
    input_grad = jnp.stack(input_grads)[:, None]
    return (
        layer_out,
        input_grad,
        shard_in,
        shard_out,
        shard_ffin,
        shard_ffout,
        gain_total,
        head_total,
        rms_values,
    )


BLOCK = 216
PADDED = 224
WIDE = 2 * PADDED
MINE = 128
PAIR = 2 * MINE
VMEM_BYTES = 62 << 20
SQRT_2_OVER_PI = math.sqrt(2.0 / math.pi)
CUBIC = 0.044715
MESH = pl.DeviceIdType.MESH
LOW = jnp.bfloat16
F32 = jnp.float32


def spots():
    me = lax.axis_index("dp")
    return me, me // 8, me // 4 % 2, me // 2 % 2, me % 2


def at(z, y, x, c):
    return z * 8 + y * 4 + x * 2 + c


def z_peer(z, k):
    if k == 0:
        return z
    if k == 1:
        return z + 1 - 2 * (z % 2)
    if k == 2:
        return (z + 2) % 4
    return 3 - z


def greet_all(me):
    barrier = pltpu.get_barrier_semaphore()

    def one(step, carry):
        pl.semaphore_signal(barrier, inc=1, device_id=((me + step) % 32,), device_id_type=MESH)
        return carry

    lax.fori_loop(1, 32, one, 0)
    pl.semaphore_wait(barrier, 31)


def nt(left, right):
    return lax.dot_general(left, right, (((1,), (1,)), ((), ())), preferred_element_type=F32)


def nn(left, right):
    return lax.dot_general(left, right, (((1,), (0,)), ((), ())), preferred_element_type=F32)


def tn(left, right):
    return lax.dot_general(left, right, (((0,), (0,)), ((), ())), preferred_element_type=F32)


def norm_back(values, gain, upstream):
    scale = lax.rsqrt(jnp.mean(values * values, -1, keepdims=True) + EPSILON)
    normed = values * scale
    gain_grad = jnp.sum(upstream * normed, 0, keepdims=True)
    inner = upstream * gain
    grad = scale * (inner - normed * jnp.mean(inner * normed, -1, keepdims=True))
    return grad, gain_grad


def added(left, right):
    return (left.astype(F32) + right.astype(F32)).astype(LOW)


class Net:
    def __init__(self, send_sems, recv_sems, anyone):
        self.send_sems, self.recv_sems, self.anyone = send_sems, recv_sems, anyone
        self.used, self.sent, self.maybe = 0, [], []

    def slots(self, count):
        first = self.used
        self.used += count
        return first

    def copy(self, src, dst, send_slot, recv_slot, device):
        return pltpu.make_async_remote_copy(
            src_ref=src,
            dst_ref=dst,
            send_sem=self.send_sems.at[send_slot],
            recv_sem=self.recv_sems.at[recv_slot],
            device_id=(device,),
            device_id_type=MESH,
        )

    def send(self, src, dst, slot, device):
        copy = self.copy(src, dst, slot, slot, device)
        copy.start()
        self.sent.append(copy)

    def move(self, stays, src, dst, send_slot, recv_slot, device):
        copy = self.copy(src, dst, send_slot, recv_slot, device)

        @pl.when(stays)
        def _():
            pltpu.make_async_copy(src, dst, self.recv_sems.at[recv_slot]).start()

        @pl.when(jnp.logical_not(stays))
        def _():
            copy.start()

        self.maybe.append((stays, copy))

    def got(self, block, slot):
        self.copy(block, block, slot, slot, self.anyone).wait_recv()

    def flush(self, gone):
        for copy in gone:
            copy.wait_send()
        names = {id(copy) for copy in gone}
        self.sent = [copy for copy in self.sent if id(copy) not in names]

    def drain(self):
        self.flush(list(self.sent))
        for stays, copy in self.maybe:

            @pl.when(jnp.logical_not(stays))
            def _():
                copy.wait_send()

        self.maybe = []


def layer_kernel(*refs):
    (
        x_ref,
        seg_ref,
        valid_ref,
        ain,
        aout,
        gu,
        dn,
        gains,
        head_gains,
        cot,
        layer_out,
        input_grad,
        o_in,
        o_out,
        o_gu,
        o_dn,
        o_small,
        all_in,
        all_out,
        all_gu,
        all_dn,
        allow,
        cosine,
        sine,
        weight,
        normed_in,
        proj,
        heads,
        probs,
        mixed,
        attn_proj,
        middle,
        rows,
        total,
        got_mid,
        got_up,
        hidden_t,
        slope_gate,
        slope_up,
        gate_t,
        up_t,
        acc,
        keep,
        send_y,
        recv_y,
        send_z,
        recv_z,
        grad_middle,
        grad_attn,
        grad_heads,
        grad_proj,
        key_acc,
        d_in,
        a1,
        a2,
        a3,
        b1,
        b2,
        b3,
        g0,
        g1,
        g2,
        n0,
        n1,
        n2,
        small,
        local,
        send_sems,
        recv_sems,
    ) = refs
    me, z, y, x, c = spots()
    xp, yp, cp = at(z, y, 1 - x, c), at(z, 1 - y, x, c), at(z, y, x, 1 - c)
    z_peers = [at(z_peer(z, k), y, x, c) for k in range(4)]
    net = Net(send_sems, recv_sems, cp)
    keep_in = pltpu.make_async_copy(ain, all_in.at[z, y, x, c], local.at[0])
    keep_out = pltpu.make_async_copy(aout, all_out.at[z, y, x, c], local.at[1])
    keep_in.start()
    keep_out.start()
    greet_all(me)

    a_z, a_x, a_y, a_c = net.slots(4), net.slots(4), net.slots(4), net.slots(2)
    b_z, b_y, b_x, b_c = net.slots(4), net.slots(4), net.slots(4), net.slots(2)
    mine_in, mine_out = all_in.at[z, y, x, c], all_out.at[z, y, x, c]
    for k in (1, 2, 3):
        net.send(ain, mine_in, a_z + k, z_peers[k])
    net.send(ain, mine_in, a_x, xp)
    for k in (1, 2, 3):
        net.send(aout, mine_out, b_z + k, z_peers[k])
    net.send(aout, mine_out, b_y, yp)
    w_one, w_two, w_c = net.slots(3), net.slots(3), net.slots(2)
    kind, goal = z // 2, 2 * (z % 2) + x
    for h in range(2):
        net.move(
            jnp.logical_and(goal == z, x == h),
            gu.at[h],
            all_gu.at[kind, h, c],
            w_one + h,
            w_one + kind,
            at(goal, y, h, c),
        )
    net.move(
        z % 2 == y,
        dn,
        all_dn.at[c, x],
        w_one + 2,
        w_one + 2,
        at(2 * (z // 2) + y, z % 2, x, c),
    )

    seg = jnp.broadcast_to(seg_ref[...].astype(F32), (MINE, MINE))
    valid = jnp.broadcast_to(valid_ref[...].astype(F32), (MINE, MINE))
    row = lax.broadcasted_iota(jnp.int32, (MINE, MINE), 0)
    col = lax.broadcasted_iota(jnp.int32, (MINE, MINE), 1)
    length = MINE // MICRO
    same = jnp.logical_and(seg == seg.T, row // length == col // length)
    position = jnp.sum(jnp.where(jnp.logical_and(same, col < row), 1.0, 0.0), -1, keepdims=True)
    usable = jnp.logical_or(valid > 0.0, row == col)
    allow[...] = jnp.where(
        jnp.logical_and(jnp.logical_and(same, col <= row), usable), 1.0, 0.0
    )
    weight[...] = valid.T
    freqs = jnp.exp(col.astype(F32) * (-2.0 * math.log(THETA) / HD))
    angles = position * freqs
    cosine[...] = jnp.cos(angles)
    sine[...] = jnp.sin(angles)
    stream = x_ref[...].astype(F32)
    normed_in[...] = norm_rows(stream, gains[0:1, :]).astype(LOW)

    for k in (1, 2, 3):
        block = all_in.at[z_peer(z, k), y, x, c]
        net.got(block, a_z + k)
        net.send(block, block, a_x + k, xp)
        block = all_out.at[z_peer(z, k), y, x, c]
        net.got(block, b_z + k)
        net.send(block, block, b_y + k, yp)
    keep_in.wait()
    keep_out.wait()
    for k in range(4):
        there = z_peer(z, k)
        net.got(all_in.at[there, y, 1 - x, c], a_x + k)
        pair = all_in.at[there, y, :, c]
        net.send(pair, pair, a_y + k, yp)
        net.got(all_out.at[there, 1 - y, x, c], b_y + k)
        pair = all_out.at[there, :, x, c]
        net.send(pair, pair, b_x + k, xp)
    near = all_in.at[:, y, :, c]
    net.send(near, near, a_c, cp)
    near = all_out.at[:, :, x, c]
    net.send(near, near, b_c, cp)
    for t in range(2):
        block = all_gu.at[t, x, c]
        net.got(block, w_one + t)
        net.send(block, block, w_two + t, xp)
    block = all_dn.at[c, x]
    net.got(block, w_one + 2)
    net.send(block, block, w_two + 2, xp)
    for k in range(4):
        net.got(all_in.at[z_peer(z, k), 1 - y, :, c], a_y + k)
    far = all_in.at[:, 1 - y, :, c]
    net.send(far, far, a_c + 1, cp)
    net.got(all_in.at[:, y, :, 1 - c], a_c)
    net.got(all_in.at[:, 1 - y, :, 1 - c], a_c + 1)

    flat_in = all_in.reshape(HEADS * HD + 2 * HD, D)
    flat_out = all_out.reshape(HEADS * HD, D)
    half = HD // 2

    def rows_of(j):
        return pl.ds(pl.multiple_of(j * HD, HD), HD)

    def project(j, carry):
        table = nt(normed_in[...], flat_in[rows_of(j), :])
        proj[j] = table

        @pl.when(j < HEADS + 1)
        def _():
            turned = norm_rows(table, head_gains[pl.ds(j // HEADS, 1), :])
            first, second = turned[:, :half], turned[:, half:]
            heads[j, :, :half] = (first * cosine[...] - second * sine[...]).astype(LOW)
            heads[j, :, half:] = (second * cosine[...] + first * sine[...]).astype(LOW)

        @pl.when(j == HEADS + 1)
        def _():
            heads[j] = table.astype(LOW)

        return carry

    lax.fori_loop(0, HEADS + 2, project, 0)
    for k in range(4):
        net.got(all_out.at[z_peer(z, k), :, 1 - x, c], b_x + k)
    far = all_out.at[:, :, 1 - x, c]
    net.send(far, far, b_c + 1, cp)

    def attend_head(j, carry):
        seen = allow[...] > 0.0
        scores = nt(heads[j], heads[HEADS]) * SCALE_FACTOR
        masked = jnp.where(seen, scores, NEGATIVE)
        peak = jnp.max(masked, -1, keepdims=True)
        expo = jnp.where(seen, jnp.exp(masked - peak), 0.0)
        prob = expo / jnp.sum(expo, -1, keepdims=True)
        probs[j] = prob
        mixed[j] = nn(prob.astype(LOW), heads[HEADS + 1]).astype(LOW)
        return carry

    lax.fori_loop(0, HEADS, attend_head, 0)
    net.got(all_out.at[:, :, x, 1 - c], b_c)
    net.got(all_out.at[:, :, 1 - x, 1 - c], b_c + 1)

    attn_proj[...] = jnp.zeros((MINE, D), F32)

    def attn_out_head(j, carry):
        attn_proj[...] += nn(mixed[j], flat_out[rows_of(j), :])
        return carry

    lax.fori_loop(0, HEADS, attn_out_head, 0)
    branch = norm_rows(attn_proj[...], gains[1:2, :])
    mid = x_ref[...].astype(F32) + branch
    middle[...] = mid
    rows[0] = norm_rows(mid, gains[2:3, :]).astype(LOW)

    def counted(values):
        return jnp.sum(weight[:, 0:1] * jnp.sum(values * values, -1, keepdims=True))

    spot = lax.broadcasted_iota(jnp.int32, (1, D), 1)
    stats = jnp.where(spot == 4, jnp.sum(weight[:, 0:1]), 0.0)
    first_values = x_ref[...].astype(F32)
    stats += jnp.where(spot == 0, counted(first_values), 0.0)
    stats += jnp.where(spot == 1, counted(mid), 0.0)
    stats += jnp.where(spot == 2, counted(branch), 0.0)
    small[0] = jnp.zeros((8, D), F32)
    small[0, 5:6, :] = stats

    def moved(which, got_all, pairs, before_pairs):
        mine = rows.at[which]
        gz, gy, sy, sz = net.slots(4), net.slots(4), net.slots(4), net.slots(4)
        for k in (1, 2, 3):
            net.send(mine, got_all.at[z, y], gz + k, z_peers[k])
        net.send(mine, got_all.at[z, y], gy, yp)
        got_all[z, y] = rows[which]
        gathered = net.sent[-4:]

        def finish(k):
            net.got(recv_y.at[k], sy + k)
            if k == 0:
                total[...] = keep[0] + recv_y[0].astype(F32)
            else:
                send_z[k - 1] = (keep[k % 2] + recv_y[k].astype(F32)).astype(LOW)
                net.send(send_z.at[k - 1], recv_z.at[k - 1], sz + k, z_peers[k])

        for k in range(4):
            there = z_peer(z, k)
            if k < 3:
                block = got_all.at[z_peer(z, k + 1), y]
                net.got(block, gz + k + 1)
                net.send(block, block, gy + k + 1, yp)
                gathered.append(net.sent[-1])
            net.got(got_all.at[there, 1 - y], gy + k)
            if k == 0:
                before_pairs()
            pairs(there)
            if k:
                finish(k - 1)
            keep[k % 2] = acc[y]
            send_y[k] = acc[1 - y].astype(LOW)
            net.send(send_y.at[k], recv_y.at[k], sy + k, yp)

        def settle():
            for k in (1, 2, 3):
                net.got(recv_z.at[k - 1], sz + k)
                total[...] += recv_z[k - 1].astype(F32)

        return finish, settle, gathered

    w_gu, w_dn = all_gu.reshape(2, 2, WIDE, D), all_dn.reshape(2, WIDE, D)

    def columns(there):
        return pl.ds(pl.multiple_of(there * PAIR, PAIR), PAIR)

    def put(h, part):
        part = part.reshape(2, MINE, D)

        @pl.when(h == 0)
        def _():
            acc[...] = part

        @pl.when(h == 1)
        def _():
            acc[...] += part

    def forward_pairs(there):
        def one(h, carry):
            block = got_mid[there].reshape(PAIR, D)
            gate = nt(block, w_gu[0, h])
            upward = nt(block, w_gu[1, h])
            square = gate * gate
            tanh = jnp.tanh(SQRT_2_OVER_PI * gate * (1.0 + CUBIC * square))
            side = 0.5 * (1.0 + tanh)
            gelu = gate * side
            slope = side + 0.5 * gate * (1.0 - tanh * tanh) * (
                SQRT_2_OVER_PI * (1.0 + 3.0 * CUBIC * square)
            )
            low = (gelu * upward).astype(LOW)
            slope_gate[h, there] = (upward * slope).astype(LOW)
            slope_up[h, there] = gelu.astype(LOW)
            put(h, nn(low, w_dn[h]))
            hidden_t[h, :, columns(there)] = low.T
            return carry

        lax.fori_loop(0, 2, one, 0)

    def weights_here():
        for t in range(2):
            net.got(all_gu.at[t, 1 - x, c], w_two + t)
        net.got(all_dn.at[c, 1 - x], w_two + 2)
        net.send(all_gu.at[:, :, c], all_gu.at[:, :, c], w_c, cp)
        net.send(all_dn.at[c], all_dn.at[c], w_c + 1, cp)
        net.got(all_gu.at[:, :, 1 - c], w_c)
        net.got(all_dn.at[1 - c], w_c + 1)

    finish, settle, _ = moved(0, got_mid, forward_pairs, weights_here)
    finish(3)
    settle()
    net.drain()

    ffw_proj = total[...]
    branch = norm_rows(ffw_proj, gains[3:4, :])
    layer_out[...] = (middle[...] + branch).astype(LOW)
    small[0, 5:6, :] += jnp.where(spot == 3, counted(branch), 0.0)
    grad, gain_grad = norm_back(ffw_proj, gains[3:4, :], cot[...].astype(F32))
    small[0, 3:4, :] = gain_grad
    rows[1] = grad.astype(LOW)

    def backward_pairs(there):
        def one(h, carry):
            block = got_up[there].reshape(PAIR, D)
            back = nt(block, w_dn[h])
            gate = (back * slope_gate[h, there].astype(F32)).astype(LOW)
            upward = (back * slope_up[h, there].astype(F32)).astype(LOW)
            put(h, nn(gate, w_gu[0, h]) + nn(upward, w_gu[1, h]))
            gate_t[h, :, columns(there)] = gate.T
            up_t[h, :, columns(there)] = upward.T
            return carry

        lax.fori_loop(0, 2, one, 0)

    finish, settle, gathered = moved(1, got_up, backward_pairs, lambda: None)
    finish(3)

    step = 384
    flat_mid, flat_up = got_mid.reshape(8 * MINE, D), got_up.reshape(8 * MINE, D)

    def down_grads(i, carry):
        h, cols = i // 3, pl.ds(pl.multiple_of(i % 3 * step, 128), step)
        w_dn[h, :, cols] = nn(hidden_t[h], flat_up[:, cols]).astype(LOW)
        return carry

    lax.fori_loop(0, 6, down_grads, 0)
    d_c, d_x, d_home = net.slots(4), net.slots(4), net.slots(3)
    net.send(all_dn.at[1 - c], n0, d_c, cp)

    def gate_up_grads(i, carry):
        h, cols = i // 3, pl.ds(pl.multiple_of(i % 3 * step, 128), step)
        w_gu[0, h, :, cols] = nn(gate_t[h], flat_mid[:, cols]).astype(LOW)
        w_gu[1, h, :, cols] = nn(up_t[h], flat_mid[:, cols]).astype(LOW)
        return carry

    lax.fori_loop(0, 6, gate_up_grads, 0)
    net.send(all_gu.at[:, :, 1 - c], g0, d_c + 1, cp)
    settle()

    mid = middle[...]
    grad, gain_grad = norm_back(mid, gains[2:3, :], total[...])
    small[0, 2:3, :] = gain_grad
    grad_mid = cot[...].astype(F32) + grad
    grad_middle[...] = grad_mid
    grad, gain_grad = norm_back(attn_proj[...], gains[1:2, :], grad_mid)
    small[0, 1:2, :] = gain_grad
    grad_attn[...] = grad.astype(LOW)
    net.flush(gathered)
    d_out = got_up.reshape(4, 2, 2, 2, 32, D)
    a0 = got_mid.reshape(8 * MINE, D).at[pl.ds(0, 16 * 48)].reshape(4, 2, 2, 48, D)
    b0 = recv_y.reshape(4, 2, 2, 32, D)
    flat_d_out, flat_d_in = got_up.reshape(HEADS * HD, D), d_in.reshape(HEADS * HD + 2 * HD, D)

    def out_grads(j, carry):
        flat_d_out[rows_of(j), :] = tn(mixed[j], grad_attn[...]).astype(LOW)
        return carry

    lax.fori_loop(0, HEADS, out_grads, 0)
    net.got(n0, d_c)
    net.got(g0, d_c + 1)
    net.send(d_out.at[:, :, :, 1 - c], b0, d_c + 2, cp)

    for q in range(2):
        all_dn[c, q] = added(all_dn[c, q], n0[q])
    net.send(all_dn.at[c, 1 - x], n1, d_x, xp)
    for t in range(2):
        for h in range(2):
            all_gu[t, h, c] = added(all_gu[t, h, c], g0[t, h])
    net.send(all_gu.at[:, 1 - x, c], g1, d_x + 1, xp)

    grad_heads[...] = jnp.zeros((6, MINE, HD), F32)

    def head_back(j, carry):
        up = nt(grad_attn[...], flat_out[rows_of(j), :]).astype(LOW)
        prob = probs[j]
        grad_prob = nt(up, heads[HEADS + 1])
        grad_heads[HEADS + 1] += tn(prob.astype(LOW), up)
        center = jnp.sum(grad_prob * prob, -1, keepdims=True)
        grad_score = (prob * (grad_prob - center)).astype(LOW)
        grad_heads[j] = nn(grad_score, heads[HEADS]) * SCALE_FACTOR
        grad_heads[HEADS] += tn(grad_score, heads[j]) * SCALE_FACTOR
        return carry

    lax.fori_loop(0, HEADS, head_back, 0)
    key_acc[...] = jnp.zeros((2, HD), F32)

    def turn_back(j, carry):
        first, second = grad_heads[j, :, :half], grad_heads[j, :, half:]
        turned = jnp.concatenate(
            [
                first * cosine[...] + second * sine[...],
                second * cosine[...] - first * sine[...],
            ],
            -1,
        )
        which = pl.ds(j // HEADS, 1)
        grad, gain_grad = norm_back(proj[j], head_gains[which, :], turned)
        key_acc[which, :] += gain_grad
        grad_proj[j] = grad.astype(LOW)
        return carry

    lax.fori_loop(0, HEADS + 1, turn_back, 0)
    grad_proj[HEADS + 1] = grad_heads[HEADS + 1].astype(LOW)
    small[0, 4:5, 0:HD] = key_acc[0:1, :]
    small[0, 4:5, HD : 2 * HD] = key_acc[1:2, :]

    r_a, r_b, r_s = net.slots(8), net.slots(8), net.slots(8)
    net.got(b0, d_c + 2)

    def sum_out(i, carry):
        p, q, r = i // 4, i // 2 % 2, i % 2
        d_out[p, q, r, c] = added(d_out[p, q, r, c], b0[p, q, r])
        return carry

    lax.fori_loop(0, 16, sum_out, 0)
    net.send(d_out.at[:, :, 1 - x, c], b1, r_b, xp)

    def in_grads(j, carry):
        flat_d_in[rows_of(j), :] = tn(grad_proj[j], normed_in[...]).astype(LOW)
        return carry

    lax.fori_loop(0, HEADS + 2, in_grads, 0)
    net.send(d_in.at[:, :, :, 1 - c], a0, d_c + 3, cp)
    total[...] = jnp.zeros((MINE, D), F32)

    def in_back(j, carry):
        total[...] += nn(grad_proj[j], flat_in[rows_of(j), :])
        return carry

    lax.fori_loop(0, HEADS + 2, in_back, 0)
    grad, gain_grad = norm_back(x_ref[...].astype(F32), gains[0:1, :], total[...])
    small[0, 0:1, :] = gain_grad
    input_grad[...] = grad_middle[...] + grad
    net.send(small.at[0], small.at[1], r_s, cp)

    net.got(a0, d_c + 3)

    def sum_in(i, carry):
        p, q, r = i // 4, i // 2 % 2, i % 2
        d_in[p, q, r, c] = added(d_in[p, q, r, c], a0[p, q, r])
        return carry

    lax.fori_loop(0, 16, sum_in, 0)
    net.send(d_in.at[:, 1 - y, :, c], a1, r_a, yp)
    net.got(small.at[1], r_s)
    small[2] = small[0] + small[1]
    net.send(small.at[2], small.at[3], r_s + 1, xp)
    net.got(b1, r_b)

    def sum_out_two(i, carry):
        p, q = i // 2, i % 2
        d_out[p, q, x, c] = added(d_out[p, q, x, c], b1[p, q])
        return carry

    lax.fori_loop(0, 8, sum_out_two, 0)
    net.send(d_out.at[:, 1 - y, x, c], b2, r_b + 1, yp)

    net.got(n1, d_x)
    all_dn[c, x] = added(all_dn[c, x], n1[...])
    net.move(
        z % 2 == y, all_dn.at[c, x], n2, d_home + 2, d_home + 2, at(2 * (z // 2) + y, z % 2, x, c)
    )
    net.got(g1, d_x + 1)
    for t in range(2):
        all_gu[t, x, c] = added(all_gu[t, x, c], g1[t])
        source = z // 2 + 2 * t
        net.move(
            jnp.logical_and(source == z, z % 2 == x),
            all_gu.at[t, x, c],
            g2.at[x],
            d_home + t,
            d_home + x,
            at(source, y, z % 2, c),
        )

    net.got(a1, r_a)

    def sum_in_two(i, carry):
        p, q = i // 2, i % 2
        d_in[p, y, q, c] = added(d_in[p, y, q, c], a1[p, q])
        return carry

    lax.fori_loop(0, 8, sum_in_two, 0)
    net.send(d_in.at[:, y, 1 - x, c], a2, r_a + 1, xp)
    net.got(small.at[3], r_s + 1)
    small[4] = small[2] + small[3]
    net.send(small.at[4], small.at[5], r_s + 2, yp)
    net.got(b2, r_b + 1)
    for p in range(4):
        d_out[p, y, x, c] = added(d_out[p, y, x, c], b2[p])
    for k in (1, 2, 3):
        net.send(d_out.at[z_peer(z, k), y, x, c], b3.at[k - 1], r_b + 1 + k, z_peers[k])
    net.got(a2, r_a + 1)
    for p in range(4):
        d_in[p, y, x, c] = added(d_in[p, y, x, c], a2[p])
    for k in (1, 2, 3):
        net.send(d_in.at[z_peer(z, k), y, x, c], a3.at[k - 1], r_a + 1 + k, z_peers[k])
    net.got(small.at[5], r_s + 2)
    small[6] = small[4] + small[5]
    for k in (1, 2, 3):
        net.send(small.at[6], small.at[6 + k], r_s + 2 + k, z_peers[k])

    for k in (1, 2, 3):
        net.got(b3.at[k - 1], r_b + 1 + k)
    o_out[...] = (d_out[z, y, x, c].astype(F32) + b3[0].astype(F32)) + (
        b3[1].astype(F32) + b3[2].astype(F32)
    )
    net.got(n2, d_home + 2)
    o_dn[...] = n2[...].astype(F32)[:BLOCK]
    for k in (1, 2, 3):
        net.got(a3.at[k - 1], r_a + 1 + k)
    o_in[...] = (d_in[z, y, x, c].astype(F32) + a3[0].astype(F32)) + (
        a3[1].astype(F32) + a3[2].astype(F32)
    )
    for k in (1, 2, 3):
        net.got(small.at[6 + k], r_s + 2 + k)
    o_small[...] = (small[6] + small[7]) + (small[8] + small[9])
    for h in range(2):
        net.got(g2.at[h], d_home + h)
        o_gu[pl.ds(h * BLOCK, BLOCK), :] = g2[h].astype(F32)[:BLOCK]
    net.drain()


def vm(*shape):
    return pltpu.VMEM(shape, LOW)


def vf(*shape):
    return pltpu.VMEM(shape, F32)


def whole_layer(x, seg, valid, ain, aout, gu, dn, gains, head_gains, cot):
    vmem = pl.BlockSpec(memory_space=pltpu.VMEM)
    scratch = [
        vm(4, 2, 2, 2, 48, D),
        vm(4, 2, 2, 2, 32, D),
        vm(2, 2, 2, PADDED, D),
        vm(2, 2, PADDED, D),
        vf(MINE, MINE),
        vf(MINE, MINE),
        vf(MINE, MINE),
        vf(MINE, MINE),
        vm(MINE, D),
        vf(6, MINE, HD),
        vm(6, MINE, HD),
        vf(4, MINE, MINE),
        vm(4, MINE, HD),
        vf(MINE, D),
        vf(MINE, D),
        vm(2, MINE, D),
        vf(MINE, D),
        vm(4, 2, MINE, D),
        vm(4, 2, MINE, D),
        vm(2, WIDE, 8 * MINE),
        vm(2, 4, PAIR, WIDE),
        vm(2, 4, PAIR, WIDE),
        vm(2, WIDE, 8 * MINE),
        vm(2, WIDE, 8 * MINE),
        vf(2, MINE, D),
        vf(2, MINE, D),
        vm(4, MINE, D),
        vm(4, MINE, D),
        vm(3, MINE, D),
        vm(3, MINE, D),
        vf(MINE, D),
        vm(MINE, D),
        vf(6, MINE, HD),
        vm(6, MINE, HD),
        vf(2, HD),
        vm(4, 2, 2, 2, 48, D),
    ]
    for count in (48, 32):
        scratch += [vm(4, 2, count, D), vm(4, count, D), vm(3, count, D)]
    scratch += [vm(2, 2, PADDED, D), vm(2, PADDED, D), vm(2, PADDED, D)]
    scratch += [vm(2, PADDED, D), vm(PADDED, D), vm(PADDED, D)]
    scratch += [vf(10, 8, D)]
    scratch += [pltpu.SemaphoreType.DMA((2,))] + [pltpu.SemaphoreType.DMA((112,))] * 2
    return pl.pallas_call(
        layer_kernel,
        out_shape=(
            jax.ShapeDtypeStruct((MINE, D), LOW),
            jax.ShapeDtypeStruct((MINE, D), F32),
            jax.ShapeDtypeStruct((48, D), F32),
            jax.ShapeDtypeStruct((32, D), F32),
            jax.ShapeDtypeStruct((2 * BLOCK, D), F32),
            jax.ShapeDtypeStruct((BLOCK, D), F32),
            jax.ShapeDtypeStruct((8, D), F32),
        ),
        in_specs=[vmem] * 10,
        out_specs=(vmem,) * 7,
        scratch_shapes=scratch,
        compiler_params=pltpu.CompilerParams(
            collective_id=1, has_side_effects=True, vmem_limit_bytes=VMEM_BYTES
        ),
        name="layer",
    )(x, seg, valid, ain, aout, gu, dn, gains, head_gains, cot)


def padded_rows(rows):
    return jnp.pad(rows, ((0, 0), (0, PADDED - BLOCK), (0, 0)))


def split_shards(
    inputs,
    segment_ids,
    valid_mask,
    attn_in,
    attn_out,
    ffw_in,
    ffw_out,
    norm_gains,
    head_gains,
    cotangent,
):
    layer_out, input_grad, shard_in, shard_out, shard_gu, shard_dn, small = whole_layer(
        inputs.reshape(MINE, D),
        segment_ids.reshape(1, MINE),
        valid_mask.reshape(1, MINE),
        attn_in,
        attn_out,
        padded_rows(ffw_in.reshape(2, BLOCK, D)),
        padded_rows(ffw_out.reshape(1, BLOCK, D))[0],
        norm_gains,
        head_gains,
        cotangent.reshape(MINE, D),
    )
    return (
        layer_out.reshape(inputs.shape),
        input_grad.reshape(inputs.shape),
        shard_in,
        shard_out,
        shard_gu,
        shard_dn,
        small[:4],
        small[4, : 2 * HD].reshape(2, HD),
        jnp.sqrt(small[5, :4] / (small[5, 4] * D)),
    )


def solution(mesh):
    placed = (
        P(None, "dp", None, None),
        P(None, "dp", None),
        P(None, "dp", None),
        P("dp", None),
        P("dp", None),
        P("dp", None),
        P("dp", None),
        P(),
        P(),
        P(None, "dp", None, None),
    )
    return jax.shard_map(
        split_shards if mesh.shape["dp"] == 32 else general_shards,
        mesh=mesh,
        in_specs=placed,
        out_specs=(
            P(None, "dp", None, None),
            P(None, "dp", None, None),
            P("dp", None),
            P("dp", None),
            P("dp", None),
            P("dp", None),
            P(),
            P(),
            P(),
        ),
        check_vma=False,
    )
```

```python
import math

import jax
import jax.numpy as jnp
from jax import lax
from jax.experimental import pallas as pl
from jax.experimental.pallas import tpu as pltpu
from jax.sharding import PartitionSpec as P

D = 1152
HEADS = 4
HD = 256
FF = 6912
MICRO = 2


EPSILON = 1e-06
SCALE_FACTOR = 0.0625
THETA = 10000.0
NEGATIVE = -1e30


def shortened(x):

    def short(part):
        return part.astype(jnp.bfloat16) if part.dtype == jnp.float32 else part

    return jax.tree.map(short, x)


def swapped(block, axis, stride):
    count = lax.axis_size(axis)
    route = []
    for low in range(count):
        high = low | 1 << stride
        if high != low and high < count:
            route += [(low, high), (high, low)]
    return lax.ppermute(block, axis, route)


def norm_rows(values, gain):
    return values * lax.rsqrt(jnp.mean(values * values, -1, keepdims=True) + EPSILON) * gain


def rotate(values, cosine, sine):
    half = values.shape[-1] // 2
    first = values[..., :half]
    second = values[..., half:]
    return jnp.concatenate([first * cosine - second * sine, second * cosine + first * sine], -1)


def doc_tables(segments, validity, head_size):
    length = segments.shape[-1]
    places = jnp.arange(length, dtype=jnp.int32)
    same_doc = segments[..., :, None] == segments[..., None, :]
    earlier = places[None, :] < places[:, None]
    position = jnp.sum(jnp.logical_and(same_doc, earlier).astype(jnp.int32), -1)
    reach = places[None, :] <= places[:, None]
    usable = jnp.logical_or(validity[..., None, :] > 0, places[None, :] == places[:, None])
    allowed = jnp.logical_and(jnp.logical_and(same_doc, reach), usable)
    freqs = jnp.exp(
        jnp.arange(head_size // 2, dtype=jnp.float32) * (-2.0 * math.log(THETA) / head_size)
    )
    angles = position.astype(jnp.float32)[..., None] * freqs
    return (allowed, jnp.cos(angles), jnp.sin(angles))


def prepare(projected, head_gains, cosine, sine):
    width = HEADS * HD
    query = projected[..., :width].reshape(projected.shape[:-1] + (HEADS, HD))
    keys = projected[..., width : width + HD]
    values = projected[..., width + HD :]
    query = rotate(norm_rows(query, head_gains[0]), cosine[..., None, :], sine[..., None, :])
    keys = rotate(norm_rows(keys, head_gains[1]), cosine, sine)
    return (query, keys, values)


def across(left, piece):
    return lax.dot_general(
        left, piece, (((1,), (1,)), ((), ())), preferred_element_type=jnp.float32
    )


def over_rows(left, right):
    return lax.dot_general(
        left, right, (((0,), (0,)), ((), ())), preferred_element_type=jnp.float32
    )


def score_table(query_low, keys_low):
    return (
        jnp.einsum("qhd,kd->hqk", query_low, keys_low, preferred_element_type=jnp.float32)
        * SCALE_FACTOR
    )


def attend(query_low, keys_low, values_low, allowed):
    scores = score_table(query_low, keys_low)
    masked = jnp.where(allowed[None], scores, NEGATIVE)
    peak = jnp.max(masked, -1, keepdims=True)
    expo = jnp.where(allowed[None], jnp.exp(masked - peak), 0.0)
    totals = jnp.sum(expo, -1, keepdims=True)
    probs = expo / totals
    mixed = jnp.einsum(
        "hqk,kd->qhd", probs.astype(jnp.bfloat16), values_low, preferred_element_type=jnp.float32
    )
    return (mixed, peak + jnp.log(totals))


def attend_back(query_low, keys_low, values_low, allowed, log_sum, grad_low):
    scores = score_table(query_low, keys_low)
    probs = jnp.where(allowed[None], jnp.exp(scores - log_sum), 0.0)
    grad_probs = jnp.einsum("qhd,kd->hqk", grad_low, values_low, preferred_element_type=jnp.float32)
    grad_values = jnp.einsum(
        "hqk,qhd->kd", probs.astype(jnp.bfloat16), grad_low, preferred_element_type=jnp.float32
    )
    center = jnp.sum(grad_probs * probs, -1, keepdims=True)
    grad_scores = (probs * (grad_probs - center)).astype(jnp.bfloat16)
    grad_query = (
        jnp.einsum("hqk,kd->qhd", grad_scores, keys_low, preferred_element_type=jnp.float32)
        * SCALE_FACTOR
    )
    grad_keys = (
        jnp.einsum("hqk,qhd->kd", grad_scores, query_low, preferred_element_type=jnp.float32)
        * SCALE_FACTOR
    )
    return (grad_query, grad_keys, grad_values)


def gated(gate, upward):
    return jax.nn.gelu(gate, approximate=True) * upward


def general_shards(
    inputs,
    segment_ids,
    valid_mask,
    attn_in,
    attn_out,
    ffw_in,
    ffw_out,
    norm_gains,
    head_gains,
    cotangent,
):
    width = HEADS * HD
    kept_proj = []
    kept_normed_in = []
    kept_mixed = []
    kept_attn = []
    kept_gate = []
    kept_normed_mid = []
    kept_hidden = []
    kept_ffw = []
    gain_sums = jnp.zeros((4, D), jnp.float32)
    head_sums = jnp.zeros((2, HD), jnp.float32)
    stats = jnp.zeros((5,), jnp.float32)
    results = []
    input_grads = []
    for step in range(MICRO):
        full_in, full_out = (
            lax.all_gather(attn_in, "dp", axis=0, tiled=True),
            lax.all_gather(attn_out, "dp", axis=0, tiled=True),
        )
        full_ffin, full_ffout = (
            lax.all_gather(ffw_in, "dp", axis=0, tiled=True),
            lax.all_gather(ffw_out, "dp", axis=0, tiled=True),
        )
        stream = inputs[step, 0].astype(jnp.float32)
        length = stream.shape[0]
        allowed, cosine, sine = doc_tables(segment_ids[step, 0], valid_mask[step, 0], HD)
        normed_in = norm_rows(stream, norm_gains[0]).astype(jnp.bfloat16)
        projected = across(normed_in, full_in)
        query, keys, values = prepare(projected, head_gains, cosine, sine)
        query_low = query.astype(jnp.bfloat16)
        keys_low = keys.astype(jnp.bfloat16)
        values_low = values.astype(jnp.bfloat16)
        mixed, log_sum = attend(query_low, keys_low, values_low, allowed)
        mixed_low = mixed.reshape(length, width).astype(jnp.bfloat16)
        attn_proj = jnp.dot(mixed_low, full_out, preferred_element_type=jnp.float32)
        attn_branch = norm_rows(attn_proj, norm_gains[1])
        middle = stream + attn_branch
        normed_mid = norm_rows(middle, norm_gains[2]).astype(jnp.bfloat16)
        gate_up = across(normed_mid, full_ffin)
        gate = gate_up[:, :FF]
        upward = gate_up[:, FF:]
        hidden = gated(gate, upward).astype(jnp.bfloat16)
        ffw_proj = jnp.dot(hidden, full_ffout, preferred_element_type=jnp.float32)
        ffw_branch = norm_rows(ffw_proj, norm_gains[3])
        results.append((middle + ffw_branch).astype(jnp.bfloat16))
        weight = valid_mask[step, 0].astype(jnp.float32)
        sums = [
            jnp.sum(weight * jnp.sum(value * value, -1))
            for value in (stream, middle, attn_branch, ffw_branch)
        ]
        sums.append(jnp.sum(weight))
        stats = stats + jnp.stack(sums)
        upstream = cotangent[step, 0].astype(jnp.float32)
        _, back_ffw = jax.vjp(norm_rows, ffw_proj, norm_gains[3])
        grad_ffw_proj, gain_three = back_ffw(upstream)
        grad_ffw_low = grad_ffw_proj.astype(jnp.bfloat16)
        grad_hidden = across(grad_ffw_low, full_ffout)
        _, back_gated = jax.vjp(gated, gate, upward)
        grad_gate, grad_upward = back_gated(grad_hidden)
        grad_gate_up = jnp.concatenate([grad_gate, grad_upward], 1).astype(jnp.bfloat16)
        grad_normed_mid = jnp.dot(grad_gate_up, full_ffin, preferred_element_type=jnp.float32)
        _, back_mid = jax.vjp(norm_rows, middle, norm_gains[2])
        grad_mid_part, gain_two = back_mid(grad_normed_mid)
        grad_middle = upstream + grad_mid_part
        _, back_attn = jax.vjp(norm_rows, attn_proj, norm_gains[1])
        grad_attn_proj, gain_one = back_attn(grad_middle)
        grad_attn_low = grad_attn_proj.astype(jnp.bfloat16)
        grad_mixed = across(grad_attn_low, full_out)
        grad_mixed_low = grad_mixed.astype(jnp.bfloat16).reshape(length, HEADS, HD)
        grad_query, grad_keys, grad_values = attend_back(
            query_low, keys_low, values_low, allowed, log_sum, grad_mixed_low
        )
        _, back_prep = jax.vjp(
            lambda table, gains: prepare(table, gains, cosine, sine), projected, head_gains
        )
        grad_projected, grad_heads = back_prep((grad_query, grad_keys, grad_values))
        grad_proj_low = grad_projected.astype(jnp.bfloat16)
        grad_normed_in = jnp.dot(grad_proj_low, full_in, preferred_element_type=jnp.float32)
        _, back_in = jax.vjp(norm_rows, stream, norm_gains[0])
        grad_stream, gain_zero = back_in(grad_normed_in)
        input_grads.append(grad_middle + grad_stream)
        gain_sums = gain_sums + jnp.stack([gain_zero, gain_one, gain_two, gain_three])
        head_sums = head_sums + grad_heads
        kept_proj.append(grad_proj_low)
        kept_normed_in.append(normed_in)
        kept_mixed.append(mixed_low)
        kept_attn.append(grad_attn_low)
        kept_gate.append(grad_gate_up)
        kept_normed_mid.append(normed_mid)
        kept_hidden.append(hidden)
        kept_ffw.append(grad_ffw_low)
    pairs = [
        (jnp.concatenate(kept_proj, 0), jnp.concatenate(kept_normed_in, 0)),
        (jnp.concatenate(kept_mixed, 0), jnp.concatenate(kept_attn, 0)),
        (jnp.concatenate(kept_gate, 0), jnp.concatenate(kept_normed_mid, 0)),
        (jnp.concatenate(kept_hidden, 0), jnp.concatenate(kept_ffw, 0)),
    ]
    levels = lax.axis_size("dp").bit_length() - 1
    place = lax.axis_index("dp")
    top_bit = place >> levels - 1 & 1
    kept_parts = []
    sent_parts = []
    for left, right in pairs:
        half_cols = left.shape[1] // 2
        kept_parts.append(
            over_rows(lax.dynamic_slice_in_dim(left, top_bit * half_cols, half_cols, 1), right)
        )
        sent_parts.append(
            over_rows(
                lax.dynamic_slice_in_dim(left, (1 - top_bit) * half_cols, half_cols, 1), right
            )
        )
    current = tuple(kept_parts)
    outgoing = tuple(sent_parts)
    for level in range(levels):
        bit = levels - 1 - level
        arrived = jax.tree.map(
            lambda part, own: part.astype(own.dtype),
            swapped(shortened(outgoing), "dp", bit),
            outgoing,
        )
        current = tuple((mine + theirs for mine, theirs in zip(current, arrived)))
        if level + 1 < levels:
            next_bit = place >> bit - 1 & 1
            halves = [piece.shape[0] // 2 for piece in current]
            outgoing = tuple(
                (
                    lax.dynamic_slice_in_dim(piece, (1 - next_bit) * rows, rows, 0)
                    for piece, rows in zip(current, halves)
                )
            )
            current = tuple(
                (
                    lax.dynamic_slice_in_dim(piece, next_bit * rows, rows, 0)
                    for piece, rows in zip(current, halves)
                )
            )
    shard_in, shard_out, shard_ffin, shard_ffout = current
    gain_total, head_total, stat_total = lax.psum((gain_sums, head_sums, stats), "dp")
    rms_values = jnp.sqrt(stat_total[:4] / (stat_total[4] * D))
    layer_out = jnp.stack(results)[:, None]
    input_grad = jnp.stack(input_grads)[:, None]
    return (
        layer_out,
        input_grad,
        shard_in,
        shard_out,
        shard_ffin,
        shard_ffout,
        gain_total,
        head_total,
        rms_values,
    )


BLOCK = 216
PADDED = 224
WIDE = 2 * PADDED
MINE = 128
PART = 64
PAIR = 2 * MINE
VMEM_BYTES = 62 << 20
SQRT_2_OVER_PI = math.sqrt(2.0 / math.pi)
CUBIC = 0.044715
MESH = pl.DeviceIdType.MESH
LOW = jnp.bfloat16
F32 = jnp.float32


def spots():
    me = lax.axis_index("dp")
    return me, me // 8, me // 4 % 2, me // 2 % 2, me % 2


def at(z, y, x, c):
    return z * 8 + y * 4 + x * 2 + c


def z_peer(z, k):
    if k == 0:
        return z
    if k == 1:
        return z + 1 - 2 * (z % 2)
    if k == 2:
        return (z + 2) % 4
    return 3 - z


def greet_all(me):
    barrier = pltpu.get_barrier_semaphore()

    def one(step, carry):
        pl.semaphore_signal(barrier, inc=1, device_id=((me + step) % 32,), device_id_type=MESH)
        return carry

    lax.fori_loop(1, 32, one, 0)
    pl.semaphore_wait(barrier, 31)


def nt(left, right):
    return lax.dot_general(left, right, (((1,), (1,)), ((), ())), preferred_element_type=F32)


def nn(left, right):
    return lax.dot_general(left, right, (((1,), (0,)), ((), ())), preferred_element_type=F32)


def tn(left, right):
    return lax.dot_general(left, right, (((0,), (0,)), ((), ())), preferred_element_type=F32)


def norm_back(values, gain, upstream):
    scale = lax.rsqrt(jnp.mean(values * values, -1, keepdims=True) + EPSILON)
    normed = values * scale
    gain_grad = jnp.sum(upstream * normed, 0, keepdims=True)
    inner = upstream * gain
    grad = scale * (inner - normed * jnp.mean(inner * normed, -1, keepdims=True))
    return grad, gain_grad


def added(left, right):
    return (left.astype(F32) + right.astype(F32)).astype(LOW)


def stream_of(ref):
    return ref[...].reshape(MINE, D).astype(F32)


class Net:
    def __init__(self, send_sems, recv_sems, anyone):
        self.send_sems, self.recv_sems, self.anyone = send_sems, recv_sems, anyone
        self.used, self.sent, self.maybe = 0, [], []

    def slots(self, count):
        first = self.used
        self.used += count
        return first

    def copy(self, src, dst, send_slot, recv_slot, device):
        return pltpu.make_async_remote_copy(
            src_ref=src,
            dst_ref=dst,
            send_sem=self.send_sems.at[send_slot],
            recv_sem=self.recv_sems.at[recv_slot],
            device_id=(device,),
            device_id_type=MESH,
        )

    def send(self, src, dst, slot, device):
        copy = self.copy(src, dst, slot, slot, device)
        copy.start()
        self.sent.append(copy)

    def move(self, stays, src, dst, send_slot, recv_slot, device):
        copy = self.copy(src, dst, send_slot, recv_slot, device)

        @pl.when(stays)
        def _():
            pltpu.make_async_copy(src, dst, self.recv_sems.at[recv_slot]).start()

        @pl.when(jnp.logical_not(stays))
        def _():
            copy.start()

        self.maybe.append((stays, copy))

    def got(self, block, slot):
        self.copy(block, block, slot, slot, self.anyone).wait_recv()

    def flush(self, gone):
        for copy in gone:
            copy.wait_send()
        names = {id(copy) for copy in gone}
        self.sent = [copy for copy in self.sent if id(copy) not in names]

    def drain(self):
        self.flush(list(self.sent))
        self.settle_moves()

    def settle_moves(self):
        for stays, copy in self.maybe:

            @pl.when(jnp.logical_not(stays))
            def _():
                copy.wait_send()

        self.maybe = []


def layer_kernel(*refs):
    (
        x_ref,
        seg_ref,
        valid_ref,
        ain,
        aout,
        gu,
        dn,
        gains,
        head_gains,
        cot,
        layer_out,
        input_grad,
        o_in,
        o_out,
        o_gu,
        o_dn,
        o_gains,
        o_heads,
        o_rms,
        all_in,
        all_out,
        all_gu,
        all_dn,
        allow,
        cosine,
        sine,
        weight,
        normed_in,
        proj,
        heads,
        probs,
        mixed,
        attn_proj,
        middle,
        rows,
        total,
        got_mid,
        got_up,
        hidden_t,
        slope_gate,
        slope_up,
        acc,
        keep,
        send_y,
        recv_y,
        send_z,
        recv_z,
        grad_middle,
        grad_attn,
        grad_heads,
        grad_proj,
        key_acc,
        d_in,
        a1,
        a2,
        a3,
        b1,
        b2,
        b3,
        g0,
        g1,
        g2,
        n0,
        n1,
        n2,
        small,
        local,
        send_sems,
        recv_sems,
    ) = refs
    me, z, y, x, c = spots()
    xp, yp, cp = at(z, y, 1 - x, c), at(z, 1 - y, x, c), at(z, y, x, 1 - c)
    z_peers = [at(z_peer(z, k), y, x, c) for k in range(4)]
    net = Net(send_sems, recv_sems, cp)
    keep_in = pltpu.make_async_copy(ain, all_in.at[z, y, x, c], local.at[0])
    keep_out = pltpu.make_async_copy(aout, all_out.at[z, y, x, c], local.at[1])
    keep_in.start()
    keep_out.start()
    greet_all(me)

    class Spread:
        def __init__(self, own, full):
            self.own, self.full = own, full
            self.az, self.ax, self.ay, self.ac = (net.slots(4) for _ in range(4))

        def block(self, k):
            return self.full.at[z_peer(z, k), y, x, c]

        def start(self):
            net.send(self.own, self.block(0), self.az + 1, z_peers[1])
            net.send(self.own, self.block(0), self.ax, xp)
            net.send(self.own, self.block(0), self.az + 2, z_peers[2])

        def hop(self, k):
            block = self.block(k)
            net.got(block, self.az + k)
            if k == 2:
                net.send(block, block, self.az + 3, z_peers[1])
            net.send(block, block, self.ax + k, xp)

        def turn(self, k):
            there = z_peer(z, k)
            net.got(self.full.at[there, y, 1 - x, c], self.ax + k)
            pair = self.full.at[there, y, :, c]
            net.send(pair, pair, self.ay + k, yp)

        def near(self):
            part = self.full.at[:, y, :, c]
            net.send(part, part, self.ac, cp)

        def far(self):
            for k in range(4):
                net.got(self.full.at[z_peer(z, k), 1 - y, :, c], self.ay + k)
            part = self.full.at[:, 1 - y, :, c]
            net.send(part, part, self.ac + 1, cp)

        def whole(self):
            net.got(self.full.at[:, y, :, 1 - c], self.ac)
            net.got(self.full.at[:, 1 - y, :, 1 - c], self.ac + 1)

    into, outof = Spread(ain, all_in), Spread(aout, all_out)
    into.start()
    w_one, w_two, w_c = net.slots(3), net.slots(3), net.slots(2)
    kind, goal = z // 2, 2 * (z % 2) + x
    blank = jnp.zeros((PADDED - BLOCK, D), F32)
    for h in range(2):
        part = gu[pl.ds(h * BLOCK, BLOCK), :].astype(F32)
        g0[0, h] = jnp.concatenate([part, blank], 0).astype(LOW)
    n0[0] = jnp.concatenate([dn[...].astype(F32), blank], 0).astype(LOW)

    def rows_out():
        for h in range(2):
            net.move(
                jnp.logical_and(goal == z, x == h),
                g0.at[0, h],
                all_gu.at[kind, h, c],
                w_one + h,
                w_one + kind,
                at(goal, y, h, c),
            )
        net.move(
            z % 2 == y,
            n0.at[0],
            all_dn.at[c, x],
            w_one + 2,
            w_one + 2,
            at(2 * (z // 2) + y, z % 2, x, c),
        )

    into.hop(1)
    into.hop(2)
    outof.start()
    keep_in.wait()
    keep_out.wait()
    into.turn(0)
    into.turn(1)
    into.hop(3)
    rows_out()

    def along_lanes(ref):
        return jnp.concatenate([ref[0].astype(F32), ref[1].astype(F32)], 1)

    seg = jnp.broadcast_to(along_lanes(seg_ref), (MINE, MINE))
    valid = jnp.broadcast_to(along_lanes(valid_ref), (MINE, MINE))
    row = lax.broadcasted_iota(jnp.int32, (MINE, MINE), 0)
    col = lax.broadcasted_iota(jnp.int32, (MINE, MINE), 1)
    length = MINE // MICRO
    same = jnp.logical_and(seg == seg.T, row // length == col // length)
    position = jnp.sum(jnp.where(jnp.logical_and(same, col < row), 1.0, 0.0), -1, keepdims=True)
    usable = jnp.logical_or(valid > 0.0, row == col)
    allow[...] = jnp.where(
        jnp.logical_and(jnp.logical_and(same, col <= row), usable), 1.0, 0.0
    )
    weight[...] = valid.T
    freqs = jnp.exp(col.astype(F32) * (-2.0 * math.log(THETA) / HD))
    angles = position * freqs
    cosine[...] = jnp.cos(angles)
    sine[...] = jnp.sin(angles)
    stream = stream_of(x_ref)
    normed_in[...] = norm_rows(stream, gains[0:1, :]).astype(LOW)

    into.turn(2)
    outof.hop(1)
    outof.hop(2)
    into.turn(3)
    into.near()
    outof.turn(0)
    outof.turn(1)
    outof.hop(3)
    into.far()
    outof.turn(2)
    outof.turn(3)
    outof.near()
    into.whole()

    flat_in = all_in.reshape(HEADS * HD + 2 * HD, D)
    flat_out = all_out.reshape(HEADS * HD, D)
    half = HD // 2

    def rows_of(j):
        return pl.ds(pl.multiple_of(j * HD, HD), HD)

    def project(j, carry):
        table = nt(normed_in[...], flat_in[rows_of(j), :])
        proj[j] = table

        @pl.when(j < HEADS + 1)
        def _():
            turned = norm_rows(table, head_gains[pl.ds(j // HEADS, 1), :])
            first, second = turned[:, :half], turned[:, half:]
            heads[j, :, :half] = (first * cosine[...] - second * sine[...]).astype(LOW)
            heads[j, :, half:] = (second * cosine[...] + first * sine[...]).astype(LOW)

        @pl.when(j == HEADS + 1)
        def _():
            heads[j] = table.astype(LOW)

        return carry

    lax.fori_loop(0, HEADS + 2, project, 0)
    outof.far()

    def attend_head(j, carry):
        seen = allow[...] > 0.0
        scores = nt(heads[j], heads[HEADS]) * SCALE_FACTOR
        masked = jnp.where(seen, scores, NEGATIVE)
        peak = jnp.max(masked, -1, keepdims=True)
        expo = jnp.where(seen, jnp.exp(masked - peak), 0.0)
        prob = expo / jnp.sum(expo, -1, keepdims=True)
        probs[j] = prob
        mixed[j] = nn(prob.astype(LOW), heads[HEADS + 1]).astype(LOW)
        return carry

    lax.fori_loop(0, HEADS, attend_head, 0)
    for t in range(2):
        block = all_gu.at[t, x, c]
        net.got(block, w_one + t)
        net.send(block, block, w_two + t, xp)
    block = all_dn.at[c, x]
    net.got(block, w_one + 2)
    net.send(block, block, w_two + 2, xp)

    outof.whole()

    attn_proj[...] = jnp.zeros((MINE, D), F32)

    def attn_out_head(j, carry):
        attn_proj[...] += nn(mixed[j], flat_out[rows_of(j), :])
        return carry

    lax.fori_loop(0, HEADS, attn_out_head, 0)
    branch = norm_rows(attn_proj[...], gains[1:2, :])
    mid = stream_of(x_ref) + branch
    middle[...] = mid
    rows[0] = norm_rows(mid, gains[2:3, :]).astype(LOW).reshape(2, PART, D)

    def counted(values):
        return jnp.sum(weight[:, 0:1] * jnp.sum(values * values, -1, keepdims=True))

    spot = lax.broadcasted_iota(jnp.int32, (1, D), 1)
    stats = jnp.where(spot == 4, jnp.sum(weight[:, 0:1]), 0.0)
    first_values = stream_of(x_ref)
    stats += jnp.where(spot == 0, counted(first_values), 0.0)
    stats += jnp.where(spot == 1, counted(mid), 0.0)
    stats += jnp.where(spot == 2, counted(branch), 0.0)
    small[0] = jnp.zeros((8, D), F32)
    small[0, 5:6, :] = stats

    zh, zl = z // 2, z % 2
    w_gu, w_dn = all_gu.reshape(2, 2, WIDE, D), all_dn.reshape(2, WIDE, D)

    class Half:
        def __init__(self, which, half, got_all, compute):
            self.which, self.half, self.got_all, self.compute = which, half, got_all, compute
            self.az, self.ay, self.ry, self.rz = (net.slots(4) for _ in range(4))
            self.gathered = []

        def block(self, k, yy):
            there = z_peer(z, k)
            return self.got_all.at[self.half, there // 2, there % 2, yy]

        def pass_on(self, block, slot, device):
            net.send(block, block, slot, device)
            self.gathered.append(net.sent[-1])

        def start(self):
            own = rows.at[self.which, self.half]
            net.send(own, self.block(0, y), self.az + 1, z_peers[1])
            self.gathered.append(net.sent[-1])
            net.send(own, self.block(0, y), self.az + 2, z_peers[2])
            self.gathered.append(net.sent[-1])
            net.send(own, self.block(0, y), self.ay, yp)
            self.gathered.append(net.sent[-1])
            self.got_all[self.half, zh, zl, y] = rows[self.which, self.half]

        def hop(self, k):
            block = self.block(k, y)
            net.got(block, self.az + k)
            if k == 2:
                self.pass_on(block, self.az + 3, z_peers[1])
            self.pass_on(block, self.ay + k, yp)

        def group(self, g):
            for k in (2 * g, 2 * g + 1):
                net.got(self.block(k, 1 - y), self.ay + k)
            self.compute(self.half, zh if g == 0 else 1 - zh)
            keep[self.half, g] = acc[:, y]
            send_y[self.half, g] = acc[:, 1 - y].astype(LOW)
            net.send(send_y.at[self.half, g], recv_y.at[self.half, g], self.ry + g, yp)

        def fold(self, g):
            net.got(recv_y.at[self.half, g], self.ry + g)
            keep[self.half, g] += recv_y[self.half, g].astype(F32)
            send_z[self.half, g] = keep[self.half, g, 1 - zl].astype(LOW)
            net.send(send_z.at[self.half, g], recv_z.at[self.half, g], self.rz + g, z_peers[1])

        def cross(self):
            net.got(recv_z.at[self.half, 1], self.rz + 1)
            send_z[self.half, 2] = (
                keep[self.half, 1, zl] + recv_z[self.half, 1].astype(F32)
            ).astype(LOW)
            net.send(send_z.at[self.half, 2], recv_z.at[self.half, 2], self.rz + 2, z_peers[2])

        def done(self):
            net.got(recv_z.at[self.half, 0], self.rz)
            net.got(recv_z.at[self.half, 2], self.rz + 2)
            total[self.half] = (
                keep[self.half, 0, zl]
                + recv_z[self.half, 0].astype(F32)
                + recv_z[self.half, 2].astype(F32)
            )

    def columns(half, pair):
        return pl.ds(pl.multiple_of((half * 2 + pair) * PAIR, PAIR), PAIR)

    def put(h, part):
        part = part.reshape(2, 2, PART, D)

        @pl.when(h == 0)
        def _():
            acc[...] = part

        @pl.when(h == 1)
        def _():
            acc[...] += part

    def forward_pairs(half, pair):
        def one(h, carry):
            block = got_mid[half, pair].reshape(PAIR, D)
            gate = nt(block, w_gu[0, h])
            upward = nt(block, w_gu[1, h])
            square = gate * gate
            tanh = jnp.tanh(SQRT_2_OVER_PI * gate * (1.0 + CUBIC * square))
            side = 0.5 * (1.0 + tanh)
            gelu = gate * side
            slope = side + 0.5 * gate * (1.0 - tanh * tanh) * (
                SQRT_2_OVER_PI * (1.0 + 3.0 * CUBIC * square)
            )
            low = (gelu * upward).astype(LOW)
            slope_gate[h, half, pair] = (upward * slope).astype(LOW)
            slope_up[h, half, pair] = gelu.astype(LOW)
            put(h, nn(low, w_dn[h]))
            hidden_t[h, :, columns(half, pair)] = low.T
            return carry

        lax.fori_loop(0, 2, one, 0)

    def weights_here():
        for t in range(2):
            net.got(all_gu.at[t, 1 - x, c], w_two + t)
        net.got(all_dn.at[c, 1 - x], w_two + 2)
        net.settle_moves()
        net.send(all_gu.at[:, :, c], all_gu.at[:, :, c], w_c, cp)
        net.send(all_dn.at[c], all_dn.at[c], w_c + 1, cp)
        net.got(all_gu.at[:, :, 1 - c], w_c)
        net.got(all_dn.at[1 - c], w_c + 1)

    def forward_end(half):
        span = pl.ds(half * PART, PART)
        ffw_proj = total[half]
        branch = norm_rows(ffw_proj, gains[3:4, :])
        layer_out[half, 0] = (middle[span, :] + branch).astype(LOW)
        counts = jnp.sum(weight[span, 0:1] * jnp.sum(branch * branch, -1, keepdims=True))
        small[0, 5:6, :] += jnp.where(spot == 3, counts, 0.0)
        grad, gain_grad = norm_back(ffw_proj, gains[3:4, :], cot[half, 0].astype(F32))
        small[0, 3:4, :] += gain_grad
        rows[1, half] = grad.astype(LOW)

    def backward_pairs(half, pair):
        def one(h, carry):
            block = got_up[half, pair].reshape(PAIR, D)
            back = nt(block, w_dn[h])
            gate = (back * slope_gate[h, half, pair].astype(F32)).astype(LOW)
            upward = (back * slope_up[h, half, pair].astype(F32)).astype(LOW)
            put(h, nn(gate, w_gu[0, h]) + nn(upward, w_gu[1, h]))
            slope_gate[h, half, pair] = gate
            slope_up[h, half, pair] = upward
            return carry

        lax.fori_loop(0, 2, one, 0)

    one, two = Half(0, 0, got_mid, forward_pairs), Half(0, 1, got_mid, forward_pairs)
    one.start()
    one.hop(1)
    two.start()
    one.hop(2)
    weights_here()
    one.group(0)
    two.hop(1)
    one.hop(3)
    two.hop(2)
    one.group(1)
    one.fold(0)
    two.hop(3)
    two.group(0)
    one.fold(1)
    two.group(1)
    one.cross()
    two.fold(0)
    one.done()
    forward_end(0)
    three, four = Half(1, 0, got_up, backward_pairs), Half(1, 1, got_up, backward_pairs)
    three.start()
    two.fold(1)
    three.hop(1)
    two.cross()
    three.hop(2)
    two.done()
    forward_end(1)
    four.start()
    net.flush([copy for copy in net.sent if not any(copy is other for other in three.gathered + four.gathered)])
    three.group(0)
    four.hop(1)
    three.hop(3)
    four.hop(2)
    three.group(1)
    three.fold(0)
    four.hop(3)
    four.group(0)
    three.fold(1)

    step = 384
    flat_mid, flat_up = got_mid.reshape(8 * MINE, D), got_up.reshape(8 * MINE, D)

    four.group(1)
    three.cross()
    four.fold(0)

    def down_grads(i, carry):
        h, cols = i // 3, pl.ds(pl.multiple_of(i % 3 * step, 128), step)
        w_dn[h, :, cols] = nn(hidden_t[h], flat_up[:, cols]).astype(LOW)
        return carry

    lax.fori_loop(0, 6, down_grads, 0)
    d_c, d_x, d_home = net.slots(5), net.slots(4), net.slots(3)
    net.send(all_dn.at[1 - c], n0, d_c, cp)
    four.fold(1)
    three.done()

    def gate_up_grads(t, h, slopes):
        hidden_t[h] = slopes[h].reshape(8 * MINE, WIDE).T

        def part(i, carry):
            cols = pl.ds(pl.multiple_of(i * step, 128), step)
            w_gu[t, h, :, cols] = nn(hidden_t[h], flat_mid[:, cols]).astype(LOW)
            return carry

        lax.fori_loop(0, 3, part, 0)

    for h in range(2):
        gate_up_grads(0, h, slope_gate)
    net.send(all_gu.at[0, :, 1 - c], g0.at[0], d_c + 1, cp)
    net.got(n0, d_c)
    for q in range(2):
        all_dn[c, q] = added(all_dn[c, q], n0[q])
    net.send(all_dn.at[c, 1 - x], n1, d_x, xp)
    four.cross()
    for h in range(2):
        gate_up_grads(1, h, slope_up)
    net.send(all_gu.at[1, :, 1 - c], g0.at[1], d_c + 2, cp)

    def share(t):
        net.got(g0.at[t], d_c + 1 + t)
        for h in range(2):
            all_gu[t, h, c] = added(all_gu[t, h, c], g0[t, h])
        net.send(all_gu.at[t, 1 - x, c], g1.at[t], d_x + 1 + t, xp)

    share(0)
    share(1)
    four.done()

    mid = middle[...]
    grad, gain_grad = norm_back(mid, gains[2:3, :], total[...].reshape(MINE, D))
    small[0, 2:3, :] = gain_grad
    grad_mid = stream_of(cot) + grad
    grad_middle[...] = grad_mid
    grad, gain_grad = norm_back(attn_proj[...], gains[1:2, :], grad_mid)
    small[0, 1:2, :] = gain_grad
    grad_attn[...] = grad.astype(LOW)
    net.flush(three.gathered + four.gathered)
    d_out = got_up.reshape(4, 2, 2, 2, 32, D)
    a0 = got_mid.reshape(8 * MINE, D).at[pl.ds(0, 16 * 48)].reshape(4, 2, 2, 48, D)
    b0 = recv_y.reshape(4, 2, 2, 32, D)
    flat_d_out, flat_d_in = got_up.reshape(HEADS * HD, D), d_in.reshape(HEADS * HD + 2 * HD, D)

    def out_grads(j, carry):
        flat_d_out[rows_of(j), :] = tn(mixed[j], grad_attn[...]).astype(LOW)
        return carry

    lax.fori_loop(0, HEADS, out_grads, 0)
    net.send(d_out.at[:, :, :, 1 - c], b0, d_c + 3, cp)

    def home_down():
        net.got(n1, d_x)
        all_dn[c, x] = added(all_dn[c, x], n1[...])
        net.move(
            z % 2 == y,
            all_dn.at[c, x],
            n2,
            d_home + 2,
            d_home + 2,
            at(2 * (z // 2) + y, z % 2, x, c),
        )

    def home_gate_up(t):
        net.got(g1.at[t], d_x + 1 + t)
        all_gu[t, x, c] = added(all_gu[t, x, c], g1[t])
        source = z // 2 + 2 * t
        net.move(
            jnp.logical_and(source == z, z % 2 == x),
            all_gu.at[t, x, c],
            g2.at[x],
            d_home + t,
            d_home + x,
            at(source, y, z % 2, c),
        )

    class Collect:
        def __init__(self, grads, core_in, y_in, x_in, z_in, core_slot):
            self.grads, self.core_in, self.y_in, self.x_in, self.z_in = (
                grads,
                core_in,
                y_in,
                x_in,
                z_in,
            )
            self.cs, self.ys, self.xs, self.zs = core_slot, net.slots(2), net.slots(2), net.slots(2)

        def cores(self):
            net.got(self.core_in, self.cs)
            for part, pair in enumerate((1 - zh, zh)):

                def one(i, carry):
                    p, q, r = 2 * pair + i // 4, i // 2 % 2, i % 2
                    self.grads[p, q, r, c] = added(self.grads[p, q, r, c], self.core_in[p, q, r])
                    return carry

                lax.fori_loop(0, 8, one, 0)
                both = pl.ds(2 * pair, 2)
                net.send(
                    self.grads.at[both, 1 - y, :, c], self.y_in.at[part], self.ys + part, yp
                )

        def ys_in(self, part):
            pair = (1 - zh, zh)[part]
            net.got(self.y_in.at[part], self.ys + part)

            def one(i, carry):
                p, q = i // 2, i % 2
                there = 2 * pair + p
                self.grads[there, y, q, c] = added(
                    self.grads[there, y, q, c], self.y_in[part, p, q]
                )
                return carry

            lax.fori_loop(0, 4, one, 0)
            net.send(
                self.grads.at[pl.ds(2 * pair, 2), y, 1 - x, c],
                self.x_in.at[part],
                self.xs + part,
                xp,
            )

        def xs_in(self, part):
            pair = (1 - zh, zh)[part]
            net.got(self.x_in.at[part], self.xs + part)
            for p in range(2):
                there = 2 * pair + p
                self.grads[there, y, x, c] = added(
                    self.grads[there, y, x, c], self.x_in[part, p]
                )
            net.send(
                self.grads.at[2 * pair + 1 - zl, y, x, c],
                self.z_in.at[part],
                self.zs + part,
                z_peers[1],
            )

        def cross(self, slot):
            net.got(self.z_in.at[0], self.zs)
            there = 2 * (1 - zh) + zl
            self.grads[there, y, x, c] = added(self.grads[there, y, x, c], self.z_in[0])
            net.send(self.grads.at[there, y, x, c], self.z_in.at[2], slot, z_peers[2])

        def done(self, slot, result):
            net.got(self.z_in.at[1], self.zs + 1)
            net.got(self.z_in.at[2], slot)
            result[...] = (
                self.grads[z, y, x, c].astype(F32)
                + self.z_in[1].astype(F32)
                + self.z_in[2].astype(F32)
            )

    r_s, r_z = net.slots(8), net.slots(2)
    outs = Collect(d_out, b0, b1, b2, b3, d_c + 3)
    ins = Collect(d_in, a0, a1, a2, a3, d_c + 4)

    grad_heads[...] = jnp.zeros((6, MINE, HD), F32)

    def head_back(j, carry):
        up = nt(grad_attn[...], flat_out[rows_of(j), :]).astype(LOW)
        prob = probs[j]
        grad_prob = nt(up, heads[HEADS + 1])
        grad_heads[HEADS + 1] += tn(prob.astype(LOW), up)
        center = jnp.sum(grad_prob * prob, -1, keepdims=True)
        grad_score = (prob * (grad_prob - center)).astype(LOW)
        grad_heads[j] = nn(grad_score, heads[HEADS]) * SCALE_FACTOR
        grad_heads[HEADS] += tn(grad_score, heads[j]) * SCALE_FACTOR
        return carry

    lax.fori_loop(0, HEADS, head_back, 0)
    key_acc[...] = jnp.zeros((2, HD), F32)

    def turn_back(j, carry):
        first, second = grad_heads[j, :, :half], grad_heads[j, :, half:]
        turned = jnp.concatenate(
            [
                first * cosine[...] + second * sine[...],
                second * cosine[...] - first * sine[...],
            ],
            -1,
        )
        which = pl.ds(j // HEADS, 1)
        grad, gain_grad = norm_back(proj[j], head_gains[which, :], turned)
        key_acc[which, :] += gain_grad
        grad_proj[j] = grad.astype(LOW)
        return carry

    lax.fori_loop(0, HEADS + 1, turn_back, 0)
    grad_proj[HEADS + 1] = grad_heads[HEADS + 1].astype(LOW)
    small[0, 4:5, 0:HD] = key_acc[0:1, :]
    small[0, 4:5, HD : 2 * HD] = key_acc[1:2, :]

    outs.cores()

    def in_grads(j, carry):
        flat_d_in[rows_of(j), :] = tn(grad_proj[j], normed_in[...]).astype(LOW)
        return carry

    lax.fori_loop(0, HEADS + 2, in_grads, 0)
    net.send(d_in.at[:, :, :, 1 - c], a0, d_c + 4, cp)
    home_down()
    total[...] = jnp.zeros((2, PART, D), F32)

    def in_back(j, carry):
        total[...] += nn(grad_proj[j], flat_in[rows_of(j), :]).reshape(2, PART, D)
        return carry

    lax.fori_loop(0, HEADS + 2, in_back, 0)
    ins.cores()
    grad, gain_grad = norm_back(stream_of(x_ref), gains[0:1, :], total[...].reshape(MINE, D))
    small[0, 0:1, :] = gain_grad
    input_grad[...] = (grad_middle[...] + grad).reshape(2, 1, PART, D)
    net.send(small.at[0], small.at[1], r_s, cp)
    home_gate_up(0)
    outs.ys_in(0)
    outs.ys_in(1)
    net.got(small.at[1], r_s)
    small[2] = small[0] + small[1]
    net.send(small.at[2], small.at[3], r_s + 1, xp)
    ins.ys_in(0)
    home_gate_up(1)
    outs.xs_in(0)
    outs.xs_in(1)
    net.got(small.at[3], r_s + 1)
    small[4] = small[2] + small[3]
    net.send(small.at[4], small.at[5], r_s + 2, yp)
    ins.ys_in(1)
    outs.cross(r_z)
    ins.xs_in(0)
    ins.xs_in(1)
    net.got(small.at[5], r_s + 2)
    small[6] = small[4] + small[5]
    for k in (1, 2, 3):
        net.send(small.at[6], small.at[6 + k], r_s + 2 + k, z_peers[k])
    ins.cross(r_z + 1)
    outs.done(r_z, o_out)
    net.got(n2, d_home + 2)
    o_dn[...] = n2[...].astype(F32)[:BLOCK]
    for k in (1, 2, 3):
        net.got(small.at[6 + k], r_s + 2 + k)
    sums = (small[6] + small[7]) + (small[8] + small[9])
    o_gains[...] = sums[0:4, :]
    o_heads[...] = jnp.concatenate([sums[4:5, 0:HD], sums[4:5, HD : 2 * HD]], 0)
    scaled = sums[5:6, :]
    tokens = jnp.sum(jnp.where(spot == 4, scaled, 0.0), -1, keepdims=True)
    means = jnp.sqrt(scaled / (tokens * D))
    for i in range(4):
        o_rms[i] = jnp.sum(jnp.where(spot == i, means, 0.0))
    ins.done(r_z + 1, o_in)
    for h in range(2):
        net.got(g2.at[h], d_home + h)
        o_gu[pl.ds(h * BLOCK, BLOCK), :] = g2[h].astype(F32)[:BLOCK]
    net.drain()


def vm(*shape):
    return pltpu.VMEM(shape, LOW)


def vf(*shape):
    return pltpu.VMEM(shape, F32)


def whole_layer(x, seg, valid, ain, aout, gu, dn, gains, head_gains, cot):
    vmem = pl.BlockSpec(memory_space=pltpu.VMEM)
    scratch = [
        vm(4, 2, 2, 2, 48, D),
        vm(4, 2, 2, 2, 32, D),
        vm(2, 2, 2, PADDED, D),
        vm(2, 2, PADDED, D),
        vf(MINE, MINE),
        vf(MINE, MINE),
        vf(MINE, MINE),
        vf(MINE, MINE),
        vm(MINE, D),
        vf(6, MINE, HD),
        vm(6, MINE, HD),
        vf(4, MINE, MINE),
        vm(4, MINE, HD),
        vf(MINE, D),
        vf(MINE, D),
        vm(2, 2, PART, D),
        vf(2, PART, D),
        vm(2, 2, 2, 2, PART, D),
        vm(2, 2, 2, 2, PART, D),
        vm(2, WIDE, 8 * MINE),
        vm(2, 2, 2, PAIR, WIDE),
        vm(2, 2, 2, PAIR, WIDE),
        vf(2, 2, PART, D),
        vf(2, 2, 2, PART, D),
        vm(2, 2, 2, PART, D),
        vm(2, 2, 2, PART, D),
        vm(2, 3, PART, D),
        vm(2, 3, PART, D),
        vf(MINE, D),
        vm(MINE, D),
        vf(6, MINE, HD),
        vm(6, MINE, HD),
        vf(2, HD),
        vm(4, 2, 2, 2, 48, D),
    ]
    for count in (48, 32):
        scratch += [vm(2, 2, 2, count, D), vm(2, 2, count, D), vm(3, count, D)]
    scratch += [vm(2, 2, PADDED, D), vm(2, PADDED, D), vm(2, PADDED, D)]
    scratch += [vm(2, PADDED, D), vm(PADDED, D), vm(PADDED, D)]
    scratch += [vf(10, 8, D)]
    scratch += [pltpu.SemaphoreType.DMA((2,))] + [pltpu.SemaphoreType.DMA((144,))] * 2
    return pl.pallas_call(
        layer_kernel,
        out_shape=(
            jax.ShapeDtypeStruct((2, 1, PART, D), LOW),
            jax.ShapeDtypeStruct((2, 1, PART, D), F32),
            jax.ShapeDtypeStruct((48, D), F32),
            jax.ShapeDtypeStruct((32, D), F32),
            jax.ShapeDtypeStruct((2 * BLOCK, D), F32),
            jax.ShapeDtypeStruct((BLOCK, D), F32),
            jax.ShapeDtypeStruct((4, D), F32),
            jax.ShapeDtypeStruct((2, HD), F32),
            jax.ShapeDtypeStruct((4,), F32),
        ),
        in_specs=[vmem] * 10,
        out_specs=(vmem,) * 8 + (pl.BlockSpec(memory_space=pltpu.SMEM),),
        scratch_shapes=scratch,
        compiler_params=pltpu.CompilerParams(
            collective_id=1, has_side_effects=True, vmem_limit_bytes=VMEM_BYTES
        ),
        name="layer",
    )(x, seg, valid, ain, aout, gu, dn, gains, head_gains, cot)


def copy_kernel(*refs):
    count = (len(refs) - 2) // 3
    given, made, held = refs[:count], refs[count : 2 * count], refs[2 * count : 3 * count]
    into = [pltpu.make_async_copy(a, b, refs[-2].at[i]) for i, (a, b) in enumerate(zip(given, held))]
    out = [pltpu.make_async_copy(a, b, refs[-1].at[i]) for i, (a, b) in enumerate(zip(held, made))]
    for copy in into:
        copy.start()
    for first, second in zip(into, out):
        first.wait()
        second.start()
    for copy in out:
        copy.wait()


def copied(arrays):
    place = pl.BlockSpec(memory_space=pl.ANY)
    return pl.pallas_call(
        copy_kernel,
        out_shape=tuple(jax.ShapeDtypeStruct(array.shape, array.dtype) for array in arrays),
        in_specs=[place] * len(arrays),
        out_specs=(place,) * len(arrays),
        scratch_shapes=[pltpu.VMEM(array.shape, array.dtype) for array in arrays]
        + [pltpu.SemaphoreType.DMA((len(arrays),))] * 2,
        name="results",
    )(*arrays)


def split_shards(
    inputs,
    segment_ids,
    valid_mask,
    attn_in,
    attn_out,
    ffw_in,
    ffw_out,
    norm_gains,
    head_gains,
    cotangent,
):
    results = whole_layer(
        inputs,
        segment_ids,
        valid_mask,
        attn_in,
        attn_out,
        ffw_in,
        ffw_out,
        norm_gains,
        head_gains,
        cotangent,
    )
    return copied(results[:-1]) + results[-1:]


def solution(mesh):
    placed = (
        P(None, "dp", None, None),
        P(None, "dp", None),
        P(None, "dp", None),
        P("dp", None),
        P("dp", None),
        P("dp", None),
        P("dp", None),
        P(),
        P(),
        P(None, "dp", None, None),
    )
    return jax.shard_map(
        split_shards if mesh.shape["dp"] == 32 else general_shards,
        mesh=mesh,
        in_specs=placed,
        out_specs=(
            P(None, "dp", None, None),
            P(None, "dp", None, None),
            P("dp", None),
            P("dp", None),
            P("dp", None),
            P("dp", None),
            P(),
            P(),
            P(),
        ),
        check_vma=False,
    )
```

```python
import math

import jax
import jax.numpy as jnp
from jax import lax
from jax.experimental import pallas as pl
from jax.experimental.pallas import tpu as pltpu
from jax.sharding import PartitionSpec as P

D = 1152
HEADS = 4
HD = 256
FF = 6912
MICRO = 2


EPSILON = 1e-06
SCALE_FACTOR = 0.0625
THETA = 10000.0
NEGATIVE = -1e30


def shortened(x):

    def short(part):
        return part.astype(jnp.bfloat16) if part.dtype == jnp.float32 else part

    return jax.tree.map(short, x)


def swapped(block, axis, stride):
    count = lax.axis_size(axis)
    route = []
    for low in range(count):
        high = low | 1 << stride
        if high != low and high < count:
            route += [(low, high), (high, low)]
    return lax.ppermute(block, axis, route)


def norm_rows(values, gain):
    return values * lax.rsqrt(jnp.mean(values * values, -1, keepdims=True) + EPSILON) * gain


def rotate(values, cosine, sine):
    half = values.shape[-1] // 2
    first = values[..., :half]
    second = values[..., half:]
    return jnp.concatenate([first * cosine - second * sine, second * cosine + first * sine], -1)


def doc_tables(segments, validity, head_size):
    length = segments.shape[-1]
    places = jnp.arange(length, dtype=jnp.int32)
    same_doc = segments[..., :, None] == segments[..., None, :]
    earlier = places[None, :] < places[:, None]
    position = jnp.sum(jnp.logical_and(same_doc, earlier).astype(jnp.int32), -1)
    reach = places[None, :] <= places[:, None]
    usable = jnp.logical_or(validity[..., None, :] > 0, places[None, :] == places[:, None])
    allowed = jnp.logical_and(jnp.logical_and(same_doc, reach), usable)
    freqs = jnp.exp(
        jnp.arange(head_size // 2, dtype=jnp.float32) * (-2.0 * math.log(THETA) / head_size)
    )
    angles = position.astype(jnp.float32)[..., None] * freqs
    return (allowed, jnp.cos(angles), jnp.sin(angles))


def prepare(projected, head_gains, cosine, sine):
    width = HEADS * HD
    query = projected[..., :width].reshape(projected.shape[:-1] + (HEADS, HD))
    keys = projected[..., width : width + HD]
    values = projected[..., width + HD :]
    query = rotate(norm_rows(query, head_gains[0]), cosine[..., None, :], sine[..., None, :])
    keys = rotate(norm_rows(keys, head_gains[1]), cosine, sine)
    return (query, keys, values)


def across(left, piece):
    return lax.dot_general(
        left, piece, (((1,), (1,)), ((), ())), preferred_element_type=jnp.float32
    )


def over_rows(left, right):
    return lax.dot_general(
        left, right, (((0,), (0,)), ((), ())), preferred_element_type=jnp.float32
    )


def score_table(query_low, keys_low):
    return (
        jnp.einsum("qhd,kd->hqk", query_low, keys_low, preferred_element_type=jnp.float32)
        * SCALE_FACTOR
    )


def attend(query_low, keys_low, values_low, allowed):
    scores = score_table(query_low, keys_low)
    masked = jnp.where(allowed[None], scores, NEGATIVE)
    peak = jnp.max(masked, -1, keepdims=True)
    expo = jnp.where(allowed[None], jnp.exp(masked - peak), 0.0)
    totals = jnp.sum(expo, -1, keepdims=True)
    probs = expo / totals
    mixed = jnp.einsum(
        "hqk,kd->qhd", probs.astype(jnp.bfloat16), values_low, preferred_element_type=jnp.float32
    )
    return (mixed, peak + jnp.log(totals))


def attend_back(query_low, keys_low, values_low, allowed, log_sum, grad_low):
    scores = score_table(query_low, keys_low)
    probs = jnp.where(allowed[None], jnp.exp(scores - log_sum), 0.0)
    grad_probs = jnp.einsum("qhd,kd->hqk", grad_low, values_low, preferred_element_type=jnp.float32)
    grad_values = jnp.einsum(
        "hqk,qhd->kd", probs.astype(jnp.bfloat16), grad_low, preferred_element_type=jnp.float32
    )
    center = jnp.sum(grad_probs * probs, -1, keepdims=True)
    grad_scores = (probs * (grad_probs - center)).astype(jnp.bfloat16)
    grad_query = (
        jnp.einsum("hqk,kd->qhd", grad_scores, keys_low, preferred_element_type=jnp.float32)
        * SCALE_FACTOR
    )
    grad_keys = (
        jnp.einsum("hqk,qhd->kd", grad_scores, query_low, preferred_element_type=jnp.float32)
        * SCALE_FACTOR
    )
    return (grad_query, grad_keys, grad_values)


def gated(gate, upward):
    return jax.nn.gelu(gate, approximate=True) * upward


def general_shards(
    inputs,
    segment_ids,
    valid_mask,
    attn_in,
    attn_out,
    ffw_in,
    ffw_out,
    norm_gains,
    head_gains,
    cotangent,
):
    width = HEADS * HD
    kept_proj = []
    kept_normed_in = []
    kept_mixed = []
    kept_attn = []
    kept_gate = []
    kept_normed_mid = []
    kept_hidden = []
    kept_ffw = []
    gain_sums = jnp.zeros((4, D), jnp.float32)
    head_sums = jnp.zeros((2, HD), jnp.float32)
    stats = jnp.zeros((5,), jnp.float32)
    results = []
    input_grads = []
    for step in range(MICRO):
        full_in, full_out = (
            lax.all_gather(attn_in, "dp", axis=0, tiled=True),
            lax.all_gather(attn_out, "dp", axis=0, tiled=True),
        )
        full_ffin, full_ffout = (
            lax.all_gather(ffw_in, "dp", axis=0, tiled=True),
            lax.all_gather(ffw_out, "dp", axis=0, tiled=True),
        )
        stream = inputs[step, 0].astype(jnp.float32)
        length = stream.shape[0]
        allowed, cosine, sine = doc_tables(segment_ids[step, 0], valid_mask[step, 0], HD)
        normed_in = norm_rows(stream, norm_gains[0]).astype(jnp.bfloat16)
        projected = across(normed_in, full_in)
        query, keys, values = prepare(projected, head_gains, cosine, sine)
        query_low = query.astype(jnp.bfloat16)
        keys_low = keys.astype(jnp.bfloat16)
        values_low = values.astype(jnp.bfloat16)
        mixed, log_sum = attend(query_low, keys_low, values_low, allowed)
        mixed_low = mixed.reshape(length, width).astype(jnp.bfloat16)
        attn_proj = jnp.dot(mixed_low, full_out, preferred_element_type=jnp.float32)
        attn_branch = norm_rows(attn_proj, norm_gains[1])
        middle = stream + attn_branch
        normed_mid = norm_rows(middle, norm_gains[2]).astype(jnp.bfloat16)
        gate_up = across(normed_mid, full_ffin)
        gate = gate_up[:, :FF]
        upward = gate_up[:, FF:]
        hidden = gated(gate, upward).astype(jnp.bfloat16)
        ffw_proj = jnp.dot(hidden, full_ffout, preferred_element_type=jnp.float32)
        ffw_branch = norm_rows(ffw_proj, norm_gains[3])
        results.append((middle + ffw_branch).astype(jnp.bfloat16))
        weight = valid_mask[step, 0].astype(jnp.float32)
        sums = [
            jnp.sum(weight * jnp.sum(value * value, -1))
            for value in (stream, middle, attn_branch, ffw_branch)
        ]
        sums.append(jnp.sum(weight))
        stats = stats + jnp.stack(sums)
        upstream = cotangent[step, 0].astype(jnp.float32)
        _, back_ffw = jax.vjp(norm_rows, ffw_proj, norm_gains[3])
        grad_ffw_proj, gain_three = back_ffw(upstream)
        grad_ffw_low = grad_ffw_proj.astype(jnp.bfloat16)
        grad_hidden = across(grad_ffw_low, full_ffout)
        _, back_gated = jax.vjp(gated, gate, upward)
        grad_gate, grad_upward = back_gated(grad_hidden)
        grad_gate_up = jnp.concatenate([grad_gate, grad_upward], 1).astype(jnp.bfloat16)
        grad_normed_mid = jnp.dot(grad_gate_up, full_ffin, preferred_element_type=jnp.float32)
        _, back_mid = jax.vjp(norm_rows, middle, norm_gains[2])
        grad_mid_part, gain_two = back_mid(grad_normed_mid)
        grad_middle = upstream + grad_mid_part
        _, back_attn = jax.vjp(norm_rows, attn_proj, norm_gains[1])
        grad_attn_proj, gain_one = back_attn(grad_middle)
        grad_attn_low = grad_attn_proj.astype(jnp.bfloat16)
        grad_mixed = across(grad_attn_low, full_out)
        grad_mixed_low = grad_mixed.astype(jnp.bfloat16).reshape(length, HEADS, HD)
        grad_query, grad_keys, grad_values = attend_back(
            query_low, keys_low, values_low, allowed, log_sum, grad_mixed_low
        )
        _, back_prep = jax.vjp(
            lambda table, gains: prepare(table, gains, cosine, sine), projected, head_gains
        )
        grad_projected, grad_heads = back_prep((grad_query, grad_keys, grad_values))
        grad_proj_low = grad_projected.astype(jnp.bfloat16)
        grad_normed_in = jnp.dot(grad_proj_low, full_in, preferred_element_type=jnp.float32)
        _, back_in = jax.vjp(norm_rows, stream, norm_gains[0])
        grad_stream, gain_zero = back_in(grad_normed_in)
        input_grads.append(grad_middle + grad_stream)
        gain_sums = gain_sums + jnp.stack([gain_zero, gain_one, gain_two, gain_three])
        head_sums = head_sums + grad_heads
        kept_proj.append(grad_proj_low)
        kept_normed_in.append(normed_in)
        kept_mixed.append(mixed_low)
        kept_attn.append(grad_attn_low)
        kept_gate.append(grad_gate_up)
        kept_normed_mid.append(normed_mid)
        kept_hidden.append(hidden)
        kept_ffw.append(grad_ffw_low)
    pairs = [
        (jnp.concatenate(kept_proj, 0), jnp.concatenate(kept_normed_in, 0)),
        (jnp.concatenate(kept_mixed, 0), jnp.concatenate(kept_attn, 0)),
        (jnp.concatenate(kept_gate, 0), jnp.concatenate(kept_normed_mid, 0)),
        (jnp.concatenate(kept_hidden, 0), jnp.concatenate(kept_ffw, 0)),
    ]
    levels = lax.axis_size("dp").bit_length() - 1
    place = lax.axis_index("dp")
    top_bit = place >> levels - 1 & 1
    kept_parts = []
    sent_parts = []
    for left, right in pairs:
        half_cols = left.shape[1] // 2
        kept_parts.append(
            over_rows(lax.dynamic_slice_in_dim(left, top_bit * half_cols, half_cols, 1), right)
        )
        sent_parts.append(
            over_rows(
                lax.dynamic_slice_in_dim(left, (1 - top_bit) * half_cols, half_cols, 1), right
            )
        )
    current = tuple(kept_parts)
    outgoing = tuple(sent_parts)
    for level in range(levels):
        bit = levels - 1 - level
        arrived = jax.tree.map(
            lambda part, own: part.astype(own.dtype),
            swapped(shortened(outgoing), "dp", bit),
            outgoing,
        )
        current = tuple((mine + theirs for mine, theirs in zip(current, arrived)))
        if level + 1 < levels:
            next_bit = place >> bit - 1 & 1
            halves = [piece.shape[0] // 2 for piece in current]
            outgoing = tuple(
                (
                    lax.dynamic_slice_in_dim(piece, (1 - next_bit) * rows, rows, 0)
                    for piece, rows in zip(current, halves)
                )
            )
            current = tuple(
                (
                    lax.dynamic_slice_in_dim(piece, next_bit * rows, rows, 0)
                    for piece, rows in zip(current, halves)
                )
            )
    shard_in, shard_out, shard_ffin, shard_ffout = current
    gain_total, head_total, stat_total = lax.psum((gain_sums, head_sums, stats), "dp")
    rms_values = jnp.sqrt(stat_total[:4] / (stat_total[4] * D))
    layer_out = jnp.stack(results)[:, None]
    input_grad = jnp.stack(input_grads)[:, None]
    return (
        layer_out,
        input_grad,
        shard_in,
        shard_out,
        shard_ffin,
        shard_ffout,
        gain_total,
        head_total,
        rms_values,
    )


BLOCK = 216
PADDED = 224
WIDE = 2 * PADDED
MINE = 128
PART = 64
PAIR = 2 * MINE
VMEM_BYTES = 62 << 20
SQRT_2_OVER_PI = math.sqrt(2.0 / math.pi)
CUBIC = 0.044715
MESH = pl.DeviceIdType.MESH
LOW = jnp.bfloat16
F32 = jnp.float32


def spots():
    me = lax.axis_index("dp")
    return me, me // 8, me // 4 % 2, me // 2 % 2, me % 2


def at(z, y, x, c):
    return z * 8 + y * 4 + x * 2 + c


def z_peer(z, k):
    if k == 0:
        return z
    if k == 1:
        return z + 1 - 2 * (z % 2)
    if k == 2:
        return (z + 2) % 4
    return 3 - z


def greet_all(me):
    barrier = pltpu.get_barrier_semaphore()

    def one(step, carry):
        pl.semaphore_signal(barrier, inc=1, device_id=((me + step) % 32,), device_id_type=MESH)
        return carry

    lax.fori_loop(1, 32, one, 0)
    pl.semaphore_wait(barrier, 31)


def nt(left, right):
    return lax.dot_general(left, right, (((1,), (1,)), ((), ())), preferred_element_type=F32)


def nn(left, right):
    return lax.dot_general(left, right, (((1,), (0,)), ((), ())), preferred_element_type=F32)


def tn(left, right):
    return lax.dot_general(left, right, (((0,), (0,)), ((), ())), preferred_element_type=F32)


def norm_back(values, gain, upstream):
    scale = lax.rsqrt(jnp.mean(values * values, -1, keepdims=True) + EPSILON)
    normed = values * scale
    gain_grad = jnp.sum(upstream * normed, 0, keepdims=True)
    inner = upstream * gain
    grad = scale * (inner - normed * jnp.mean(inner * normed, -1, keepdims=True))
    return grad, gain_grad


def added(left, right):
    return (left.astype(F32) + right.astype(F32)).astype(LOW)


def stream_of(ref):
    return ref[...].reshape(MINE, D).astype(F32)


class Net:
    def __init__(self, send_sems, recv_sems, anyone):
        self.send_sems, self.recv_sems, self.anyone = send_sems, recv_sems, anyone
        self.used, self.sent, self.maybe = 0, [], []

    def slots(self, count):
        first = self.used
        self.used += count
        return first

    def copy(self, src, dst, send_slot, recv_slot, device):
        return pltpu.make_async_remote_copy(
            src_ref=src,
            dst_ref=dst,
            send_sem=self.send_sems.at[send_slot],
            recv_sem=self.recv_sems.at[recv_slot],
            device_id=(device,),
            device_id_type=MESH,
        )

    def send(self, src, dst, slot, device):
        copy = self.copy(src, dst, slot, slot, device)
        copy.start()
        self.sent.append(copy)

    def move(self, stays, src, dst, send_slot, recv_slot, device):
        copy = self.copy(src, dst, send_slot, recv_slot, device)

        @pl.when(stays)
        def _():
            pltpu.make_async_copy(src, dst, self.recv_sems.at[recv_slot]).start()

        @pl.when(jnp.logical_not(stays))
        def _():
            copy.start()

        self.maybe.append((stays, copy))

    def got(self, block, slot):
        self.copy(block, block, slot, slot, self.anyone).wait_recv()

    def flush(self, gone):
        for copy in gone:
            copy.wait_send()
        names = {id(copy) for copy in gone}
        self.sent = [copy for copy in self.sent if id(copy) not in names]

    def drain(self):
        self.flush(list(self.sent))
        self.settle_moves()

    def settle_moves(self):
        for stays, copy in self.maybe:

            @pl.when(jnp.logical_not(stays))
            def _():
                copy.wait_send()

        self.maybe = []


def layer_kernel(*refs):
    (
        x_ref,
        seg_ref,
        valid_ref,
        ain,
        aout,
        gu,
        dn,
        gains,
        head_gains,
        cot,
        layer_out,
        input_grad,
        o_in,
        o_out,
        o_gu,
        o_dn,
        o_gains,
        o_heads,
        o_rms,
        all_in,
        all_out,
        all_gu,
        all_dn,
        allow,
        cosine,
        sine,
        weight,
        normed_in,
        proj,
        heads,
        probs,
        mixed,
        attn_proj,
        middle,
        rows,
        total,
        got_mid,
        got_up,
        hidden_t,
        slope_gate,
        slope_up,
        acc,
        keep,
        send_y,
        recv_y,
        send_z,
        recv_z,
        grad_middle,
        grad_attn,
        grad_heads,
        grad_proj,
        key_acc,
        d_in,
        a1,
        a2,
        a3,
        b1,
        b2,
        b3,
        g0,
        g1,
        g2,
        d_dn,
        n0,
        n1,
        n2,
        small,
        local,
        send_sems,
        recv_sems,
    ) = refs
    me, z, y, x, c = spots()
    xp, yp, cp = at(z, y, 1 - x, c), at(z, 1 - y, x, c), at(z, y, x, 1 - c)
    z_peers = [at(z_peer(z, k), y, x, c) for k in range(4)]
    net = Net(send_sems, recv_sems, cp)
    keep_in = pltpu.make_async_copy(ain, all_in.at[z, y, x, c], local.at[0])
    keep_out = pltpu.make_async_copy(aout, all_out.at[z, y, x, c], local.at[1])
    keep_in.start()
    keep_out.start()
    greet_all(me)

    class Spread:
        def __init__(self, own, full, x_first):
            self.own, self.full, self.x_first = own, full, x_first
            self.first, self.second = (xp, yp) if x_first else (yp, xp)
            self.az, self.ax, self.ay, self.ac = (net.slots(4) for _ in range(4))

        def block(self, k):
            return self.full.at[z_peer(z, k), y, x, c]

        def crossed(self, k):
            there = z_peer(z, k)
            return self.full.at[there, y, 1 - x, c] if self.x_first else self.full.at[there, 1 - y, x, c]

        def pair(self, there, own, core):
            if self.x_first:
                return self.full.at[there, y if own else 1 - y, :, core]
            return self.full.at[there, :, x if own else 1 - x, core]

        def start(self):
            net.send(self.own, self.block(0), self.az + 1, z_peers[1])
            net.send(self.own, self.block(0), self.ax, self.first)
            net.send(self.own, self.block(0), self.az + 2, z_peers[2])

        def hop(self, k):
            block = self.block(k)
            net.got(block, self.az + k)
            if k == 2:
                net.send(block, block, self.az + 3, z_peers[1])
            net.send(block, block, self.ax + k, self.first)

        def turn(self, k):
            net.got(self.crossed(k), self.ax + k)
            pair = self.pair(z_peer(z, k), True, c)
            net.send(pair, pair, self.ay + k, self.second)

        def near(self):
            part = self.pair(slice(None), True, c)
            net.send(part, part, self.ac, cp)

        def far(self):
            for k in range(4):
                net.got(self.pair(z_peer(z, k), False, c), self.ay + k)
            part = self.pair(slice(None), False, c)
            net.send(part, part, self.ac + 1, cp)

        def whole(self):
            net.got(self.pair(slice(None), True, 1 - c), self.ac)
            net.got(self.pair(slice(None), False, 1 - c), self.ac + 1)

    into, outof = Spread(ain, all_in, True), Spread(aout, all_out, False)
    into.start()
    w_one, w_two, w_c, w_d = net.slots(2), net.slots(2), net.slots(2), net.slots(2)
    v_x, v_one, v_c = net.slots(1), net.slots(2), net.slots(1)
    kind, goal = z // 2, 2 * (z % 2) + c
    blank = jnp.zeros((PADDED - BLOCK, D), F32)
    for h in range(2):
        part = gu[pl.ds(h * BLOCK, BLOCK), :].astype(F32)
        g0[0, h] = jnp.concatenate([part, blank], 0).astype(LOW)
    n0[0] = jnp.concatenate([dn[...].astype(F32), blank], 0).astype(LOW)

    def rows_out():
        for h in range(2):
            net.move(
                jnp.logical_and(goal == z, c == h),
                g0.at[0, h],
                all_gu.at[kind, h, x],
                w_one + h,
                w_one + kind,
                at(goal, y, x, h),
            )

    def rows_on(which):
        t = (kind, 1 - kind)[which]
        block = all_gu.at[t, c, x]
        net.got(block, w_one + t)
        net.send(block, block, w_two + which, xp)
        net.send(block, block, w_c + which, cp)

    def rows_across(which):
        block = all_gu.at[(kind, 1 - kind)[which], c, 1 - x]
        net.got(block, w_two + which)
        net.send(block, block, w_d + which, cp)

    def rows_whole():
        for which in range(2):
            t = (kind, 1 - kind)[which]
            net.got(all_gu.at[t, 1 - c, x], w_c + which)
            net.got(all_gu.at[t, 1 - c, 1 - x], w_d + which)
        net.got(all_dn.at[1 - c], v_c)

    net.send(n0.at[0], n0.at[1], v_x, xp)
    across_x = net.sent[-1]

    def down_out():
        net.got(n0.at[1], v_x)
        for other in range(2):
            block_x = 1 - x if other else x
            net.move(
                jnp.logical_and(z % 2 == block_x, z % 2 == y),
                n0.at[other],
                all_dn.at[c, y],
                v_one + other,
                v_one + y,
                at(2 * (z // 2) + block_x, z % 2, x, c),
            )

    def down_on():
        for q in range(2):
            net.got(all_dn.at[c, q], v_one + q)
        net.send(all_dn.at[c], all_dn.at[c], v_c, cp)

    rows_out()
    into.hop(1)
    into.hop(2)
    outof.start()
    keep_in.wait()
    keep_out.wait()
    into.turn(0)
    into.turn(1)
    into.hop(3)

    def along_lanes(ref):
        return jnp.concatenate([ref[0].astype(F32), ref[1].astype(F32)], 1)

    seg = jnp.broadcast_to(along_lanes(seg_ref), (MINE, MINE))
    valid = jnp.broadcast_to(along_lanes(valid_ref), (MINE, MINE))
    row = lax.broadcasted_iota(jnp.int32, (MINE, MINE), 0)
    col = lax.broadcasted_iota(jnp.int32, (MINE, MINE), 1)
    length = MINE // MICRO
    same = jnp.logical_and(seg == seg.T, row // length == col // length)
    position = jnp.sum(jnp.where(jnp.logical_and(same, col < row), 1.0, 0.0), -1, keepdims=True)
    usable = jnp.logical_or(valid > 0.0, row == col)
    allow[...] = jnp.where(
        jnp.logical_and(jnp.logical_and(same, col <= row), usable), 1.0, 0.0
    )
    weight[...] = valid.T
    freqs = jnp.exp(col.astype(F32) * (-2.0 * math.log(THETA) / HD))
    angles = position * freqs
    cosine[...] = jnp.cos(angles)
    sine[...] = jnp.sin(angles)
    stream = stream_of(x_ref)
    normed_in[...] = norm_rows(stream, gains[0:1, :]).astype(LOW)

    into.turn(2)
    outof.hop(1)
    outof.hop(2)
    into.turn(3)
    down_out()
    into.near()
    outof.turn(0)
    outof.turn(1)
    outof.hop(3)
    rows_on(0)
    into.far()
    outof.turn(2)
    outof.turn(3)
    outof.near()
    rows_on(1)
    into.whole()

    flat_in = all_in.reshape(HEADS * HD + 2 * HD, D)
    flat_out = all_out.reshape(HEADS * HD, D)
    half = HD // 2

    def rows_of(j):
        return pl.ds(pl.multiple_of(j * HD, HD), HD)

    def project(j, carry):
        table = nt(normed_in[...], flat_in[rows_of(j), :])
        proj[j] = table

        @pl.when(j < HEADS + 1)
        def _():
            turned = norm_rows(table, head_gains[pl.ds(j // HEADS, 1), :])
            first, second = turned[:, :half], turned[:, half:]
            heads[j, :, :half] = (first * cosine[...] - second * sine[...]).astype(LOW)
            heads[j, :, half:] = (second * cosine[...] + first * sine[...]).astype(LOW)

        @pl.when(j == HEADS + 1)
        def _():
            heads[j] = table.astype(LOW)

        return carry

    lax.fori_loop(0, HEADS + 2, project, 0)
    down_on()
    outof.far()

    def attend_head(j, carry):
        seen = allow[...] > 0.0
        scores = nt(heads[j], heads[HEADS]) * SCALE_FACTOR
        masked = jnp.where(seen, scores, NEGATIVE)
        peak = jnp.max(masked, -1, keepdims=True)
        expo = jnp.where(seen, jnp.exp(masked - peak), 0.0)
        prob = expo / jnp.sum(expo, -1, keepdims=True)
        probs[j] = prob
        mixed[j] = nn(prob.astype(LOW), heads[HEADS + 1]).astype(LOW)
        return carry

    lax.fori_loop(0, HEADS, attend_head, 0)
    rows_across(0)
    outof.whole()

    attn_proj[...] = jnp.zeros((MINE, D), F32)

    def attn_out_head(j, carry):
        attn_proj[...] += nn(mixed[j], flat_out[rows_of(j), :])
        return carry

    lax.fori_loop(0, HEADS, attn_out_head, 0)
    branch = norm_rows(attn_proj[...], gains[1:2, :])
    mid = stream_of(x_ref) + branch
    middle[...] = mid
    rows[0] = norm_rows(mid, gains[2:3, :]).astype(LOW).reshape(2, PART, D)

    def counted(values):
        return jnp.sum(weight[:, 0:1] * jnp.sum(values * values, -1, keepdims=True))

    spot = lax.broadcasted_iota(jnp.int32, (1, D), 1)
    stats = jnp.where(spot == 4, jnp.sum(weight[:, 0:1]), 0.0)
    first_values = stream_of(x_ref)
    stats += jnp.where(spot == 0, counted(first_values), 0.0)
    stats += jnp.where(spot == 1, counted(mid), 0.0)
    stats += jnp.where(spot == 2, counted(branch), 0.0)
    small[0] = jnp.zeros((8, D), F32)
    small[0, 5:6, :] = stats

    zh, zl = z // 2, z % 2
    w_gu, w_dn = all_gu.reshape(2, 2, WIDE, D), all_dn.reshape(2, WIDE, D)

    class Half:
        def __init__(self, which, half, got_all, compute):
            self.which, self.half, self.got_all, self.compute = which, half, got_all, compute
            self.az, self.ay, self.ry, self.rz = (net.slots(4) for _ in range(4))
            self.gathered, self.here = [], set()

        def block(self, k, yy):
            there = z_peer(z, k)
            return self.got_all.at[self.half, there // 2, there % 2, yy]

        def pass_on(self, block, slot, device):
            net.send(block, block, slot, device)
            self.gathered.append(net.sent[-1])

        def start(self):
            own = rows.at[self.which, self.half]
            net.send(own, self.block(0, y), self.az + 1, z_peers[1])
            self.gathered.append(net.sent[-1])
            net.send(own, self.block(0, y), self.az + 2, z_peers[2])
            self.gathered.append(net.sent[-1])
            net.send(own, self.block(0, y), self.ay, yp)
            self.gathered.append(net.sent[-1])
            self.got_all[self.half, zh, zl, y] = rows[self.which, self.half]

        def hop(self, k):
            block = self.block(k, y)
            net.got(block, self.az + k)
            if k == 2:
                self.pass_on(block, self.az + 3, z_peers[1])
            self.pass_on(block, self.ay + k, yp)

        def arrive(self, g):
            if g not in self.here:
                for k in (2 * g, 2 * g + 1):
                    net.got(self.block(k, 1 - y), self.ay + k)
            self.here.add(g)

        def group(self, g):
            self.arrive(g)
            self.compute(self.half, zh if g == 0 else 1 - zh)
            keep[self.half, g] = acc[:, y]
            send_y[self.half, g] = acc[:, 1 - y].astype(LOW)
            net.send(send_y.at[self.half, g], recv_y.at[self.half, g], self.ry + g, yp)

        def fold(self, g):
            net.got(recv_y.at[self.half, g], self.ry + g)
            keep[self.half, g] += recv_y[self.half, g].astype(F32)
            send_z[self.half, g] = keep[self.half, g, 1 - zl].astype(LOW)
            net.send(send_z.at[self.half, g], recv_z.at[self.half, g], self.rz + g, z_peers[1])

        def cross(self):
            net.got(recv_z.at[self.half, 1], self.rz + 1)
            send_z[self.half, 2] = (
                keep[self.half, 1, zl] + recv_z[self.half, 1].astype(F32)
            ).astype(LOW)
            net.send(send_z.at[self.half, 2], recv_z.at[self.half, 2], self.rz + 2, z_peers[2])

        def done(self):
            net.got(recv_z.at[self.half, 0], self.rz)
            net.got(recv_z.at[self.half, 2], self.rz + 2)
            total[self.half] = (
                keep[self.half, 0, zl]
                + recv_z[self.half, 0].astype(F32)
                + recv_z[self.half, 2].astype(F32)
            )

    def columns(half, pair):
        return pl.ds(pl.multiple_of((half * 2 + pair) * PAIR, PAIR), PAIR)

    def put(h, part):
        part = part.reshape(2, 2, PART, D)

        @pl.when(h == 0)
        def _():
            acc[...] = part

        @pl.when(h == 1)
        def _():
            acc[...] += part

    def forward_pairs(half, pair):
        def one(h, carry):
            block = got_mid[half, pair].reshape(PAIR, D)
            gate = nt(block, w_gu[0, h])
            upward = nt(block, w_gu[1, h])
            square = gate * gate
            tanh = jnp.tanh(SQRT_2_OVER_PI * gate * (1.0 + CUBIC * square))
            side = 0.5 * (1.0 + tanh)
            gelu = gate * side
            slope = side + 0.5 * gate * (1.0 - tanh * tanh) * (
                SQRT_2_OVER_PI * (1.0 + 3.0 * CUBIC * square)
            )
            low = (gelu * upward).astype(LOW)
            slope_gate[h, half, pair] = (upward * slope).astype(LOW)
            slope_up[h, half, pair] = gelu.astype(LOW)
            put(h, nn(low, w_dn[h]))
            hidden_t[h, :, columns(half, pair)] = low.T
            return carry

        lax.fori_loop(0, 2, one, 0)

    def weights_here():
        net.settle_moves()
        net.flush([across_x])
        rows_across(1)
        rows_whole()

    def forward_end(half):
        span = pl.ds(half * PART, PART)
        ffw_proj = total[half]
        branch = norm_rows(ffw_proj, gains[3:4, :])
        layer_out[half, 0] = (middle[span, :] + branch).astype(LOW)
        counts = jnp.sum(weight[span, 0:1] * jnp.sum(branch * branch, -1, keepdims=True))
        small[0, 5:6, :] += jnp.where(spot == 3, counts, 0.0)
        grad, gain_grad = norm_back(ffw_proj, gains[3:4, :], cot[half, 0].astype(F32))
        small[0, 3:4, :] += gain_grad
        rows[1, half] = grad.astype(LOW)

    def backward_pairs(half, pair):
        def one(h, carry):
            block = got_up[half, pair].reshape(PAIR, D)
            back = nt(block, w_dn[h])
            gate = (back * slope_gate[h, half, pair].astype(F32)).astype(LOW)
            upward = (back * slope_up[h, half, pair].astype(F32)).astype(LOW)
            put(h, nn(gate, w_gu[0, h]) + nn(upward, w_gu[1, h]))
            slope_gate[h, half, pair] = gate
            slope_up[h, half, pair] = upward
            return carry

        lax.fori_loop(0, 2, one, 0)

    one, two = Half(0, 0, got_mid, forward_pairs), Half(0, 1, got_mid, forward_pairs)
    one.start()
    one.hop(1)
    two.start()
    one.hop(2)
    weights_here()
    one.group(0)
    two.hop(1)
    one.hop(3)
    two.hop(2)
    one.group(1)
    one.fold(0)
    two.hop(3)
    two.group(0)
    one.fold(1)
    two.group(1)
    one.cross()
    two.fold(0)
    one.done()
    forward_end(0)
    three, four = Half(1, 0, got_up, backward_pairs), Half(1, 1, got_up, backward_pairs)
    three.start()
    two.fold(1)
    three.hop(1)
    two.cross()
    three.hop(2)
    two.done()
    forward_end(1)
    four.start()
    net.flush([copy for copy in net.sent if not any(copy is other for other in three.gathered + four.gathered)])
    three.group(0)
    four.hop(1)
    three.hop(3)
    four.hop(2)
    three.group(1)
    three.fold(0)
    four.hop(3)
    four.group(0)
    three.fold(1)

    step = 384
    flat_mid, flat_up = got_mid.reshape(8 * MINE, D), got_up.reshape(8 * MINE, D)

    four.arrive(1)

    def down_grads(i, carry):
        h, cols = i // 3, pl.ds(pl.multiple_of(i % 3 * step, 128), step)
        d_dn.reshape(2, WIDE, D)[h, :, cols] = nn(hidden_t[h], flat_up[:, cols]).astype(LOW)
        return carry

    lax.fori_loop(0, 6, down_grads, 0)
    d_c, d_x, d_home, d_y = net.slots(5), net.slots(2), net.slots(2), net.slots(2)
    kept = (x + y + z) % 2
    net.send(d_dn.at[1 - c], n0, d_c, cp)
    four.group(1)
    three.cross()
    four.fold(0)

    def gate_up_grads(t, h, slopes):
        hidden_t[h] = slopes[h].reshape(8 * MINE, WIDE).T

        def part(i, carry):
            cols = pl.ds(pl.multiple_of(i * step, 128), step)
            w_gu[t, h, :, cols] = nn(hidden_t[h], flat_mid[:, cols]).astype(LOW)
            return carry

        lax.fori_loop(0, 3, part, 0)

    for h in range(2):
        gate_up_grads(0, h, slope_gate)
    net.send(all_gu.at[0, 1 - c], g0.at[0], d_c + 1, cp)
    net.got(n0, d_c)
    for q in range(2):
        d_dn[c, q] = added(d_dn[c, q], n0[q])
    net.send(d_dn.at[c, 1 - kept], n1, d_y, xp)
    four.fold(1)
    three.done()
    four.cross()
    for h in range(2):
        gate_up_grads(1, h, slope_up)
    net.send(all_gu.at[1, 1 - c], g0.at[1], d_c + 2, cp)

    def share(t):
        net.got(g0.at[t], d_c + 1 + t)
        for q in range(2):
            all_gu[t, c, q] = added(all_gu[t, c, q], g0[t, q])
        net.send(all_gu.at[t, c, 1 - x], g1.at[t], d_x + t, xp)

    share(0)
    share(1)
    four.done()

    mid = middle[...]
    grad, gain_grad = norm_back(mid, gains[2:3, :], total[...].reshape(MINE, D))
    small[0, 2:3, :] = gain_grad
    grad_mid = stream_of(cot) + grad
    grad_middle[...] = grad_mid
    grad, gain_grad = norm_back(attn_proj[...], gains[1:2, :], grad_mid)
    small[0, 1:2, :] = gain_grad
    grad_attn[...] = grad.astype(LOW)
    net.flush(three.gathered + four.gathered)
    d_out = got_up.reshape(4, 2, 2, 2, 32, D)
    a0 = got_mid.reshape(8 * MINE, D).at[pl.ds(0, 16 * 48)].reshape(4, 2, 2, 48, D)
    b0 = recv_y.reshape(4, 2, 2, 32, D)
    flat_d_out, flat_d_in = got_up.reshape(HEADS * HD, D), d_in.reshape(HEADS * HD + 2 * HD, D)

    def out_grads(j, carry):
        flat_d_out[rows_of(j), :] = tn(mixed[j], grad_attn[...]).astype(LOW)
        return carry

    lax.fori_loop(0, HEADS, out_grads, 0)
    net.send(d_out.at[:, :, :, 1 - c], b0, d_c + 3, cp)

    def home_down():
        net.got(n1, d_y)
        d_dn[c, kept] = added(d_dn[c, kept], n1[...])
        net.move(
            jnp.logical_and(z % 2 == y, x == y),
            d_dn.at[c, kept],
            n2,
            d_y + 1,
            d_y + 1,
            at(2 * (z // 2) + y, kept, z % 2, c),
        )

    def home_gate_up(t):
        net.got(g1.at[t], d_x + t)
        all_gu[t, c, x] = added(all_gu[t, c, x], g1[t])
        source = z // 2 + 2 * t
        net.move(
            jnp.logical_and(source == z, z % 2 == c),
            all_gu.at[t, c, x],
            g2.at[c],
            d_home + t,
            d_home + c,
            at(source, y, x, z % 2),
        )

    class Collect:
        def __init__(self, grads, core_in, y_in, x_in, z_in, core_slot):
            self.grads, self.core_in, self.y_in, self.x_in, self.z_in = (
                grads,
                core_in,
                y_in,
                x_in,
                z_in,
            )
            self.cs, self.ys, self.xs, self.zs = core_slot, net.slots(2), net.slots(2), net.slots(2)

        def cores(self):
            net.got(self.core_in, self.cs)
            for part, pair in enumerate((1 - zh, zh)):

                def one(i, carry):
                    p, q, r = 2 * pair + i // 4, i // 2 % 2, i % 2
                    self.grads[p, q, r, c] = added(self.grads[p, q, r, c], self.core_in[p, q, r])
                    return carry

                lax.fori_loop(0, 8, one, 0)
                both = pl.ds(2 * pair, 2)
                net.send(
                    self.grads.at[both, 1 - y, :, c], self.y_in.at[part], self.ys + part, yp
                )

        def ys_in(self, part):
            pair = (1 - zh, zh)[part]
            net.got(self.y_in.at[part], self.ys + part)

            def one(i, carry):
                p, q = i // 2, i % 2
                there = 2 * pair + p
                self.grads[there, y, q, c] = added(
                    self.grads[there, y, q, c], self.y_in[part, p, q]
                )
                return carry

            lax.fori_loop(0, 4, one, 0)
            net.send(
                self.grads.at[pl.ds(2 * pair, 2), y, 1 - x, c],
                self.x_in.at[part],
                self.xs + part,
                xp,
            )

        def xs_in(self, part):
            pair = (1 - zh, zh)[part]
            net.got(self.x_in.at[part], self.xs + part)
            for p in range(2):
                there = 2 * pair + p
                self.grads[there, y, x, c] = added(
                    self.grads[there, y, x, c], self.x_in[part, p]
                )
            net.send(
                self.grads.at[2 * pair + 1 - zl, y, x, c],
                self.z_in.at[part],
                self.zs + part,
                z_peers[1],
            )

        def cross(self, slot):
            net.got(self.z_in.at[0], self.zs)
            there = 2 * (1 - zh) + zl
            self.grads[there, y, x, c] = added(self.grads[there, y, x, c], self.z_in[0])
            net.send(self.grads.at[there, y, x, c], self.z_in.at[2], slot, z_peers[2])

        def done(self, slot, result):
            net.got(self.z_in.at[1], self.zs + 1)
            net.got(self.z_in.at[2], slot)
            result[...] = (
                self.grads[z, y, x, c].astype(F32)
                + self.z_in[1].astype(F32)
                + self.z_in[2].astype(F32)
            )

    r_s, r_z = net.slots(8), net.slots(2)
    outs = Collect(d_out, b0, b1, b2, b3, d_c + 3)
    ins = Collect(d_in, a0, a1, a2, a3, d_c + 4)

    grad_heads[...] = jnp.zeros((6, MINE, HD), F32)

    def head_back(j, carry):
        up = nt(grad_attn[...], flat_out[rows_of(j), :]).astype(LOW)
        prob = probs[j]
        grad_prob = nt(up, heads[HEADS + 1])
        grad_heads[HEADS + 1] += tn(prob.astype(LOW), up)
        center = jnp.sum(grad_prob * prob, -1, keepdims=True)
        grad_score = (prob * (grad_prob - center)).astype(LOW)
        grad_heads[j] = nn(grad_score, heads[HEADS]) * SCALE_FACTOR
        grad_heads[HEADS] += tn(grad_score, heads[j]) * SCALE_FACTOR
        return carry

    lax.fori_loop(0, HEADS, head_back, 0)
    key_acc[...] = jnp.zeros((2, HD), F32)

    def turn_back(j, carry):
        first, second = grad_heads[j, :, :half], grad_heads[j, :, half:]
        turned = jnp.concatenate(
            [
                first * cosine[...] + second * sine[...],
                second * cosine[...] - first * sine[...],
            ],
            -1,
        )
        which = pl.ds(j // HEADS, 1)
        grad, gain_grad = norm_back(proj[j], head_gains[which, :], turned)
        key_acc[which, :] += gain_grad
        grad_proj[j] = grad.astype(LOW)
        return carry

    lax.fori_loop(0, HEADS + 1, turn_back, 0)
    grad_proj[HEADS + 1] = grad_heads[HEADS + 1].astype(LOW)
    small[0, 4:5, 0:HD] = key_acc[0:1, :]
    small[0, 4:5, HD : 2 * HD] = key_acc[1:2, :]

    outs.cores()

    def in_grads(j, carry):
        flat_d_in[rows_of(j), :] = tn(grad_proj[j], normed_in[...]).astype(LOW)
        return carry

    lax.fori_loop(0, HEADS + 2, in_grads, 0)
    net.send(d_in.at[:, :, :, 1 - c], a0, d_c + 4, cp)
    home_down()
    total[...] = jnp.zeros((2, PART, D), F32)

    def in_back(j, carry):
        total[...] += nn(grad_proj[j], flat_in[rows_of(j), :]).reshape(2, PART, D)
        return carry

    lax.fori_loop(0, HEADS + 2, in_back, 0)
    ins.cores()
    grad, gain_grad = norm_back(stream_of(x_ref), gains[0:1, :], total[...].reshape(MINE, D))
    small[0, 0:1, :] = gain_grad
    input_grad[...] = (grad_middle[...] + grad).reshape(2, 1, PART, D)
    net.send(small.at[0], small.at[1], r_s, cp)
    home_gate_up(0)
    outs.ys_in(0)
    outs.ys_in(1)
    net.got(small.at[1], r_s)
    small[2] = small[0] + small[1]
    net.send(small.at[2], small.at[3], r_s + 1, xp)
    ins.ys_in(0)
    home_gate_up(1)
    outs.xs_in(0)
    outs.xs_in(1)
    net.got(small.at[3], r_s + 1)
    small[4] = small[2] + small[3]
    net.send(small.at[4], small.at[5], r_s + 2, yp)
    ins.ys_in(1)
    outs.cross(r_z)
    ins.xs_in(0)
    ins.xs_in(1)
    net.got(small.at[5], r_s + 2)
    small[6] = small[4] + small[5]
    for k in (1, 2, 3):
        net.send(small.at[6], small.at[6 + k], r_s + 2 + k, z_peers[k])
    ins.cross(r_z + 1)
    outs.done(r_z, o_out)
    net.got(n2, d_y + 1)
    o_dn[...] = n2[...].astype(F32)[:BLOCK]
    for k in (1, 2, 3):
        net.got(small.at[6 + k], r_s + 2 + k)
    sums = (small[6] + small[7]) + (small[8] + small[9])
    o_gains[...] = sums[0:4, :]
    o_heads[...] = jnp.concatenate([sums[4:5, 0:HD], sums[4:5, HD : 2 * HD]], 0)
    scaled = sums[5:6, :]
    tokens = jnp.sum(jnp.where(spot == 4, scaled, 0.0), -1, keepdims=True)
    means = jnp.sqrt(scaled / (tokens * D))
    for i in range(4):
        o_rms[i] = jnp.sum(jnp.where(spot == i, means, 0.0))
    ins.done(r_z + 1, o_in)
    for h in range(2):
        net.got(g2.at[h], d_home + h)
        o_gu[pl.ds(h * BLOCK, BLOCK), :] = g2[h].astype(F32)[:BLOCK]
    net.drain()


def vm(*shape):
    return pltpu.VMEM(shape, LOW)


def vf(*shape):
    return pltpu.VMEM(shape, F32)


def whole_layer(x, seg, valid, ain, aout, gu, dn, gains, head_gains, cot):
    vmem = pl.BlockSpec(memory_space=pltpu.VMEM)
    scratch = [
        vm(4, 2, 2, 2, 48, D),
        vm(4, 2, 2, 2, 32, D),
        vm(2, 2, 2, PADDED, D),
        vm(2, 2, PADDED, D),
        vf(MINE, MINE),
        vf(MINE, MINE),
        vf(MINE, MINE),
        vf(MINE, MINE),
        vm(MINE, D),
        vf(6, MINE, HD),
        vm(6, MINE, HD),
        vf(4, MINE, MINE),
        vm(4, MINE, HD),
        vf(MINE, D),
        vf(MINE, D),
        vm(2, 2, PART, D),
        vf(2, PART, D),
        vm(2, 2, 2, 2, PART, D),
        vm(2, 2, 2, 2, PART, D),
        vm(2, WIDE, 8 * MINE),
        vm(2, 2, 2, PAIR, WIDE),
        vm(2, 2, 2, PAIR, WIDE),
        vf(2, 2, PART, D),
        vf(2, 2, 2, PART, D),
        vm(2, 2, 2, PART, D),
        vm(2, 2, 2, PART, D),
        vm(2, 3, PART, D),
        vm(2, 3, PART, D),
        vf(MINE, D),
        vm(MINE, D),
        vf(6, MINE, HD),
        vm(6, MINE, HD),
        vf(2, HD),
        vm(4, 2, 2, 2, 48, D),
    ]
    for count in (48, 32):
        scratch += [vm(2, 2, 2, count, D), vm(2, 2, count, D), vm(3, count, D)]
    scratch += [vm(2, 2, PADDED, D), vm(2, PADDED, D), vm(2, PADDED, D)]
    scratch += [vm(2, 2, PADDED, D), vm(2, PADDED, D), vm(PADDED, D), vm(PADDED, D)]
    scratch += [vf(10, 8, D)]
    scratch += [pltpu.SemaphoreType.DMA((2,))] + [pltpu.SemaphoreType.DMA((144,))] * 2
    return pl.pallas_call(
        layer_kernel,
        out_shape=(
            jax.ShapeDtypeStruct((2, 1, PART, D), LOW),
            jax.ShapeDtypeStruct((2, 1, PART, D), F32),
            jax.ShapeDtypeStruct((48, D), F32),
            jax.ShapeDtypeStruct((32, D), F32),
            jax.ShapeDtypeStruct((2 * BLOCK, D), F32),
            jax.ShapeDtypeStruct((BLOCK, D), F32),
            jax.ShapeDtypeStruct((4, D), F32),
            jax.ShapeDtypeStruct((2, HD), F32),
            jax.ShapeDtypeStruct((4,), F32),
        ),
        in_specs=[vmem] * 10,
        out_specs=(vmem,) * 8 + (pl.BlockSpec(memory_space=pltpu.SMEM),),
        scratch_shapes=scratch,
        compiler_params=pltpu.CompilerParams(
            collective_id=1, has_side_effects=True, vmem_limit_bytes=VMEM_BYTES
        ),
        name="layer",
    )(x, seg, valid, ain, aout, gu, dn, gains, head_gains, cot)


def copy_kernel(*refs):
    count = (len(refs) - 2) // 3
    given, made, held = refs[:count], refs[count : 2 * count], refs[2 * count : 3 * count]
    into = [pltpu.make_async_copy(a, b, refs[-2].at[i]) for i, (a, b) in enumerate(zip(given, held))]
    out = [pltpu.make_async_copy(a, b, refs[-1].at[i]) for i, (a, b) in enumerate(zip(held, made))]
    for copy in into:
        copy.start()
    for first, second in zip(into, out):
        first.wait()
        second.start()
    for copy in out:
        copy.wait()


def copied(arrays):
    place = pl.BlockSpec(memory_space=pl.ANY)
    return pl.pallas_call(
        copy_kernel,
        out_shape=tuple(jax.ShapeDtypeStruct(array.shape, array.dtype) for array in arrays),
        in_specs=[place] * len(arrays),
        out_specs=(place,) * len(arrays),
        scratch_shapes=[pltpu.VMEM(array.shape, array.dtype) for array in arrays]
        + [pltpu.SemaphoreType.DMA((len(arrays),))] * 2,
        name="results",
    )(*arrays)


def split_shards(
    inputs,
    segment_ids,
    valid_mask,
    attn_in,
    attn_out,
    ffw_in,
    ffw_out,
    norm_gains,
    head_gains,
    cotangent,
):
    results = whole_layer(
        inputs,
        segment_ids,
        valid_mask,
        attn_in,
        attn_out,
        ffw_in,
        ffw_out,
        norm_gains,
        head_gains,
        cotangent,
    )
    return copied(results[:-1]) + results[-1:]


def solution(mesh):
    placed = (
        P(None, "dp", None, None),
        P(None, "dp", None),
        P(None, "dp", None),
        P("dp", None),
        P("dp", None),
        P("dp", None),
        P("dp", None),
        P(),
        P(),
        P(None, "dp", None, None),
    )
    return jax.shard_map(
        split_shards if mesh.shape["dp"] == 32 else general_shards,
        mesh=mesh,
        in_specs=placed,
        out_specs=(
            P(None, "dp", None, None),
            P(None, "dp", None, None),
            P("dp", None),
            P("dp", None),
            P("dp", None),
            P("dp", None),
            P(),
            P(),
            P(),
        ),
        check_vma=False,
    )
```

```python
import math

import jax
import jax.numpy as jnp
from jax import lax
from jax.experimental import pallas as pl
from jax.experimental.pallas import tpu as pltpu
from jax.sharding import PartitionSpec as P

D = 1152
HEADS = 4
HD = 256
FF = 6912
MICRO = 2


EPSILON = 1e-06
SCALE_FACTOR = 0.0625
THETA = 10000.0
NEGATIVE = -1e30


def shortened(x):

    def short(part):
        return part.astype(jnp.bfloat16) if part.dtype == jnp.float32 else part

    return jax.tree.map(short, x)


def swapped(block, axis, stride):
    count = lax.axis_size(axis)
    route = []
    for low in range(count):
        high = low | 1 << stride
        if high != low and high < count:
            route += [(low, high), (high, low)]
    return lax.ppermute(block, axis, route)


def norm_rows(values, gain):
    return values * lax.rsqrt(jnp.mean(values * values, -1, keepdims=True) + EPSILON) * gain


def rotate(values, cosine, sine):
    half = values.shape[-1] // 2
    first = values[..., :half]
    second = values[..., half:]
    return jnp.concatenate([first * cosine - second * sine, second * cosine + first * sine], -1)


def doc_tables(segments, validity, head_size):
    length = segments.shape[-1]
    places = jnp.arange(length, dtype=jnp.int32)
    same_doc = segments[..., :, None] == segments[..., None, :]
    earlier = places[None, :] < places[:, None]
    position = jnp.sum(jnp.logical_and(same_doc, earlier).astype(jnp.int32), -1)
    reach = places[None, :] <= places[:, None]
    usable = jnp.logical_or(validity[..., None, :] > 0, places[None, :] == places[:, None])
    allowed = jnp.logical_and(jnp.logical_and(same_doc, reach), usable)
    freqs = jnp.exp(
        jnp.arange(head_size // 2, dtype=jnp.float32) * (-2.0 * math.log(THETA) / head_size)
    )
    angles = position.astype(jnp.float32)[..., None] * freqs
    return (allowed, jnp.cos(angles), jnp.sin(angles))


def prepare(projected, head_gains, cosine, sine):
    width = HEADS * HD
    query = projected[..., :width].reshape(projected.shape[:-1] + (HEADS, HD))
    keys = projected[..., width : width + HD]
    values = projected[..., width + HD :]
    query = rotate(norm_rows(query, head_gains[0]), cosine[..., None, :], sine[..., None, :])
    keys = rotate(norm_rows(keys, head_gains[1]), cosine, sine)
    return (query, keys, values)


def across(left, piece):
    return lax.dot_general(
        left, piece, (((1,), (1,)), ((), ())), preferred_element_type=jnp.float32
    )


def over_rows(left, right):
    return lax.dot_general(
        left, right, (((0,), (0,)), ((), ())), preferred_element_type=jnp.float32
    )


def score_table(query_low, keys_low):
    return (
        jnp.einsum("qhd,kd->hqk", query_low, keys_low, preferred_element_type=jnp.float32)
        * SCALE_FACTOR
    )


def attend(query_low, keys_low, values_low, allowed):
    scores = score_table(query_low, keys_low)
    masked = jnp.where(allowed[None], scores, NEGATIVE)
    peak = jnp.max(masked, -1, keepdims=True)
    expo = jnp.where(allowed[None], jnp.exp(masked - peak), 0.0)
    totals = jnp.sum(expo, -1, keepdims=True)
    probs = expo / totals
    mixed = jnp.einsum(
        "hqk,kd->qhd", probs.astype(jnp.bfloat16), values_low, preferred_element_type=jnp.float32
    )
    return (mixed, peak + jnp.log(totals))


def attend_back(query_low, keys_low, values_low, allowed, log_sum, grad_low):
    scores = score_table(query_low, keys_low)
    probs = jnp.where(allowed[None], jnp.exp(scores - log_sum), 0.0)
    grad_probs = jnp.einsum("qhd,kd->hqk", grad_low, values_low, preferred_element_type=jnp.float32)
    grad_values = jnp.einsum(
        "hqk,qhd->kd", probs.astype(jnp.bfloat16), grad_low, preferred_element_type=jnp.float32
    )
    center = jnp.sum(grad_probs * probs, -1, keepdims=True)
    grad_scores = (probs * (grad_probs - center)).astype(jnp.bfloat16)
    grad_query = (
        jnp.einsum("hqk,kd->qhd", grad_scores, keys_low, preferred_element_type=jnp.float32)
        * SCALE_FACTOR
    )
    grad_keys = (
        jnp.einsum("hqk,qhd->kd", grad_scores, query_low, preferred_element_type=jnp.float32)
        * SCALE_FACTOR
    )
    return (grad_query, grad_keys, grad_values)


def gated(gate, upward):
    return jax.nn.gelu(gate, approximate=True) * upward


def general_shards(
    inputs,
    segment_ids,
    valid_mask,
    attn_in,
    attn_out,
    ffw_in,
    ffw_out,
    norm_gains,
    head_gains,
    cotangent,
):
    width = HEADS * HD
    kept_proj = []
    kept_normed_in = []
    kept_mixed = []
    kept_attn = []
    kept_gate = []
    kept_normed_mid = []
    kept_hidden = []
    kept_ffw = []
    gain_sums = jnp.zeros((4, D), jnp.float32)
    head_sums = jnp.zeros((2, HD), jnp.float32)
    stats = jnp.zeros((5,), jnp.float32)
    results = []
    input_grads = []
    for step in range(MICRO):
        full_in, full_out = (
            lax.all_gather(attn_in, "dp", axis=0, tiled=True),
            lax.all_gather(attn_out, "dp", axis=0, tiled=True),
        )
        full_ffin, full_ffout = (
            lax.all_gather(ffw_in, "dp", axis=0, tiled=True),
            lax.all_gather(ffw_out, "dp", axis=0, tiled=True),
        )
        stream = inputs[step, 0].astype(jnp.float32)
        length = stream.shape[0]
        allowed, cosine, sine = doc_tables(segment_ids[step, 0], valid_mask[step, 0], HD)
        normed_in = norm_rows(stream, norm_gains[0]).astype(jnp.bfloat16)
        projected = across(normed_in, full_in)
        query, keys, values = prepare(projected, head_gains, cosine, sine)
        query_low = query.astype(jnp.bfloat16)
        keys_low = keys.astype(jnp.bfloat16)
        values_low = values.astype(jnp.bfloat16)
        mixed, log_sum = attend(query_low, keys_low, values_low, allowed)
        mixed_low = mixed.reshape(length, width).astype(jnp.bfloat16)
        attn_proj = jnp.dot(mixed_low, full_out, preferred_element_type=jnp.float32)
        attn_branch = norm_rows(attn_proj, norm_gains[1])
        middle = stream + attn_branch
        normed_mid = norm_rows(middle, norm_gains[2]).astype(jnp.bfloat16)
        gate_up = across(normed_mid, full_ffin)
        gate = gate_up[:, :FF]
        upward = gate_up[:, FF:]
        hidden = gated(gate, upward).astype(jnp.bfloat16)
        ffw_proj = jnp.dot(hidden, full_ffout, preferred_element_type=jnp.float32)
        ffw_branch = norm_rows(ffw_proj, norm_gains[3])
        results.append((middle + ffw_branch).astype(jnp.bfloat16))
        weight = valid_mask[step, 0].astype(jnp.float32)
        sums = [
            jnp.sum(weight * jnp.sum(value * value, -1))
            for value in (stream, middle, attn_branch, ffw_branch)
        ]
        sums.append(jnp.sum(weight))
        stats = stats + jnp.stack(sums)
        upstream = cotangent[step, 0].astype(jnp.float32)
        _, back_ffw = jax.vjp(norm_rows, ffw_proj, norm_gains[3])
        grad_ffw_proj, gain_three = back_ffw(upstream)
        grad_ffw_low = grad_ffw_proj.astype(jnp.bfloat16)
        grad_hidden = across(grad_ffw_low, full_ffout)
        _, back_gated = jax.vjp(gated, gate, upward)
        grad_gate, grad_upward = back_gated(grad_hidden)
        grad_gate_up = jnp.concatenate([grad_gate, grad_upward], 1).astype(jnp.bfloat16)
        grad_normed_mid = jnp.dot(grad_gate_up, full_ffin, preferred_element_type=jnp.float32)
        _, back_mid = jax.vjp(norm_rows, middle, norm_gains[2])
        grad_mid_part, gain_two = back_mid(grad_normed_mid)
        grad_middle = upstream + grad_mid_part
        _, back_attn = jax.vjp(norm_rows, attn_proj, norm_gains[1])
        grad_attn_proj, gain_one = back_attn(grad_middle)
        grad_attn_low = grad_attn_proj.astype(jnp.bfloat16)
        grad_mixed = across(grad_attn_low, full_out)
        grad_mixed_low = grad_mixed.astype(jnp.bfloat16).reshape(length, HEADS, HD)
        grad_query, grad_keys, grad_values = attend_back(
            query_low, keys_low, values_low, allowed, log_sum, grad_mixed_low
        )
        _, back_prep = jax.vjp(
            lambda table, gains: prepare(table, gains, cosine, sine), projected, head_gains
        )
        grad_projected, grad_heads = back_prep((grad_query, grad_keys, grad_values))
        grad_proj_low = grad_projected.astype(jnp.bfloat16)
        grad_normed_in = jnp.dot(grad_proj_low, full_in, preferred_element_type=jnp.float32)
        _, back_in = jax.vjp(norm_rows, stream, norm_gains[0])
        grad_stream, gain_zero = back_in(grad_normed_in)
        input_grads.append(grad_middle + grad_stream)
        gain_sums = gain_sums + jnp.stack([gain_zero, gain_one, gain_two, gain_three])
        head_sums = head_sums + grad_heads
        kept_proj.append(grad_proj_low)
        kept_normed_in.append(normed_in)
        kept_mixed.append(mixed_low)
        kept_attn.append(grad_attn_low)
        kept_gate.append(grad_gate_up)
        kept_normed_mid.append(normed_mid)
        kept_hidden.append(hidden)
        kept_ffw.append(grad_ffw_low)
    pairs = [
        (jnp.concatenate(kept_proj, 0), jnp.concatenate(kept_normed_in, 0)),
        (jnp.concatenate(kept_mixed, 0), jnp.concatenate(kept_attn, 0)),
        (jnp.concatenate(kept_gate, 0), jnp.concatenate(kept_normed_mid, 0)),
        (jnp.concatenate(kept_hidden, 0), jnp.concatenate(kept_ffw, 0)),
    ]
    levels = lax.axis_size("dp").bit_length() - 1
    place = lax.axis_index("dp")
    top_bit = place >> levels - 1 & 1
    kept_parts = []
    sent_parts = []
    for left, right in pairs:
        half_cols = left.shape[1] // 2
        kept_parts.append(
            over_rows(lax.dynamic_slice_in_dim(left, top_bit * half_cols, half_cols, 1), right)
        )
        sent_parts.append(
            over_rows(
                lax.dynamic_slice_in_dim(left, (1 - top_bit) * half_cols, half_cols, 1), right
            )
        )
    current = tuple(kept_parts)
    outgoing = tuple(sent_parts)
    for level in range(levels):
        bit = levels - 1 - level
        arrived = jax.tree.map(
            lambda part, own: part.astype(own.dtype),
            swapped(shortened(outgoing), "dp", bit),
            outgoing,
        )
        current = tuple((mine + theirs for mine, theirs in zip(current, arrived)))
        if level + 1 < levels:
            next_bit = place >> bit - 1 & 1
            halves = [piece.shape[0] // 2 for piece in current]
            outgoing = tuple(
                (
                    lax.dynamic_slice_in_dim(piece, (1 - next_bit) * rows, rows, 0)
                    for piece, rows in zip(current, halves)
                )
            )
            current = tuple(
                (
                    lax.dynamic_slice_in_dim(piece, next_bit * rows, rows, 0)
                    for piece, rows in zip(current, halves)
                )
            )
    shard_in, shard_out, shard_ffin, shard_ffout = current
    gain_total, head_total, stat_total = lax.psum((gain_sums, head_sums, stats), "dp")
    rms_values = jnp.sqrt(stat_total[:4] / (stat_total[4] * D))
    layer_out = jnp.stack(results)[:, None]
    input_grad = jnp.stack(input_grads)[:, None]
    return (
        layer_out,
        input_grad,
        shard_in,
        shard_out,
        shard_ffin,
        shard_ffout,
        gain_total,
        head_total,
        rms_values,
    )


BLOCK = 216
PADDED = 224
WIDE = 2 * PADDED
MINE = 128
PART = 64
PAIR = 2 * MINE
VMEM_BYTES = 62 << 20
SQRT_2_OVER_PI = math.sqrt(2.0 / math.pi)
CUBIC = 0.044715
MESH = pl.DeviceIdType.MESH
LOW = jnp.bfloat16
F32 = jnp.float32


def spots():
    me = lax.axis_index("dp")
    return me, me // 8, me // 4 % 2, me // 2 % 2, me % 2


def at(z, y, x, c):
    return z * 8 + y * 4 + x * 2 + c


def z_peer(z, k):
    if k == 0:
        return z
    if k == 1:
        return z + 1 - 2 * (z % 2)
    if k == 2:
        return (z + 2) % 4
    return 3 - z


def greet_all(me):
    barrier = pltpu.get_barrier_semaphore()

    def one(step, carry):
        pl.semaphore_signal(barrier, inc=1, device_id=((me + step) % 32,), device_id_type=MESH)
        return carry

    lax.fori_loop(1, 32, one, 0)
    pl.semaphore_wait(barrier, 31)


def nt(left, right):
    return lax.dot_general(left, right, (((1,), (1,)), ((), ())), preferred_element_type=F32)


def nn(left, right):
    return lax.dot_general(left, right, (((1,), (0,)), ((), ())), preferred_element_type=F32)


def tn(left, right):
    return lax.dot_general(left, right, (((0,), (0,)), ((), ())), preferred_element_type=F32)


def norm_back(values, gain, upstream):
    scale = lax.rsqrt(jnp.mean(values * values, -1, keepdims=True) + EPSILON)
    normed = values * scale
    gain_grad = jnp.sum(upstream * normed, 0, keepdims=True)
    inner = upstream * gain
    grad = scale * (inner - normed * jnp.mean(inner * normed, -1, keepdims=True))
    return grad, gain_grad


def added(left, right):
    return (left.astype(F32) + right.astype(F32)).astype(LOW)


def stream_of(ref):
    return ref[...].reshape(MINE, D).astype(F32)


class Net:
    def __init__(self, send_sems, recv_sems, anyone):
        self.send_sems, self.recv_sems, self.anyone = send_sems, recv_sems, anyone
        self.used, self.sent, self.maybe = 0, [], []

    def slots(self, count):
        first = self.used
        self.used += count
        return first

    def copy(self, src, dst, send_slot, recv_slot, device):
        return pltpu.make_async_remote_copy(
            src_ref=src,
            dst_ref=dst,
            send_sem=self.send_sems.at[send_slot],
            recv_sem=self.recv_sems.at[recv_slot],
            device_id=(device,),
            device_id_type=MESH,
        )

    def send(self, src, dst, slot, device):
        copy = self.copy(src, dst, slot, slot, device)
        copy.start()
        self.sent.append(copy)

    def move(self, stays, src, dst, send_slot, recv_slot, device):
        copy = self.copy(src, dst, send_slot, recv_slot, device)

        @pl.when(stays)
        def _():
            pltpu.make_async_copy(src, dst, self.recv_sems.at[recv_slot]).start()

        @pl.when(jnp.logical_not(stays))
        def _():
            copy.start()

        self.maybe.append((stays, copy))

    def got(self, block, slot):
        self.copy(block, block, slot, slot, self.anyone).wait_recv()

    def flush(self, gone):
        for copy in gone:
            copy.wait_send()
        names = {id(copy) for copy in gone}
        self.sent = [copy for copy in self.sent if id(copy) not in names]

    def drain(self):
        self.flush(list(self.sent))
        self.settle_moves()

    def settle_moves(self):
        for stays, copy in self.maybe:

            @pl.when(jnp.logical_not(stays))
            def _():
                copy.wait_send()

        self.maybe = []


def layer_kernel(*refs):
    (
        x_ref,
        seg_ref,
        valid_ref,
        ain,
        aout,
        gu,
        dn,
        gains,
        head_gains,
        cot,
        layer_out,
        input_grad,
        o_in,
        o_out,
        o_gu,
        o_dn,
        o_gains,
        o_heads,
        o_rms,
        all_in,
        all_out,
        all_gu,
        all_dn,
        allow,
        cosine,
        sine,
        weight,
        normed_in,
        proj,
        heads,
        probs,
        mixed,
        attn_proj,
        middle,
        rows,
        total,
        got_mid,
        got_up,
        hidden_t,
        slope_gate,
        slope_up,
        acc,
        keep,
        send_y,
        recv_y,
        send_z,
        recv_z,
        grad_middle,
        grad_attn,
        grad_heads,
        grad_proj,
        key_acc,
        d_in,
        a1,
        a2,
        a3,
        b1,
        b2,
        b3,
        g0,
        g1,
        g2,
        d_dn,
        n0,
        n1,
        n2,
        small,
        local,
        send_sems,
        recv_sems,
    ) = refs
    me, z, y, x, c = spots()
    xp, yp, cp = at(z, y, 1 - x, c), at(z, 1 - y, x, c), at(z, y, x, 1 - c)
    z_peers = [at(z_peer(z, k), y, x, c) for k in range(4)]
    net = Net(send_sems, recv_sems, cp)
    keep_in = pltpu.make_async_copy(ain, all_in.at[z, y, x, c], local.at[0])
    keep_out = pltpu.make_async_copy(aout, all_out.at[z, y, x, c], local.at[1])
    keep_in.start()
    keep_out.start()
    greet_all(me)

    class Spread:
        def __init__(self, own, full, x_first):
            self.own, self.full, self.x_first = own, full, x_first
            self.first, self.second = (xp, yp) if x_first else (yp, xp)
            self.az, self.ax, self.ay, self.ac = (net.slots(4) for _ in range(4))

        def block(self, k):
            return self.full.at[z_peer(z, k), y, x, c]

        def crossed(self, k):
            there = z_peer(z, k)
            return self.full.at[there, y, 1 - x, c] if self.x_first else self.full.at[there, 1 - y, x, c]

        def pair(self, there, own, core):
            if self.x_first:
                return self.full.at[there, y if own else 1 - y, :, core]
            return self.full.at[there, :, x if own else 1 - x, core]

        def start(self):
            net.send(self.own, self.block(0), self.az + 1, z_peers[1])
            net.send(self.own, self.block(0), self.ax, self.first)
            net.send(self.own, self.block(0), self.az + 2, z_peers[2])

        def hop(self, k):
            block = self.block(k)
            net.got(block, self.az + k)
            if k == 2:
                net.send(block, block, self.az + 3, z_peers[1])
            net.send(block, block, self.ax + k, self.first)

        def turn(self, k):
            net.got(self.crossed(k), self.ax + k)
            pair = self.pair(z_peer(z, k), True, c)
            net.send(pair, pair, self.ay + k, self.second)

        def near(self):
            part = self.pair(slice(None), True, c)
            net.send(part, part, self.ac, cp)

        def far(self):
            for k in range(4):
                net.got(self.pair(z_peer(z, k), False, c), self.ay + k)
            part = self.pair(slice(None), False, c)
            net.send(part, part, self.ac + 1, cp)

        def whole(self):
            net.got(self.pair(slice(None), True, 1 - c), self.ac)
            net.got(self.pair(slice(None), False, 1 - c), self.ac + 1)

    into, outof = Spread(ain, all_in, True), Spread(aout, all_out, False)
    into.start()
    w_one, w_two, w_c, w_d = net.slots(2), net.slots(2), net.slots(2), net.slots(2)
    v_x, v_one, v_c = net.slots(1), net.slots(2), net.slots(1)
    kind, goal = z // 2, 2 * (z % 2) + c
    blank = jnp.zeros((PADDED - BLOCK, D), F32)
    for h in range(2):
        part = gu[pl.ds(h * BLOCK, BLOCK), :].astype(F32)
        g0[0, h] = jnp.concatenate([part, blank], 0).astype(LOW)
    n0[0] = jnp.concatenate([dn[...].astype(F32), blank], 0).astype(LOW)

    def rows_out():
        for h in range(2):
            net.move(
                jnp.logical_and(goal == z, c == h),
                g0.at[0, h],
                all_gu.at[kind, h, x],
                w_one + h,
                w_one + kind,
                at(goal, y, x, h),
            )

    def rows_on(which):
        t = (kind, 1 - kind)[which]
        block = all_gu.at[t, c, x]
        net.got(block, w_one + t)
        net.send(block, block, w_two + which, xp)
        net.send(block, block, w_c + which, cp)

    def rows_across(which):
        block = all_gu.at[(kind, 1 - kind)[which], c, 1 - x]
        net.got(block, w_two + which)
        net.send(block, block, w_d + which, cp)

    def rows_whole():
        for which in range(2):
            t = (kind, 1 - kind)[which]
            net.got(all_gu.at[t, 1 - c, x], w_c + which)
            net.got(all_gu.at[t, 1 - c, 1 - x], w_d + which)
        net.got(all_dn.at[1 - c], v_c)

    across_x = []

    def down_x():
        net.send(n0.at[0], n0.at[1], v_x, xp)
        across_x.append(net.sent[-1])


    def down_out():
        net.got(n0.at[1], v_x)
        for other in range(2):
            block_x = 1 - x if other else x
            net.move(
                jnp.logical_and(z % 2 == block_x, z % 2 == y),
                n0.at[other],
                all_dn.at[c, y],
                v_one + other,
                v_one + y,
                at(2 * (z // 2) + block_x, z % 2, x, c),
            )

    def down_on():
        for q in range(2):
            net.got(all_dn.at[c, q], v_one + q)
        net.send(all_dn.at[c], all_dn.at[c], v_c, cp)

    into.hop(1)
    into.hop(2)
    outof.start()
    keep_in.wait()
    keep_out.wait()
    into.turn(0)
    into.turn(1)
    into.hop(3)

    def along_lanes(ref):
        return jnp.concatenate([ref[0].astype(F32), ref[1].astype(F32)], 1)

    seg = jnp.broadcast_to(along_lanes(seg_ref), (MINE, MINE))
    valid = jnp.broadcast_to(along_lanes(valid_ref), (MINE, MINE))
    row = lax.broadcasted_iota(jnp.int32, (MINE, MINE), 0)
    col = lax.broadcasted_iota(jnp.int32, (MINE, MINE), 1)
    length = MINE // MICRO
    same = jnp.logical_and(seg == seg.T, row // length == col // length)
    position = jnp.sum(jnp.where(jnp.logical_and(same, col < row), 1.0, 0.0), -1, keepdims=True)
    usable = jnp.logical_or(valid > 0.0, row == col)
    allow[...] = jnp.where(
        jnp.logical_and(jnp.logical_and(same, col <= row), usable), 1.0, 0.0
    )
    weight[...] = valid.T
    freqs = jnp.exp(col.astype(F32) * (-2.0 * math.log(THETA) / HD))
    angles = position * freqs
    cosine[...] = jnp.cos(angles)
    sine[...] = jnp.sin(angles)
    stream = stream_of(x_ref)
    normed_in[...] = norm_rows(stream, gains[0:1, :]).astype(LOW)

    rows_out()
    down_x()
    into.turn(2)
    outof.hop(1)
    outof.hop(2)
    into.turn(3)
    into.near()
    outof.turn(0)
    outof.turn(1)
    outof.hop(3)
    into.far()
    outof.turn(2)
    outof.turn(3)
    outof.near()
    into.whole()

    down_out()
    flat_in = all_in.reshape(HEADS * HD + 2 * HD, D)
    flat_out = all_out.reshape(HEADS * HD, D)
    half = HD // 2

    def rows_of(j):
        return pl.ds(pl.multiple_of(j * HD, HD), HD)

    def project(j, carry):
        table = nt(normed_in[...], flat_in[rows_of(j), :])
        proj[j] = table

        @pl.when(j < HEADS + 1)
        def _():
            turned = norm_rows(table, head_gains[pl.ds(j // HEADS, 1), :])
            first, second = turned[:, :half], turned[:, half:]
            heads[j, :, :half] = (first * cosine[...] - second * sine[...]).astype(LOW)
            heads[j, :, half:] = (second * cosine[...] + first * sine[...]).astype(LOW)

        @pl.when(j == HEADS + 1)
        def _():
            heads[j] = table.astype(LOW)

        return carry

    lax.fori_loop(0, HEADS + 2, project, 0)
    outof.far()

    def attend_head(j, carry):
        seen = allow[...] > 0.0
        scores = nt(heads[j], heads[HEADS]) * SCALE_FACTOR
        masked = jnp.where(seen, scores, NEGATIVE)
        peak = jnp.max(masked, -1, keepdims=True)
        expo = jnp.where(seen, jnp.exp(masked - peak), 0.0)
        prob = expo / jnp.sum(expo, -1, keepdims=True)
        probs[j] = prob
        mixed[j] = nn(prob.astype(LOW), heads[HEADS + 1]).astype(LOW)
        return carry

    lax.fori_loop(0, HEADS, attend_head, 0)
    rows_on(0)
    outof.whole()

    attn_proj[...] = jnp.zeros((MINE, D), F32)

    def attn_out_head(j, carry):
        attn_proj[...] += nn(mixed[j], flat_out[rows_of(j), :])
        return carry

    lax.fori_loop(0, HEADS, attn_out_head, 0)
    branch = norm_rows(attn_proj[...], gains[1:2, :])
    mid = stream_of(x_ref) + branch
    middle[...] = mid
    rows[0] = norm_rows(mid, gains[2:3, :]).astype(LOW).reshape(2, PART, D)

    def counted(values):
        return jnp.sum(weight[:, 0:1] * jnp.sum(values * values, -1, keepdims=True))

    spot = lax.broadcasted_iota(jnp.int32, (1, D), 1)
    stats = jnp.where(spot == 4, jnp.sum(weight[:, 0:1]), 0.0)
    first_values = stream_of(x_ref)
    stats += jnp.where(spot == 0, counted(first_values), 0.0)
    stats += jnp.where(spot == 1, counted(mid), 0.0)
    stats += jnp.where(spot == 2, counted(branch), 0.0)
    small[0] = jnp.zeros((8, D), F32)
    small[0, 5:6, :] = stats

    zh, zl = z // 2, z % 2
    w_gu, w_dn = all_gu.reshape(2, 2, WIDE, D), all_dn.reshape(2, WIDE, D)

    class Half:
        def __init__(self, which, half, got_all, compute):
            self.which, self.half, self.got_all, self.compute = which, half, got_all, compute
            self.az, self.ay, self.ry, self.rz = (net.slots(4) for _ in range(4))
            self.gathered, self.here = [], set()

        def block(self, k, yy):
            there = z_peer(z, k)
            return self.got_all.at[self.half, there // 2, there % 2, yy]

        def pass_on(self, block, slot, device):
            net.send(block, block, slot, device)
            self.gathered.append(net.sent[-1])

        def start(self):
            own = rows.at[self.which, self.half]
            net.send(own, self.block(0, y), self.az + 1, z_peers[1])
            self.gathered.append(net.sent[-1])
            net.send(own, self.block(0, y), self.az + 2, z_peers[2])
            self.gathered.append(net.sent[-1])
            net.send(own, self.block(0, y), self.ay, yp)
            self.gathered.append(net.sent[-1])
            self.got_all[self.half, zh, zl, y] = rows[self.which, self.half]

        def hop(self, k):
            block = self.block(k, y)
            net.got(block, self.az + k)
            if k == 2:
                self.pass_on(block, self.az + 3, z_peers[1])
            self.pass_on(block, self.ay + k, yp)

        def arrive(self, g):
            if g not in self.here:
                for k in (2 * g, 2 * g + 1):
                    net.got(self.block(k, 1 - y), self.ay + k)
            self.here.add(g)

        def group(self, g):
            self.arrive(g)
            self.compute(self.half, zh if g == 0 else 1 - zh)
            keep[self.half, g] = acc[:, y]
            send_y[self.half, g] = acc[:, 1 - y].astype(LOW)
            net.send(send_y.at[self.half, g], recv_y.at[self.half, g], self.ry + g, yp)

        def fold(self, g):
            net.got(recv_y.at[self.half, g], self.ry + g)
            keep[self.half, g] += recv_y[self.half, g].astype(F32)
            send_z[self.half, g] = keep[self.half, g, 1 - zl].astype(LOW)
            net.send(send_z.at[self.half, g], recv_z.at[self.half, g], self.rz + g, z_peers[1])

        def cross(self):
            net.got(recv_z.at[self.half, 1], self.rz + 1)
            send_z[self.half, 2] = (
                keep[self.half, 1, zl] + recv_z[self.half, 1].astype(F32)
            ).astype(LOW)
            net.send(send_z.at[self.half, 2], recv_z.at[self.half, 2], self.rz + 2, z_peers[2])

        def done(self):
            net.got(recv_z.at[self.half, 0], self.rz)
            net.got(recv_z.at[self.half, 2], self.rz + 2)
            total[self.half] = (
                keep[self.half, 0, zl]
                + recv_z[self.half, 0].astype(F32)
                + recv_z[self.half, 2].astype(F32)
            )

    def columns(half, pair):
        return pl.ds(pl.multiple_of((half * 2 + pair) * PAIR, PAIR), PAIR)

    def put(h, part):
        part = part.reshape(2, 2, PART, D)

        @pl.when(h == 0)
        def _():
            acc[...] = part

        @pl.when(h == 1)
        def _():
            acc[...] += part

    def forward_pairs(half, pair):
        def one(h, carry):
            block = got_mid[half, pair].reshape(PAIR, D)
            gate = nt(block, w_gu[0, h])
            upward = nt(block, w_gu[1, h])
            square = gate * gate
            tanh = jnp.tanh(SQRT_2_OVER_PI * gate * (1.0 + CUBIC * square))
            side = 0.5 * (1.0 + tanh)
            gelu = gate * side
            slope = side + 0.5 * gate * (1.0 - tanh * tanh) * (
                SQRT_2_OVER_PI * (1.0 + 3.0 * CUBIC * square)
            )
            low = (gelu * upward).astype(LOW)
            slope_gate[h, half, pair] = (upward * slope).astype(LOW)
            slope_up[h, half, pair] = gelu.astype(LOW)
            put(h, nn(low, w_dn[h]))
            hidden_t[h, :, columns(half, pair)] = low.T
            return carry

        lax.fori_loop(0, 2, one, 0)

    def weights_here():
        net.settle_moves()
        net.flush(across_x)
        rows_across(1)
        rows_whole()

    def forward_end(half):
        span = pl.ds(half * PART, PART)
        ffw_proj = total[half]
        branch = norm_rows(ffw_proj, gains[3:4, :])
        layer_out[half, 0] = (middle[span, :] + branch).astype(LOW)
        counts = jnp.sum(weight[span, 0:1] * jnp.sum(branch * branch, -1, keepdims=True))
        small[0, 5:6, :] += jnp.where(spot == 3, counts, 0.0)
        grad, gain_grad = norm_back(ffw_proj, gains[3:4, :], cot[half, 0].astype(F32))
        small[0, 3:4, :] += gain_grad
        rows[1, half] = grad.astype(LOW)

    def backward_pairs(half, pair):
        def one(h, carry):
            block = got_up[half, pair].reshape(PAIR, D)
            back = nt(block, w_dn[h])
            gate = (back * slope_gate[h, half, pair].astype(F32)).astype(LOW)
            upward = (back * slope_up[h, half, pair].astype(F32)).astype(LOW)
            put(h, nn(gate, w_gu[0, h]) + nn(upward, w_gu[1, h]))
            slope_gate[h, half, pair] = gate
            slope_up[h, half, pair] = upward
            return carry

        lax.fori_loop(0, 2, one, 0)

    one, two = Half(0, 0, got_mid, forward_pairs), Half(0, 1, got_mid, forward_pairs)
    one.start()
    rows_on(1)
    rows_across(0)
    down_on()
    two.start()
    one.hop(1)
    two.hop(1)
    one.hop(2)
    two.hop(2)
    one.hop(3)
    two.hop(3)
    weights_here()
    one.group(0)
    one.group(1)
    one.fold(0)
    two.group(0)
    one.fold(1)
    two.group(1)
    one.cross()
    two.fold(0)
    one.done()
    forward_end(0)
    three, four = Half(1, 0, got_up, backward_pairs), Half(1, 1, got_up, backward_pairs)
    three.start()
    two.fold(1)
    three.hop(1)
    two.cross()
    three.hop(2)
    two.done()
    forward_end(1)
    four.start()
    net.flush([copy for copy in net.sent if not any(copy is other for other in three.gathered + four.gathered)])
    three.group(0)
    four.hop(1)
    three.hop(3)
    four.hop(2)
    three.group(1)
    three.fold(0)
    four.hop(3)
    four.group(0)
    three.fold(1)

    step = 384
    flat_mid, flat_up = got_mid.reshape(8 * MINE, D), got_up.reshape(8 * MINE, D)

    four.arrive(1)

    def down_grads(i, carry):
        h, cols = i // 3, pl.ds(pl.multiple_of(i % 3 * step, 128), step)
        d_dn.reshape(2, WIDE, D)[h, :, cols] = nn(hidden_t[h], flat_up[:, cols]).astype(LOW)
        return carry

    lax.fori_loop(0, 6, down_grads, 0)
    d_c, d_x, d_home, d_y = net.slots(5), net.slots(2), net.slots(2), net.slots(2)
    kept = (x + y + z) % 2
    net.send(d_dn.at[1 - c], n0, d_c, cp)
    four.group(1)
    three.cross()
    four.fold(0)

    def gate_up_grads(t, h, slopes):
        hidden_t[h] = slopes[h].reshape(8 * MINE, WIDE).T

        def part(i, carry):
            cols = pl.ds(pl.multiple_of(i * step, 128), step)
            w_gu[t, h, :, cols] = nn(hidden_t[h], flat_mid[:, cols]).astype(LOW)
            return carry

        lax.fori_loop(0, 3, part, 0)

    for h in range(2):
        gate_up_grads(0, h, slope_gate)
    net.send(all_gu.at[0, 1 - c], g0.at[0], d_c + 1, cp)
    net.got(n0, d_c)
    for q in range(2):
        d_dn[c, q] = added(d_dn[c, q], n0[q])
    net.send(d_dn.at[c, 1 - kept], n1, d_y, xp)
    four.fold(1)
    three.done()
    four.cross()
    for h in range(2):
        gate_up_grads(1, h, slope_up)
    net.send(all_gu.at[1, 1 - c], g0.at[1], d_c + 2, cp)

    def share(t):
        net.got(g0.at[t], d_c + 1 + t)
        for q in range(2):
            all_gu[t, c, q] = added(all_gu[t, c, q], g0[t, q])
        net.send(all_gu.at[t, c, 1 - x], g1.at[t], d_x + t, xp)

    share(0)
    share(1)
    four.done()

    mid = middle[...]
    grad, gain_grad = norm_back(mid, gains[2:3, :], total[...].reshape(MINE, D))
    small[0, 2:3, :] = gain_grad
    grad_mid = stream_of(cot) + grad
    grad_middle[...] = grad_mid
    grad, gain_grad = norm_back(attn_proj[...], gains[1:2, :], grad_mid)
    small[0, 1:2, :] = gain_grad
    grad_attn[...] = grad.astype(LOW)
    net.flush(three.gathered + four.gathered)
    d_out = got_up.reshape(4, 2, 2, 2, 32, D)
    a0 = got_mid.reshape(8 * MINE, D).at[pl.ds(0, 16 * 48)].reshape(4, 2, 2, 48, D)
    b0 = recv_y.reshape(4, 2, 2, 32, D)
    flat_d_out, flat_d_in = got_up.reshape(HEADS * HD, D), d_in.reshape(HEADS * HD + 2 * HD, D)

    def out_grads(j, carry):
        flat_d_out[rows_of(j), :] = tn(mixed[j], grad_attn[...]).astype(LOW)
        return carry

    lax.fori_loop(0, HEADS, out_grads, 0)
    net.send(d_out.at[:, :, :, 1 - c], b0, d_c + 3, cp)

    def home_down():
        net.got(n1, d_y)
        d_dn[c, kept] = added(d_dn[c, kept], n1[...])
        net.move(
            jnp.logical_and(z % 2 == y, x == y),
            d_dn.at[c, kept],
            n2,
            d_y + 1,
            d_y + 1,
            at(2 * (z // 2) + y, kept, z % 2, c),
        )

    def home_gate_up(t):
        net.got(g1.at[t], d_x + t)
        all_gu[t, c, x] = added(all_gu[t, c, x], g1[t])
        source = z // 2 + 2 * t
        net.move(
            jnp.logical_and(source == z, z % 2 == c),
            all_gu.at[t, c, x],
            g2.at[c],
            d_home + t,
            d_home + c,
            at(source, y, x, z % 2),
        )

    class Collect:
        def __init__(self, grads, core_in, y_in, x_in, z_in, core_slot):
            self.grads, self.core_in, self.y_in, self.x_in, self.z_in = (
                grads,
                core_in,
                y_in,
                x_in,
                z_in,
            )
            self.cs, self.ys, self.xs, self.zs = core_slot, net.slots(2), net.slots(2), net.slots(2)

        def cores(self):
            net.got(self.core_in, self.cs)
            for part, pair in enumerate((1 - zh, zh)):

                def one(i, carry):
                    p, q, r = 2 * pair + i // 4, i // 2 % 2, i % 2
                    self.grads[p, q, r, c] = added(self.grads[p, q, r, c], self.core_in[p, q, r])
                    return carry

                lax.fori_loop(0, 8, one, 0)
                both = pl.ds(2 * pair, 2)
                net.send(
                    self.grads.at[both, 1 - y, :, c], self.y_in.at[part], self.ys + part, yp
                )

        def ys_in(self, part):
            pair = (1 - zh, zh)[part]
            net.got(self.y_in.at[part], self.ys + part)

            def one(i, carry):
                p, q = i // 2, i % 2
                there = 2 * pair + p
                self.grads[there, y, q, c] = added(
                    self.grads[there, y, q, c], self.y_in[part, p, q]
                )
                return carry

            lax.fori_loop(0, 4, one, 0)
            net.send(
                self.grads.at[pl.ds(2 * pair, 2), y, 1 - x, c],
                self.x_in.at[part],
                self.xs + part,
                xp,
            )

        def xs_in(self, part):
            pair = (1 - zh, zh)[part]
            net.got(self.x_in.at[part], self.xs + part)
            for p in range(2):
                there = 2 * pair + p
                self.grads[there, y, x, c] = added(
                    self.grads[there, y, x, c], self.x_in[part, p]
                )
            net.send(
                self.grads.at[2 * pair + 1 - zl, y, x, c],
                self.z_in.at[part],
                self.zs + part,
                z_peers[1],
            )

        def cross(self, slot):
            net.got(self.z_in.at[0], self.zs)
            there = 2 * (1 - zh) + zl
            self.grads[there, y, x, c] = added(self.grads[there, y, x, c], self.z_in[0])
            net.send(self.grads.at[there, y, x, c], self.z_in.at[2], slot, z_peers[2])

        def done(self, slot, result):
            net.got(self.z_in.at[1], self.zs + 1)
            net.got(self.z_in.at[2], slot)
            result[...] = (
                self.grads[z, y, x, c].astype(F32)
                + self.z_in[1].astype(F32)
                + self.z_in[2].astype(F32)
            )

    r_s, r_z = net.slots(8), net.slots(2)
    outs = Collect(d_out, b0, b1, b2, b3, d_c + 3)
    ins = Collect(d_in, a0, a1, a2, a3, d_c + 4)

    grad_heads[...] = jnp.zeros((6, MINE, HD), F32)

    def head_back(j, carry):
        up = nt(grad_attn[...], flat_out[rows_of(j), :]).astype(LOW)
        prob = probs[j]
        grad_prob = nt(up, heads[HEADS + 1])
        grad_heads[HEADS + 1] += tn(prob.astype(LOW), up)
        center = jnp.sum(grad_prob * prob, -1, keepdims=True)
        grad_score = (prob * (grad_prob - center)).astype(LOW)
        grad_heads[j] = nn(grad_score, heads[HEADS]) * SCALE_FACTOR
        grad_heads[HEADS] += tn(grad_score, heads[j]) * SCALE_FACTOR
        return carry

    lax.fori_loop(0, HEADS, head_back, 0)
    key_acc[...] = jnp.zeros((2, HD), F32)

    def turn_back(j, carry):
        first, second = grad_heads[j, :, :half], grad_heads[j, :, half:]
        turned = jnp.concatenate(
            [
                first * cosine[...] + second * sine[...],
                second * cosine[...] - first * sine[...],
            ],
            -1,
        )
        which = pl.ds(j // HEADS, 1)
        grad, gain_grad = norm_back(proj[j], head_gains[which, :], turned)
        key_acc[which, :] += gain_grad
        grad_proj[j] = grad.astype(LOW)
        return carry

    lax.fori_loop(0, HEADS + 1, turn_back, 0)
    grad_proj[HEADS + 1] = grad_heads[HEADS + 1].astype(LOW)
    small[0, 4:5, 0:HD] = key_acc[0:1, :]
    small[0, 4:5, HD : 2 * HD] = key_acc[1:2, :]

    outs.cores()

    def in_grads(j, carry):
        flat_d_in[rows_of(j), :] = tn(grad_proj[j], normed_in[...]).astype(LOW)
        return carry

    lax.fori_loop(0, HEADS + 2, in_grads, 0)
    net.send(d_in.at[:, :, :, 1 - c], a0, d_c + 4, cp)
    home_down()
    total[...] = jnp.zeros((2, PART, D), F32)

    def in_back(j, carry):
        total[...] += nn(grad_proj[j], flat_in[rows_of(j), :]).reshape(2, PART, D)
        return carry

    lax.fori_loop(0, HEADS + 2, in_back, 0)
    ins.cores()
    grad, gain_grad = norm_back(stream_of(x_ref), gains[0:1, :], total[...].reshape(MINE, D))
    small[0, 0:1, :] = gain_grad
    input_grad[...] = (grad_middle[...] + grad).reshape(2, 1, PART, D)
    net.send(small.at[0], small.at[1], r_s, cp)
    home_gate_up(0)
    outs.ys_in(0)
    outs.ys_in(1)
    net.got(small.at[1], r_s)
    small[2] = small[0] + small[1]
    net.send(small.at[2], small.at[3], r_s + 1, xp)
    ins.ys_in(0)
    home_gate_up(1)
    outs.xs_in(0)
    outs.xs_in(1)
    net.got(small.at[3], r_s + 1)
    small[4] = small[2] + small[3]
    net.send(small.at[4], small.at[5], r_s + 2, yp)
    ins.ys_in(1)
    outs.cross(r_z)
    ins.xs_in(0)
    ins.xs_in(1)
    net.got(small.at[5], r_s + 2)
    small[6] = small[4] + small[5]
    for k in (1, 2, 3):
        net.send(small.at[6], small.at[6 + k], r_s + 2 + k, z_peers[k])
    ins.cross(r_z + 1)
    outs.done(r_z, o_out)
    net.got(n2, d_y + 1)
    o_dn[...] = n2[...].astype(F32)[:BLOCK]
    for k in (1, 2, 3):
        net.got(small.at[6 + k], r_s + 2 + k)
    sums = (small[6] + small[7]) + (small[8] + small[9])
    o_gains[...] = sums[0:4, :]
    o_heads[...] = jnp.concatenate([sums[4:5, 0:HD], sums[4:5, HD : 2 * HD]], 0)
    scaled = sums[5:6, :]
    tokens = jnp.sum(jnp.where(spot == 4, scaled, 0.0), -1, keepdims=True)
    means = jnp.sqrt(scaled / (tokens * D))
    for i in range(4):
        o_rms[i] = jnp.sum(jnp.where(spot == i, means, 0.0))
    ins.done(r_z + 1, o_in)
    for h in range(2):
        net.got(g2.at[h], d_home + h)
        o_gu[pl.ds(h * BLOCK, BLOCK), :] = g2[h].astype(F32)[:BLOCK]
    net.drain()


def vm(*shape):
    return pltpu.VMEM(shape, LOW)


def vf(*shape):
    return pltpu.VMEM(shape, F32)


def whole_layer(x, seg, valid, ain, aout, gu, dn, gains, head_gains, cot):
    vmem = pl.BlockSpec(memory_space=pltpu.VMEM)
    scratch = [
        vm(4, 2, 2, 2, 48, D),
        vm(4, 2, 2, 2, 32, D),
        vm(2, 2, 2, PADDED, D),
        vm(2, 2, PADDED, D),
        vf(MINE, MINE),
        vf(MINE, MINE),
        vf(MINE, MINE),
        vf(MINE, MINE),
        vm(MINE, D),
        vf(6, MINE, HD),
        vm(6, MINE, HD),
        vf(4, MINE, MINE),
        vm(4, MINE, HD),
        vf(MINE, D),
        vf(MINE, D),
        vm(2, 2, PART, D),
        vf(2, PART, D),
        vm(2, 2, 2, 2, PART, D),
        vm(2, 2, 2, 2, PART, D),
        vm(2, WIDE, 8 * MINE),
        vm(2, 2, 2, PAIR, WIDE),
        vm(2, 2, 2, PAIR, WIDE),
        vf(2, 2, PART, D),
        vf(2, 2, 2, PART, D),
        vm(2, 2, 2, PART, D),
        vm(2, 2, 2, PART, D),
        vm(2, 3, PART, D),
        vm(2, 3, PART, D),
        vf(MINE, D),
        vm(MINE, D),
        vf(6, MINE, HD),
        vm(6, MINE, HD),
        vf(2, HD),
        vm(4, 2, 2, 2, 48, D),
    ]
    for count in (48, 32):
        scratch += [vm(2, 2, 2, count, D), vm(2, 2, count, D), vm(3, count, D)]
    scratch += [vm(2, 2, PADDED, D), vm(2, PADDED, D), vm(2, PADDED, D)]
    scratch += [vm(2, 2, PADDED, D), vm(2, PADDED, D), vm(PADDED, D), vm(PADDED, D)]
    scratch += [vf(10, 8, D)]
    scratch += [pltpu.SemaphoreType.DMA((2,))] + [pltpu.SemaphoreType.DMA((144,))] * 2
    return pl.pallas_call(
        layer_kernel,
        out_shape=(
            jax.ShapeDtypeStruct((2, 1, PART, D), LOW),
            jax.ShapeDtypeStruct((2, 1, PART, D), F32),
            jax.ShapeDtypeStruct((48, D), F32),
            jax.ShapeDtypeStruct((32, D), F32),
            jax.ShapeDtypeStruct((2 * BLOCK, D), F32),
            jax.ShapeDtypeStruct((BLOCK, D), F32),
            jax.ShapeDtypeStruct((4, D), F32),
            jax.ShapeDtypeStruct((2, HD), F32),
            jax.ShapeDtypeStruct((4,), F32),
        ),
        in_specs=[vmem] * 10,
        out_specs=(vmem,) * 8 + (pl.BlockSpec(memory_space=pltpu.SMEM),),
        scratch_shapes=scratch,
        compiler_params=pltpu.CompilerParams(
            collective_id=1, has_side_effects=True, vmem_limit_bytes=VMEM_BYTES
        ),
        name="layer",
    )(x, seg, valid, ain, aout, gu, dn, gains, head_gains, cot)


def copy_kernel(*refs):
    count = (len(refs) - 2) // 3
    given, made, held = refs[:count], refs[count : 2 * count], refs[2 * count : 3 * count]
    into = [pltpu.make_async_copy(a, b, refs[-2].at[i]) for i, (a, b) in enumerate(zip(given, held))]
    out = [pltpu.make_async_copy(a, b, refs[-1].at[i]) for i, (a, b) in enumerate(zip(held, made))]
    for copy in into:
        copy.start()
    for first, second in zip(into, out):
        first.wait()
        second.start()
    for copy in out:
        copy.wait()


def copied(arrays):
    place = pl.BlockSpec(memory_space=pl.ANY)
    return pl.pallas_call(
        copy_kernel,
        out_shape=tuple(jax.ShapeDtypeStruct(array.shape, array.dtype) for array in arrays),
        in_specs=[place] * len(arrays),
        out_specs=(place,) * len(arrays),
        scratch_shapes=[pltpu.VMEM(array.shape, array.dtype) for array in arrays]
        + [pltpu.SemaphoreType.DMA((len(arrays),))] * 2,
        name="results",
    )(*arrays)


def split_shards(
    inputs,
    segment_ids,
    valid_mask,
    attn_in,
    attn_out,
    ffw_in,
    ffw_out,
    norm_gains,
    head_gains,
    cotangent,
):
    results = whole_layer(
        inputs,
        segment_ids,
        valid_mask,
        attn_in,
        attn_out,
        ffw_in,
        ffw_out,
        norm_gains,
        head_gains,
        cotangent,
    )
    return copied(results[:-1]) + results[-1:]


def solution(mesh):
    placed = (
        P(None, "dp", None, None),
        P(None, "dp", None),
        P(None, "dp", None),
        P("dp", None),
        P("dp", None),
        P("dp", None),
        P("dp", None),
        P(),
        P(),
        P(None, "dp", None, None),
    )
    return jax.shard_map(
        split_shards if mesh.shape["dp"] == 32 else general_shards,
        mesh=mesh,
        in_specs=placed,
        out_specs=(
            P(None, "dp", None, None),
            P(None, "dp", None, None),
            P("dp", None),
            P("dp", None),
            P("dp", None),
            P("dp", None),
            P(),
            P(),
            P(),
        ),
        check_vma=False,
    )
```

```python
import math

import jax
import jax.numpy as jnp
from jax import lax
from jax.experimental import pallas as pl
from jax.experimental.pallas import tpu as pltpu
from jax.sharding import PartitionSpec as P

D = 1152
HEADS = 4
HD = 256
FF = 6912
MICRO = 2


EPSILON = 1e-06
SCALE_FACTOR = 0.0625
THETA = 10000.0
NEGATIVE = -1e30


def shortened(x):

    def short(part):
        return part.astype(jnp.bfloat16) if part.dtype == jnp.float32 else part

    return jax.tree.map(short, x)


def swapped(block, axis, stride):
    count = lax.axis_size(axis)
    route = []
    for low in range(count):
        high = low | 1 << stride
        if high != low and high < count:
            route += [(low, high), (high, low)]
    return lax.ppermute(block, axis, route)


def norm_rows(values, gain):
    return values * lax.rsqrt(jnp.mean(values * values, -1, keepdims=True) + EPSILON) * gain


def rotate(values, cosine, sine):
    half = values.shape[-1] // 2
    first = values[..., :half]
    second = values[..., half:]
    return jnp.concatenate([first * cosine - second * sine, second * cosine + first * sine], -1)


def doc_tables(segments, validity, head_size):
    length = segments.shape[-1]
    places = jnp.arange(length, dtype=jnp.int32)
    same_doc = segments[..., :, None] == segments[..., None, :]
    earlier = places[None, :] < places[:, None]
    position = jnp.sum(jnp.logical_and(same_doc, earlier).astype(jnp.int32), -1)
    reach = places[None, :] <= places[:, None]
    usable = jnp.logical_or(validity[..., None, :] > 0, places[None, :] == places[:, None])
    allowed = jnp.logical_and(jnp.logical_and(same_doc, reach), usable)
    freqs = jnp.exp(
        jnp.arange(head_size // 2, dtype=jnp.float32) * (-2.0 * math.log(THETA) / head_size)
    )
    angles = position.astype(jnp.float32)[..., None] * freqs
    return (allowed, jnp.cos(angles), jnp.sin(angles))


def prepare(projected, head_gains, cosine, sine):
    width = HEADS * HD
    query = projected[..., :width].reshape(projected.shape[:-1] + (HEADS, HD))
    keys = projected[..., width : width + HD]
    values = projected[..., width + HD :]
    query = rotate(norm_rows(query, head_gains[0]), cosine[..., None, :], sine[..., None, :])
    keys = rotate(norm_rows(keys, head_gains[1]), cosine, sine)
    return (query, keys, values)


def across(left, piece):
    return lax.dot_general(
        left, piece, (((1,), (1,)), ((), ())), preferred_element_type=jnp.float32
    )


def over_rows(left, right):
    return lax.dot_general(
        left, right, (((0,), (0,)), ((), ())), preferred_element_type=jnp.float32
    )


def score_table(query_low, keys_low):
    return (
        jnp.einsum("qhd,kd->hqk", query_low, keys_low, preferred_element_type=jnp.float32)
        * SCALE_FACTOR
    )


def attend(query_low, keys_low, values_low, allowed):
    scores = score_table(query_low, keys_low)
    masked = jnp.where(allowed[None], scores, NEGATIVE)
    peak = jnp.max(masked, -1, keepdims=True)
    expo = jnp.where(allowed[None], jnp.exp(masked - peak), 0.0)
    totals = jnp.sum(expo, -1, keepdims=True)
    probs = expo / totals
    mixed = jnp.einsum(
        "hqk,kd->qhd", probs.astype(jnp.bfloat16), values_low, preferred_element_type=jnp.float32
    )
    return (mixed, peak + jnp.log(totals))


def attend_back(query_low, keys_low, values_low, allowed, log_sum, grad_low):
    scores = score_table(query_low, keys_low)
    probs = jnp.where(allowed[None], jnp.exp(scores - log_sum), 0.0)
    grad_probs = jnp.einsum("qhd,kd->hqk", grad_low, values_low, preferred_element_type=jnp.float32)
    grad_values = jnp.einsum(
        "hqk,qhd->kd", probs.astype(jnp.bfloat16), grad_low, preferred_element_type=jnp.float32
    )
    center = jnp.sum(grad_probs * probs, -1, keepdims=True)
    grad_scores = (probs * (grad_probs - center)).astype(jnp.bfloat16)
    grad_query = (
        jnp.einsum("hqk,kd->qhd", grad_scores, keys_low, preferred_element_type=jnp.float32)
        * SCALE_FACTOR
    )
    grad_keys = (
        jnp.einsum("hqk,qhd->kd", grad_scores, query_low, preferred_element_type=jnp.float32)
        * SCALE_FACTOR
    )
    return (grad_query, grad_keys, grad_values)


def gated(gate, upward):
    return jax.nn.gelu(gate, approximate=True) * upward


def general_shards(
    inputs,
    segment_ids,
    valid_mask,
    attn_in,
    attn_out,
    ffw_in,
    ffw_out,
    norm_gains,
    head_gains,
    cotangent,
):
    width = HEADS * HD
    kept_proj = []
    kept_normed_in = []
    kept_mixed = []
    kept_attn = []
    kept_gate = []
    kept_normed_mid = []
    kept_hidden = []
    kept_ffw = []
    gain_sums = jnp.zeros((4, D), jnp.float32)
    head_sums = jnp.zeros((2, HD), jnp.float32)
    stats = jnp.zeros((5,), jnp.float32)
    results = []
    input_grads = []
    for step in range(MICRO):
        full_in, full_out = (
            lax.all_gather(attn_in, "dp", axis=0, tiled=True),
            lax.all_gather(attn_out, "dp", axis=0, tiled=True),
        )
        full_ffin, full_ffout = (
            lax.all_gather(ffw_in, "dp", axis=0, tiled=True),
            lax.all_gather(ffw_out, "dp", axis=0, tiled=True),
        )
        stream = inputs[step, 0].astype(jnp.float32)
        length = stream.shape[0]
        allowed, cosine, sine = doc_tables(segment_ids[step, 0], valid_mask[step, 0], HD)
        normed_in = norm_rows(stream, norm_gains[0]).astype(jnp.bfloat16)
        projected = across(normed_in, full_in)
        query, keys, values = prepare(projected, head_gains, cosine, sine)
        query_low = query.astype(jnp.bfloat16)
        keys_low = keys.astype(jnp.bfloat16)
        values_low = values.astype(jnp.bfloat16)
        mixed, log_sum = attend(query_low, keys_low, values_low, allowed)
        mixed_low = mixed.reshape(length, width).astype(jnp.bfloat16)
        attn_proj = jnp.dot(mixed_low, full_out, preferred_element_type=jnp.float32)
        attn_branch = norm_rows(attn_proj, norm_gains[1])
        middle = stream + attn_branch
        normed_mid = norm_rows(middle, norm_gains[2]).astype(jnp.bfloat16)
        gate_up = across(normed_mid, full_ffin)
        gate = gate_up[:, :FF]
        upward = gate_up[:, FF:]
        hidden = gated(gate, upward).astype(jnp.bfloat16)
        ffw_proj = jnp.dot(hidden, full_ffout, preferred_element_type=jnp.float32)
        ffw_branch = norm_rows(ffw_proj, norm_gains[3])
        results.append((middle + ffw_branch).astype(jnp.bfloat16))
        weight = valid_mask[step, 0].astype(jnp.float32)
        sums = [
            jnp.sum(weight * jnp.sum(value * value, -1))
            for value in (stream, middle, attn_branch, ffw_branch)
        ]
        sums.append(jnp.sum(weight))
        stats = stats + jnp.stack(sums)
        upstream = cotangent[step, 0].astype(jnp.float32)
        _, back_ffw = jax.vjp(norm_rows, ffw_proj, norm_gains[3])
        grad_ffw_proj, gain_three = back_ffw(upstream)
        grad_ffw_low = grad_ffw_proj.astype(jnp.bfloat16)
        grad_hidden = across(grad_ffw_low, full_ffout)
        _, back_gated = jax.vjp(gated, gate, upward)
        grad_gate, grad_upward = back_gated(grad_hidden)
        grad_gate_up = jnp.concatenate([grad_gate, grad_upward], 1).astype(jnp.bfloat16)
        grad_normed_mid = jnp.dot(grad_gate_up, full_ffin, preferred_element_type=jnp.float32)
        _, back_mid = jax.vjp(norm_rows, middle, norm_gains[2])
        grad_mid_part, gain_two = back_mid(grad_normed_mid)
        grad_middle = upstream + grad_mid_part
        _, back_attn = jax.vjp(norm_rows, attn_proj, norm_gains[1])
        grad_attn_proj, gain_one = back_attn(grad_middle)
        grad_attn_low = grad_attn_proj.astype(jnp.bfloat16)
        grad_mixed = across(grad_attn_low, full_out)
        grad_mixed_low = grad_mixed.astype(jnp.bfloat16).reshape(length, HEADS, HD)
        grad_query, grad_keys, grad_values = attend_back(
            query_low, keys_low, values_low, allowed, log_sum, grad_mixed_low
        )
        _, back_prep = jax.vjp(
            lambda table, gains: prepare(table, gains, cosine, sine), projected, head_gains
        )
        grad_projected, grad_heads = back_prep((grad_query, grad_keys, grad_values))
        grad_proj_low = grad_projected.astype(jnp.bfloat16)
        grad_normed_in = jnp.dot(grad_proj_low, full_in, preferred_element_type=jnp.float32)
        _, back_in = jax.vjp(norm_rows, stream, norm_gains[0])
        grad_stream, gain_zero = back_in(grad_normed_in)
        input_grads.append(grad_middle + grad_stream)
        gain_sums = gain_sums + jnp.stack([gain_zero, gain_one, gain_two, gain_three])
        head_sums = head_sums + grad_heads
        kept_proj.append(grad_proj_low)
        kept_normed_in.append(normed_in)
        kept_mixed.append(mixed_low)
        kept_attn.append(grad_attn_low)
        kept_gate.append(grad_gate_up)
        kept_normed_mid.append(normed_mid)
        kept_hidden.append(hidden)
        kept_ffw.append(grad_ffw_low)
    pairs = [
        (jnp.concatenate(kept_proj, 0), jnp.concatenate(kept_normed_in, 0)),
        (jnp.concatenate(kept_mixed, 0), jnp.concatenate(kept_attn, 0)),
        (jnp.concatenate(kept_gate, 0), jnp.concatenate(kept_normed_mid, 0)),
        (jnp.concatenate(kept_hidden, 0), jnp.concatenate(kept_ffw, 0)),
    ]
    levels = lax.axis_size("dp").bit_length() - 1
    place = lax.axis_index("dp")
    top_bit = place >> levels - 1 & 1
    kept_parts = []
    sent_parts = []
    for left, right in pairs:
        half_cols = left.shape[1] // 2
        kept_parts.append(
            over_rows(lax.dynamic_slice_in_dim(left, top_bit * half_cols, half_cols, 1), right)
        )
        sent_parts.append(
            over_rows(
                lax.dynamic_slice_in_dim(left, (1 - top_bit) * half_cols, half_cols, 1), right
            )
        )
    current = tuple(kept_parts)
    outgoing = tuple(sent_parts)
    for level in range(levels):
        bit = levels - 1 - level
        arrived = jax.tree.map(
            lambda part, own: part.astype(own.dtype),
            swapped(shortened(outgoing), "dp", bit),
            outgoing,
        )
        current = tuple((mine + theirs for mine, theirs in zip(current, arrived)))
        if level + 1 < levels:
            next_bit = place >> bit - 1 & 1
            halves = [piece.shape[0] // 2 for piece in current]
            outgoing = tuple(
                (
                    lax.dynamic_slice_in_dim(piece, (1 - next_bit) * rows, rows, 0)
                    for piece, rows in zip(current, halves)
                )
            )
            current = tuple(
                (
                    lax.dynamic_slice_in_dim(piece, next_bit * rows, rows, 0)
                    for piece, rows in zip(current, halves)
                )
            )
    shard_in, shard_out, shard_ffin, shard_ffout = current
    gain_total, head_total, stat_total = lax.psum((gain_sums, head_sums, stats), "dp")
    rms_values = jnp.sqrt(stat_total[:4] / (stat_total[4] * D))
    layer_out = jnp.stack(results)[:, None]
    input_grad = jnp.stack(input_grads)[:, None]
    return (
        layer_out,
        input_grad,
        shard_in,
        shard_out,
        shard_ffin,
        shard_ffout,
        gain_total,
        head_total,
        rms_values,
    )


BLOCK = 216
PADDED = 224
WIDE = 2 * PADDED
MINE = 128
PART = 64
PAIR = 2 * MINE
VMEM_BYTES = 62 << 20
SQRT_2_OVER_PI = math.sqrt(2.0 / math.pi)
CUBIC = 0.044715
MESH = pl.DeviceIdType.MESH
LOW = jnp.bfloat16
F32 = jnp.float32


def spots():
    me = lax.axis_index("dp")
    return me, me // 8, me // 4 % 2, me // 2 % 2, me % 2


def at(z, y, x, c):
    return z * 8 + y * 4 + x * 2 + c


def z_peer(z, k):
    if k == 0:
        return z
    if k == 1:
        return z + 1 - 2 * (z % 2)
    if k == 2:
        return (z + 2) % 4
    return 3 - z


def greet(z, y, x, c):
    barrier = pltpu.get_barrier_semaphore()
    others = [at(z_peer(z, k), y, x, core) for k in (1, 2, 3) for core in (c, 1 - c)]
    others.append(at(z, y, x, 1 - c))
    for k in range(2):
        for there_y, there_x in ((1 - y, x), (y, 1 - x), (1 - y, 1 - x)):
            others.append(at(z_peer(z, k), there_y, there_x, c))
    for device in others:
        pl.semaphore_signal(barrier, inc=1, device_id=(device,), device_id_type=MESH)
    pl.semaphore_wait(barrier, len(others))


def nt(left, right):
    return lax.dot_general(left, right, (((1,), (1,)), ((), ())), preferred_element_type=F32)


def nn(left, right):
    return lax.dot_general(left, right, (((1,), (0,)), ((), ())), preferred_element_type=F32)


def tn(left, right):
    return lax.dot_general(left, right, (((0,), (0,)), ((), ())), preferred_element_type=F32)


def norm_back(values, gain, upstream):
    scale = lax.rsqrt(jnp.mean(values * values, -1, keepdims=True) + EPSILON)
    normed = values * scale
    gain_grad = jnp.sum(upstream * normed, 0, keepdims=True)
    inner = upstream * gain
    grad = scale * (inner - normed * jnp.mean(inner * normed, -1, keepdims=True))
    return grad, gain_grad


def added(left, right):
    return (left.astype(F32) + right.astype(F32)).astype(LOW)


def stream_of(ref):
    return ref[...].reshape(MINE, D).astype(F32)


class Net:
    def __init__(self, send_sems, recv_sems, anyone):
        self.send_sems, self.recv_sems, self.anyone = send_sems, recv_sems, anyone
        self.used, self.sent, self.maybe = 0, [], []

    def slots(self, count):
        first = self.used
        self.used += count
        return first

    def copy(self, src, dst, send_slot, recv_slot, device):
        return pltpu.make_async_remote_copy(
            src_ref=src,
            dst_ref=dst,
            send_sem=self.send_sems.at[send_slot],
            recv_sem=self.recv_sems.at[recv_slot],
            device_id=(device,),
            device_id_type=MESH,
        )

    def send(self, src, dst, slot, device):
        copy = self.copy(src, dst, slot, slot, device)
        copy.start()
        self.sent.append(copy)

    def move(self, stays, src, dst, send_slot, recv_slot, device):
        copy = self.copy(src, dst, send_slot, recv_slot, device)

        @pl.when(stays)
        def _():
            pltpu.make_async_copy(src, dst, self.recv_sems.at[recv_slot]).start()

        @pl.when(jnp.logical_not(stays))
        def _():
            copy.start()

        self.maybe.append((stays, copy))

    def got(self, block, slot):
        self.copy(block, block, slot, slot, self.anyone).wait_recv()

    def flush(self, gone):
        for copy in gone:
            copy.wait_send()
        names = {id(copy) for copy in gone}
        self.sent = [copy for copy in self.sent if id(copy) not in names]

    def drain(self):
        self.flush(list(self.sent))
        self.settle_moves()

    def settle_moves(self):
        for stays, copy in self.maybe:

            @pl.when(jnp.logical_not(stays))
            def _():
                copy.wait_send()

        self.maybe = []


def layer_kernel(*refs):
    (
        x_ref,
        seg_ref,
        valid_ref,
        ain,
        aout,
        gu,
        dn,
        gains,
        head_gains,
        cot,
        layer_out,
        input_grad,
        o_in,
        o_out,
        o_gu,
        o_dn,
        o_gains,
        o_heads,
        o_rms,
        all_in,
        all_out,
        all_gu,
        all_dn,
        allow,
        cosine,
        sine,
        weight,
        normed_in,
        proj,
        heads,
        probs,
        mixed,
        attn_proj,
        middle,
        rows,
        total,
        got_mid,
        got_up,
        hidden_t,
        slope_gate,
        slope_up,
        acc,
        keep,
        send_y,
        recv_y,
        send_z,
        recv_z,
        grad_middle,
        grad_attn,
        grad_heads,
        grad_proj,
        key_acc,
        d_in,
        a1,
        a2,
        a3,
        b1,
        b2,
        b3,
        g0,
        g1,
        g2,
        d_dn,
        n0,
        n1,
        n2,
        small,
        local,
        send_sems,
        recv_sems,
    ) = refs
    me, z, y, x, c = spots()
    xp, yp, cp = at(z, y, 1 - x, c), at(z, 1 - y, x, c), at(z, y, x, 1 - c)
    z_peers = [at(z_peer(z, k), y, x, c) for k in range(4)]
    net = Net(send_sems, recv_sems, cp)
    keep_in = pltpu.make_async_copy(ain, all_in.at[z, y, x, c], local.at[0])
    keep_out = pltpu.make_async_copy(aout, all_out.at[z, y, x, c], local.at[1])
    keep_in.start()
    keep_out.start()
    greet(z, y, x, c)

    class Spread:
        def __init__(self, own, full, x_first):
            self.own, self.full, self.x_first = own, full, x_first
            self.first, self.second = (xp, yp) if x_first else (yp, xp)
            self.az, self.ax, self.ay, self.ac = (net.slots(4) for _ in range(4))

        def block(self, k):
            return self.full.at[z_peer(z, k), y, x, c]

        def crossed(self, k):
            there = z_peer(z, k)
            return self.full.at[there, y, 1 - x, c] if self.x_first else self.full.at[there, 1 - y, x, c]

        def pair(self, there, own, core):
            if self.x_first:
                return self.full.at[there, y if own else 1 - y, :, core]
            return self.full.at[there, :, x if own else 1 - x, core]

        def start(self):
            net.send(self.own, self.block(0), self.az + 1, z_peers[1])
            net.send(self.own, self.block(0), self.ax, self.first)
            net.send(self.own, self.block(0), self.az + 2, z_peers[2])

        def hop(self, k):
            block = self.block(k)
            net.got(block, self.az + k)
            if k == 2:
                net.send(block, block, self.az + 3, z_peers[1])
            net.send(block, block, self.ax + k, self.first)

        def turn(self, k):
            net.got(self.crossed(k), self.ax + k)
            pair = self.pair(z_peer(z, k), True, c)
            net.send(pair, pair, self.ay + k, self.second)

        def near(self):
            part = self.pair(slice(None), True, c)
            net.send(part, part, self.ac, cp)

        def far(self):
            for k in range(4):
                net.got(self.pair(z_peer(z, k), False, c), self.ay + k)
            part = self.pair(slice(None), False, c)
            net.send(part, part, self.ac + 1, cp)

        def whole(self):
            net.got(self.pair(slice(None), True, 1 - c), self.ac)
            net.got(self.pair(slice(None), False, 1 - c), self.ac + 1)

    into, outof = Spread(ain, all_in, True), Spread(aout, all_out, False)
    into.start()
    w_one, w_two, w_c, w_d = net.slots(2), net.slots(2), net.slots(2), net.slots(2)
    v_x, v_one, v_c = net.slots(1), net.slots(2), net.slots(1)
    kind, goal = z // 2, 2 * (z % 2) + c
    blank = jnp.zeros((PADDED - BLOCK, D), F32)
    for h in range(2):
        part = gu[pl.ds(h * BLOCK, BLOCK), :].astype(F32)
        g0[0, h] = jnp.concatenate([part, blank], 0).astype(LOW)
    n0[0] = jnp.concatenate([dn[...].astype(F32), blank], 0).astype(LOW)

    def rows_out():
        for h in range(2):
            net.move(
                jnp.logical_and(goal == z, c == h),
                g0.at[0, h],
                all_gu.at[kind, h, x],
                w_one + h,
                w_one + kind,
                at(goal, y, x, h),
            )

    def rows_on(which):
        t = (kind, 1 - kind)[which]
        block = all_gu.at[t, c, x]
        net.got(block, w_one + t)
        net.send(block, block, w_two + which, xp)
        net.send(block, block, w_c + which, cp)

    def rows_across(which):
        block = all_gu.at[(kind, 1 - kind)[which], c, 1 - x]
        net.got(block, w_two + which)
        net.send(block, block, w_d + which, cp)

    def rows_whole():
        for which in range(2):
            t = (kind, 1 - kind)[which]
            net.got(all_gu.at[t, 1 - c, x], w_c + which)
            net.got(all_gu.at[t, 1 - c, 1 - x], w_d + which)
        net.got(all_dn.at[1 - c], v_c)

    across_x = []

    def down_x():
        net.send(n0.at[0], n0.at[1], v_x, xp)
        across_x.append(net.sent[-1])


    def down_out():
        net.got(n0.at[1], v_x)
        for other in range(2):
            block_x = 1 - x if other else x
            net.move(
                jnp.logical_and(z % 2 == block_x, z % 2 == y),
                n0.at[other],
                all_dn.at[c, y],
                v_one + other,
                v_one + y,
                at(2 * (z // 2) + block_x, z % 2, x, c),
            )

    def down_on():
        for q in range(2):
            net.got(all_dn.at[c, q], v_one + q)
        net.send(all_dn.at[c], all_dn.at[c], v_c, cp)

    into.hop(1)
    into.hop(2)
    outof.start()
    keep_in.wait()
    keep_out.wait()
    into.turn(0)
    into.turn(1)
    into.hop(3)

    def along_lanes(ref):
        return jnp.concatenate([ref[0].astype(F32), ref[1].astype(F32)], 1)

    seg = jnp.broadcast_to(along_lanes(seg_ref), (MINE, MINE))
    valid = jnp.broadcast_to(along_lanes(valid_ref), (MINE, MINE))
    row = lax.broadcasted_iota(jnp.int32, (MINE, MINE), 0)
    col = lax.broadcasted_iota(jnp.int32, (MINE, MINE), 1)
    length = MINE // MICRO
    same = jnp.logical_and(seg == seg.T, row // length == col // length)
    position = jnp.sum(jnp.where(jnp.logical_and(same, col < row), 1.0, 0.0), -1, keepdims=True)
    usable = jnp.logical_or(valid > 0.0, row == col)
    allow[...] = jnp.where(
        jnp.logical_and(jnp.logical_and(same, col <= row), usable), 1.0, 0.0
    )
    weight[...] = valid.T
    freqs = jnp.exp(col.astype(F32) * (-2.0 * math.log(THETA) / HD))
    angles = position * freqs
    cosine[...] = jnp.cos(angles)
    sine[...] = jnp.sin(angles)
    stream = stream_of(x_ref)
    normed_in[...] = norm_rows(stream, gains[0:1, :]).astype(LOW)

    rows_out()
    down_x()
    into.turn(2)
    outof.hop(1)
    outof.hop(2)
    into.turn(3)
    into.near()
    outof.turn(0)
    outof.turn(1)
    outof.hop(3)
    into.far()
    outof.turn(2)
    outof.turn(3)
    outof.near()
    into.whole()

    down_out()
    flat_in = all_in.reshape(HEADS * HD + 2 * HD, D)
    flat_out = all_out.reshape(HEADS * HD, D)
    half = HD // 2

    def rows_of(j):
        return pl.ds(pl.multiple_of(j * HD, HD), HD)

    def project(j, carry):
        table = nt(normed_in[...], flat_in[rows_of(j), :])
        proj[j] = table

        @pl.when(j < HEADS + 1)
        def _():
            turned = norm_rows(table, head_gains[pl.ds(j // HEADS, 1), :])
            first, second = turned[:, :half], turned[:, half:]
            heads[j, :, :half] = (first * cosine[...] - second * sine[...]).astype(LOW)
            heads[j, :, half:] = (second * cosine[...] + first * sine[...]).astype(LOW)

        @pl.when(j == HEADS + 1)
        def _():
            heads[j] = table.astype(LOW)

        return carry

    lax.fori_loop(0, HEADS + 2, project, 0)
    outof.far()

    def attend_head(j, carry):
        seen = allow[...] > 0.0
        scores = nt(heads[j], heads[HEADS]) * SCALE_FACTOR
        masked = jnp.where(seen, scores, NEGATIVE)
        peak = jnp.max(masked, -1, keepdims=True)
        expo = jnp.where(seen, jnp.exp(masked - peak), 0.0)
        prob = expo / jnp.sum(expo, -1, keepdims=True)
        probs[j] = prob
        mixed[j] = nn(prob.astype(LOW), heads[HEADS + 1]).astype(LOW)
        return carry

    lax.fori_loop(0, HEADS, attend_head, 0)
    rows_on(0)
    outof.whole()

    attn_proj[...] = jnp.zeros((MINE, D), F32)

    def attn_out_head(j, carry):
        attn_proj[...] += nn(mixed[j], flat_out[rows_of(j), :])
        return carry

    lax.fori_loop(0, HEADS, attn_out_head, 0)
    branch = norm_rows(attn_proj[...], gains[1:2, :])
    mid = stream_of(x_ref) + branch
    middle[...] = mid
    rows[0] = norm_rows(mid, gains[2:3, :]).astype(LOW).reshape(2, PART, D)

    def counted(values):
        return jnp.sum(weight[:, 0:1] * jnp.sum(values * values, -1, keepdims=True))

    spot = lax.broadcasted_iota(jnp.int32, (1, D), 1)
    stats = jnp.where(spot == 4, jnp.sum(weight[:, 0:1]), 0.0)
    first_values = stream_of(x_ref)
    stats += jnp.where(spot == 0, counted(first_values), 0.0)
    stats += jnp.where(spot == 1, counted(mid), 0.0)
    stats += jnp.where(spot == 2, counted(branch), 0.0)
    small[0] = jnp.zeros((8, D), F32)
    small[0, 5:6, :] = stats

    zh, zl = z // 2, z % 2
    w_gu, w_dn = all_gu.reshape(2, 2, WIDE, D), all_dn.reshape(2, WIDE, D)

    class Half:
        def __init__(self, which, half, got_all, compute):
            self.which, self.half, self.got_all, self.compute = which, half, got_all, compute
            self.az, self.ay, self.ry, self.rz = (net.slots(4) for _ in range(4))
            self.gathered, self.here = [], set()

        def block(self, k, yy):
            there = z_peer(z, k)
            return self.got_all.at[self.half, there // 2, there % 2, yy]

        def pass_on(self, block, slot, device):
            net.send(block, block, slot, device)
            self.gathered.append(net.sent[-1])

        def start(self):
            own = rows.at[self.which, self.half]
            net.send(own, self.block(0, y), self.az + 1, z_peers[1])
            self.gathered.append(net.sent[-1])
            net.send(own, self.block(0, y), self.az + 2, z_peers[2])
            self.gathered.append(net.sent[-1])
            net.send(own, self.block(0, y), self.ay, yp)
            self.gathered.append(net.sent[-1])
            self.got_all[self.half, zh, zl, y] = rows[self.which, self.half]

        def hop(self, k):
            block = self.block(k, y)
            net.got(block, self.az + k)
            if k == 2:
                self.pass_on(block, self.az + 3, z_peers[1])
            self.pass_on(block, self.ay + k, yp)

        def arrive(self, g):
            if g not in self.here:
                for k in (2 * g, 2 * g + 1):
                    net.got(self.block(k, 1 - y), self.ay + k)
            self.here.add(g)

        def group(self, g):
            self.arrive(g)
            self.compute(self.half, zh if g == 0 else 1 - zh)
            keep[self.half, g] = acc[:, y]
            send_y[self.half, g] = acc[:, 1 - y].astype(LOW)
            net.send(send_y.at[self.half, g], recv_y.at[self.half, g], self.ry + g, yp)

        def fold(self, g):
            net.got(recv_y.at[self.half, g], self.ry + g)
            keep[self.half, g] += recv_y[self.half, g].astype(F32)
            send_z[self.half, g] = keep[self.half, g, 1 - zl].astype(LOW)
            net.send(send_z.at[self.half, g], recv_z.at[self.half, g], self.rz + g, z_peers[1])

        def cross(self):
            net.got(recv_z.at[self.half, 1], self.rz + 1)
            send_z[self.half, 2] = (
                keep[self.half, 1, zl] + recv_z[self.half, 1].astype(F32)
            ).astype(LOW)
            net.send(send_z.at[self.half, 2], recv_z.at[self.half, 2], self.rz + 2, z_peers[2])

        def done(self):
            net.got(recv_z.at[self.half, 0], self.rz)
            net.got(recv_z.at[self.half, 2], self.rz + 2)
            total[self.half] = (
                keep[self.half, 0, zl]
                + recv_z[self.half, 0].astype(F32)
                + recv_z[self.half, 2].astype(F32)
            )

    def columns(half, pair):
        return pl.ds(pl.multiple_of((half * 2 + pair) * PAIR, PAIR), PAIR)

    def put(h, part):
        part = part.reshape(2, 2, PART, D)

        @pl.when(h == 0)
        def _():
            acc[...] = part

        @pl.when(h == 1)
        def _():
            acc[...] += part

    def forward_pairs(half, pair):
        def one(h, carry):
            block = got_mid[half, pair].reshape(PAIR, D)
            gate = nt(block, w_gu[0, h])
            upward = nt(block, w_gu[1, h])
            square = gate * gate
            tanh = jnp.tanh(SQRT_2_OVER_PI * gate * (1.0 + CUBIC * square))
            side = 0.5 * (1.0 + tanh)
            gelu = gate * side
            slope = side + 0.5 * gate * (1.0 - tanh * tanh) * (
                SQRT_2_OVER_PI * (1.0 + 3.0 * CUBIC * square)
            )
            low = (gelu * upward).astype(LOW)
            slope_gate[h, half, pair] = (upward * slope).astype(LOW)
            slope_up[h, half, pair] = gelu.astype(LOW)
            put(h, nn(low, w_dn[h]))
            hidden_t[h, :, columns(half, pair)] = low.T
            return carry

        lax.fori_loop(0, 2, one, 0)

    def weights_here():
        net.settle_moves()
        net.flush(across_x)
        rows_across(1)
        rows_whole()

    def forward_end(half):
        span = pl.ds(half * PART, PART)
        ffw_proj = total[half]
        branch = norm_rows(ffw_proj, gains[3:4, :])
        layer_out[half, 0] = (middle[span, :] + branch).astype(LOW)
        counts = jnp.sum(weight[span, 0:1] * jnp.sum(branch * branch, -1, keepdims=True))
        small[0, 5:6, :] += jnp.where(spot == 3, counts, 0.0)
        grad, gain_grad = norm_back(ffw_proj, gains[3:4, :], cot[half, 0].astype(F32))
        small[0, 3:4, :] += gain_grad
        rows[1, half] = grad.astype(LOW)

    def backward_pairs(half, pair):
        def one(h, carry):
            block = got_up[half, pair].reshape(PAIR, D)
            back = nt(block, w_dn[h])
            gate = (back * slope_gate[h, half, pair].astype(F32)).astype(LOW)
            upward = (back * slope_up[h, half, pair].astype(F32)).astype(LOW)
            put(h, nn(gate, w_gu[0, h]) + nn(upward, w_gu[1, h]))
            slope_gate[h, half, pair] = gate
            slope_up[h, half, pair] = upward
            return carry

        lax.fori_loop(0, 2, one, 0)

    one, two = Half(0, 0, got_mid, forward_pairs), Half(0, 1, got_mid, forward_pairs)
    one.start()
    rows_on(1)
    rows_across(0)
    down_on()
    two.start()
    one.hop(1)
    two.hop(1)
    one.hop(2)
    two.hop(2)
    one.hop(3)
    two.hop(3)
    weights_here()
    one.group(0)
    one.group(1)
    one.fold(0)
    two.group(0)
    one.fold(1)
    two.group(1)
    one.cross()
    two.fold(0)
    one.done()
    forward_end(0)
    three, four = Half(1, 0, got_up, backward_pairs), Half(1, 1, got_up, backward_pairs)
    three.start()
    two.fold(1)
    three.hop(1)
    two.cross()
    three.hop(2)
    two.done()
    forward_end(1)
    four.start()
    net.flush([copy for copy in net.sent if not any(copy is other for other in three.gathered + four.gathered)])
    three.group(0)
    four.hop(1)
    three.hop(3)
    four.hop(2)
    three.group(1)
    three.fold(0)
    four.hop(3)
    four.group(0)
    three.fold(1)

    step = 384
    flat_mid, flat_up = got_mid.reshape(8 * MINE, D), got_up.reshape(8 * MINE, D)

    four.arrive(1)

    def down_grads(i, carry):
        h, cols = i // 3, pl.ds(pl.multiple_of(i % 3 * step, 128), step)
        d_dn.reshape(2, WIDE, D)[h, :, cols] = nn(hidden_t[h], flat_up[:, cols]).astype(LOW)
        return carry

    lax.fori_loop(0, 6, down_grads, 0)
    d_c, d_x, d_home, d_y = net.slots(5), net.slots(2), net.slots(2), net.slots(2)
    kept = (x + y + z) % 2
    net.send(d_dn.at[1 - c], n0, d_c, cp)
    four.group(1)
    three.cross()
    four.fold(0)

    def gate_up_grads(t, h, slopes):
        hidden_t[h] = slopes[h].reshape(8 * MINE, WIDE).T

        def part(i, carry):
            cols = pl.ds(pl.multiple_of(i * step, 128), step)
            w_gu[t, h, :, cols] = nn(hidden_t[h], flat_mid[:, cols]).astype(LOW)
            return carry

        lax.fori_loop(0, 3, part, 0)

    for h in range(2):
        gate_up_grads(0, h, slope_gate)
    net.send(all_gu.at[0, 1 - c], g0.at[0], d_c + 1, cp)
    net.got(n0, d_c)
    for q in range(2):
        d_dn[c, q] = added(d_dn[c, q], n0[q])
    net.send(d_dn.at[c, 1 - kept], n1, d_y, xp)
    four.fold(1)
    three.done()
    four.cross()
    for h in range(2):
        gate_up_grads(1, h, slope_up)
    net.send(all_gu.at[1, 1 - c], g0.at[1], d_c + 2, cp)

    def share(t):
        net.got(g0.at[t], d_c + 1 + t)
        for q in range(2):
            all_gu[t, c, q] = added(all_gu[t, c, q], g0[t, q])
        net.send(all_gu.at[t, c, 1 - x], g1.at[t], d_x + t, xp)

    def home_down():
        net.got(n1, d_y)
        d_dn[c, kept] = added(d_dn[c, kept], n1[...])
        net.move(
            jnp.logical_and(z % 2 == y, x == y),
            d_dn.at[c, kept],
            n2,
            d_y + 1,
            d_y + 1,
            at(2 * (z // 2) + y, kept, z % 2, c),
        )

    def home_gate_up(t):
        net.got(g1.at[t], d_x + t)
        all_gu[t, c, x] = added(all_gu[t, c, x], g1[t])
        source = z // 2 + 2 * t
        net.move(
            jnp.logical_and(source == z, z % 2 == c),
            all_gu.at[t, c, x],
            g2.at[c],
            d_home + t,
            d_home + c,
            at(source, y, x, z % 2),
        )

    share(0)
    share(1)
    four.done()

    home_down()
    mid = middle[...]
    grad, gain_grad = norm_back(mid, gains[2:3, :], total[...].reshape(MINE, D))
    small[0, 2:3, :] = gain_grad
    grad_mid = stream_of(cot) + grad
    grad_middle[...] = grad_mid
    grad, gain_grad = norm_back(attn_proj[...], gains[1:2, :], grad_mid)
    small[0, 1:2, :] = gain_grad
    grad_attn[...] = grad.astype(LOW)
    net.flush(three.gathered + four.gathered)
    d_out = got_up.reshape(4, 2, 2, 2, 32, D)
    a0 = got_mid.reshape(8 * MINE, D).at[pl.ds(0, 16 * 48)].reshape(4, 2, 2, 48, D)
    b0 = recv_y.reshape(4, 2, 2, 32, D)
    flat_d_out, flat_d_in = got_up.reshape(HEADS * HD, D), d_in.reshape(HEADS * HD + 2 * HD, D)

    def out_grads(j, carry):
        flat_d_out[rows_of(j), :] = tn(mixed[j], grad_attn[...]).astype(LOW)
        return carry

    lax.fori_loop(0, HEADS, out_grads, 0)
    net.send(d_out.at[:, :, :, 1 - c], b0, d_c + 3, cp)

    class Collect:
        def __init__(self, grads, core_in, y_in, x_in, z_in, core_slot, y_first):
            self.y_first = y_first
            self.grads, self.core_in, self.y_in, self.x_in, self.z_in = (
                grads,
                core_in,
                y_in,
                x_in,
                z_in,
            )
            self.cs, self.ys, self.xs, self.zs = core_slot, net.slots(2), net.slots(2), net.slots(2)

        def cores(self):
            net.got(self.core_in, self.cs)
            for part, pair in enumerate((1 - zh, zh)):

                def one(i, carry):
                    p, q, r = 2 * pair + i // 4, i // 2 % 2, i % 2
                    self.grads[p, q, r, c] = added(self.grads[p, q, r, c], self.core_in[p, q, r])
                    return carry

                lax.fori_loop(0, 8, one, 0)
                both = pl.ds(2 * pair, 2)
                if self.y_first:
                    away, device = self.grads.at[both, 1 - y, :, c], yp
                else:
                    away, device = self.grads.at[both, :, 1 - x, c], xp
                net.send(away, self.y_in.at[part], self.ys + part, device)

        def ys_in(self, part):
            pair = (1 - zh, zh)[part]
            net.got(self.y_in.at[part], self.ys + part)

            def one(i, carry):
                p, q = i // 2, i % 2
                there = 2 * pair + p
                if self.y_first:
                    self.grads[there, y, q, c] = added(
                        self.grads[there, y, q, c], self.y_in[part, p, q]
                    )
                else:
                    self.grads[there, q, x, c] = added(
                        self.grads[there, q, x, c], self.y_in[part, p, q]
                    )
                return carry

            lax.fori_loop(0, 4, one, 0)
            both = pl.ds(2 * pair, 2)
            if self.y_first:
                away, device = self.grads.at[both, y, 1 - x, c], xp
            else:
                away, device = self.grads.at[both, 1 - y, x, c], yp
            net.send(away, self.x_in.at[part], self.xs + part, device)

        def xs_in(self, part):
            pair = (1 - zh, zh)[part]
            net.got(self.x_in.at[part], self.xs + part)
            for p in range(2):
                there = 2 * pair + p
                self.grads[there, y, x, c] = added(
                    self.grads[there, y, x, c], self.x_in[part, p]
                )
            net.send(
                self.grads.at[2 * pair + 1 - zl, y, x, c],
                self.z_in.at[part],
                self.zs + part,
                z_peers[1],
            )

        def cross(self, slot):
            net.got(self.z_in.at[0], self.zs)
            there = 2 * (1 - zh) + zl
            self.grads[there, y, x, c] = added(self.grads[there, y, x, c], self.z_in[0])
            net.send(self.grads.at[there, y, x, c], self.z_in.at[2], slot, z_peers[2])

        def done(self, slot, result):
            net.got(self.z_in.at[1], self.zs + 1)
            net.got(self.z_in.at[2], slot)
            result[...] = (
                self.grads[z, y, x, c].astype(F32)
                + self.z_in[1].astype(F32)
                + self.z_in[2].astype(F32)
            )

    r_s, r_z = net.slots(8), net.slots(2)
    outs = Collect(d_out, b0, b1, b2, b3, d_c + 3, False)
    ins = Collect(d_in, a0, a1, a2, a3, d_c + 4, True)

    grad_heads[...] = jnp.zeros((6, MINE, HD), F32)

    def head_back(j, carry):
        up = nt(grad_attn[...], flat_out[rows_of(j), :]).astype(LOW)
        prob = probs[j]
        grad_prob = nt(up, heads[HEADS + 1])
        grad_heads[HEADS + 1] += tn(prob.astype(LOW), up)
        center = jnp.sum(grad_prob * prob, -1, keepdims=True)
        grad_score = (prob * (grad_prob - center)).astype(LOW)
        grad_heads[j] = nn(grad_score, heads[HEADS]) * SCALE_FACTOR
        grad_heads[HEADS] += tn(grad_score, heads[j]) * SCALE_FACTOR
        return carry

    lax.fori_loop(0, HEADS, head_back, 0)
    key_acc[...] = jnp.zeros((2, HD), F32)

    def turn_back(j, carry):
        first, second = grad_heads[j, :, :half], grad_heads[j, :, half:]
        turned = jnp.concatenate(
            [
                first * cosine[...] + second * sine[...],
                second * cosine[...] - first * sine[...],
            ],
            -1,
        )
        which = pl.ds(j // HEADS, 1)
        grad, gain_grad = norm_back(proj[j], head_gains[which, :], turned)
        key_acc[which, :] += gain_grad
        grad_proj[j] = grad.astype(LOW)
        return carry

    lax.fori_loop(0, HEADS + 1, turn_back, 0)
    grad_proj[HEADS + 1] = grad_heads[HEADS + 1].astype(LOW)
    small[0, 4:5, 0:HD] = key_acc[0:1, :]
    small[0, 4:5, HD : 2 * HD] = key_acc[1:2, :]

    outs.cores()

    def in_grads(j, carry):
        flat_d_in[rows_of(j), :] = tn(grad_proj[j], normed_in[...]).astype(LOW)
        return carry

    lax.fori_loop(0, HEADS + 2, in_grads, 0)
    net.send(d_in.at[:, :, :, 1 - c], a0, d_c + 4, cp)
    total[...] = jnp.zeros((2, PART, D), F32)

    def in_back(j, carry):
        total[...] += nn(grad_proj[j], flat_in[rows_of(j), :]).reshape(2, PART, D)
        return carry

    home_gate_up(0)
    lax.fori_loop(0, HEADS + 2, in_back, 0)
    ins.cores()
    grad, gain_grad = norm_back(stream_of(x_ref), gains[0:1, :], total[...].reshape(MINE, D))
    small[0, 0:1, :] = gain_grad
    input_grad[...] = (grad_middle[...] + grad).reshape(2, 1, PART, D)
    net.send(small.at[0], small.at[1], r_s, cp)
    home_gate_up(1)
    outs.ys_in(0)
    outs.ys_in(1)
    net.got(small.at[1], r_s)
    small[2] = small[0] + small[1]
    net.send(small.at[2], small.at[3], r_s + 1, xp)
    ins.ys_in(0)
    outs.xs_in(0)
    outs.xs_in(1)
    net.got(small.at[3], r_s + 1)
    small[4] = small[2] + small[3]
    net.send(small.at[4], small.at[5], r_s + 2, yp)
    ins.ys_in(1)
    outs.cross(r_z)
    ins.xs_in(0)
    ins.xs_in(1)
    net.got(small.at[5], r_s + 2)
    small[6] = small[4] + small[5]
    for k in (1, 2, 3):
        net.send(small.at[6], small.at[6 + k], r_s + 2 + k, z_peers[k])
    ins.cross(r_z + 1)
    outs.done(r_z, o_out)
    net.got(n2, d_y + 1)
    o_dn[...] = n2[...].astype(F32)[:BLOCK]
    for k in (1, 2, 3):
        net.got(small.at[6 + k], r_s + 2 + k)
    sums = (small[6] + small[7]) + (small[8] + small[9])
    o_gains[...] = sums[0:4, :]
    o_heads[...] = jnp.concatenate([sums[4:5, 0:HD], sums[4:5, HD : 2 * HD]], 0)
    scaled = sums[5:6, :]
    tokens = jnp.sum(jnp.where(spot == 4, scaled, 0.0), -1, keepdims=True)
    means = jnp.sqrt(scaled / (tokens * D))
    for i in range(4):
        o_rms[i] = jnp.sum(jnp.where(spot == i, means, 0.0))
    ins.done(r_z + 1, o_in)
    for h in range(2):
        net.got(g2.at[h], d_home + h)
        o_gu[pl.ds(h * BLOCK, BLOCK), :] = g2[h].astype(F32)[:BLOCK]
    net.drain()


def vm(*shape):
    return pltpu.VMEM(shape, LOW)


def vf(*shape):
    return pltpu.VMEM(shape, F32)


def whole_layer(x, seg, valid, ain, aout, gu, dn, gains, head_gains, cot):
    vmem = pl.BlockSpec(memory_space=pltpu.VMEM)
    scratch = [
        vm(4, 2, 2, 2, 48, D),
        vm(4, 2, 2, 2, 32, D),
        vm(2, 2, 2, PADDED, D),
        vm(2, 2, PADDED, D),
        vf(MINE, MINE),
        vf(MINE, MINE),
        vf(MINE, MINE),
        vf(MINE, MINE),
        vm(MINE, D),
        vf(6, MINE, HD),
        vm(6, MINE, HD),
        vf(4, MINE, MINE),
        vm(4, MINE, HD),
        vf(MINE, D),
        vf(MINE, D),
        vm(2, 2, PART, D),
        vf(2, PART, D),
        vm(2, 2, 2, 2, PART, D),
        vm(2, 2, 2, 2, PART, D),
        vm(2, WIDE, 8 * MINE),
        vm(2, 2, 2, PAIR, WIDE),
        vm(2, 2, 2, PAIR, WIDE),
        vf(2, 2, PART, D),
        vf(2, 2, 2, PART, D),
        vm(2, 2, 2, PART, D),
        vm(2, 2, 2, PART, D),
        vm(2, 3, PART, D),
        vm(2, 3, PART, D),
        vf(MINE, D),
        vm(MINE, D),
        vf(6, MINE, HD),
        vm(6, MINE, HD),
        vf(2, HD),
        vm(4, 2, 2, 2, 48, D),
    ]
    for count in (48, 32):
        scratch += [vm(2, 2, 2, count, D), vm(2, 2, count, D), vm(3, count, D)]
    scratch += [vm(2, 2, PADDED, D), vm(2, PADDED, D), vm(2, PADDED, D)]
    scratch += [vm(2, 2, PADDED, D), vm(2, PADDED, D), vm(PADDED, D), vm(PADDED, D)]
    scratch += [vf(10, 8, D)]
    scratch += [pltpu.SemaphoreType.DMA((2,))] + [pltpu.SemaphoreType.DMA((144,))] * 2
    return pl.pallas_call(
        layer_kernel,
        out_shape=(
            jax.ShapeDtypeStruct((2, 1, PART, D), LOW),
            jax.ShapeDtypeStruct((2, 1, PART, D), F32),
            jax.ShapeDtypeStruct((48, D), F32),
            jax.ShapeDtypeStruct((32, D), F32),
            jax.ShapeDtypeStruct((2 * BLOCK, D), F32),
            jax.ShapeDtypeStruct((BLOCK, D), F32),
            jax.ShapeDtypeStruct((4, D), F32),
            jax.ShapeDtypeStruct((2, HD), F32),
            jax.ShapeDtypeStruct((4,), F32),
        ),
        in_specs=[vmem] * 10,
        out_specs=(vmem,) * 8 + (pl.BlockSpec(memory_space=pltpu.SMEM),),
        scratch_shapes=scratch,
        compiler_params=pltpu.CompilerParams(
            collective_id=1, has_side_effects=True, vmem_limit_bytes=VMEM_BYTES
        ),
        name="layer",
    )(x, seg, valid, ain, aout, gu, dn, gains, head_gains, cot)


def copy_kernel(*refs):
    count = (len(refs) - 2) // 3
    given, made, held = refs[:count], refs[count : 2 * count], refs[2 * count : 3 * count]
    into = [pltpu.make_async_copy(a, b, refs[-2].at[i]) for i, (a, b) in enumerate(zip(given, held))]
    out = [pltpu.make_async_copy(a, b, refs[-1].at[i]) for i, (a, b) in enumerate(zip(held, made))]
    for copy in into:
        copy.start()
    for first, second in zip(into, out):
        first.wait()
        second.start()
    for copy in out:
        copy.wait()


def copied(arrays):
    place = pl.BlockSpec(memory_space=pl.ANY)
    return pl.pallas_call(
        copy_kernel,
        out_shape=tuple(jax.ShapeDtypeStruct(array.shape, array.dtype) for array in arrays),
        in_specs=[place] * len(arrays),
        out_specs=(place,) * len(arrays),
        scratch_shapes=[pltpu.VMEM(array.shape, array.dtype) for array in arrays]
        + [pltpu.SemaphoreType.DMA((len(arrays),))] * 2,
        name="results",
    )(*arrays)


def split_shards(
    inputs,
    segment_ids,
    valid_mask,
    attn_in,
    attn_out,
    ffw_in,
    ffw_out,
    norm_gains,
    head_gains,
    cotangent,
):
    results = whole_layer(
        inputs,
        segment_ids,
        valid_mask,
        attn_in,
        attn_out,
        ffw_in,
        ffw_out,
        norm_gains,
        head_gains,
        cotangent,
    )
    return copied(results[:-1]) + results[-1:]


def solution(mesh):
    placed = (
        P(None, "dp", None, None),
        P(None, "dp", None),
        P(None, "dp", None),
        P("dp", None),
        P("dp", None),
        P("dp", None),
        P("dp", None),
        P(),
        P(),
        P(None, "dp", None, None),
    )
    return jax.shard_map(
        split_shards if mesh.shape["dp"] == 32 else general_shards,
        mesh=mesh,
        in_specs=placed,
        out_specs=(
            P(None, "dp", None, None),
            P(None, "dp", None, None),
            P("dp", None),
            P("dp", None),
            P("dp", None),
            P("dp", None),
            P(),
            P(),
            P(),
        ),
        check_vma=False,
    )
```

```python
import math

import jax
import jax.numpy as jnp
from jax import lax
from jax.experimental import pallas as pl
from jax.experimental.pallas import tpu as pltpu
from jax.sharding import PartitionSpec as P

D = 1152
HEADS = 4
HD = 256
FF = 6912
MICRO = 2


EPSILON = 1e-06
SCALE_FACTOR = 0.0625
THETA = 10000.0
NEGATIVE = -1e30


def shortened(x):

    def short(part):
        return part.astype(jnp.bfloat16) if part.dtype == jnp.float32 else part

    return jax.tree.map(short, x)


def swapped(block, axis, stride):
    count = lax.axis_size(axis)
    route = []
    for low in range(count):
        high = low | 1 << stride
        if high != low and high < count:
            route += [(low, high), (high, low)]
    return lax.ppermute(block, axis, route)


def norm_rows(values, gain):
    return values * lax.rsqrt(jnp.mean(values * values, -1, keepdims=True) + EPSILON) * gain


def rotate(values, cosine, sine):
    half = values.shape[-1] // 2
    first = values[..., :half]
    second = values[..., half:]
    return jnp.concatenate([first * cosine - second * sine, second * cosine + first * sine], -1)


def doc_tables(segments, validity, head_size):
    length = segments.shape[-1]
    places = jnp.arange(length, dtype=jnp.int32)
    same_doc = segments[..., :, None] == segments[..., None, :]
    earlier = places[None, :] < places[:, None]
    position = jnp.sum(jnp.logical_and(same_doc, earlier).astype(jnp.int32), -1)
    reach = places[None, :] <= places[:, None]
    usable = jnp.logical_or(validity[..., None, :] > 0, places[None, :] == places[:, None])
    allowed = jnp.logical_and(jnp.logical_and(same_doc, reach), usable)
    freqs = jnp.exp(
        jnp.arange(head_size // 2, dtype=jnp.float32) * (-2.0 * math.log(THETA) / head_size)
    )
    angles = position.astype(jnp.float32)[..., None] * freqs
    return (allowed, jnp.cos(angles), jnp.sin(angles))


def prepare(projected, head_gains, cosine, sine):
    width = HEADS * HD
    query = projected[..., :width].reshape(projected.shape[:-1] + (HEADS, HD))
    keys = projected[..., width : width + HD]
    values = projected[..., width + HD :]
    query = rotate(norm_rows(query, head_gains[0]), cosine[..., None, :], sine[..., None, :])
    keys = rotate(norm_rows(keys, head_gains[1]), cosine, sine)
    return (query, keys, values)


def across(left, piece):
    return lax.dot_general(
        left, piece, (((1,), (1,)), ((), ())), preferred_element_type=jnp.float32
    )


def over_rows(left, right):
    return lax.dot_general(
        left, right, (((0,), (0,)), ((), ())), preferred_element_type=jnp.float32
    )


def score_table(query_low, keys_low):
    return (
        jnp.einsum("qhd,kd->hqk", query_low, keys_low, preferred_element_type=jnp.float32)
        * SCALE_FACTOR
    )


def attend(query_low, keys_low, values_low, allowed):
    scores = score_table(query_low, keys_low)
    masked = jnp.where(allowed[None], scores, NEGATIVE)
    peak = jnp.max(masked, -1, keepdims=True)
    expo = jnp.where(allowed[None], jnp.exp(masked - peak), 0.0)
    totals = jnp.sum(expo, -1, keepdims=True)
    probs = expo / totals
    mixed = jnp.einsum(
        "hqk,kd->qhd", probs.astype(jnp.bfloat16), values_low, preferred_element_type=jnp.float32
    )
    return (mixed, peak + jnp.log(totals))


def attend_back(query_low, keys_low, values_low, allowed, log_sum, grad_low):
    scores = score_table(query_low, keys_low)
    probs = jnp.where(allowed[None], jnp.exp(scores - log_sum), 0.0)
    grad_probs = jnp.einsum("qhd,kd->hqk", grad_low, values_low, preferred_element_type=jnp.float32)
    grad_values = jnp.einsum(
        "hqk,qhd->kd", probs.astype(jnp.bfloat16), grad_low, preferred_element_type=jnp.float32
    )
    center = jnp.sum(grad_probs * probs, -1, keepdims=True)
    grad_scores = (probs * (grad_probs - center)).astype(jnp.bfloat16)
    grad_query = (
        jnp.einsum("hqk,kd->qhd", grad_scores, keys_low, preferred_element_type=jnp.float32)
        * SCALE_FACTOR
    )
    grad_keys = (
        jnp.einsum("hqk,qhd->kd", grad_scores, query_low, preferred_element_type=jnp.float32)
        * SCALE_FACTOR
    )
    return (grad_query, grad_keys, grad_values)


def gated(gate, upward):
    return jax.nn.gelu(gate, approximate=True) * upward


def general_shards(
    inputs,
    segment_ids,
    valid_mask,
    attn_in,
    attn_out,
    ffw_in,
    ffw_out,
    norm_gains,
    head_gains,
    cotangent,
):
    width = HEADS * HD
    kept_proj = []
    kept_normed_in = []
    kept_mixed = []
    kept_attn = []
    kept_gate = []
    kept_normed_mid = []
    kept_hidden = []
    kept_ffw = []
    gain_sums = jnp.zeros((4, D), jnp.float32)
    head_sums = jnp.zeros((2, HD), jnp.float32)
    stats = jnp.zeros((5,), jnp.float32)
    results = []
    input_grads = []
    for step in range(MICRO):
        full_in, full_out = (
            lax.all_gather(attn_in, "dp", axis=0, tiled=True),
            lax.all_gather(attn_out, "dp", axis=0, tiled=True),
        )
        full_ffin, full_ffout = (
            lax.all_gather(ffw_in, "dp", axis=0, tiled=True),
            lax.all_gather(ffw_out, "dp", axis=0, tiled=True),
        )
        stream = inputs[step, 0].astype(jnp.float32)
        length = stream.shape[0]
        allowed, cosine, sine = doc_tables(segment_ids[step, 0], valid_mask[step, 0], HD)
        normed_in = norm_rows(stream, norm_gains[0]).astype(jnp.bfloat16)
        projected = across(normed_in, full_in)
        query, keys, values = prepare(projected, head_gains, cosine, sine)
        query_low = query.astype(jnp.bfloat16)
        keys_low = keys.astype(jnp.bfloat16)
        values_low = values.astype(jnp.bfloat16)
        mixed, log_sum = attend(query_low, keys_low, values_low, allowed)
        mixed_low = mixed.reshape(length, width).astype(jnp.bfloat16)
        attn_proj = jnp.dot(mixed_low, full_out, preferred_element_type=jnp.float32)
        attn_branch = norm_rows(attn_proj, norm_gains[1])
        middle = stream + attn_branch
        normed_mid = norm_rows(middle, norm_gains[2]).astype(jnp.bfloat16)
        gate_up = across(normed_mid, full_ffin)
        gate = gate_up[:, :FF]
        upward = gate_up[:, FF:]
        hidden = gated(gate, upward).astype(jnp.bfloat16)
        ffw_proj = jnp.dot(hidden, full_ffout, preferred_element_type=jnp.float32)
        ffw_branch = norm_rows(ffw_proj, norm_gains[3])
        results.append((middle + ffw_branch).astype(jnp.bfloat16))
        weight = valid_mask[step, 0].astype(jnp.float32)
        sums = [
            jnp.sum(weight * jnp.sum(value * value, -1))
            for value in (stream, middle, attn_branch, ffw_branch)
        ]
        sums.append(jnp.sum(weight))
        stats = stats + jnp.stack(sums)
        upstream = cotangent[step, 0].astype(jnp.float32)
        _, back_ffw = jax.vjp(norm_rows, ffw_proj, norm_gains[3])
        grad_ffw_proj, gain_three = back_ffw(upstream)
        grad_ffw_low = grad_ffw_proj.astype(jnp.bfloat16)
        grad_hidden = across(grad_ffw_low, full_ffout)
        _, back_gated = jax.vjp(gated, gate, upward)
        grad_gate, grad_upward = back_gated(grad_hidden)
        grad_gate_up = jnp.concatenate([grad_gate, grad_upward], 1).astype(jnp.bfloat16)
        grad_normed_mid = jnp.dot(grad_gate_up, full_ffin, preferred_element_type=jnp.float32)
        _, back_mid = jax.vjp(norm_rows, middle, norm_gains[2])
        grad_mid_part, gain_two = back_mid(grad_normed_mid)
        grad_middle = upstream + grad_mid_part
        _, back_attn = jax.vjp(norm_rows, attn_proj, norm_gains[1])
        grad_attn_proj, gain_one = back_attn(grad_middle)
        grad_attn_low = grad_attn_proj.astype(jnp.bfloat16)
        grad_mixed = across(grad_attn_low, full_out)
        grad_mixed_low = grad_mixed.astype(jnp.bfloat16).reshape(length, HEADS, HD)
        grad_query, grad_keys, grad_values = attend_back(
            query_low, keys_low, values_low, allowed, log_sum, grad_mixed_low
        )
        _, back_prep = jax.vjp(
            lambda table, gains: prepare(table, gains, cosine, sine), projected, head_gains
        )
        grad_projected, grad_heads = back_prep((grad_query, grad_keys, grad_values))
        grad_proj_low = grad_projected.astype(jnp.bfloat16)
        grad_normed_in = jnp.dot(grad_proj_low, full_in, preferred_element_type=jnp.float32)
        _, back_in = jax.vjp(norm_rows, stream, norm_gains[0])
        grad_stream, gain_zero = back_in(grad_normed_in)
        input_grads.append(grad_middle + grad_stream)
        gain_sums = gain_sums + jnp.stack([gain_zero, gain_one, gain_two, gain_three])
        head_sums = head_sums + grad_heads
        kept_proj.append(grad_proj_low)
        kept_normed_in.append(normed_in)
        kept_mixed.append(mixed_low)
        kept_attn.append(grad_attn_low)
        kept_gate.append(grad_gate_up)
        kept_normed_mid.append(normed_mid)
        kept_hidden.append(hidden)
        kept_ffw.append(grad_ffw_low)
    pairs = [
        (jnp.concatenate(kept_proj, 0), jnp.concatenate(kept_normed_in, 0)),
        (jnp.concatenate(kept_mixed, 0), jnp.concatenate(kept_attn, 0)),
        (jnp.concatenate(kept_gate, 0), jnp.concatenate(kept_normed_mid, 0)),
        (jnp.concatenate(kept_hidden, 0), jnp.concatenate(kept_ffw, 0)),
    ]
    levels = lax.axis_size("dp").bit_length() - 1
    place = lax.axis_index("dp")
    top_bit = place >> levels - 1 & 1
    kept_parts = []
    sent_parts = []
    for left, right in pairs:
        half_cols = left.shape[1] // 2
        kept_parts.append(
            over_rows(lax.dynamic_slice_in_dim(left, top_bit * half_cols, half_cols, 1), right)
        )
        sent_parts.append(
            over_rows(
                lax.dynamic_slice_in_dim(left, (1 - top_bit) * half_cols, half_cols, 1), right
            )
        )
    current = tuple(kept_parts)
    outgoing = tuple(sent_parts)
    for level in range(levels):
        bit = levels - 1 - level
        arrived = jax.tree.map(
            lambda part, own: part.astype(own.dtype),
            swapped(shortened(outgoing), "dp", bit),
            outgoing,
        )
        current = tuple((mine + theirs for mine, theirs in zip(current, arrived)))
        if level + 1 < levels:
            next_bit = place >> bit - 1 & 1
            halves = [piece.shape[0] // 2 for piece in current]
            outgoing = tuple(
                (
                    lax.dynamic_slice_in_dim(piece, (1 - next_bit) * rows, rows, 0)
                    for piece, rows in zip(current, halves)
                )
            )
            current = tuple(
                (
                    lax.dynamic_slice_in_dim(piece, next_bit * rows, rows, 0)
                    for piece, rows in zip(current, halves)
                )
            )
    shard_in, shard_out, shard_ffin, shard_ffout = current
    gain_total, head_total, stat_total = lax.psum((gain_sums, head_sums, stats), "dp")
    rms_values = jnp.sqrt(stat_total[:4] / (stat_total[4] * D))
    layer_out = jnp.stack(results)[:, None]
    input_grad = jnp.stack(input_grads)[:, None]
    return (
        layer_out,
        input_grad,
        shard_in,
        shard_out,
        shard_ffin,
        shard_ffout,
        gain_total,
        head_total,
        rms_values,
    )


BLOCK = 216
PADDED = 224
WIDE = 2 * PADDED
MINE = 128
PART = 64
PAIR = 2 * MINE
VMEM_BYTES = 62 << 20
SQRT_2_OVER_PI = math.sqrt(2.0 / math.pi)
CUBIC = 0.044715
MESH = pl.DeviceIdType.MESH
LOW = jnp.bfloat16
F32 = jnp.float32


def spots():
    me = lax.axis_index("dp")
    return me, me // 8, me // 4 % 2, me // 2 % 2, me % 2


def at(z, y, x, c):
    return z * 8 + y * 4 + x * 2 + c


def z_peer(z, k):
    if k == 0:
        return z
    if k == 1:
        return z + 1 - 2 * (z % 2)
    if k == 2:
        return (z + 2) % 4
    return 3 - z


def greet(z, y, x, c):
    barrier = pltpu.get_barrier_semaphore()
    others = [at(z_peer(z, k), y, x, core) for k in (1, 2, 3) for core in (c, 1 - c)]
    others.append(at(z, y, x, 1 - c))
    for k in range(2):
        for there_y, there_x in ((1 - y, x), (y, 1 - x), (1 - y, 1 - x)):
            others.append(at(z_peer(z, k), there_y, there_x, c))
    for device in others:
        pl.semaphore_signal(barrier, inc=1, device_id=(device,), device_id_type=MESH)
    pl.semaphore_wait(barrier, len(others))


def nt(left, right):
    return lax.dot_general(left, right, (((1,), (1,)), ((), ())), preferred_element_type=F32)


def nn(left, right):
    return lax.dot_general(left, right, (((1,), (0,)), ((), ())), preferred_element_type=F32)


def tn(left, right):
    return lax.dot_general(left, right, (((0,), (0,)), ((), ())), preferred_element_type=F32)


def norm_back(values, gain, upstream):
    scale = lax.rsqrt(jnp.mean(values * values, -1, keepdims=True) + EPSILON)
    normed = values * scale
    gain_grad = jnp.sum(upstream * normed, 0, keepdims=True)
    inner = upstream * gain
    grad = scale * (inner - normed * jnp.mean(inner * normed, -1, keepdims=True))
    return grad, gain_grad


def added(left, right):
    return (left.astype(F32) + right.astype(F32)).astype(LOW)


def stream_of(ref):
    return ref[...].reshape(MINE, D).astype(F32)


class Net:
    def __init__(self, send_sems, recv_sems, anyone):
        self.send_sems, self.recv_sems, self.anyone = send_sems, recv_sems, anyone
        self.used, self.sent, self.maybe = 0, [], []

    def slots(self, count):
        first = self.used
        self.used += count
        return first

    def copy(self, src, dst, send_slot, recv_slot, device):
        return pltpu.make_async_remote_copy(
            src_ref=src,
            dst_ref=dst,
            send_sem=self.send_sems.at[send_slot],
            recv_sem=self.recv_sems.at[recv_slot],
            device_id=(device,),
            device_id_type=MESH,
        )

    def send(self, src, dst, slot, device):
        copy = self.copy(src, dst, slot, slot, device)
        copy.start()
        self.sent.append(copy)

    def move(self, stays, src, dst, send_slot, recv_slot, device):
        copy = self.copy(src, dst, send_slot, recv_slot, device)

        @pl.when(stays)
        def _():
            pltpu.make_async_copy(src, dst, self.recv_sems.at[recv_slot]).start()

        @pl.when(jnp.logical_not(stays))
        def _():
            copy.start()

        self.maybe.append((stays, copy))

    def got(self, block, slot):
        self.copy(block, block, slot, slot, self.anyone).wait_recv()

    def flush(self, gone):
        for copy in gone:
            copy.wait_send()
        names = {id(copy) for copy in gone}
        self.sent = [copy for copy in self.sent if id(copy) not in names]

    def drain(self):
        self.flush(list(self.sent))
        self.settle_moves()

    def settle_moves(self):
        for stays, copy in self.maybe:

            @pl.when(jnp.logical_not(stays))
            def _():
                copy.wait_send()

        self.maybe = []


def layer_kernel(*refs):
    (
        x_ref,
        seg_ref,
        valid_ref,
        ain,
        aout,
        gu,
        dn,
        gains,
        head_gains,
        cot,
        layer_out,
        input_grad,
        o_in,
        o_out,
        o_gu,
        o_dn,
        o_gains,
        o_heads,
        o_rms,
        all_in,
        all_out,
        all_gu,
        all_dn,
        allow,
        cosine,
        sine,
        weight,
        normed_in,
        proj,
        heads,
        probs,
        mixed,
        attn_proj,
        middle,
        rows,
        total,
        got_mid,
        got_up,
        hidden_t,
        slope_gate,
        slope_up,
        acc,
        keep,
        send_y,
        recv_y,
        send_z,
        recv_z,
        grad_middle,
        grad_attn,
        grad_heads,
        grad_proj,
        key_acc,
        d_in,
        a1,
        a2,
        a3,
        b1,
        b2,
        b3,
        g0,
        g1,
        g2,
        d_dn,
        n0,
        n1,
        n2,
        small,
        local,
        send_sems,
        recv_sems,
    ) = refs
    me, z, y, x, c = spots()
    xp, yp, cp = at(z, y, 1 - x, c), at(z, 1 - y, x, c), at(z, y, x, 1 - c)
    z_peers = [at(z_peer(z, k), y, x, c) for k in range(4)]
    net = Net(send_sems, recv_sems, cp)
    keep_in = pltpu.make_async_copy(ain, all_in.at[z, y, x, c], local.at[0])
    keep_out = pltpu.make_async_copy(aout, all_out.at[z, y, x, c], local.at[1])
    keep_in.start()
    keep_out.start()
    greet(z, y, x, c)

    class Spread:
        def __init__(self, own, full, x_first):
            self.own, self.full, self.x_first = own, full, x_first
            self.first, self.second = (xp, yp) if x_first else (yp, xp)
            self.az, self.ax, self.ay, self.ac = (net.slots(4) for _ in range(4))

        def block(self, k):
            return self.full.at[z_peer(z, k), y, x, c]

        def crossed(self, k):
            there = z_peer(z, k)
            return self.full.at[there, y, 1 - x, c] if self.x_first else self.full.at[there, 1 - y, x, c]

        def pair(self, there, own, core):
            if self.x_first:
                return self.full.at[there, y if own else 1 - y, :, core]
            return self.full.at[there, :, x if own else 1 - x, core]

        def start(self):
            net.send(self.own, self.block(0), self.az + 1, z_peers[1])
            net.send(self.own, self.block(0), self.ax, self.first)
            net.send(self.own, self.block(0), self.az + 2, z_peers[2])

        def hop(self, k):
            block = self.block(k)
            net.got(block, self.az + k)
            if k == 2:
                net.send(block, block, self.az + 3, z_peers[1])
            net.send(block, block, self.ax + k, self.first)

        def turn(self, k):
            net.got(self.crossed(k), self.ax + k)
            pair = self.pair(z_peer(z, k), True, c)
            net.send(pair, pair, self.ay + k, self.second)

        def near(self):
            part = self.pair(slice(None), True, c)
            net.send(part, part, self.ac, cp)

        def far(self):
            for k in range(4):
                net.got(self.pair(z_peer(z, k), False, c), self.ay + k)
            part = self.pair(slice(None), False, c)
            net.send(part, part, self.ac + 1, cp)

        def whole(self):
            net.got(self.pair(slice(None), True, 1 - c), self.ac)
            net.got(self.pair(slice(None), False, 1 - c), self.ac + 1)

    into, outof = Spread(ain, all_in, True), Spread(aout, all_out, False)
    into.start()
    w_one, w_two, w_c, w_d = net.slots(2), net.slots(2), net.slots(2), net.slots(2)
    v_x, v_one, v_c = net.slots(1), net.slots(2), net.slots(1)
    kind, goal = z // 2, 2 * (z % 2) + c
    blank = jnp.zeros((PADDED - BLOCK, D), F32)
    for h in range(2):
        part = gu[pl.ds(h * BLOCK, BLOCK), :].astype(F32)
        g0[0, h] = jnp.concatenate([part, blank], 0).astype(LOW)
    n0[0] = jnp.concatenate([dn[...].astype(F32), blank], 0).astype(LOW)

    def rows_out():
        for h in range(2):
            net.move(
                jnp.logical_and(goal == z, c == h),
                g0.at[0, h],
                all_gu.at[kind, h, x],
                w_one + h,
                w_one + kind,
                at(goal, y, x, h),
            )

    def rows_on(which):
        t = (kind, 1 - kind)[which]
        block = all_gu.at[t, c, x]
        net.got(block, w_one + t)
        net.send(block, block, w_two + which, xp)
        net.send(block, block, w_c + which, cp)

    def rows_across(which):
        block = all_gu.at[(kind, 1 - kind)[which], c, 1 - x]
        net.got(block, w_two + which)
        net.send(block, block, w_d + which, cp)

    def rows_whole():
        for which in range(2):
            t = (kind, 1 - kind)[which]
            net.got(all_gu.at[t, 1 - c, x], w_c + which)
            net.got(all_gu.at[t, 1 - c, 1 - x], w_d + which)
        net.got(all_dn.at[1 - c], v_c)

    across_x = []

    def down_x():
        net.send(n0.at[0], n0.at[1], v_x, xp)
        across_x.append(net.sent[-1])


    def down_out():
        net.got(n0.at[1], v_x)
        for other in range(2):
            block_x = 1 - x if other else x
            net.move(
                jnp.logical_and(z % 2 == block_x, z % 2 == y),
                n0.at[other],
                all_dn.at[c, y],
                v_one + other,
                v_one + y,
                at(2 * (z // 2) + block_x, z % 2, x, c),
            )

    def down_on():
        for q in range(2):
            net.got(all_dn.at[c, q], v_one + q)
        net.send(all_dn.at[c], all_dn.at[c], v_c, cp)

    into.hop(1)
    into.hop(2)
    outof.start()
    keep_in.wait()
    keep_out.wait()
    into.turn(0)
    into.turn(1)
    into.hop(3)

    def along_lanes(ref):
        return jnp.concatenate([ref[0].astype(F32), ref[1].astype(F32)], 1)

    seg = jnp.broadcast_to(along_lanes(seg_ref), (MINE, MINE))
    valid = jnp.broadcast_to(along_lanes(valid_ref), (MINE, MINE))
    row = lax.broadcasted_iota(jnp.int32, (MINE, MINE), 0)
    col = lax.broadcasted_iota(jnp.int32, (MINE, MINE), 1)
    length = MINE // MICRO
    same = jnp.logical_and(seg == seg.T, row // length == col // length)
    position = jnp.sum(jnp.where(jnp.logical_and(same, col < row), 1.0, 0.0), -1, keepdims=True)
    usable = jnp.logical_or(valid > 0.0, row == col)
    allow[...] = jnp.where(
        jnp.logical_and(jnp.logical_and(same, col <= row), usable), 1.0, 0.0
    )
    weight[...] = valid.T
    freqs = jnp.exp(col.astype(F32) * (-2.0 * math.log(THETA) / HD))
    angles = position * freqs
    cosine[...] = jnp.cos(angles)
    sine[...] = jnp.sin(angles)
    stream = stream_of(x_ref)
    normed_in[...] = norm_rows(stream, gains[0:1, :]).astype(LOW)

    rows_out()
    down_x()
    into.turn(2)
    outof.hop(1)
    outof.hop(2)
    into.turn(3)
    into.near()
    outof.turn(0)
    outof.turn(1)
    outof.hop(3)
    into.far()
    outof.turn(2)
    outof.turn(3)
    outof.near()
    into.whole()

    down_out()
    flat_in = all_in.reshape(HEADS * HD + 2 * HD, D)
    flat_out = all_out.reshape(HEADS * HD, D)
    half = HD // 2

    def rows_of(j):
        return pl.ds(pl.multiple_of(j * HD, HD), HD)

    def project(j, carry):
        table = nt(normed_in[...], flat_in[rows_of(j), :])
        proj[j] = table

        @pl.when(j < HEADS + 1)
        def _():
            turned = norm_rows(table, head_gains[pl.ds(j // HEADS, 1), :])
            first, second = turned[:, :half], turned[:, half:]
            heads[j, :, :half] = (first * cosine[...] - second * sine[...]).astype(LOW)
            heads[j, :, half:] = (second * cosine[...] + first * sine[...]).astype(LOW)

        @pl.when(j == HEADS + 1)
        def _():
            heads[j] = table.astype(LOW)

        return carry

    lax.fori_loop(0, HEADS + 2, project, 0)
    outof.far()

    def attend_head(j, carry):
        seen = allow[...] > 0.0
        scores = nt(heads[j], heads[HEADS]) * SCALE_FACTOR
        masked = jnp.where(seen, scores, NEGATIVE)
        peak = jnp.max(masked, -1, keepdims=True)
        expo = jnp.where(seen, jnp.exp(masked - peak), 0.0)
        prob = expo / jnp.sum(expo, -1, keepdims=True)
        probs[j] = prob
        mixed[j] = nn(prob.astype(LOW), heads[HEADS + 1]).astype(LOW)
        return carry

    lax.fori_loop(0, HEADS, attend_head, 0)
    rows_on(0)
    outof.whole()

    attn_proj[...] = jnp.zeros((MINE, D), F32)

    def attn_out_head(j, carry):
        attn_proj[...] += nn(mixed[j], flat_out[rows_of(j), :])
        return carry

    lax.fori_loop(0, HEADS, attn_out_head, 0)
    branch = norm_rows(attn_proj[...], gains[1:2, :])
    mid = stream_of(x_ref) + branch
    middle[...] = mid
    rows[0] = norm_rows(mid, gains[2:3, :]).astype(LOW).reshape(2, PART, D)

    def counted(values):
        return jnp.sum(weight[:, 0:1] * jnp.sum(values * values, -1, keepdims=True))

    spot = lax.broadcasted_iota(jnp.int32, (1, D), 1)
    stats = jnp.where(spot == 4, jnp.sum(weight[:, 0:1]), 0.0)
    first_values = stream_of(x_ref)
    stats += jnp.where(spot == 0, counted(first_values), 0.0)
    stats += jnp.where(spot == 1, counted(mid), 0.0)
    stats += jnp.where(spot == 2, counted(branch), 0.0)
    small[0] = jnp.zeros((8, D), F32)
    small[0, 5:6, :] = stats

    zh, zl = z // 2, z % 2
    w_gu, w_dn = all_gu.reshape(2, 2, WIDE, D), all_dn.reshape(2, WIDE, D)

    class Half:
        def __init__(self, which, half, got_all, compute):
            self.which, self.half, self.got_all, self.compute = which, half, got_all, compute
            self.az, self.ay, self.ry, self.rz = (net.slots(4) for _ in range(4))
            self.gathered, self.here = [], set()

        def block(self, k, yy):
            there = z_peer(z, k)
            return self.got_all.at[self.half, there // 2, there % 2, yy]

        def pass_on(self, block, slot, device):
            net.send(block, block, slot, device)
            self.gathered.append(net.sent[-1])

        def start(self):
            own = rows.at[self.which, self.half]
            net.send(own, self.block(0, y), self.az + 1, z_peers[1])
            self.gathered.append(net.sent[-1])
            net.send(own, self.block(0, y), self.az + 2, z_peers[2])
            self.gathered.append(net.sent[-1])
            net.send(own, self.block(0, y), self.ay, yp)
            self.gathered.append(net.sent[-1])
            self.got_all[self.half, zh, zl, y] = rows[self.which, self.half]

        def hop(self, k):
            block = self.block(k, y)
            net.got(block, self.az + k)
            if k == 2:
                self.pass_on(block, self.az + 3, z_peers[1])
            self.pass_on(block, self.ay + k, yp)

        def arrive(self, g):
            if g not in self.here:
                for k in (2 * g, 2 * g + 1):
                    net.got(self.block(k, 1 - y), self.ay + k)
            self.here.add(g)

        def group(self, g):
            self.arrive(g)
            self.compute(self.half, zh if g == 0 else 1 - zh)
            keep[self.half, g] = acc[:, y]
            send_y[self.half, g] = acc[:, 1 - y].astype(LOW)
            net.send(send_y.at[self.half, g], recv_y.at[self.half, g], self.ry + g, yp)

        def fold(self, g):
            net.got(recv_y.at[self.half, g], self.ry + g)
            keep[self.half, g] += recv_y[self.half, g].astype(F32)
            send_z[self.half, g] = keep[self.half, g, 1 - zl].astype(LOW)
            net.send(send_z.at[self.half, g], recv_z.at[self.half, g], self.rz + g, z_peers[1])

        def cross(self):
            net.got(recv_z.at[self.half, 1], self.rz + 1)
            send_z[self.half, 2] = (
                keep[self.half, 1, zl] + recv_z[self.half, 1].astype(F32)
            ).astype(LOW)
            net.send(send_z.at[self.half, 2], recv_z.at[self.half, 2], self.rz + 2, z_peers[2])

        def done(self):
            net.got(recv_z.at[self.half, 0], self.rz)
            net.got(recv_z.at[self.half, 2], self.rz + 2)
            total[self.half] = (
                keep[self.half, 0, zl]
                + recv_z[self.half, 0].astype(F32)
                + recv_z[self.half, 2].astype(F32)
            )

    def columns(half, pair):
        return pl.ds(pl.multiple_of((half * 2 + pair) * PAIR, PAIR), PAIR)

    def put(h, part):
        part = part.reshape(2, 2, PART, D)

        @pl.when(h == 0)
        def _():
            acc[...] = part

        @pl.when(h == 1)
        def _():
            acc[...] += part

    def forward_pairs(half, pair):
        def one(h, carry):
            block = got_mid[half, pair].reshape(PAIR, D)
            gate = nt(block, w_gu[0, h])
            upward = nt(block, w_gu[1, h])
            square = gate * gate
            tanh = jnp.tanh(SQRT_2_OVER_PI * gate * (1.0 + CUBIC * square))
            side = 0.5 * (1.0 + tanh)
            gelu = gate * side
            slope = side + 0.5 * gate * (1.0 - tanh * tanh) * (
                SQRT_2_OVER_PI * (1.0 + 3.0 * CUBIC * square)
            )
            low = (gelu * upward).astype(LOW)
            slope_gate[h, half, pair] = (upward * slope).astype(LOW)
            slope_up[h, half, pair] = gelu.astype(LOW)
            put(h, nn(low, w_dn[h]))
            hidden_t[h, :, columns(half, pair)] = low.T
            return carry

        lax.fori_loop(0, 2, one, 0)

    def weights_here():
        net.settle_moves()
        net.flush(across_x)
        rows_across(1)
        rows_whole()

    def forward_end(half):
        span = pl.ds(half * PART, PART)
        ffw_proj = total[half]
        branch = norm_rows(ffw_proj, gains[3:4, :])
        layer_out[half, 0] = (middle[span, :] + branch).astype(LOW)
        counts = jnp.sum(weight[span, 0:1] * jnp.sum(branch * branch, -1, keepdims=True))
        small[0, 5:6, :] += jnp.where(spot == 3, counts, 0.0)
        grad, gain_grad = norm_back(ffw_proj, gains[3:4, :], cot[half, 0].astype(F32))
        small[0, 3:4, :] += gain_grad
        rows[1, half] = grad.astype(LOW)

    def backward_pairs(half, pair):
        def one(h, carry):
            block = got_up[half, pair].reshape(PAIR, D)
            back = nt(block, w_dn[h])
            gate = (back * slope_gate[h, half, pair].astype(F32)).astype(LOW)
            upward = (back * slope_up[h, half, pair].astype(F32)).astype(LOW)
            put(h, nn(gate, w_gu[0, h]) + nn(upward, w_gu[1, h]))
            slope_gate[h, half, pair] = gate
            slope_up[h, half, pair] = upward
            return carry

        lax.fori_loop(0, 2, one, 0)

    one, two = Half(0, 0, got_mid, forward_pairs), Half(0, 1, got_mid, forward_pairs)
    one.start()
    rows_on(1)
    rows_across(0)
    down_on()
    two.start()
    one.hop(1)
    two.hop(1)
    one.hop(2)
    two.hop(2)
    one.hop(3)
    two.hop(3)
    weights_here()
    one.group(0)
    one.group(1)
    one.fold(0)
    two.group(0)
    one.fold(1)
    two.group(1)
    one.cross()
    two.fold(0)
    one.done()
    forward_end(0)
    three, four = Half(1, 0, got_up, backward_pairs), Half(1, 1, got_up, backward_pairs)
    three.start()
    two.fold(1)
    three.hop(1)
    two.cross()
    three.hop(2)
    two.done()
    forward_end(1)
    four.start()
    net.flush([copy for copy in net.sent if not any(copy is other for other in three.gathered + four.gathered)])
    three.group(0)
    four.hop(1)
    three.hop(3)
    four.hop(2)
    three.group(1)
    three.fold(0)
    four.hop(3)
    four.group(0)
    three.fold(1)

    step = 384
    flat_mid, flat_up = got_mid.reshape(8 * MINE, D), got_up.reshape(8 * MINE, D)

    four.arrive(1)

    def down_grads(i, carry):
        h, cols = i // 3, pl.ds(pl.multiple_of(i % 3 * step, 128), step)
        d_dn.reshape(2, WIDE, D)[h, :, cols] = nn(hidden_t[h], flat_up[:, cols]).astype(LOW)
        return carry

    lax.fori_loop(0, 6, down_grads, 0)
    d_c, d_x, d_home, d_y = net.slots(5), net.slots(2), net.slots(2), net.slots(2)
    kept = (x + y + z) % 2
    net.send(d_dn.at[1 - c], n0, d_c, cp)
    four.group(1)
    three.cross()
    four.fold(0)

    def gate_up_grads(t, h, slopes):
        hidden_t[h] = slopes[h].reshape(8 * MINE, WIDE).T

        def part(i, carry):
            cols = pl.ds(pl.multiple_of(i * step, 128), step)
            w_gu[t, h, :, cols] = nn(hidden_t[h], flat_mid[:, cols]).astype(LOW)
            return carry

        lax.fori_loop(0, 3, part, 0)

    for h in range(2):
        gate_up_grads(0, h, slope_gate)
    net.send(all_gu.at[0, 1 - c], g0.at[0], d_c + 1, cp)
    net.got(n0, d_c)
    for q in range(2):
        d_dn[c, q] = added(d_dn[c, q], n0[q])
    net.send(d_dn.at[c, 1 - kept], n1, d_y, xp)
    four.fold(1)
    three.done()
    four.cross()
    for h in range(2):
        gate_up_grads(1, h, slope_up)
    net.send(all_gu.at[1, 1 - c], g0.at[1], d_c + 2, cp)

    def share(t):
        net.got(g0.at[t], d_c + 1 + t)
        for q in range(2):
            all_gu[t, c, q] = added(all_gu[t, c, q], g0[t, q])
        net.send(all_gu.at[t, c, 1 - x], g1.at[t], d_x + t, xp)

    def home_down():
        net.got(n1, d_y)
        d_dn[c, kept] = added(d_dn[c, kept], n1[...])
        net.move(
            jnp.logical_and(z % 2 == y, x == y),
            d_dn.at[c, kept],
            n2,
            d_y + 1,
            d_y + 1,
            at(2 * (z // 2) + y, kept, z % 2, c),
        )

    def home_gate_up(t):
        net.got(g1.at[t], d_x + t)
        all_gu[t, c, x] = added(all_gu[t, c, x], g1[t])
        source = z // 2 + 2 * t
        net.move(
            jnp.logical_and(source == z, z % 2 == c),
            all_gu.at[t, c, x],
            g2.at[c],
            d_home + t,
            d_home + c,
            at(source, y, x, z % 2),
        )

    share(0)
    share(1)
    four.done()

    home_down()
    mid = middle[...]
    grad, gain_grad = norm_back(mid, gains[2:3, :], total[...].reshape(MINE, D))
    small[0, 2:3, :] = gain_grad
    grad_mid = stream_of(cot) + grad
    grad_middle[...] = grad_mid
    grad, gain_grad = norm_back(attn_proj[...], gains[1:2, :], grad_mid)
    small[0, 1:2, :] = gain_grad
    grad_attn[...] = grad.astype(LOW)
    net.flush(three.gathered + four.gathered)
    d_out = got_up.reshape(4, 2, 2, 2, 32, D)
    a0 = got_mid.reshape(8 * MINE, D).at[pl.ds(0, 16 * 48)].reshape(4, 2, 2, 48, D)
    b0 = recv_y.reshape(4, 2, 2, 32, D)
    flat_d_out, flat_d_in = got_up.reshape(HEADS * HD, D), d_in.reshape(HEADS * HD + 2 * HD, D)

    def out_grads(j, carry):
        flat_d_out[rows_of(j), :] = tn(mixed[j], grad_attn[...]).astype(LOW)
        return carry

    lax.fori_loop(0, HEADS, out_grads, 0)
    net.send(d_out.at[:, :, :, 1 - c], b0, d_c + 3, cp)

    class Collect:
        def __init__(self, grads, core_in, y_in, x_in, z_in, core_slot, y_first):
            self.y_first = y_first
            self.grads, self.core_in, self.y_in, self.x_in, self.z_in = (
                grads,
                core_in,
                y_in,
                x_in,
                z_in,
            )
            self.cs, self.ys, self.xs, self.zs = core_slot, net.slots(2), net.slots(2), net.slots(2)

        def cores(self):
            net.got(self.core_in, self.cs)
            for part, pair in enumerate((1 - zh, zh)):

                def one(i, carry):
                    p, q, r = 2 * pair + i // 4, i // 2 % 2, i % 2
                    self.grads[p, q, r, c] = added(self.grads[p, q, r, c], self.core_in[p, q, r])
                    return carry

                lax.fori_loop(0, 8, one, 0)
                both = pl.ds(2 * pair, 2)
                if self.y_first:
                    away, device = self.grads.at[both, 1 - y, :, c], yp
                else:
                    away, device = self.grads.at[both, :, 1 - x, c], xp
                net.send(away, self.y_in.at[part], self.ys + part, device)

        def ys_in(self, part):
            pair = (1 - zh, zh)[part]
            net.got(self.y_in.at[part], self.ys + part)

            def one(i, carry):
                p, q = i // 2, i % 2
                there = 2 * pair + p
                if self.y_first:
                    self.grads[there, y, q, c] = added(
                        self.grads[there, y, q, c], self.y_in[part, p, q]
                    )
                else:
                    self.grads[there, q, x, c] = added(
                        self.grads[there, q, x, c], self.y_in[part, p, q]
                    )
                return carry

            lax.fori_loop(0, 4, one, 0)
            both = pl.ds(2 * pair, 2)
            if self.y_first:
                away, device = self.grads.at[both, y, 1 - x, c], xp
            else:
                away, device = self.grads.at[both, 1 - y, x, c], yp
            net.send(away, self.x_in.at[part], self.xs + part, device)

        def xs_in(self, part):
            pair = (1 - zh, zh)[part]
            net.got(self.x_in.at[part], self.xs + part)
            for p in range(2):
                there = 2 * pair + p
                self.grads[there, y, x, c] = added(
                    self.grads[there, y, x, c], self.x_in[part, p]
                )
            net.send(
                self.grads.at[2 * pair + 1 - zl, y, x, c],
                self.z_in.at[part],
                self.zs + part,
                z_peers[1],
            )

        def cross(self, slot):
            net.got(self.z_in.at[0], self.zs)
            there = 2 * (1 - zh) + zl
            self.grads[there, y, x, c] = added(self.grads[there, y, x, c], self.z_in[0])
            net.send(self.grads.at[there, y, x, c], self.z_in.at[2], slot, z_peers[2])

        def done(self, slot, result):
            net.got(self.z_in.at[1], self.zs + 1)
            net.got(self.z_in.at[2], slot)
            result[...] = (
                self.grads[z, y, x, c].astype(F32)
                + self.z_in[1].astype(F32)
                + self.z_in[2].astype(F32)
            )

    r_s, r_z = net.slots(8), net.slots(2)
    outs = Collect(d_out, b0, b1, b2, b3, d_c + 3, True)
    ins = Collect(d_in, a0, a1, a2, a3, d_c + 4, True)

    grad_heads[...] = jnp.zeros((6, MINE, HD), F32)

    def head_back(j, carry):
        up = nt(grad_attn[...], flat_out[rows_of(j), :]).astype(LOW)
        prob = probs[j]
        grad_prob = nt(up, heads[HEADS + 1])
        grad_heads[HEADS + 1] += tn(prob.astype(LOW), up)
        center = jnp.sum(grad_prob * prob, -1, keepdims=True)
        grad_score = (prob * (grad_prob - center)).astype(LOW)
        grad_heads[j] = nn(grad_score, heads[HEADS]) * SCALE_FACTOR
        grad_heads[HEADS] += tn(grad_score, heads[j]) * SCALE_FACTOR
        return carry

    outs.cores()
    lax.fori_loop(0, HEADS, head_back, 0)
    key_acc[...] = jnp.zeros((2, HD), F32)

    def turn_back(j, carry):
        first, second = grad_heads[j, :, :half], grad_heads[j, :, half:]
        turned = jnp.concatenate(
            [
                first * cosine[...] + second * sine[...],
                second * cosine[...] - first * sine[...],
            ],
            -1,
        )
        which = pl.ds(j // HEADS, 1)
        grad, gain_grad = norm_back(proj[j], head_gains[which, :], turned)
        key_acc[which, :] += gain_grad
        grad_proj[j] = grad.astype(LOW)
        return carry

    lax.fori_loop(0, HEADS + 1, turn_back, 0)
    grad_proj[HEADS + 1] = grad_heads[HEADS + 1].astype(LOW)
    small[0, 4:5, 0:HD] = key_acc[0:1, :]
    small[0, 4:5, HD : 2 * HD] = key_acc[1:2, :]


    def in_grads(j, carry):
        flat_d_in[rows_of(j), :] = tn(grad_proj[j], normed_in[...]).astype(LOW)
        return carry

    lax.fori_loop(0, HEADS + 2, in_grads, 0)
    net.send(d_in.at[:, :, :, 1 - c], a0, d_c + 4, cp)
    total[...] = jnp.zeros((2, PART, D), F32)

    def in_back(j, carry):
        total[...] += nn(grad_proj[j], flat_in[rows_of(j), :]).reshape(2, PART, D)
        return carry

    home_gate_up(0)
    lax.fori_loop(0, HEADS + 2, in_back, 0)
    ins.cores()
    grad, gain_grad = norm_back(stream_of(x_ref), gains[0:1, :], total[...].reshape(MINE, D))
    small[0, 0:1, :] = gain_grad
    input_grad[...] = (grad_middle[...] + grad).reshape(2, 1, PART, D)
    net.send(small.at[0], small.at[1], r_s, cp)
    home_gate_up(1)
    outs.ys_in(0)
    outs.ys_in(1)
    net.got(small.at[1], r_s)
    small[2] = small[0] + small[1]
    net.send(small.at[2], small.at[3], r_s + 1, xp)
    ins.ys_in(0)
    outs.xs_in(0)
    outs.xs_in(1)
    net.got(small.at[3], r_s + 1)
    small[4] = small[2] + small[3]
    net.send(small.at[4], small.at[5], r_s + 2, yp)
    ins.ys_in(1)
    outs.cross(r_z)
    ins.xs_in(0)
    ins.xs_in(1)
    net.got(small.at[5], r_s + 2)
    small[6] = small[4] + small[5]
    for k in (1, 2, 3):
        net.send(small.at[6], small.at[6 + k], r_s + 2 + k, z_peers[k])
    ins.cross(r_z + 1)
    outs.done(r_z, o_out)
    net.got(n2, d_y + 1)
    o_dn[...] = n2[...].astype(F32)[:BLOCK]
    for k in (1, 2, 3):
        net.got(small.at[6 + k], r_s + 2 + k)
    sums = (small[6] + small[7]) + (small[8] + small[9])
    o_gains[...] = sums[0:4, :]
    o_heads[...] = jnp.concatenate([sums[4:5, 0:HD], sums[4:5, HD : 2 * HD]], 0)
    scaled = sums[5:6, :]
    tokens = jnp.sum(jnp.where(spot == 4, scaled, 0.0), -1, keepdims=True)
    means = jnp.sqrt(scaled / (tokens * D))
    for i in range(4):
        o_rms[i] = jnp.sum(jnp.where(spot == i, means, 0.0))
    ins.done(r_z + 1, o_in)
    for h in range(2):
        net.got(g2.at[h], d_home + h)
        o_gu[pl.ds(h * BLOCK, BLOCK), :] = g2[h].astype(F32)[:BLOCK]
    net.drain()


def vm(*shape):
    return pltpu.VMEM(shape, LOW)


def vf(*shape):
    return pltpu.VMEM(shape, F32)


def whole_layer(x, seg, valid, ain, aout, gu, dn, gains, head_gains, cot):
    vmem = pl.BlockSpec(memory_space=pltpu.VMEM)
    scratch = [
        vm(4, 2, 2, 2, 48, D),
        vm(4, 2, 2, 2, 32, D),
        vm(2, 2, 2, PADDED, D),
        vm(2, 2, PADDED, D),
        vf(MINE, MINE),
        vf(MINE, MINE),
        vf(MINE, MINE),
        vf(MINE, MINE),
        vm(MINE, D),
        vf(6, MINE, HD),
        vm(6, MINE, HD),
        vf(4, MINE, MINE),
        vm(4, MINE, HD),
        vf(MINE, D),
        vf(MINE, D),
        vm(2, 2, PART, D),
        vf(2, PART, D),
        vm(2, 2, 2, 2, PART, D),
        vm(2, 2, 2, 2, PART, D),
        vm(2, WIDE, 8 * MINE),
        vm(2, 2, 2, PAIR, WIDE),
        vm(2, 2, 2, PAIR, WIDE),
        vf(2, 2, PART, D),
        vf(2, 2, 2, PART, D),
        vm(2, 2, 2, PART, D),
        vm(2, 2, 2, PART, D),
        vm(2, 3, PART, D),
        vm(2, 3, PART, D),
        vf(MINE, D),
        vm(MINE, D),
        vf(6, MINE, HD),
        vm(6, MINE, HD),
        vf(2, HD),
        vm(4, 2, 2, 2, 48, D),
    ]
    for count in (48, 32):
        scratch += [vm(2, 2, 2, count, D), vm(2, 2, count, D), vm(3, count, D)]
    scratch += [vm(2, 2, PADDED, D), vm(2, PADDED, D), vm(2, PADDED, D)]
    scratch += [vm(2, 2, PADDED, D), vm(2, PADDED, D), vm(PADDED, D), vm(PADDED, D)]
    scratch += [vf(10, 8, D)]
    scratch += [pltpu.SemaphoreType.DMA((2,))] + [pltpu.SemaphoreType.DMA((144,))] * 2
    return pl.pallas_call(
        layer_kernel,
        out_shape=(
            jax.ShapeDtypeStruct((2, 1, PART, D), LOW),
            jax.ShapeDtypeStruct((2, 1, PART, D), F32),
            jax.ShapeDtypeStruct((48, D), F32),
            jax.ShapeDtypeStruct((32, D), F32),
            jax.ShapeDtypeStruct((2 * BLOCK, D), F32),
            jax.ShapeDtypeStruct((BLOCK, D), F32),
            jax.ShapeDtypeStruct((4, D), F32),
            jax.ShapeDtypeStruct((2, HD), F32),
            jax.ShapeDtypeStruct((4,), F32),
        ),
        in_specs=[vmem] * 10,
        out_specs=(vmem,) * 8 + (pl.BlockSpec(memory_space=pltpu.SMEM),),
        scratch_shapes=scratch,
        compiler_params=pltpu.CompilerParams(
            collective_id=1, has_side_effects=True, vmem_limit_bytes=VMEM_BYTES
        ),
        name="layer",
    )(x, seg, valid, ain, aout, gu, dn, gains, head_gains, cot)


def copy_kernel(*refs):
    count = (len(refs) - 2) // 3
    given, made, held = refs[:count], refs[count : 2 * count], refs[2 * count : 3 * count]
    into = [pltpu.make_async_copy(a, b, refs[-2].at[i]) for i, (a, b) in enumerate(zip(given, held))]
    out = [pltpu.make_async_copy(a, b, refs[-1].at[i]) for i, (a, b) in enumerate(zip(held, made))]
    for copy in into:
        copy.start()
    for first, second in zip(into, out):
        first.wait()
        second.start()
    for copy in out:
        copy.wait()


def copied(arrays):
    place = pl.BlockSpec(memory_space=pl.ANY)
    return pl.pallas_call(
        copy_kernel,
        out_shape=tuple(jax.ShapeDtypeStruct(array.shape, array.dtype) for array in arrays),
        in_specs=[place] * len(arrays),
        out_specs=(place,) * len(arrays),
        scratch_shapes=[pltpu.VMEM(array.shape, array.dtype) for array in arrays]
        + [pltpu.SemaphoreType.DMA((len(arrays),))] * 2,
        name="results",
    )(*arrays)


def split_shards(
    inputs,
    segment_ids,
    valid_mask,
    attn_in,
    attn_out,
    ffw_in,
    ffw_out,
    norm_gains,
    head_gains,
    cotangent,
):
    results = whole_layer(
        inputs,
        segment_ids,
        valid_mask,
        attn_in,
        attn_out,
        ffw_in,
        ffw_out,
        norm_gains,
        head_gains,
        cotangent,
    )
    return copied(results[:-1]) + results[-1:]


def solution(mesh):
    placed = (
        P(None, "dp", None, None),
        P(None, "dp", None),
        P(None, "dp", None),
        P("dp", None),
        P("dp", None),
        P("dp", None),
        P("dp", None),
        P(),
        P(),
        P(None, "dp", None, None),
    )
    return jax.shard_map(
        split_shards if mesh.shape["dp"] == 32 else general_shards,
        mesh=mesh,
        in_specs=placed,
        out_specs=(
            P(None, "dp", None, None),
            P(None, "dp", None, None),
            P("dp", None),
            P("dp", None),
            P("dp", None),
            P("dp", None),
            P(),
            P(),
            P(),
        ),
        check_vma=False,
    )
```

```python
import math

import jax
import jax.numpy as jnp
from jax import lax
from jax.experimental import pallas as pl
from jax.experimental.pallas import tpu as pltpu
from jax.sharding import PartitionSpec as P

D = 1152
HEADS = 4
HD = 256
FF = 6912
MICRO = 2


EPSILON = 1e-06
SCALE_FACTOR = 0.0625
THETA = 10000.0
NEGATIVE = -1e30


def shortened(x):

    def short(part):
        return part.astype(jnp.bfloat16) if part.dtype == jnp.float32 else part

    return jax.tree.map(short, x)


def swapped(block, axis, stride):
    count = lax.axis_size(axis)
    route = []
    for low in range(count):
        high = low | 1 << stride
        if high != low and high < count:
            route += [(low, high), (high, low)]
    return lax.ppermute(block, axis, route)


def norm_rows(values, gain):
    return values * lax.rsqrt(jnp.mean(values * values, -1, keepdims=True) + EPSILON) * gain


def rotate(values, cosine, sine):
    half = values.shape[-1] // 2
    first = values[..., :half]
    second = values[..., half:]
    return jnp.concatenate([first * cosine - second * sine, second * cosine + first * sine], -1)


def doc_tables(segments, validity, head_size):
    length = segments.shape[-1]
    places = jnp.arange(length, dtype=jnp.int32)
    same_doc = segments[..., :, None] == segments[..., None, :]
    earlier = places[None, :] < places[:, None]
    position = jnp.sum(jnp.logical_and(same_doc, earlier).astype(jnp.int32), -1)
    reach = places[None, :] <= places[:, None]
    usable = jnp.logical_or(validity[..., None, :] > 0, places[None, :] == places[:, None])
    allowed = jnp.logical_and(jnp.logical_and(same_doc, reach), usable)
    freqs = jnp.exp(
        jnp.arange(head_size // 2, dtype=jnp.float32) * (-2.0 * math.log(THETA) / head_size)
    )
    angles = position.astype(jnp.float32)[..., None] * freqs
    return (allowed, jnp.cos(angles), jnp.sin(angles))


def prepare(projected, head_gains, cosine, sine):
    width = HEADS * HD
    query = projected[..., :width].reshape(projected.shape[:-1] + (HEADS, HD))
    keys = projected[..., width : width + HD]
    values = projected[..., width + HD :]
    query = rotate(norm_rows(query, head_gains[0]), cosine[..., None, :], sine[..., None, :])
    keys = rotate(norm_rows(keys, head_gains[1]), cosine, sine)
    return (query, keys, values)


def across(left, piece):
    return lax.dot_general(
        left, piece, (((1,), (1,)), ((), ())), preferred_element_type=jnp.float32
    )


def over_rows(left, right):
    return lax.dot_general(
        left, right, (((0,), (0,)), ((), ())), preferred_element_type=jnp.float32
    )


def score_table(query_low, keys_low):
    return (
        jnp.einsum("qhd,kd->hqk", query_low, keys_low, preferred_element_type=jnp.float32)
        * SCALE_FACTOR
    )


def attend(query_low, keys_low, values_low, allowed):
    scores = score_table(query_low, keys_low)
    masked = jnp.where(allowed[None], scores, NEGATIVE)
    peak = jnp.max(masked, -1, keepdims=True)
    expo = jnp.where(allowed[None], jnp.exp(masked - peak), 0.0)
    totals = jnp.sum(expo, -1, keepdims=True)
    probs = expo / totals
    mixed = jnp.einsum(
        "hqk,kd->qhd", probs.astype(jnp.bfloat16), values_low, preferred_element_type=jnp.float32
    )
    return (mixed, peak + jnp.log(totals))


def attend_back(query_low, keys_low, values_low, allowed, log_sum, grad_low):
    scores = score_table(query_low, keys_low)
    probs = jnp.where(allowed[None], jnp.exp(scores - log_sum), 0.0)
    grad_probs = jnp.einsum("qhd,kd->hqk", grad_low, values_low, preferred_element_type=jnp.float32)
    grad_values = jnp.einsum(
        "hqk,qhd->kd", probs.astype(jnp.bfloat16), grad_low, preferred_element_type=jnp.float32
    )
    center = jnp.sum(grad_probs * probs, -1, keepdims=True)
    grad_scores = (probs * (grad_probs - center)).astype(jnp.bfloat16)
    grad_query = (
        jnp.einsum("hqk,kd->qhd", grad_scores, keys_low, preferred_element_type=jnp.float32)
        * SCALE_FACTOR
    )
    grad_keys = (
        jnp.einsum("hqk,qhd->kd", grad_scores, query_low, preferred_element_type=jnp.float32)
        * SCALE_FACTOR
    )
    return (grad_query, grad_keys, grad_values)


def gated(gate, upward):
    return jax.nn.gelu(gate, approximate=True) * upward


def general_shards(
    inputs,
    segment_ids,
    valid_mask,
    attn_in,
    attn_out,
    ffw_in,
    ffw_out,
    norm_gains,
    head_gains,
    cotangent,
):
    width = HEADS * HD
    kept_proj = []
    kept_normed_in = []
    kept_mixed = []
    kept_attn = []
    kept_gate = []
    kept_normed_mid = []
    kept_hidden = []
    kept_ffw = []
    gain_sums = jnp.zeros((4, D), jnp.float32)
    head_sums = jnp.zeros((2, HD), jnp.float32)
    stats = jnp.zeros((5,), jnp.float32)
    results = []
    input_grads = []
    for step in range(MICRO):
        full_in, full_out = (
            lax.all_gather(attn_in, "dp", axis=0, tiled=True),
            lax.all_gather(attn_out, "dp", axis=0, tiled=True),
        )
        full_ffin, full_ffout = (
            lax.all_gather(ffw_in, "dp", axis=0, tiled=True),
            lax.all_gather(ffw_out, "dp", axis=0, tiled=True),
        )
        stream = inputs[step, 0].astype(jnp.float32)
        length = stream.shape[0]
        allowed, cosine, sine = doc_tables(segment_ids[step, 0], valid_mask[step, 0], HD)
        normed_in = norm_rows(stream, norm_gains[0]).astype(jnp.bfloat16)
        projected = across(normed_in, full_in)
        query, keys, values = prepare(projected, head_gains, cosine, sine)
        query_low = query.astype(jnp.bfloat16)
        keys_low = keys.astype(jnp.bfloat16)
        values_low = values.astype(jnp.bfloat16)
        mixed, log_sum = attend(query_low, keys_low, values_low, allowed)
        mixed_low = mixed.reshape(length, width).astype(jnp.bfloat16)
        attn_proj = jnp.dot(mixed_low, full_out, preferred_element_type=jnp.float32)
        attn_branch = norm_rows(attn_proj, norm_gains[1])
        middle = stream + attn_branch
        normed_mid = norm_rows(middle, norm_gains[2]).astype(jnp.bfloat16)
        gate_up = across(normed_mid, full_ffin)
        gate = gate_up[:, :FF]
        upward = gate_up[:, FF:]
        hidden = gated(gate, upward).astype(jnp.bfloat16)
        ffw_proj = jnp.dot(hidden, full_ffout, preferred_element_type=jnp.float32)
        ffw_branch = norm_rows(ffw_proj, norm_gains[3])
        results.append((middle + ffw_branch).astype(jnp.bfloat16))
        weight = valid_mask[step, 0].astype(jnp.float32)
        sums = [
            jnp.sum(weight * jnp.sum(value * value, -1))
            for value in (stream, middle, attn_branch, ffw_branch)
        ]
        sums.append(jnp.sum(weight))
        stats = stats + jnp.stack(sums)
        upstream = cotangent[step, 0].astype(jnp.float32)
        _, back_ffw = jax.vjp(norm_rows, ffw_proj, norm_gains[3])
        grad_ffw_proj, gain_three = back_ffw(upstream)
        grad_ffw_low = grad_ffw_proj.astype(jnp.bfloat16)
        grad_hidden = across(grad_ffw_low, full_ffout)
        _, back_gated = jax.vjp(gated, gate, upward)
        grad_gate, grad_upward = back_gated(grad_hidden)
        grad_gate_up = jnp.concatenate([grad_gate, grad_upward], 1).astype(jnp.bfloat16)
        grad_normed_mid = jnp.dot(grad_gate_up, full_ffin, preferred_element_type=jnp.float32)
        _, back_mid = jax.vjp(norm_rows, middle, norm_gains[2])
        grad_mid_part, gain_two = back_mid(grad_normed_mid)
        grad_middle = upstream + grad_mid_part
        _, back_attn = jax.vjp(norm_rows, attn_proj, norm_gains[1])
        grad_attn_proj, gain_one = back_attn(grad_middle)
        grad_attn_low = grad_attn_proj.astype(jnp.bfloat16)
        grad_mixed = across(grad_attn_low, full_out)
        grad_mixed_low = grad_mixed.astype(jnp.bfloat16).reshape(length, HEADS, HD)
        grad_query, grad_keys, grad_values = attend_back(
            query_low, keys_low, values_low, allowed, log_sum, grad_mixed_low
        )
        _, back_prep = jax.vjp(
            lambda table, gains: prepare(table, gains, cosine, sine), projected, head_gains
        )
        grad_projected, grad_heads = back_prep((grad_query, grad_keys, grad_values))
        grad_proj_low = grad_projected.astype(jnp.bfloat16)
        grad_normed_in = jnp.dot(grad_proj_low, full_in, preferred_element_type=jnp.float32)
        _, back_in = jax.vjp(norm_rows, stream, norm_gains[0])
        grad_stream, gain_zero = back_in(grad_normed_in)
        input_grads.append(grad_middle + grad_stream)
        gain_sums = gain_sums + jnp.stack([gain_zero, gain_one, gain_two, gain_three])
        head_sums = head_sums + grad_heads
        kept_proj.append(grad_proj_low)
        kept_normed_in.append(normed_in)
        kept_mixed.append(mixed_low)
        kept_attn.append(grad_attn_low)
        kept_gate.append(grad_gate_up)
        kept_normed_mid.append(normed_mid)
        kept_hidden.append(hidden)
        kept_ffw.append(grad_ffw_low)
    pairs = [
        (jnp.concatenate(kept_proj, 0), jnp.concatenate(kept_normed_in, 0)),
        (jnp.concatenate(kept_mixed, 0), jnp.concatenate(kept_attn, 0)),
        (jnp.concatenate(kept_gate, 0), jnp.concatenate(kept_normed_mid, 0)),
        (jnp.concatenate(kept_hidden, 0), jnp.concatenate(kept_ffw, 0)),
    ]
    levels = lax.axis_size("dp").bit_length() - 1
    place = lax.axis_index("dp")
    top_bit = place >> levels - 1 & 1
    kept_parts = []
    sent_parts = []
    for left, right in pairs:
        half_cols = left.shape[1] // 2
        kept_parts.append(
            over_rows(lax.dynamic_slice_in_dim(left, top_bit * half_cols, half_cols, 1), right)
        )
        sent_parts.append(
            over_rows(
                lax.dynamic_slice_in_dim(left, (1 - top_bit) * half_cols, half_cols, 1), right
            )
        )
    current = tuple(kept_parts)
    outgoing = tuple(sent_parts)
    for level in range(levels):
        bit = levels - 1 - level
        arrived = jax.tree.map(
            lambda part, own: part.astype(own.dtype),
            swapped(shortened(outgoing), "dp", bit),
            outgoing,
        )
        current = tuple((mine + theirs for mine, theirs in zip(current, arrived)))
        if level + 1 < levels:
            next_bit = place >> bit - 1 & 1
            halves = [piece.shape[0] // 2 for piece in current]
            outgoing = tuple(
                (
                    lax.dynamic_slice_in_dim(piece, (1 - next_bit) * rows, rows, 0)
                    for piece, rows in zip(current, halves)
                )
            )
            current = tuple(
                (
                    lax.dynamic_slice_in_dim(piece, next_bit * rows, rows, 0)
                    for piece, rows in zip(current, halves)
                )
            )
    shard_in, shard_out, shard_ffin, shard_ffout = current
    gain_total, head_total, stat_total = lax.psum((gain_sums, head_sums, stats), "dp")
    rms_values = jnp.sqrt(stat_total[:4] / (stat_total[4] * D))
    layer_out = jnp.stack(results)[:, None]
    input_grad = jnp.stack(input_grads)[:, None]
    return (
        layer_out,
        input_grad,
        shard_in,
        shard_out,
        shard_ffin,
        shard_ffout,
        gain_total,
        head_total,
        rms_values,
    )


BLOCK = 216
PADDED = 224
WIDE = 2 * PADDED
MINE = 128
PART = 64
PAIR = 2 * MINE
VMEM_BYTES = 62 << 20
SQRT_2_OVER_PI = math.sqrt(2.0 / math.pi)
CUBIC = 0.044715
MESH = pl.DeviceIdType.MESH
LOW = jnp.bfloat16
F32 = jnp.float32


def spots():
    me = lax.axis_index("dp")
    return me, me // 8, me // 4 % 2, me // 2 % 2, me % 2


def at(z, y, x, c):
    return z * 8 + y * 4 + x * 2 + c


def z_peer(z, k):
    if k == 0:
        return z
    if k == 1:
        return z + 1 - 2 * (z % 2)
    if k == 2:
        return (z + 2) % 4
    return 3 - z


def greet(z, y, x, c):
    barrier = pltpu.get_barrier_semaphore()
    others = [at(z_peer(z, k), y, x, core) for k in (1, 2, 3) for core in (c, 1 - c)]
    others.append(at(z, y, x, 1 - c))
    for k in range(2):
        for there_y, there_x in ((1 - y, x), (y, 1 - x), (1 - y, 1 - x)):
            others.append(at(z_peer(z, k), there_y, there_x, c))
    for device in others:
        pl.semaphore_signal(barrier, inc=1, device_id=(device,), device_id_type=MESH)
    pl.semaphore_wait(barrier, len(others))


def nt(left, right):
    return lax.dot_general(left, right, (((1,), (1,)), ((), ())), preferred_element_type=F32)


def nn(left, right):
    return lax.dot_general(left, right, (((1,), (0,)), ((), ())), preferred_element_type=F32)


def tn(left, right):
    return lax.dot_general(left, right, (((0,), (0,)), ((), ())), preferred_element_type=F32)


def norm_back(values, gain, upstream):
    scale = lax.rsqrt(jnp.mean(values * values, -1, keepdims=True) + EPSILON)
    normed = values * scale
    gain_grad = jnp.sum(upstream * normed, 0, keepdims=True)
    inner = upstream * gain
    grad = scale * (inner - normed * jnp.mean(inner * normed, -1, keepdims=True))
    return grad, gain_grad


def added(left, right):
    return (left.astype(F32) + right.astype(F32)).astype(LOW)


def stream_of(ref):
    return ref[...].reshape(MINE, D).astype(F32)


class Net:
    def __init__(self, send_sems, recv_sems, anyone):
        self.send_sems, self.recv_sems, self.anyone = send_sems, recv_sems, anyone
        self.used, self.sent, self.maybe = 0, [], []

    def slots(self, count):
        first = self.used
        self.used += count
        return first

    def copy(self, src, dst, send_slot, recv_slot, device):
        return pltpu.make_async_remote_copy(
            src_ref=src,
            dst_ref=dst,
            send_sem=self.send_sems.at[send_slot],
            recv_sem=self.recv_sems.at[recv_slot],
            device_id=(device,),
            device_id_type=MESH,
        )

    def send(self, src, dst, slot, device):
        copy = self.copy(src, dst, slot, slot, device)
        copy.start()
        self.sent.append(copy)

    def move(self, stays, src, dst, send_slot, recv_slot, device):
        copy = self.copy(src, dst, send_slot, recv_slot, device)

        @pl.when(stays)
        def _():
            pltpu.make_async_copy(src, dst, self.recv_sems.at[recv_slot]).start()

        @pl.when(jnp.logical_not(stays))
        def _():
            copy.start()

        self.maybe.append((stays, copy))

    def got(self, block, slot):
        self.copy(block, block, slot, slot, self.anyone).wait_recv()

    def flush(self, gone):
        for copy in gone:
            copy.wait_send()
        names = {id(copy) for copy in gone}
        self.sent = [copy for copy in self.sent if id(copy) not in names]

    def drain(self):
        self.flush(list(self.sent))
        self.settle_moves()

    def settle_moves(self):
        for stays, copy in self.maybe:

            @pl.when(jnp.logical_not(stays))
            def _():
                copy.wait_send()

        self.maybe = []


def layer_kernel(*refs):
    (
        x_ref,
        seg_ref,
        valid_ref,
        ain,
        aout,
        gu,
        dn,
        gains,
        head_gains,
        cot,
        layer_out,
        input_grad,
        o_in,
        o_out,
        o_gu,
        o_dn,
        o_gains,
        o_heads,
        o_rms,
        all_in,
        all_out,
        all_gu,
        all_dn,
        allow,
        cosine,
        sine,
        weight,
        normed_in,
        proj,
        heads,
        probs,
        mixed,
        attn_proj,
        middle,
        rows,
        total,
        got_mid,
        got_up,
        hidden_t,
        slope_gate,
        slope_up,
        acc,
        keep,
        send_y,
        recv_y,
        send_z,
        recv_z,
        grad_middle,
        grad_attn,
        grad_heads,
        grad_proj,
        key_acc,
        d_in,
        a1,
        a2,
        a3,
        b1,
        b2,
        b3,
        g0,
        g1,
        g2,
        d_dn,
        n0,
        n1,
        n2,
        small,
        local,
        send_sems,
        recv_sems,
    ) = refs
    me, z, y, x, c = spots()
    xp, yp, cp = at(z, y, 1 - x, c), at(z, 1 - y, x, c), at(z, y, x, 1 - c)
    z_peers = [at(z_peer(z, k), y, x, c) for k in range(4)]
    net = Net(send_sems, recv_sems, cp)
    keep_in = pltpu.make_async_copy(ain, all_in.at[z, y, x, c], local.at[0])
    keep_out = pltpu.make_async_copy(aout, all_out.at[z, y, x, c], local.at[1])
    keep_in.start()
    keep_out.start()
    greet(z, y, x, c)

    class Spread:
        def __init__(self, own, full, x_first):
            self.own, self.full, self.x_first = own, full, x_first
            self.first, self.second = (xp, yp) if x_first else (yp, xp)
            self.az, self.ax, self.ay, self.ac = (net.slots(4) for _ in range(4))

        def block(self, k):
            return self.full.at[z_peer(z, k), y, x, c]

        def crossed(self, k):
            there = z_peer(z, k)
            return self.full.at[there, y, 1 - x, c] if self.x_first else self.full.at[there, 1 - y, x, c]

        def pair(self, there, own, core):
            if self.x_first:
                return self.full.at[there, y if own else 1 - y, :, core]
            return self.full.at[there, :, x if own else 1 - x, core]

        def start(self):
            net.send(self.own, self.block(0), self.az + 1, z_peers[1])
            net.send(self.own, self.block(0), self.ax, self.first)
            net.send(self.own, self.block(0), self.az + 2, z_peers[2])

        def hop(self, k):
            block = self.block(k)
            net.got(block, self.az + k)
            if k == 2:
                net.send(block, block, self.az + 3, z_peers[1])
            net.send(block, block, self.ax + k, self.first)

        def turn(self, k):
            net.got(self.crossed(k), self.ax + k)
            pair = self.pair(z_peer(z, k), True, c)
            net.send(pair, pair, self.ay + k, self.second)

        def near(self):
            part = self.pair(slice(None), True, c)
            net.send(part, part, self.ac, cp)

        def far(self):
            for k in range(4):
                net.got(self.pair(z_peer(z, k), False, c), self.ay + k)
            part = self.pair(slice(None), False, c)
            net.send(part, part, self.ac + 1, cp)

        def whole(self):
            net.got(self.pair(slice(None), True, 1 - c), self.ac)
            net.got(self.pair(slice(None), False, 1 - c), self.ac + 1)

    into, outof = Spread(ain, all_in, True), Spread(aout, all_out, False)
    into.start()
    w_one, w_two, w_c, w_d = net.slots(2), net.slots(2), net.slots(2), net.slots(2)
    v_x, v_one, v_c = net.slots(1), net.slots(2), net.slots(1)
    kind, goal = z // 2, 2 * (z % 2) + c
    blank = jnp.zeros((PADDED - BLOCK, D), F32)
    both_parts = gu[...].astype(F32)
    for h in range(2):
        part = both_parts[h * BLOCK : (h + 1) * BLOCK]
        g0[0, h] = jnp.concatenate([part, blank], 0).astype(LOW)
    n0[0] = jnp.concatenate([dn[...].astype(F32), blank], 0).astype(LOW)

    def rows_out():
        for h in range(2):
            net.move(
                jnp.logical_and(goal == z, c == h),
                g0.at[0, h],
                all_gu.at[kind, h, x],
                w_one + h,
                w_one + kind,
                at(goal, y, x, h),
            )

    def rows_on(which):
        t = (kind, 1 - kind)[which]
        block = all_gu.at[t, c, x]
        net.got(block, w_one + t)
        net.send(block, block, w_two + which, xp)
        net.send(block, block, w_c + which, cp)

    def rows_across(which):
        block = all_gu.at[(kind, 1 - kind)[which], c, 1 - x]
        net.got(block, w_two + which)
        net.send(block, block, w_d + which, cp)

    def rows_whole():
        for which in range(2):
            t = (kind, 1 - kind)[which]
            net.got(all_gu.at[t, 1 - c, x], w_c + which)
            net.got(all_gu.at[t, 1 - c, 1 - x], w_d + which)
        net.got(all_dn.at[1 - c], v_c)

    across_x = []

    def down_x():
        net.send(n0.at[0], n0.at[1], v_x, xp)
        across_x.append(net.sent[-1])


    def down_out():
        net.got(n0.at[1], v_x)
        for other in range(2):
            block_x = 1 - x if other else x
            net.move(
                jnp.logical_and(z % 2 == block_x, z % 2 == y),
                n0.at[other],
                all_dn.at[c, y],
                v_one + other,
                v_one + y,
                at(2 * (z // 2) + block_x, z % 2, x, c),
            )

    def down_on():
        for q in range(2):
            net.got(all_dn.at[c, q], v_one + q)
        net.send(all_dn.at[c], all_dn.at[c], v_c, cp)

    into.hop(1)
    into.hop(2)
    outof.start()
    keep_in.wait()
    keep_out.wait()
    into.turn(0)
    into.turn(1)
    into.hop(3)

    def along_lanes(ref):
        return jnp.concatenate([ref[0].astype(F32), ref[1].astype(F32)], 1)

    seg = jnp.broadcast_to(along_lanes(seg_ref), (MINE, MINE))
    valid = jnp.broadcast_to(along_lanes(valid_ref), (MINE, MINE))
    row = lax.broadcasted_iota(jnp.int32, (MINE, MINE), 0)
    col = lax.broadcasted_iota(jnp.int32, (MINE, MINE), 1)
    length = MINE // MICRO
    same = jnp.logical_and(seg == seg.T, row // length == col // length)
    position = jnp.sum(jnp.where(jnp.logical_and(same, col < row), 1.0, 0.0), -1, keepdims=True)
    usable = jnp.logical_or(valid > 0.0, row == col)
    allow[...] = jnp.where(
        jnp.logical_and(jnp.logical_and(same, col <= row), usable), 1.0, 0.0
    )
    weight[...] = valid.T
    freqs = jnp.exp(col.astype(F32) * (-2.0 * math.log(THETA) / HD))
    angles = position * freqs
    cosine[...] = jnp.cos(angles)
    sine[...] = jnp.sin(angles)
    stream = stream_of(x_ref)
    normed_in[...] = norm_rows(stream, gains[0:1, :]).astype(LOW)

    rows_out()
    down_x()
    into.turn(2)
    outof.hop(1)
    outof.hop(2)
    into.turn(3)
    into.near()
    outof.turn(0)
    outof.turn(1)
    outof.hop(3)
    into.far()
    outof.turn(2)
    outof.turn(3)
    outof.near()
    into.whole()

    down_out()
    flat_in = all_in.reshape(HEADS * HD + 2 * HD, D)
    flat_out = all_out.reshape(HEADS * HD, D)
    half = HD // 2

    def rows_of(j):
        return pl.ds(pl.multiple_of(j * HD, HD), HD)

    def project(j, carry):
        table = nt(normed_in[...], flat_in[rows_of(j), :])
        proj[j] = table

        @pl.when(j < HEADS + 1)
        def _():
            turned = norm_rows(table, head_gains[pl.ds(j // HEADS, 1), :])
            first, second = turned[:, :half], turned[:, half:]
            heads[j, :, :half] = (first * cosine[...] - second * sine[...]).astype(LOW)
            heads[j, :, half:] = (second * cosine[...] + first * sine[...]).astype(LOW)

        @pl.when(j == HEADS + 1)
        def _():
            heads[j] = table.astype(LOW)

        return carry

    lax.fori_loop(0, HEADS + 2, project, 0)
    outof.far()

    def attend_head(j, carry):
        seen = allow[...] > 0.0
        scores = nt(heads[j], heads[HEADS]) * SCALE_FACTOR
        masked = jnp.where(seen, scores, NEGATIVE)
        peak = jnp.max(masked, -1, keepdims=True)
        expo = jnp.where(seen, jnp.exp(masked - peak), 0.0)
        prob = expo / jnp.sum(expo, -1, keepdims=True)
        probs[j] = prob
        mixed[j] = nn(prob.astype(LOW), heads[HEADS + 1]).astype(LOW)
        return carry

    lax.fori_loop(0, HEADS, attend_head, 0)
    rows_on(0)
    outof.whole()

    attn_proj[...] = jnp.zeros((MINE, D), F32)

    def attn_out_head(j, carry):
        attn_proj[...] += nn(mixed[j], flat_out[rows_of(j), :])
        return carry

    lax.fori_loop(0, HEADS, attn_out_head, 0)
    branch = norm_rows(attn_proj[...], gains[1:2, :])
    mid = stream_of(x_ref) + branch
    middle[...] = mid
    rows[0] = norm_rows(mid, gains[2:3, :]).astype(LOW).reshape(2, PART, D)

    def counted(values):
        return jnp.sum(weight[:, 0:1] * jnp.sum(values * values, -1, keepdims=True))

    spot = lax.broadcasted_iota(jnp.int32, (1, D), 1)
    stats = jnp.where(spot == 4, jnp.sum(weight[:, 0:1]), 0.0)
    first_values = stream_of(x_ref)
    stats += jnp.where(spot == 0, counted(first_values), 0.0)
    stats += jnp.where(spot == 1, counted(mid), 0.0)
    stats += jnp.where(spot == 2, counted(branch), 0.0)
    small[0] = jnp.zeros((8, D), F32)
    small[0, 5:6, :] = stats

    zh, zl = z // 2, z % 2
    w_gu, w_dn = all_gu.reshape(2, 2, WIDE, D), all_dn.reshape(2, WIDE, D)

    class Half:
        def __init__(self, which, half, got_all, compute):
            self.which, self.half, self.got_all, self.compute = which, half, got_all, compute
            self.az, self.ay, self.ry, self.rz = (net.slots(4) for _ in range(4))
            self.gathered, self.here = [], set()

        def block(self, k, yy):
            there = z_peer(z, k)
            return self.got_all.at[self.half, there // 2, there % 2, yy]

        def pass_on(self, block, slot, device):
            net.send(block, block, slot, device)
            self.gathered.append(net.sent[-1])

        def start(self):
            own = rows.at[self.which, self.half]
            net.send(own, self.block(0, y), self.az + 1, z_peers[1])
            self.gathered.append(net.sent[-1])
            net.send(own, self.block(0, y), self.az + 2, z_peers[2])
            self.gathered.append(net.sent[-1])
            net.send(own, self.block(0, y), self.ay, yp)
            self.gathered.append(net.sent[-1])
            self.got_all[self.half, zh, zl, y] = rows[self.which, self.half]

        def hop(self, k):
            block = self.block(k, y)
            net.got(block, self.az + k)
            if k == 2:
                self.pass_on(block, self.az + 3, z_peers[1])
            self.pass_on(block, self.ay + k, yp)

        def arrive(self, g):
            if g not in self.here:
                for k in (2 * g, 2 * g + 1):
                    net.got(self.block(k, 1 - y), self.ay + k)
            self.here.add(g)

        def group(self, g):
            self.arrive(g)
            self.compute(self.half, zh if g == 0 else 1 - zh)
            keep[self.half, g] = acc[:, y]
            send_y[self.half, g] = acc[:, 1 - y].astype(LOW)
            net.send(send_y.at[self.half, g], recv_y.at[self.half, g], self.ry + g, yp)

        def fold(self, g):
            net.got(recv_y.at[self.half, g], self.ry + g)
            keep[self.half, g] += recv_y[self.half, g].astype(F32)
            send_z[self.half, g] = keep[self.half, g, 1 - zl].astype(LOW)
            net.send(send_z.at[self.half, g], recv_z.at[self.half, g], self.rz + g, z_peers[1])

        def cross(self):
            net.got(recv_z.at[self.half, 1], self.rz + 1)
            send_z[self.half, 2] = (
                keep[self.half, 1, zl] + recv_z[self.half, 1].astype(F32)
            ).astype(LOW)
            net.send(send_z.at[self.half, 2], recv_z.at[self.half, 2], self.rz + 2, z_peers[2])

        def done(self):
            net.got(recv_z.at[self.half, 0], self.rz)
            net.got(recv_z.at[self.half, 2], self.rz + 2)
            total[self.half] = (
                keep[self.half, 0, zl]
                + recv_z[self.half, 0].astype(F32)
                + recv_z[self.half, 2].astype(F32)
            )

    def columns(half, pair):
        return pl.ds(pl.multiple_of((half * 2 + pair) * PAIR, PAIR), PAIR)

    def put(h, part):
        part = part.reshape(2, 2, PART, D)

        @pl.when(h == 0)
        def _():
            acc[...] = part

        @pl.when(h == 1)
        def _():
            acc[...] += part

    def forward_pairs(half, pair):
        def one(h, carry):
            block = got_mid[half, pair].reshape(PAIR, D)
            gate = nt(block, w_gu[0, h])
            upward = nt(block, w_gu[1, h])
            square = gate * gate
            tanh = jnp.tanh(SQRT_2_OVER_PI * gate * (1.0 + CUBIC * square))
            side = 0.5 * (1.0 + tanh)
            gelu = gate * side
            slope = side + 0.5 * gate * (1.0 - tanh * tanh) * (
                SQRT_2_OVER_PI * (1.0 + 3.0 * CUBIC * square)
            )
            low = (gelu * upward).astype(LOW)
            slope_gate[h, half, pair] = (upward * slope).astype(LOW)
            slope_up[h, half, pair] = gelu.astype(LOW)
            put(h, nn(low, w_dn[h]))
            hidden_t[h, :, columns(half, pair)] = low.T
            return carry

        lax.fori_loop(0, 2, one, 0)

    def weights_here():
        net.settle_moves()
        net.flush(across_x)
        rows_across(1)
        rows_whole()

    def forward_end(half):
        span = pl.ds(half * PART, PART)
        ffw_proj = total[half]
        branch = norm_rows(ffw_proj, gains[3:4, :])
        layer_out[half, 0] = (middle[span, :] + branch).astype(LOW)
        counts = jnp.sum(weight[span, 0:1] * jnp.sum(branch * branch, -1, keepdims=True))
        small[0, 5:6, :] += jnp.where(spot == 3, counts, 0.0)
        grad, gain_grad = norm_back(ffw_proj, gains[3:4, :], cot[half, 0].astype(F32))
        small[0, 3:4, :] += gain_grad
        rows[1, half] = grad.astype(LOW)

    def backward_pairs(half, pair):
        def one(h, carry):
            block = got_up[half, pair].reshape(PAIR, D)
            back = nt(block, w_dn[h])
            gate = (back * slope_gate[h, half, pair].astype(F32)).astype(LOW)
            upward = (back * slope_up[h, half, pair].astype(F32)).astype(LOW)
            put(h, nn(gate, w_gu[0, h]) + nn(upward, w_gu[1, h]))
            slope_gate[h, half, pair] = gate
            slope_up[h, half, pair] = upward
            return carry

        lax.fori_loop(0, 2, one, 0)

    one, two = Half(0, 0, got_mid, forward_pairs), Half(0, 1, got_mid, forward_pairs)
    one.start()
    rows_on(1)
    rows_across(0)
    down_on()
    two.start()
    one.hop(1)
    two.hop(1)
    one.hop(2)
    two.hop(2)
    one.hop(3)
    two.hop(3)
    weights_here()
    one.group(0)
    one.group(1)
    one.fold(0)
    two.group(0)
    one.fold(1)
    two.group(1)
    one.cross()
    two.fold(0)
    one.done()
    forward_end(0)
    three, four = Half(1, 0, got_up, backward_pairs), Half(1, 1, got_up, backward_pairs)
    three.start()
    two.fold(1)
    three.hop(1)
    two.cross()
    three.hop(2)
    two.done()
    forward_end(1)
    four.start()
    net.flush([copy for copy in net.sent if not any(copy is other for other in three.gathered + four.gathered)])
    three.group(0)
    four.hop(1)
    three.hop(3)
    four.hop(2)
    three.group(1)
    three.fold(0)
    four.hop(3)
    four.group(0)
    three.fold(1)

    step = 384
    flat_mid, flat_up = got_mid.reshape(8 * MINE, D), got_up.reshape(8 * MINE, D)

    four.arrive(1)

    def down_grads(i, carry):
        h, cols = i // 3, pl.ds(pl.multiple_of(i % 3 * step, 128), step)
        d_dn.reshape(2, WIDE, D)[h, :, cols] = nn(hidden_t[h], flat_up[:, cols]).astype(LOW)
        return carry

    lax.fori_loop(0, 6, down_grads, 0)
    d_c, d_x, d_home, d_y = net.slots(5), net.slots(2), net.slots(2), net.slots(2)
    kept = (x + y + z) % 2
    net.send(d_dn.at[1 - c], n0, d_c, cp)
    four.group(1)
    three.cross()
    four.fold(0)

    def gate_up_grads(t, h, slopes):
        hidden_t[h] = slopes[h].reshape(8 * MINE, WIDE).T

        def part(i, carry):
            cols = pl.ds(pl.multiple_of(i * step, 128), step)
            w_gu[t, h, :, cols] = nn(hidden_t[h], flat_mid[:, cols]).astype(LOW)
            return carry

        lax.fori_loop(0, 3, part, 0)

    for h in range(2):
        gate_up_grads(0, h, slope_gate)
    net.send(all_gu.at[0, 1 - c], g0.at[0], d_c + 1, cp)
    net.got(n0, d_c)
    for q in range(2):
        d_dn[c, q] = added(d_dn[c, q], n0[q])
    net.send(d_dn.at[c, 1 - kept], n1, d_y, xp)
    four.fold(1)
    three.done()
    four.cross()
    for h in range(2):
        gate_up_grads(1, h, slope_up)
    net.send(all_gu.at[1, 1 - c], g0.at[1], d_c + 2, cp)

    def share(t):
        net.got(g0.at[t], d_c + 1 + t)
        for q in range(2):
            all_gu[t, c, q] = added(all_gu[t, c, q], g0[t, q])
        net.send(all_gu.at[t, c, 1 - x], g1.at[t], d_x + t, xp)

    def home_down():
        net.got(n1, d_y)
        d_dn[c, kept] = added(d_dn[c, kept], n1[...])
        net.move(
            jnp.logical_and(z % 2 == y, x == y),
            d_dn.at[c, kept],
            n2,
            d_y + 1,
            d_y + 1,
            at(2 * (z // 2) + y, kept, z % 2, c),
        )

    def home_gate_up(t):
        net.got(g1.at[t], d_x + t)
        all_gu[t, c, x] = added(all_gu[t, c, x], g1[t])
        source = z // 2 + 2 * t
        net.move(
            jnp.logical_and(source == z, z % 2 == c),
            all_gu.at[t, c, x],
            g2.at[c],
            d_home + t,
            d_home + c,
            at(source, y, x, z % 2),
        )

    share(0)
    share(1)
    four.done()

    home_down()
    mid = middle[...]
    grad, gain_grad = norm_back(mid, gains[2:3, :], total[...].reshape(MINE, D))
    small[0, 2:3, :] = gain_grad
    grad_mid = stream_of(cot) + grad
    grad_middle[...] = grad_mid
    grad, gain_grad = norm_back(attn_proj[...], gains[1:2, :], grad_mid)
    small[0, 1:2, :] = gain_grad
    grad_attn[...] = grad.astype(LOW)
    net.flush(three.gathered + four.gathered)
    d_out = got_up.reshape(4, 2, 2, 2, 32, D)
    a0 = got_mid.reshape(8 * MINE, D).at[pl.ds(0, 16 * 48)].reshape(4, 2, 2, 48, D)
    b0 = recv_y.reshape(4, 2, 2, 32, D)
    flat_d_out, flat_d_in = got_up.reshape(HEADS * HD, D), d_in.reshape(HEADS * HD + 2 * HD, D)

    def out_grads(j, carry):
        flat_d_out[rows_of(j), :] = tn(mixed[j], grad_attn[...]).astype(LOW)
        return carry

    lax.fori_loop(0, HEADS, out_grads, 0)
    net.send(d_out.at[:, :, :, 1 - c], b0, d_c + 3, cp)

    class Collect:
        def __init__(self, grads, core_in, y_in, x_in, z_in, core_slot, y_first):
            self.y_first = y_first
            self.grads, self.core_in, self.y_in, self.x_in, self.z_in = (
                grads,
                core_in,
                y_in,
                x_in,
                z_in,
            )
            self.cs, self.ys, self.xs, self.zs = core_slot, net.slots(2), net.slots(2), net.slots(2)

        def cores(self):
            net.got(self.core_in, self.cs)
            for part, pair in enumerate((1 - zh, zh)):

                def one(i, carry):
                    p, q, r = 2 * pair + i // 4, i // 2 % 2, i % 2
                    self.grads[p, q, r, c] = added(self.grads[p, q, r, c], self.core_in[p, q, r])
                    return carry

                lax.fori_loop(0, 8, one, 0)
                both = pl.ds(2 * pair, 2)
                if self.y_first:
                    away, device = self.grads.at[both, 1 - y, :, c], yp
                else:
                    away, device = self.grads.at[both, :, 1 - x, c], xp
                net.send(away, self.y_in.at[part], self.ys + part, device)

        def ys_in(self, part):
            pair = (1 - zh, zh)[part]
            net.got(self.y_in.at[part], self.ys + part)

            def one(i, carry):
                p, q = i // 2, i % 2
                there = 2 * pair + p
                if self.y_first:
                    self.grads[there, y, q, c] = added(
                        self.grads[there, y, q, c], self.y_in[part, p, q]
                    )
                else:
                    self.grads[there, q, x, c] = added(
                        self.grads[there, q, x, c], self.y_in[part, p, q]
                    )
                return carry

            lax.fori_loop(0, 4, one, 0)
            both = pl.ds(2 * pair, 2)
            if self.y_first:
                away, device = self.grads.at[both, y, 1 - x, c], xp
            else:
                away, device = self.grads.at[both, 1 - y, x, c], yp
            net.send(away, self.x_in.at[part], self.xs + part, device)

        def xs_in(self, part):
            pair = (1 - zh, zh)[part]
            net.got(self.x_in.at[part], self.xs + part)
            for p in range(2):
                there = 2 * pair + p
                self.grads[there, y, x, c] = added(
                    self.grads[there, y, x, c], self.x_in[part, p]
                )
            net.send(
                self.grads.at[2 * pair + 1 - zl, y, x, c],
                self.z_in.at[part],
                self.zs + part,
                z_peers[1],
            )

        def cross(self, slot):
            net.got(self.z_in.at[0], self.zs)
            there = 2 * (1 - zh) + zl
            self.grads[there, y, x, c] = added(self.grads[there, y, x, c], self.z_in[0])
            net.send(self.grads.at[there, y, x, c], self.z_in.at[2], slot, z_peers[2])

        def done(self, slot, result):
            net.got(self.z_in.at[1], self.zs + 1)
            net.got(self.z_in.at[2], slot)
            result[...] = (
                self.grads[z, y, x, c].astype(F32)
                + self.z_in[1].astype(F32)
                + self.z_in[2].astype(F32)
            )

    r_s, r_z = net.slots(8), net.slots(2)
    outs = Collect(d_out, b0, b1, b2, b3, d_c + 3, True)
    ins = Collect(d_in, a0, a1, a2, a3, d_c + 4, True)

    grad_heads[...] = jnp.zeros((6, MINE, HD), F32)

    def head_back(j, carry):
        up = nt(grad_attn[...], flat_out[rows_of(j), :]).astype(LOW)
        prob = probs[j]
        grad_prob = nt(up, heads[HEADS + 1])
        grad_heads[HEADS + 1] += tn(prob.astype(LOW), up)
        center = jnp.sum(grad_prob * prob, -1, keepdims=True)
        grad_score = (prob * (grad_prob - center)).astype(LOW)
        grad_heads[j] = nn(grad_score, heads[HEADS]) * SCALE_FACTOR
        grad_heads[HEADS] += tn(grad_score, heads[j]) * SCALE_FACTOR
        return carry

    outs.cores()
    lax.fori_loop(0, HEADS, head_back, 0)
    key_acc[...] = jnp.zeros((2, HD), F32)

    def turn_back(j, carry):
        first, second = grad_heads[j, :, :half], grad_heads[j, :, half:]
        turned = jnp.concatenate(
            [
                first * cosine[...] + second * sine[...],
                second * cosine[...] - first * sine[...],
            ],
            -1,
        )
        which = pl.ds(j // HEADS, 1)
        grad, gain_grad = norm_back(proj[j], head_gains[which, :], turned)
        key_acc[which, :] += gain_grad
        grad_proj[j] = grad.astype(LOW)
        return carry

    lax.fori_loop(0, HEADS + 1, turn_back, 0)
    grad_proj[HEADS + 1] = grad_heads[HEADS + 1].astype(LOW)
    small[0, 4:5, 0:HD] = key_acc[0:1, :]
    small[0, 4:5, HD : 2 * HD] = key_acc[1:2, :]


    def in_grads(j, carry):
        flat_d_in[rows_of(j), :] = tn(grad_proj[j], normed_in[...]).astype(LOW)
        return carry

    lax.fori_loop(0, HEADS + 2, in_grads, 0)
    net.send(d_in.at[:, :, :, 1 - c], a0, d_c + 4, cp)
    total[...] = jnp.zeros((2, PART, D), F32)

    def in_back(j, carry):
        total[...] += nn(grad_proj[j], flat_in[rows_of(j), :]).reshape(2, PART, D)
        return carry

    home_gate_up(0)
    lax.fori_loop(0, HEADS + 2, in_back, 0)
    ins.cores()
    grad, gain_grad = norm_back(stream_of(x_ref), gains[0:1, :], total[...].reshape(MINE, D))
    small[0, 0:1, :] = gain_grad
    input_grad[...] = (grad_middle[...] + grad).reshape(2, 1, PART, D)
    net.send(small.at[0], small.at[1], r_s, cp)
    home_gate_up(1)
    outs.ys_in(0)
    outs.ys_in(1)
    net.got(small.at[1], r_s)
    small[2] = small[0] + small[1]
    net.send(small.at[2], small.at[3], r_s + 1, xp)
    ins.ys_in(0)
    outs.xs_in(0)
    outs.xs_in(1)
    net.got(small.at[3], r_s + 1)
    small[4] = small[2] + small[3]
    net.send(small.at[4], small.at[5], r_s + 2, yp)
    ins.ys_in(1)
    outs.cross(r_z)
    ins.xs_in(0)
    ins.xs_in(1)
    net.got(small.at[5], r_s + 2)
    small[6] = small[4] + small[5]
    for k in (1, 2, 3):
        net.send(small.at[6], small.at[6 + k], r_s + 2 + k, z_peers[k])
    ins.cross(r_z + 1)
    outs.done(r_z, o_out)
    net.got(n2, d_y + 1)
    o_dn[...] = n2[...].astype(F32)[:BLOCK]
    for k in (1, 2, 3):
        net.got(small.at[6 + k], r_s + 2 + k)
    sums = (small[6] + small[7]) + (small[8] + small[9])
    o_gains[...] = sums[0:4, :]
    o_heads[...] = jnp.concatenate([sums[4:5, 0:HD], sums[4:5, HD : 2 * HD]], 0)
    scaled = sums[5:6, :]
    tokens = jnp.sum(jnp.where(spot == 4, scaled, 0.0), -1, keepdims=True)
    means = jnp.sqrt(scaled / (tokens * D))
    for i in range(4):
        o_rms[i] = jnp.sum(jnp.where(spot == i, means, 0.0))
    ins.done(r_z + 1, o_in)
    for h in range(2):
        net.got(g2.at[h], d_home + h)
        o_gu[pl.ds(h * BLOCK, BLOCK), :] = g2[h].astype(F32)[:BLOCK]
    net.drain()


def vm(*shape):
    return pltpu.VMEM(shape, LOW)


def vf(*shape):
    return pltpu.VMEM(shape, F32)


def whole_layer(x, seg, valid, ain, aout, gu, dn, gains, head_gains, cot):
    vmem = pl.BlockSpec(memory_space=pltpu.VMEM)
    scratch = [
        vm(4, 2, 2, 2, 48, D),
        vm(4, 2, 2, 2, 32, D),
        vm(2, 2, 2, PADDED, D),
        vm(2, 2, PADDED, D),
        vf(MINE, MINE),
        vf(MINE, MINE),
        vf(MINE, MINE),
        vf(MINE, MINE),
        vm(MINE, D),
        vf(6, MINE, HD),
        vm(6, MINE, HD),
        vf(4, MINE, MINE),
        vm(4, MINE, HD),
        vf(MINE, D),
        vf(MINE, D),
        vm(2, 2, PART, D),
        vf(2, PART, D),
        vm(2, 2, 2, 2, PART, D),
        vm(2, 2, 2, 2, PART, D),
        vm(2, WIDE, 8 * MINE),
        vm(2, 2, 2, PAIR, WIDE),
        vm(2, 2, 2, PAIR, WIDE),
        vf(2, 2, PART, D),
        vf(2, 2, 2, PART, D),
        vm(2, 2, 2, PART, D),
        vm(2, 2, 2, PART, D),
        vm(2, 3, PART, D),
        vm(2, 3, PART, D),
        vf(MINE, D),
        vm(MINE, D),
        vf(6, MINE, HD),
        vm(6, MINE, HD),
        vf(2, HD),
        vm(4, 2, 2, 2, 48, D),
    ]
    for count in (48, 32):
        scratch += [vm(2, 2, 2, count, D), vm(2, 2, count, D), vm(3, count, D)]
    scratch += [vm(2, 2, PADDED, D), vm(2, PADDED, D), vm(2, PADDED, D)]
    scratch += [vm(2, 2, PADDED, D), vm(2, PADDED, D), vm(PADDED, D), vm(PADDED, D)]
    scratch += [vf(10, 8, D)]
    scratch += [pltpu.SemaphoreType.DMA((2,))] + [pltpu.SemaphoreType.DMA((144,))] * 2
    return pl.pallas_call(
        layer_kernel,
        out_shape=(
            jax.ShapeDtypeStruct((2, 1, PART, D), LOW),
            jax.ShapeDtypeStruct((2, 1, PART, D), F32),
            jax.ShapeDtypeStruct((48, D), F32),
            jax.ShapeDtypeStruct((32, D), F32),
            jax.ShapeDtypeStruct((2 * BLOCK, D), F32),
            jax.ShapeDtypeStruct((BLOCK, D), F32),
            jax.ShapeDtypeStruct((4, D), F32),
            jax.ShapeDtypeStruct((2, HD), F32),
            jax.ShapeDtypeStruct((4,), F32),
        ),
        in_specs=[vmem] * 10,
        out_specs=(vmem,) * 8 + (pl.BlockSpec(memory_space=pltpu.SMEM),),
        scratch_shapes=scratch,
        compiler_params=pltpu.CompilerParams(
            collective_id=1, has_side_effects=True, vmem_limit_bytes=VMEM_BYTES
        ),
        name="layer",
    )(x, seg, valid, ain, aout, gu, dn, gains, head_gains, cot)


def copy_kernel(*refs):
    count = (len(refs) - 2) // 3
    given, made, held = refs[:count], refs[count : 2 * count], refs[2 * count : 3 * count]
    into = [pltpu.make_async_copy(a, b, refs[-2].at[i]) for i, (a, b) in enumerate(zip(given, held))]
    out = [pltpu.make_async_copy(a, b, refs[-1].at[i]) for i, (a, b) in enumerate(zip(held, made))]
    for copy in into:
        copy.start()
    for first, second in zip(into, out):
        first.wait()
        second.start()
    for copy in out:
        copy.wait()


def copied(arrays):
    place = pl.BlockSpec(memory_space=pl.ANY)
    return pl.pallas_call(
        copy_kernel,
        out_shape=tuple(jax.ShapeDtypeStruct(array.shape, array.dtype) for array in arrays),
        in_specs=[place] * len(arrays),
        out_specs=(place,) * len(arrays),
        scratch_shapes=[pltpu.VMEM(array.shape, array.dtype) for array in arrays]
        + [pltpu.SemaphoreType.DMA((len(arrays),))] * 2,
        name="results",
    )(*arrays)


def split_shards(
    inputs,
    segment_ids,
    valid_mask,
    attn_in,
    attn_out,
    ffw_in,
    ffw_out,
    norm_gains,
    head_gains,
    cotangent,
):
    results = whole_layer(
        inputs,
        segment_ids,
        valid_mask,
        attn_in,
        attn_out,
        ffw_in,
        ffw_out,
        norm_gains,
        head_gains,
        cotangent,
    )
    return copied(results[:-1]) + results[-1:]


def solution(mesh):
    placed = (
        P(None, "dp", None, None),
        P(None, "dp", None),
        P(None, "dp", None),
        P("dp", None),
        P("dp", None),
        P("dp", None),
        P("dp", None),
        P(),
        P(),
        P(None, "dp", None, None),
    )
    return jax.shard_map(
        split_shards if mesh.shape["dp"] == 32 else general_shards,
        mesh=mesh,
        in_specs=placed,
        out_specs=(
            P(None, "dp", None, None),
            P(None, "dp", None, None),
            P("dp", None),
            P("dp", None),
            P("dp", None),
            P("dp", None),
            P(),
            P(),
            P(),
        ),
        check_vma=False,
    )
```

```python
import math

import jax
import jax.numpy as jnp
from jax import lax
from jax.experimental import pallas as pl
from jax.experimental.pallas import tpu as pltpu
from jax.sharding import PartitionSpec as P

D = 1152
HEADS = 4
HD = 256
FF = 6912
MICRO = 2


EPSILON = 1e-06
SCALE_FACTOR = 0.0625
THETA = 10000.0
NEGATIVE = -1e30


def shortened(x):

    def short(part):
        return part.astype(jnp.bfloat16) if part.dtype == jnp.float32 else part

    return jax.tree.map(short, x)


def swapped(block, axis, stride):
    count = lax.axis_size(axis)
    route = []
    for low in range(count):
        high = low | 1 << stride
        if high != low and high < count:
            route += [(low, high), (high, low)]
    return lax.ppermute(block, axis, route)


def norm_rows(values, gain):
    return values * lax.rsqrt(jnp.mean(values * values, -1, keepdims=True) + EPSILON) * gain


def rotate(values, cosine, sine):
    half = values.shape[-1] // 2
    first = values[..., :half]
    second = values[..., half:]
    return jnp.concatenate([first * cosine - second * sine, second * cosine + first * sine], -1)


def doc_tables(segments, validity, head_size):
    length = segments.shape[-1]
    places = jnp.arange(length, dtype=jnp.int32)
    same_doc = segments[..., :, None] == segments[..., None, :]
    earlier = places[None, :] < places[:, None]
    position = jnp.sum(jnp.logical_and(same_doc, earlier).astype(jnp.int32), -1)
    reach = places[None, :] <= places[:, None]
    usable = jnp.logical_or(validity[..., None, :] > 0, places[None, :] == places[:, None])
    allowed = jnp.logical_and(jnp.logical_and(same_doc, reach), usable)
    freqs = jnp.exp(
        jnp.arange(head_size // 2, dtype=jnp.float32) * (-2.0 * math.log(THETA) / head_size)
    )
    angles = position.astype(jnp.float32)[..., None] * freqs
    return (allowed, jnp.cos(angles), jnp.sin(angles))


def prepare(projected, head_gains, cosine, sine):
    width = HEADS * HD
    query = projected[..., :width].reshape(projected.shape[:-1] + (HEADS, HD))
    keys = projected[..., width : width + HD]
    values = projected[..., width + HD :]
    query = rotate(norm_rows(query, head_gains[0]), cosine[..., None, :], sine[..., None, :])
    keys = rotate(norm_rows(keys, head_gains[1]), cosine, sine)
    return (query, keys, values)


def across(left, piece):
    return lax.dot_general(
        left, piece, (((1,), (1,)), ((), ())), preferred_element_type=jnp.float32
    )


def over_rows(left, right):
    return lax.dot_general(
        left, right, (((0,), (0,)), ((), ())), preferred_element_type=jnp.float32
    )


def score_table(query_low, keys_low):
    return (
        jnp.einsum("qhd,kd->hqk", query_low, keys_low, preferred_element_type=jnp.float32)
        * SCALE_FACTOR
    )


def attend(query_low, keys_low, values_low, allowed):
    scores = score_table(query_low, keys_low)
    masked = jnp.where(allowed[None], scores, NEGATIVE)
    peak = jnp.max(masked, -1, keepdims=True)
    expo = jnp.where(allowed[None], jnp.exp(masked - peak), 0.0)
    totals = jnp.sum(expo, -1, keepdims=True)
    probs = expo / totals
    mixed = jnp.einsum(
        "hqk,kd->qhd", probs.astype(jnp.bfloat16), values_low, preferred_element_type=jnp.float32
    )
    return (mixed, peak + jnp.log(totals))


def attend_back(query_low, keys_low, values_low, allowed, log_sum, grad_low):
    scores = score_table(query_low, keys_low)
    probs = jnp.where(allowed[None], jnp.exp(scores - log_sum), 0.0)
    grad_probs = jnp.einsum("qhd,kd->hqk", grad_low, values_low, preferred_element_type=jnp.float32)
    grad_values = jnp.einsum(
        "hqk,qhd->kd", probs.astype(jnp.bfloat16), grad_low, preferred_element_type=jnp.float32
    )
    center = jnp.sum(grad_probs * probs, -1, keepdims=True)
    grad_scores = (probs * (grad_probs - center)).astype(jnp.bfloat16)
    grad_query = (
        jnp.einsum("hqk,kd->qhd", grad_scores, keys_low, preferred_element_type=jnp.float32)
        * SCALE_FACTOR
    )
    grad_keys = (
        jnp.einsum("hqk,qhd->kd", grad_scores, query_low, preferred_element_type=jnp.float32)
        * SCALE_FACTOR
    )
    return (grad_query, grad_keys, grad_values)


def gated(gate, upward):
    return jax.nn.gelu(gate, approximate=True) * upward


def general_shards(
    inputs,
    segment_ids,
    valid_mask,
    attn_in,
    attn_out,
    ffw_in,
    ffw_out,
    norm_gains,
    head_gains,
    cotangent,
):
    width = HEADS * HD
    kept_proj = []
    kept_normed_in = []
    kept_mixed = []
    kept_attn = []
    kept_gate = []
    kept_normed_mid = []
    kept_hidden = []
    kept_ffw = []
    gain_sums = jnp.zeros((4, D), jnp.float32)
    head_sums = jnp.zeros((2, HD), jnp.float32)
    stats = jnp.zeros((5,), jnp.float32)
    results = []
    input_grads = []
    for step in range(MICRO):
        full_in, full_out = (
            lax.all_gather(attn_in, "dp", axis=0, tiled=True),
            lax.all_gather(attn_out, "dp", axis=0, tiled=True),
        )
        full_ffin, full_ffout = (
            lax.all_gather(ffw_in, "dp", axis=0, tiled=True),
            lax.all_gather(ffw_out, "dp", axis=0, tiled=True),
        )
        stream = inputs[step, 0].astype(jnp.float32)
        length = stream.shape[0]
        allowed, cosine, sine = doc_tables(segment_ids[step, 0], valid_mask[step, 0], HD)
        normed_in = norm_rows(stream, norm_gains[0]).astype(jnp.bfloat16)
        projected = across(normed_in, full_in)
        query, keys, values = prepare(projected, head_gains, cosine, sine)
        query_low = query.astype(jnp.bfloat16)
        keys_low = keys.astype(jnp.bfloat16)
        values_low = values.astype(jnp.bfloat16)
        mixed, log_sum = attend(query_low, keys_low, values_low, allowed)
        mixed_low = mixed.reshape(length, width).astype(jnp.bfloat16)
        attn_proj = jnp.dot(mixed_low, full_out, preferred_element_type=jnp.float32)
        attn_branch = norm_rows(attn_proj, norm_gains[1])
        middle = stream + attn_branch
        normed_mid = norm_rows(middle, norm_gains[2]).astype(jnp.bfloat16)
        gate_up = across(normed_mid, full_ffin)
        gate = gate_up[:, :FF]
        upward = gate_up[:, FF:]
        hidden = gated(gate, upward).astype(jnp.bfloat16)
        ffw_proj = jnp.dot(hidden, full_ffout, preferred_element_type=jnp.float32)
        ffw_branch = norm_rows(ffw_proj, norm_gains[3])
        results.append((middle + ffw_branch).astype(jnp.bfloat16))
        weight = valid_mask[step, 0].astype(jnp.float32)
        sums = [
            jnp.sum(weight * jnp.sum(value * value, -1))
            for value in (stream, middle, attn_branch, ffw_branch)
        ]
        sums.append(jnp.sum(weight))
        stats = stats + jnp.stack(sums)
        upstream = cotangent[step, 0].astype(jnp.float32)
        _, back_ffw = jax.vjp(norm_rows, ffw_proj, norm_gains[3])
        grad_ffw_proj, gain_three = back_ffw(upstream)
        grad_ffw_low = grad_ffw_proj.astype(jnp.bfloat16)
        grad_hidden = across(grad_ffw_low, full_ffout)
        _, back_gated = jax.vjp(gated, gate, upward)
        grad_gate, grad_upward = back_gated(grad_hidden)
        grad_gate_up = jnp.concatenate([grad_gate, grad_upward], 1).astype(jnp.bfloat16)
        grad_normed_mid = jnp.dot(grad_gate_up, full_ffin, preferred_element_type=jnp.float32)
        _, back_mid = jax.vjp(norm_rows, middle, norm_gains[2])
        grad_mid_part, gain_two = back_mid(grad_normed_mid)
        grad_middle = upstream + grad_mid_part
        _, back_attn = jax.vjp(norm_rows, attn_proj, norm_gains[1])
        grad_attn_proj, gain_one = back_attn(grad_middle)
        grad_attn_low = grad_attn_proj.astype(jnp.bfloat16)
        grad_mixed = across(grad_attn_low, full_out)
        grad_mixed_low = grad_mixed.astype(jnp.bfloat16).reshape(length, HEADS, HD)
        grad_query, grad_keys, grad_values = attend_back(
            query_low, keys_low, values_low, allowed, log_sum, grad_mixed_low
        )
        _, back_prep = jax.vjp(
            lambda table, gains: prepare(table, gains, cosine, sine), projected, head_gains
        )
        grad_projected, grad_heads = back_prep((grad_query, grad_keys, grad_values))
        grad_proj_low = grad_projected.astype(jnp.bfloat16)
        grad_normed_in = jnp.dot(grad_proj_low, full_in, preferred_element_type=jnp.float32)
        _, back_in = jax.vjp(norm_rows, stream, norm_gains[0])
        grad_stream, gain_zero = back_in(grad_normed_in)
        input_grads.append(grad_middle + grad_stream)
        gain_sums = gain_sums + jnp.stack([gain_zero, gain_one, gain_two, gain_three])
        head_sums = head_sums + grad_heads
        kept_proj.append(grad_proj_low)
        kept_normed_in.append(normed_in)
        kept_mixed.append(mixed_low)
        kept_attn.append(grad_attn_low)
        kept_gate.append(grad_gate_up)
        kept_normed_mid.append(normed_mid)
        kept_hidden.append(hidden)
        kept_ffw.append(grad_ffw_low)
    pairs = [
        (jnp.concatenate(kept_proj, 0), jnp.concatenate(kept_normed_in, 0)),
        (jnp.concatenate(kept_mixed, 0), jnp.concatenate(kept_attn, 0)),
        (jnp.concatenate(kept_gate, 0), jnp.concatenate(kept_normed_mid, 0)),
        (jnp.concatenate(kept_hidden, 0), jnp.concatenate(kept_ffw, 0)),
    ]
    levels = lax.axis_size("dp").bit_length() - 1
    place = lax.axis_index("dp")
    top_bit = place >> levels - 1 & 1
    kept_parts = []
    sent_parts = []
    for left, right in pairs:
        half_cols = left.shape[1] // 2
        kept_parts.append(
            over_rows(lax.dynamic_slice_in_dim(left, top_bit * half_cols, half_cols, 1), right)
        )
        sent_parts.append(
            over_rows(
                lax.dynamic_slice_in_dim(left, (1 - top_bit) * half_cols, half_cols, 1), right
            )
        )
    current = tuple(kept_parts)
    outgoing = tuple(sent_parts)
    for level in range(levels):
        bit = levels - 1 - level
        arrived = jax.tree.map(
            lambda part, own: part.astype(own.dtype),
            swapped(shortened(outgoing), "dp", bit),
            outgoing,
        )
        current = tuple((mine + theirs for mine, theirs in zip(current, arrived)))
        if level + 1 < levels:
            next_bit = place >> bit - 1 & 1
            halves = [piece.shape[0] // 2 for piece in current]
            outgoing = tuple(
                (
                    lax.dynamic_slice_in_dim(piece, (1 - next_bit) * rows, rows, 0)
                    for piece, rows in zip(current, halves)
                )
            )
            current = tuple(
                (
                    lax.dynamic_slice_in_dim(piece, next_bit * rows, rows, 0)
                    for piece, rows in zip(current, halves)
                )
            )
    shard_in, shard_out, shard_ffin, shard_ffout = current
    gain_total, head_total, stat_total = lax.psum((gain_sums, head_sums, stats), "dp")
    rms_values = jnp.sqrt(stat_total[:4] / (stat_total[4] * D))
    layer_out = jnp.stack(results)[:, None]
    input_grad = jnp.stack(input_grads)[:, None]
    return (
        layer_out,
        input_grad,
        shard_in,
        shard_out,
        shard_ffin,
        shard_ffout,
        gain_total,
        head_total,
        rms_values,
    )


BLOCK = 216
PADDED = 224
WIDE = 2 * PADDED
MINE = 128
PART = 64
PAIR = 2 * MINE
VMEM_BYTES = 62 << 20
SQRT_2_OVER_PI = math.sqrt(2.0 / math.pi)
CUBIC = 0.044715
MESH = pl.DeviceIdType.MESH
LOW = jnp.bfloat16
F32 = jnp.float32


def spots():
    me = lax.axis_index("dp")
    return me, me // 8, me // 4 % 2, me // 2 % 2, me % 2


def at(z, y, x, c):
    return z * 8 + y * 4 + x * 2 + c


def z_peer(z, k):
    if k == 0:
        return z
    if k == 1:
        return z + 1 - 2 * (z % 2)
    if k == 2:
        return (z + 2) % 4
    return 3 - z


def greet(z, y, x, c):
    barrier = pltpu.get_barrier_semaphore()
    others = [at(z_peer(z, k), y, x, core) for k in (1, 2, 3) for core in (c, 1 - c)]
    others.append(at(z, y, x, 1 - c))
    for k in range(2):
        for there_y, there_x in ((1 - y, x), (y, 1 - x), (1 - y, 1 - x)):
            others.append(at(z_peer(z, k), there_y, there_x, c))
    for device in others:
        pl.semaphore_signal(barrier, inc=1, device_id=(device,), device_id_type=MESH)
    pl.semaphore_wait(barrier, len(others))


def nt(left, right):
    return lax.dot_general(left, right, (((1,), (1,)), ((), ())), preferred_element_type=F32)


def nn(left, right):
    return lax.dot_general(left, right, (((1,), (0,)), ((), ())), preferred_element_type=F32)


def tn(left, right):
    return lax.dot_general(left, right, (((0,), (0,)), ((), ())), preferred_element_type=F32)


def norm_back(values, gain, upstream):
    scale = lax.rsqrt(jnp.mean(values * values, -1, keepdims=True) + EPSILON)
    normed = values * scale
    gain_grad = jnp.sum(upstream * normed, 0, keepdims=True)
    inner = upstream * gain
    grad = scale * (inner - normed * jnp.mean(inner * normed, -1, keepdims=True))
    return grad, gain_grad


def added(left, right):
    return (left.astype(F32) + right.astype(F32)).astype(LOW)


def stream_of(ref):
    return ref[...].reshape(MINE, D).astype(F32)


class Net:
    def __init__(self, send_sems, recv_sems, anyone):
        self.send_sems, self.recv_sems, self.anyone = send_sems, recv_sems, anyone
        self.used, self.sent, self.maybe = 0, [], []

    def slots(self, count):
        first = self.used
        self.used += count
        return first

    def copy(self, src, dst, send_slot, recv_slot, device):
        return pltpu.make_async_remote_copy(
            src_ref=src,
            dst_ref=dst,
            send_sem=self.send_sems.at[send_slot],
            recv_sem=self.recv_sems.at[recv_slot],
            device_id=(device,),
            device_id_type=MESH,
        )

    def send(self, src, dst, slot, device):
        copy = self.copy(src, dst, slot, slot, device)
        copy.start()
        self.sent.append(copy)

    def move(self, stays, src, dst, send_slot, recv_slot, device):
        copy = self.copy(src, dst, send_slot, recv_slot, device)

        @pl.when(stays)
        def _():
            pltpu.make_async_copy(src, dst, self.recv_sems.at[recv_slot]).start()

        @pl.when(jnp.logical_not(stays))
        def _():
            copy.start()

        self.maybe.append((stays, copy))

    def got(self, block, slot):
        self.copy(block, block, slot, slot, self.anyone).wait_recv()

    def flush(self, gone):
        for copy in gone:
            copy.wait_send()
        names = {id(copy) for copy in gone}
        self.sent = [copy for copy in self.sent if id(copy) not in names]

    def drain(self):
        self.flush(list(self.sent))
        self.settle_moves()

    def settle_moves(self):
        for stays, copy in self.maybe:

            @pl.when(jnp.logical_not(stays))
            def _():
                copy.wait_send()

        self.maybe = []


def layer_kernel(*refs):
    (
        x_ref,
        seg_ref,
        valid_ref,
        ain,
        aout,
        gu,
        dn,
        gains,
        head_gains,
        cot,
        layer_out,
        input_grad,
        o_in,
        o_out,
        o_gu,
        o_dn,
        o_gains,
        o_heads,
        o_rms,
        all_in,
        all_out,
        all_gu,
        all_dn,
        allow,
        cosine,
        sine,
        weight,
        normed_in,
        proj,
        heads,
        probs,
        mixed,
        attn_proj,
        middle,
        rows,
        total,
        got_mid,
        got_up,
        hidden_t,
        slope_gate,
        slope_up,
        acc,
        keep,
        send_y,
        recv_y,
        send_z,
        recv_z,
        grad_middle,
        grad_attn,
        grad_heads,
        grad_proj,
        key_acc,
        d_in,
        a1,
        a2,
        a3,
        b1,
        b2,
        b3,
        g0,
        g1,
        g2,
        d_dn,
        n0,
        n1,
        n2,
        small,
        local,
        send_sems,
        recv_sems,
    ) = refs
    me, z, y, x, c = spots()
    xp, yp, cp = at(z, y, 1 - x, c), at(z, 1 - y, x, c), at(z, y, x, 1 - c)
    z_peers = [at(z_peer(z, k), y, x, c) for k in range(4)]
    net = Net(send_sems, recv_sems, cp)
    keep_in = pltpu.make_async_copy(ain, all_in.at[z, y, x, c], local.at[0])
    keep_out = pltpu.make_async_copy(aout, all_out.at[z, y, x, c], local.at[1])
    keep_in.start()
    keep_out.start()
    greet(z, y, x, c)

    class Spread:
        def __init__(self, own, full, x_first):
            self.own, self.full, self.x_first = own, full, x_first
            self.first, self.second = (xp, yp) if x_first else (yp, xp)
            self.az, self.ax, self.ay, self.ac = (net.slots(4) for _ in range(4))

        def block(self, k):
            return self.full.at[z_peer(z, k), y, x, c]

        def crossed(self, k):
            there = z_peer(z, k)
            return self.full.at[there, y, 1 - x, c] if self.x_first else self.full.at[there, 1 - y, x, c]

        def pair(self, there, own, core):
            if self.x_first:
                return self.full.at[there, y if own else 1 - y, :, core]
            return self.full.at[there, :, x if own else 1 - x, core]

        def start(self):
            net.send(self.own, self.block(0), self.az + 1, z_peers[1])
            net.send(self.own, self.block(0), self.ax, self.first)
            net.send(self.own, self.block(0), self.az + 2, z_peers[2])

        def hop(self, k):
            block = self.block(k)
            net.got(block, self.az + k)
            if k == 2:
                net.send(block, block, self.az + 3, z_peers[1])
            net.send(block, block, self.ax + k, self.first)

        def turn(self, k):
            net.got(self.crossed(k), self.ax + k)
            pair = self.pair(z_peer(z, k), True, c)
            net.send(pair, pair, self.ay + k, self.second)

        def near(self):
            part = self.pair(slice(None), True, c)
            net.send(part, part, self.ac, cp)

        def far(self):
            for k in range(4):
                net.got(self.pair(z_peer(z, k), False, c), self.ay + k)
            part = self.pair(slice(None), False, c)
            net.send(part, part, self.ac + 1, cp)

        def whole(self):
            net.got(self.pair(slice(None), True, 1 - c), self.ac)
            net.got(self.pair(slice(None), False, 1 - c), self.ac + 1)

    into, outof = Spread(ain, all_in, True), Spread(aout, all_out, False)
    into.start()
    w_one, w_two, w_c, w_d = net.slots(2), net.slots(2), net.slots(2), net.slots(2)
    v_x, v_one, v_c = net.slots(1), net.slots(2), net.slots(1)
    kind, goal = z // 2, 2 * (z % 2) + c
    blank = jnp.zeros((PADDED - BLOCK, D), F32)
    both_parts = gu[...].astype(F32)
    for h in range(2):
        part = both_parts[h * BLOCK : (h + 1) * BLOCK]
        g0[0, h] = jnp.concatenate([part, blank], 0).astype(LOW)
    n0[0] = jnp.concatenate([dn[...].astype(F32), blank], 0).astype(LOW)

    def rows_out():
        for h in range(2):
            net.move(
                jnp.logical_and(goal == z, c == h),
                g0.at[0, h],
                all_gu.at[kind, h, x],
                w_one + h,
                w_one + kind,
                at(goal, y, x, h),
            )

    def rows_on(which):
        t = (kind, 1 - kind)[which]
        block = all_gu.at[t, c, x]
        net.got(block, w_one + t)
        net.send(block, block, w_two + which, xp)
        net.send(block, block, w_c + which, cp)

    def rows_across(which):
        block = all_gu.at[(kind, 1 - kind)[which], c, 1 - x]
        net.got(block, w_two + which)
        net.send(block, block, w_d + which, cp)

    def rows_whole():
        for which in range(2):
            t = (kind, 1 - kind)[which]
            net.got(all_gu.at[t, 1 - c, x], w_c + which)
            net.got(all_gu.at[t, 1 - c, 1 - x], w_d + which)
        net.got(all_dn.at[1 - c], v_c)

    across_x = []

    def down_x():
        net.send(n0.at[0], n0.at[1], v_x, xp)
        across_x.append(net.sent[-1])


    def down_out():
        net.got(n0.at[1], v_x)
        for other in range(2):
            block_x = 1 - x if other else x
            net.move(
                jnp.logical_and(z % 2 == block_x, z % 2 == y),
                n0.at[other],
                all_dn.at[c, y],
                v_one + other,
                v_one + y,
                at(2 * (z // 2) + block_x, z % 2, x, c),
            )

    def down_on():
        for q in range(2):
            net.got(all_dn.at[c, q], v_one + q)
        net.send(all_dn.at[c], all_dn.at[c], v_c, cp)

    into.hop(1)
    into.hop(2)
    outof.start()
    keep_in.wait()
    keep_out.wait()
    into.turn(0)
    into.turn(1)
    into.hop(3)

    def along_lanes(ref):
        return jnp.concatenate([ref[0].astype(F32), ref[1].astype(F32)], 1)

    seg = jnp.broadcast_to(along_lanes(seg_ref), (MINE, MINE))
    valid = jnp.broadcast_to(along_lanes(valid_ref), (MINE, MINE))
    row = lax.broadcasted_iota(jnp.int32, (MINE, MINE), 0)
    col = lax.broadcasted_iota(jnp.int32, (MINE, MINE), 1)
    length = MINE // MICRO
    same = jnp.logical_and(seg == seg.T, row // length == col // length)
    position = jnp.sum(jnp.where(jnp.logical_and(same, col < row), 1.0, 0.0), -1, keepdims=True)
    usable = jnp.logical_or(valid > 0.0, row == col)
    allow[...] = jnp.where(
        jnp.logical_and(jnp.logical_and(same, col <= row), usable), 1.0, 0.0
    )
    weight[...] = valid.T
    freqs = jnp.exp(col.astype(F32) * (-2.0 * math.log(THETA) / HD))
    angles = position * freqs
    cosine[...] = jnp.cos(angles)
    sine[...] = jnp.sin(angles)
    stream = stream_of(x_ref)
    normed_in[...] = norm_rows(stream, gains[0:1, :]).astype(LOW)

    rows_out()
    down_x()
    into.turn(2)
    outof.hop(1)
    outof.hop(2)
    into.turn(3)
    into.near()
    outof.turn(0)
    outof.turn(1)
    outof.hop(3)
    into.far()
    outof.turn(2)
    outof.turn(3)
    outof.near()
    into.whole()

    down_out()
    flat_in = all_in.reshape(HEADS * HD + 2 * HD, D)
    flat_out = all_out.reshape(HEADS * HD, D)
    half = HD // 2

    def rows_of(j):
        return pl.ds(pl.multiple_of(j * HD, HD), HD)

    def project(j, carry):
        table = nt(normed_in[...], flat_in[rows_of(j), :])
        proj[j] = table

        @pl.when(j < HEADS + 1)
        def _():
            turned = norm_rows(table, head_gains[pl.ds(j // HEADS, 1), :])
            first, second = turned[:, :half], turned[:, half:]
            heads[j, :, :half] = (first * cosine[...] - second * sine[...]).astype(LOW)
            heads[j, :, half:] = (second * cosine[...] + first * sine[...]).astype(LOW)

        @pl.when(j == HEADS + 1)
        def _():
            heads[j] = table.astype(LOW)

        return carry

    lax.fori_loop(0, HEADS + 2, project, 0)
    outof.far()

    def attend_head(j, carry):
        seen = allow[...] > 0.0
        scores = nt(heads[j], heads[HEADS]) * SCALE_FACTOR
        masked = jnp.where(seen, scores, NEGATIVE)
        peak = jnp.max(masked, -1, keepdims=True)
        expo = jnp.where(seen, jnp.exp(masked - peak), 0.0)
        prob = expo / jnp.sum(expo, -1, keepdims=True)
        probs[j] = prob
        mixed[j] = nn(prob.astype(LOW), heads[HEADS + 1]).astype(LOW)
        return carry

    lax.fori_loop(0, HEADS, attend_head, 0)
    rows_on(0)
    outof.whole()

    attn_proj[...] = jnp.zeros((MINE, D), F32)

    def attn_out_head(j, carry):
        attn_proj[...] += nn(mixed[j], flat_out[rows_of(j), :])
        return carry

    lax.fori_loop(0, HEADS, attn_out_head, 0)
    branch = norm_rows(attn_proj[...], gains[1:2, :])
    mid = stream_of(x_ref) + branch
    middle[...] = mid
    rows[0] = norm_rows(mid, gains[2:3, :]).astype(LOW).reshape(2, PART, D)

    def counted(values):
        return jnp.sum(weight[:, 0:1] * jnp.sum(values * values, -1, keepdims=True))

    spot = lax.broadcasted_iota(jnp.int32, (1, D), 1)
    stats = jnp.where(spot == 4, jnp.sum(weight[:, 0:1]), 0.0)
    first_values = stream_of(x_ref)
    stats += jnp.where(spot == 0, counted(first_values), 0.0)
    stats += jnp.where(spot == 1, counted(mid), 0.0)
    stats += jnp.where(spot == 2, counted(branch), 0.0)
    small[0] = jnp.zeros((8, D), F32)
    small[0, 5:6, :] = stats

    zh, zl = z // 2, z % 2
    w_gu, w_dn = all_gu.reshape(2, 2, WIDE, D), all_dn.reshape(2, WIDE, D)

    class Half:
        def __init__(self, which, half, got_all, compute):
            self.which, self.half, self.got_all, self.compute = which, half, got_all, compute
            self.az, self.ay, self.ry, self.rz = (net.slots(4) for _ in range(4))
            self.gathered, self.here = [], set()

        def block(self, k, yy):
            there = z_peer(z, k)
            return self.got_all.at[self.half, there // 2, there % 2, yy]

        def pass_on(self, block, slot, device):
            net.send(block, block, slot, device)
            self.gathered.append(net.sent[-1])

        def start(self):
            own = rows.at[self.which, self.half]
            net.send(own, self.block(0, y), self.az + 1, z_peers[1])
            self.gathered.append(net.sent[-1])
            net.send(own, self.block(0, y), self.az + 2, z_peers[2])
            self.gathered.append(net.sent[-1])
            net.send(own, self.block(0, y), self.ay, yp)
            self.gathered.append(net.sent[-1])
            self.got_all[self.half, zh, zl, y] = rows[self.which, self.half]

        def hop(self, k):
            block = self.block(k, y)
            net.got(block, self.az + k)
            if k == 2:
                self.pass_on(block, self.az + 3, z_peers[1])
            self.pass_on(block, self.ay + k, yp)

        def arrive(self, g):
            if g not in self.here:
                for k in (2 * g, 2 * g + 1):
                    net.got(self.block(k, 1 - y), self.ay + k)
            self.here.add(g)

        def group(self, g):
            self.arrive(g)
            self.compute(self.half, zh if g == 0 else 1 - zh)
            keep[self.half, g] = acc[:, y]
            send_y[self.half, g] = acc[:, 1 - y].astype(LOW)
            net.send(send_y.at[self.half, g], recv_y.at[self.half, g], self.ry + g, yp)

        def fold(self, g):
            net.got(recv_y.at[self.half, g], self.ry + g)
            keep[self.half, g] += recv_y[self.half, g].astype(F32)
            send_z[self.half, g] = keep[self.half, g, 1 - zl].astype(LOW)
            net.send(send_z.at[self.half, g], recv_z.at[self.half, g], self.rz + g, z_peers[1])

        def cross(self):
            net.got(recv_z.at[self.half, 1], self.rz + 1)
            send_z[self.half, 2] = (
                keep[self.half, 1, zl] + recv_z[self.half, 1].astype(F32)
            ).astype(LOW)
            net.send(send_z.at[self.half, 2], recv_z.at[self.half, 2], self.rz + 2, z_peers[2])

        def done(self):
            net.got(recv_z.at[self.half, 0], self.rz)
            net.got(recv_z.at[self.half, 2], self.rz + 2)
            total[self.half] = (
                keep[self.half, 0, zl]
                + recv_z[self.half, 0].astype(F32)
                + recv_z[self.half, 2].astype(F32)
            )

    def columns(half, pair):
        return pl.ds(pl.multiple_of((half * 2 + pair) * PAIR, PAIR), PAIR)

    def put(h, part):
        part = part.reshape(2, 2, PART, D)

        @pl.when(h == 0)
        def _():
            acc[...] = part

        @pl.when(h == 1)
        def _():
            acc[...] += part

    def forward_pairs(half, pair):
        def one(h, carry):
            block = got_mid[half, pair].reshape(PAIR, D)
            gate = nt(block, w_gu[0, h])
            upward = nt(block, w_gu[1, h])
            square = gate * gate
            tanh = jnp.tanh(SQRT_2_OVER_PI * gate * (1.0 + CUBIC * square))
            side = 0.5 * (1.0 + tanh)
            gelu = gate * side
            slope = side + 0.5 * gate * (1.0 - tanh * tanh) * (
                SQRT_2_OVER_PI * (1.0 + 3.0 * CUBIC * square)
            )
            low = (gelu * upward).astype(LOW)
            slope_gate[h, half, pair] = (upward * slope).astype(LOW)
            slope_up[h, half, pair] = gelu.astype(LOW)
            put(h, nn(low, w_dn[h]))
            hidden_t[h, :, columns(half, pair)] = low.T
            return carry

        lax.fori_loop(0, 2, one, 0)

    def weights_here():
        net.settle_moves()
        net.flush(across_x)
        rows_across(1)
        rows_whole()

    def forward_end(half):
        span = pl.ds(half * PART, PART)
        ffw_proj = total[half]
        branch = norm_rows(ffw_proj, gains[3:4, :])
        layer_out[half, 0] = (middle[span, :] + branch).astype(LOW)
        counts = jnp.sum(weight[span, 0:1] * jnp.sum(branch * branch, -1, keepdims=True))
        small[0, 5:6, :] += jnp.where(spot == 3, counts, 0.0)
        grad, gain_grad = norm_back(ffw_proj, gains[3:4, :], cot[half, 0].astype(F32))
        small[0, 3:4, :] += gain_grad
        rows[1, half] = grad.astype(LOW)

    def backward_pairs(half, pair):
        def one(h, carry):
            block = got_up[half, pair].reshape(PAIR, D)
            back = nt(block, w_dn[h])
            gate = (back * slope_gate[h, half, pair].astype(F32)).astype(LOW)
            upward = (back * slope_up[h, half, pair].astype(F32)).astype(LOW)
            put(h, nn(gate, w_gu[0, h]) + nn(upward, w_gu[1, h]))
            slope_gate[h, half, pair] = gate
            slope_up[h, half, pair] = upward
            return carry

        lax.fori_loop(0, 2, one, 0)

    one, two = Half(0, 0, got_mid, forward_pairs), Half(0, 1, got_mid, forward_pairs)
    one.start()
    rows_on(1)
    rows_across(0)
    down_on()
    two.start()
    one.hop(1)
    two.hop(1)
    one.hop(2)
    two.hop(2)
    one.hop(3)
    two.hop(3)
    weights_here()
    one.group(0)
    one.group(1)
    two.group(0)
    one.fold(0)
    one.fold(1)
    two.group(1)
    one.cross()
    two.fold(0)
    one.done()
    forward_end(0)
    three, four = Half(1, 0, got_up, backward_pairs), Half(1, 1, got_up, backward_pairs)
    three.start()
    two.fold(1)
    three.hop(1)
    two.cross()
    three.hop(2)
    two.done()
    forward_end(1)
    four.start()
    net.flush([copy for copy in net.sent if not any(copy is other for other in three.gathered + four.gathered)])
    three.group(0)
    four.hop(1)
    three.hop(3)
    four.hop(2)
    three.group(1)
    three.fold(0)
    four.hop(3)
    four.group(0)
    three.fold(1)

    step = 384
    flat_mid, flat_up = got_mid.reshape(8 * MINE, D), got_up.reshape(8 * MINE, D)

    four.arrive(1)

    def down_grads(i, carry):
        h, cols = i // 3, pl.ds(pl.multiple_of(i % 3 * step, 128), step)
        d_dn.reshape(2, WIDE, D)[h, :, cols] = nn(hidden_t[h], flat_up[:, cols]).astype(LOW)
        return carry

    lax.fori_loop(0, 6, down_grads, 0)
    d_c, d_x, d_home, d_y = net.slots(5), net.slots(2), net.slots(2), net.slots(2)
    kept = (x + y + z) % 2
    net.send(d_dn.at[1 - c], n0, d_c, cp)
    four.group(1)
    three.cross()
    four.fold(0)

    def gate_up_grads(t, h, slopes):
        hidden_t[h] = slopes[h].reshape(8 * MINE, WIDE).T

        def part(i, carry):
            cols = pl.ds(pl.multiple_of(i * step, 128), step)
            w_gu[t, h, :, cols] = nn(hidden_t[h], flat_mid[:, cols]).astype(LOW)
            return carry

        lax.fori_loop(0, 3, part, 0)

    for h in range(2):
        gate_up_grads(0, h, slope_gate)
    net.send(all_gu.at[0, 1 - c], g0.at[0], d_c + 1, cp)
    net.got(n0, d_c)
    for q in range(2):
        d_dn[c, q] = added(d_dn[c, q], n0[q])
    net.send(d_dn.at[c, 1 - kept], n1, d_y, xp)
    four.fold(1)
    three.done()
    four.cross()
    for h in range(2):
        gate_up_grads(1, h, slope_up)
    net.send(all_gu.at[1, 1 - c], g0.at[1], d_c + 2, cp)

    def share(t):
        net.got(g0.at[t], d_c + 1 + t)
        for q in range(2):
            all_gu[t, c, q] = added(all_gu[t, c, q], g0[t, q])
        net.send(all_gu.at[t, c, 1 - x], g1.at[t], d_x + t, xp)

    def home_down():
        net.got(n1, d_y)
        d_dn[c, kept] = added(d_dn[c, kept], n1[...])
        net.move(
            jnp.logical_and(z % 2 == y, x == y),
            d_dn.at[c, kept],
            n2,
            d_y + 1,
            d_y + 1,
            at(2 * (z // 2) + y, kept, z % 2, c),
        )

    def home_gate_up(t):
        net.got(g1.at[t], d_x + t)
        all_gu[t, c, x] = added(all_gu[t, c, x], g1[t])
        source = z // 2 + 2 * t
        net.move(
            jnp.logical_and(source == z, z % 2 == c),
            all_gu.at[t, c, x],
            g2.at[c],
            d_home + t,
            d_home + c,
            at(source, y, x, z % 2),
        )

    share(0)
    share(1)
    four.done()

    home_down()
    mid = middle[...]
    grad, gain_grad = norm_back(mid, gains[2:3, :], total[...].reshape(MINE, D))
    small[0, 2:3, :] = gain_grad
    grad_mid = stream_of(cot) + grad
    grad_middle[...] = grad_mid
    grad, gain_grad = norm_back(attn_proj[...], gains[1:2, :], grad_mid)
    small[0, 1:2, :] = gain_grad
    grad_attn[...] = grad.astype(LOW)
    net.flush(three.gathered + four.gathered)
    d_out = got_up.reshape(4, 2, 2, 2, 32, D)
    a0 = got_mid.reshape(8 * MINE, D).at[pl.ds(0, 16 * 48)].reshape(4, 2, 2, 48, D)
    b0 = recv_y.reshape(4, 2, 2, 32, D)
    flat_d_out, flat_d_in = got_up.reshape(HEADS * HD, D), d_in.reshape(HEADS * HD + 2 * HD, D)

    def out_grads(j, carry):
        flat_d_out[rows_of(j), :] = tn(mixed[j], grad_attn[...]).astype(LOW)
        return carry

    lax.fori_loop(0, HEADS, out_grads, 0)
    net.send(d_out.at[:, :, :, 1 - c], b0, d_c + 3, cp)

    class Collect:
        def __init__(self, grads, core_in, y_in, x_in, z_in, core_slot, y_first):
            self.y_first = y_first
            self.grads, self.core_in, self.y_in, self.x_in, self.z_in = (
                grads,
                core_in,
                y_in,
                x_in,
                z_in,
            )
            self.cs, self.ys, self.xs, self.zs = core_slot, net.slots(2), net.slots(2), net.slots(2)

        def cores(self):
            net.got(self.core_in, self.cs)
            for part, pair in enumerate((1 - zh, zh)):

                def one(i, carry):
                    p, q, r = 2 * pair + i // 4, i // 2 % 2, i % 2
                    self.grads[p, q, r, c] = added(self.grads[p, q, r, c], self.core_in[p, q, r])
                    return carry

                lax.fori_loop(0, 8, one, 0)
                both = pl.ds(2 * pair, 2)
                if self.y_first:
                    away, device = self.grads.at[both, 1 - y, :, c], yp
                else:
                    away, device = self.grads.at[both, :, 1 - x, c], xp
                net.send(away, self.y_in.at[part], self.ys + part, device)

        def ys_in(self, part):
            pair = (1 - zh, zh)[part]
            net.got(self.y_in.at[part], self.ys + part)

            def one(i, carry):
                p, q = i // 2, i % 2
                there = 2 * pair + p
                if self.y_first:
                    self.grads[there, y, q, c] = added(
                        self.grads[there, y, q, c], self.y_in[part, p, q]
                    )
                else:
                    self.grads[there, q, x, c] = added(
                        self.grads[there, q, x, c], self.y_in[part, p, q]
                    )
                return carry

            lax.fori_loop(0, 4, one, 0)
            both = pl.ds(2 * pair, 2)
            if self.y_first:
                away, device = self.grads.at[both, y, 1 - x, c], xp
            else:
                away, device = self.grads.at[both, 1 - y, x, c], yp
            net.send(away, self.x_in.at[part], self.xs + part, device)

        def xs_in(self, part):
            pair = (1 - zh, zh)[part]
            net.got(self.x_in.at[part], self.xs + part)
            for p in range(2):
                there = 2 * pair + p
                self.grads[there, y, x, c] = added(
                    self.grads[there, y, x, c], self.x_in[part, p]
                )
            net.send(
                self.grads.at[2 * pair + 1 - zl, y, x, c],
                self.z_in.at[part],
                self.zs + part,
                z_peers[1],
            )

        def cross(self, slot):
            net.got(self.z_in.at[0], self.zs)
            there = 2 * (1 - zh) + zl
            self.grads[there, y, x, c] = added(self.grads[there, y, x, c], self.z_in[0])
            net.send(self.grads.at[there, y, x, c], self.z_in.at[2], slot, z_peers[2])

        def done(self, slot, result):
            net.got(self.z_in.at[1], self.zs + 1)
            net.got(self.z_in.at[2], slot)
            result[...] = (
                self.grads[z, y, x, c].astype(F32)
                + self.z_in[1].astype(F32)
                + self.z_in[2].astype(F32)
            )

    r_s, r_z = net.slots(8), net.slots(2)
    outs = Collect(d_out, b0, b1, b2, b3, d_c + 3, True)
    ins = Collect(d_in, a0, a1, a2, a3, d_c + 4, True)

    grad_heads[...] = jnp.zeros((6, MINE, HD), F32)

    def head_back(j, carry):
        up = nt(grad_attn[...], flat_out[rows_of(j), :]).astype(LOW)
        prob = probs[j]
        grad_prob = nt(up, heads[HEADS + 1])
        grad_heads[HEADS + 1] += tn(prob.astype(LOW), up)
        center = jnp.sum(grad_prob * prob, -1, keepdims=True)
        grad_score = (prob * (grad_prob - center)).astype(LOW)
        grad_heads[j] = nn(grad_score, heads[HEADS]) * SCALE_FACTOR
        grad_heads[HEADS] += tn(grad_score, heads[j]) * SCALE_FACTOR
        return carry

    outs.cores()
    lax.fori_loop(0, HEADS, head_back, 0)
    key_acc[...] = jnp.zeros((2, HD), F32)

    def turn_back(j, carry):
        first, second = grad_heads[j, :, :half], grad_heads[j, :, half:]
        turned = jnp.concatenate(
            [
                first * cosine[...] + second * sine[...],
                second * cosine[...] - first * sine[...],
            ],
            -1,
        )
        which = pl.ds(j // HEADS, 1)
        grad, gain_grad = norm_back(proj[j], head_gains[which, :], turned)
        key_acc[which, :] += gain_grad
        grad_proj[j] = grad.astype(LOW)
        return carry

    lax.fori_loop(0, HEADS + 1, turn_back, 0)
    grad_proj[HEADS + 1] = grad_heads[HEADS + 1].astype(LOW)
    small[0, 4:5, 0:HD] = key_acc[0:1, :]
    small[0, 4:5, HD : 2 * HD] = key_acc[1:2, :]


    def in_grads(j, carry):
        flat_d_in[rows_of(j), :] = tn(grad_proj[j], normed_in[...]).astype(LOW)
        return carry

    lax.fori_loop(0, HEADS + 2, in_grads, 0)
    net.send(d_in.at[:, :, :, 1 - c], a0, d_c + 4, cp)
    total[...] = jnp.zeros((2, PART, D), F32)

    def in_back(j, carry):
        total[...] += nn(grad_proj[j], flat_in[rows_of(j), :]).reshape(2, PART, D)
        return carry

    home_gate_up(0)
    lax.fori_loop(0, HEADS + 2, in_back, 0)
    ins.cores()
    grad, gain_grad = norm_back(stream_of(x_ref), gains[0:1, :], total[...].reshape(MINE, D))
    small[0, 0:1, :] = gain_grad
    input_grad[...] = (grad_middle[...] + grad).reshape(2, 1, PART, D)
    net.send(small.at[0], small.at[1], r_s, cp)
    home_gate_up(1)
    outs.ys_in(0)
    outs.ys_in(1)
    net.got(small.at[1], r_s)
    small[2] = small[0] + small[1]
    net.send(small.at[2], small.at[3], r_s + 1, xp)
    ins.ys_in(0)
    outs.xs_in(0)
    outs.xs_in(1)
    net.got(small.at[3], r_s + 1)
    small[4] = small[2] + small[3]
    net.send(small.at[4], small.at[5], r_s + 2, yp)
    ins.ys_in(1)
    outs.cross(r_z)
    ins.xs_in(0)
    ins.xs_in(1)
    net.got(small.at[5], r_s + 2)
    small[6] = small[4] + small[5]
    for k in (1, 2, 3):
        net.send(small.at[6], small.at[6 + k], r_s + 2 + k, z_peers[k])
    ins.cross(r_z + 1)
    outs.done(r_z, o_out)
    net.got(n2, d_y + 1)
    o_dn[...] = n2[...].astype(F32)[:BLOCK]
    for k in (1, 2, 3):
        net.got(small.at[6 + k], r_s + 2 + k)
    sums = (small[6] + small[7]) + (small[8] + small[9])
    o_gains[...] = sums[0:4, :]
    o_heads[...] = jnp.concatenate([sums[4:5, 0:HD], sums[4:5, HD : 2 * HD]], 0)
    scaled = sums[5:6, :]
    tokens = jnp.sum(jnp.where(spot == 4, scaled, 0.0), -1, keepdims=True)
    means = jnp.sqrt(scaled / (tokens * D))
    for i in range(4):
        o_rms[i] = jnp.sum(jnp.where(spot == i, means, 0.0))
    ins.done(r_z + 1, o_in)
    for h in range(2):
        net.got(g2.at[h], d_home + h)
        o_gu[pl.ds(h * BLOCK, BLOCK), :] = g2[h].astype(F32)[:BLOCK]
    net.drain()


def vm(*shape):
    return pltpu.VMEM(shape, LOW)


def vf(*shape):
    return pltpu.VMEM(shape, F32)


def whole_layer(x, seg, valid, ain, aout, gu, dn, gains, head_gains, cot):
    vmem = pl.BlockSpec(memory_space=pltpu.VMEM)
    scratch = [
        vm(4, 2, 2, 2, 48, D),
        vm(4, 2, 2, 2, 32, D),
        vm(2, 2, 2, PADDED, D),
        vm(2, 2, PADDED, D),
        vf(MINE, MINE),
        vf(MINE, MINE),
        vf(MINE, MINE),
        vf(MINE, MINE),
        vm(MINE, D),
        vf(6, MINE, HD),
        vm(6, MINE, HD),
        vf(4, MINE, MINE),
        vm(4, MINE, HD),
        vf(MINE, D),
        vf(MINE, D),
        vm(2, 2, PART, D),
        vf(2, PART, D),
        vm(2, 2, 2, 2, PART, D),
        vm(2, 2, 2, 2, PART, D),
        vm(2, WIDE, 8 * MINE),
        vm(2, 2, 2, PAIR, WIDE),
        vm(2, 2, 2, PAIR, WIDE),
        vf(2, 2, PART, D),
        vf(2, 2, 2, PART, D),
        vm(2, 2, 2, PART, D),
        vm(2, 2, 2, PART, D),
        vm(2, 3, PART, D),
        vm(2, 3, PART, D),
        vf(MINE, D),
        vm(MINE, D),
        vf(6, MINE, HD),
        vm(6, MINE, HD),
        vf(2, HD),
        vm(4, 2, 2, 2, 48, D),
    ]
    for count in (48, 32):
        scratch += [vm(2, 2, 2, count, D), vm(2, 2, count, D), vm(3, count, D)]
    scratch += [vm(2, 2, PADDED, D), vm(2, PADDED, D), vm(2, PADDED, D)]
    scratch += [vm(2, 2, PADDED, D), vm(2, PADDED, D), vm(PADDED, D), vm(PADDED, D)]
    scratch += [vf(10, 8, D)]
    scratch += [pltpu.SemaphoreType.DMA((2,))] + [pltpu.SemaphoreType.DMA((144,))] * 2
    return pl.pallas_call(
        layer_kernel,
        out_shape=(
            jax.ShapeDtypeStruct((2, 1, PART, D), LOW),
            jax.ShapeDtypeStruct((2, 1, PART, D), F32),
            jax.ShapeDtypeStruct((48, D), F32),
            jax.ShapeDtypeStruct((32, D), F32),
            jax.ShapeDtypeStruct((2 * BLOCK, D), F32),
            jax.ShapeDtypeStruct((BLOCK, D), F32),
            jax.ShapeDtypeStruct((4, D), F32),
            jax.ShapeDtypeStruct((2, HD), F32),
            jax.ShapeDtypeStruct((4,), F32),
        ),
        in_specs=[vmem] * 10,
        out_specs=(vmem,) * 8 + (pl.BlockSpec(memory_space=pltpu.SMEM),),
        scratch_shapes=scratch,
        compiler_params=pltpu.CompilerParams(
            collective_id=1, has_side_effects=True, vmem_limit_bytes=VMEM_BYTES
        ),
        name="layer",
    )(x, seg, valid, ain, aout, gu, dn, gains, head_gains, cot)


def copy_kernel(*refs):
    count = (len(refs) - 2) // 3
    given, made, held = refs[:count], refs[count : 2 * count], refs[2 * count : 3 * count]
    into = [pltpu.make_async_copy(a, b, refs[-2].at[i]) for i, (a, b) in enumerate(zip(given, held))]
    out = [pltpu.make_async_copy(a, b, refs[-1].at[i]) for i, (a, b) in enumerate(zip(held, made))]
    for copy in into:
        copy.start()
    for first, second in zip(into, out):
        first.wait()
        second.start()
    for copy in out:
        copy.wait()


def copied(arrays):
    place = pl.BlockSpec(memory_space=pl.ANY)
    return pl.pallas_call(
        copy_kernel,
        out_shape=tuple(jax.ShapeDtypeStruct(array.shape, array.dtype) for array in arrays),
        in_specs=[place] * len(arrays),
        out_specs=(place,) * len(arrays),
        scratch_shapes=[pltpu.VMEM(array.shape, array.dtype) for array in arrays]
        + [pltpu.SemaphoreType.DMA((len(arrays),))] * 2,
        name="results",
    )(*arrays)


def split_shards(
    inputs,
    segment_ids,
    valid_mask,
    attn_in,
    attn_out,
    ffw_in,
    ffw_out,
    norm_gains,
    head_gains,
    cotangent,
):
    results = whole_layer(
        inputs,
        segment_ids,
        valid_mask,
        attn_in,
        attn_out,
        ffw_in,
        ffw_out,
        norm_gains,
        head_gains,
        cotangent,
    )
    return copied(results[:-1]) + results[-1:]


def solution(mesh):
    placed = (
        P(None, "dp", None, None),
        P(None, "dp", None),
        P(None, "dp", None),
        P("dp", None),
        P("dp", None),
        P("dp", None),
        P("dp", None),
        P(),
        P(),
        P(None, "dp", None, None),
    )
    return jax.shard_map(
        split_shards if mesh.shape["dp"] == 32 else general_shards,
        mesh=mesh,
        in_specs=placed,
        out_specs=(
            P(None, "dp", None, None),
            P(None, "dp", None, None),
            P("dp", None),
            P("dp", None),
            P("dp", None),
            P("dp", None),
            P(),
            P(),
            P(),
        ),
        check_vma=False,
    )
```
